32 devices in a mesh: dp: 2 (over y), ctx: 16 (over z, x, core).
Axes of the slice: x: 2, y: 2, z: 4, core: 2. Of those that a mesh axis runs over, the one named last changes fastest.
Arguments:
- query_in: bfloat16 [2, 2048, 1792], P('dp', 'ctx'), may hold values from -8 to 8
- key_in: bfloat16 [2, 2048, 256], P('dp', 'ctx'), may hold values from -4 to 4
- value_input: bfloat16 [2, 2048, 256], P('dp', 'ctx'), may hold values from -4 to 4
- output_gradient: bfloat16 [2, 2048, 1792], P('dp', 'ctx'), may hold values from -5 to 5
- doc_ids: int32 [2, 2048], P('dp', 'ctx'), may hold values from 0 to 1, as said below
- query_bias: float32 [1792], replicated, may hold values from -2 to 2
Outputs:
- attended: bfloat16 [2, 2048, 1792], P('dp', 'ctx')
- grad_query: bfloat16 [2, 2048, 1792], P('dp', 'ctx')
- key_gradient: bfloat16 [2, 2048, 256], P('dp', 'ctx')
- value_gradient: bfloat16 [2, 2048, 256], P('dp', 'ctx')
- grad_bias: float32 [1792], replicated
The draws below stay inside these ranges and needn't reach their ends.
Inputs may be any that keep to these rules, and one draw needn't show every extreme that they name: `doc_ids`: ids never fall along a sequence; each of the 2 documents of a sequence holds 512 to 1536 tokens, and together they fill all 2048 tokens.
All inputs are finite; a program needn't handle non-finite values.
Results may differ from the reference program's by a relative error of at most 0.019.
Values may be sent and summed in bfloat16 or wider, within the bound.
No kernel may reach another device: no remote copies, remote signals or barrier semaphores. Data moves between devices by JAX's collectives and lax.ppermute only.
A program may use at most 64 MiB of HBM per device.

```python
import math
import jax
import jax.numpy as jnp
from jax import lax

QUERY_HEADS = 14
KEY_VALUE_HEADS = 2
HEAD_SIZE = 128
GROUP_SIZE = 7
BLK = 128
WB = 16
SEQUENCE_LENGTH = 2048
BATCH_COUNT = 2
DOC_MOST = 1536


def draw_query_in(key, part):
    value_rows = jnp.clip(jax.random.normal(jax.random.fold_in(key, 23), (BATCH_COUNT, SEQUENCE_LENGTH, QUERY_HEADS * HEAD_SIZE), jnp.float32), -4.0, 4.0)
    return value_rows.astype(jnp.bfloat16)


def draw_key_in(key, part):
    value_rows = jnp.clip(jax.random.normal(jax.random.fold_in(key, 33), (BATCH_COUNT, SEQUENCE_LENGTH, KEY_VALUE_HEADS * HEAD_SIZE), jnp.float32), -4.0, 4.0)
    return value_rows.astype(jnp.bfloat16)


def draw_doc_ids(key, part):
    first_length = jax.random.randint(jax.random.fold_in(key, 4471), (BATCH_COUNT, 1), SEQUENCE_LENGTH - DOC_MOST, DOC_MOST + 1)
    positions = jnp.arange(SEQUENCE_LENGTH, dtype=jnp.int32)[None, :]
    return (positions >= first_length).astype(jnp.int32)


def shard_levels(stream_key, shape, split, low, top_value):
    level = 1.0
    for axis_at, blocks in split:
        heights = jax.random.uniform(jax.random.fold_in(jax.random.fold_in(stream_key, 6), axis_at), (blocks,), jnp.float32, low / len(split), top_value / len(split))
        level = level * jnp.repeat(jnp.exp(heights), shape[axis_at] // blocks).reshape((-1,) + (1,) * (len(shape) - 1 - axis_at))
    return level


def scatter_about(stream_key, shape, width, bound, pieces=(), kind=jnp.bfloat16):
    gain = shard_levels(stream_key, shape, pieces, -0.22, 0.18) if pieces else 1.0
    entries = jax.random.normal(stream_key, shape, jnp.float32) * width * gain
    return jnp.minimum(jnp.maximum(entries, -bound), bound).astype(kind)


def setup_inputs(seed: int = 0) -> dict:
    key_of = jax.random.split(jax.random.key(seed), 7)
    return {
        "query_in": draw_query_in(jax.random.fold_in(key_of[6], 71), 0),
        "key_in": draw_key_in(jax.random.fold_in(key_of[6], 71), 0),
        "value_input": scatter_about(key_of[2], (BATCH_COUNT, SEQUENCE_LENGTH, KEY_VALUE_HEADS * HEAD_SIZE), 1.0, 4.0, ((0, 2), (1, 16))),
        "output_gradient": scatter_about(key_of[3], (BATCH_COUNT, SEQUENCE_LENGTH, QUERY_HEADS * HEAD_SIZE), 1.0, 5.0, ((0, 2), (1, 16))),
        "doc_ids": draw_doc_ids(jax.random.fold_in(key_of[6], 71), 0),
        "query_bias": scatter_about(key_of[5], (QUERY_HEADS * HEAD_SIZE,), 0.5, 2.0, (), jnp.float32),
    }


def reference(query_in, key_in, value_input, output_gradient, doc_ids, query_bias):
    score_scale = 1.0 / math.sqrt(HEAD_SIZE)
    padding_rows = (WB - 1) * BLK
    block_count = SEQUENCE_LENGTH // BLK

    def one_sequence(inputs):
        query_seq, key_sequence, value_sequence, gradient_sequence, docs_seq = inputs
        rounded_length = lax.optimization_barrier((query_seq.astype(jnp.float32) + query_bias).astype(jnp.bfloat16))
        query_rows = rounded_length.astype(jnp.float32).reshape(SEQUENCE_LENGTH, KEY_VALUE_HEADS, GROUP_SIZE, HEAD_SIZE)
        padded_keys = jnp.pad(key_sequence.astype(jnp.float32).reshape(SEQUENCE_LENGTH, KEY_VALUE_HEADS, HEAD_SIZE), ((padding_rows, 0), (0, 0), (0, 0)))
        padded_values = jnp.pad(value_sequence.astype(jnp.float32).reshape(SEQUENCE_LENGTH, KEY_VALUE_HEADS, HEAD_SIZE), ((padding_rows, 0), (0, 0), (0, 0)))
        gradient_list = gradient_sequence.astype(jnp.float32).reshape(SEQUENCE_LENGTH, KEY_VALUE_HEADS, GROUP_SIZE, HEAD_SIZE)
        docs_padded = jnp.pad(docs_seq, (padding_rows, 0), constant_values=-1)

        def block_step(running, block_index):
            key_accumulator, value_accumulator = running
            start = (block_index * BLK).astype(jnp.int32)
            query_block = lax.dynamic_slice_in_dim(query_rows, start, BLK, 0)
            grad_block = lax.dynamic_slice_in_dim(gradient_list, start, BLK, 0)
            query_docs = lax.dynamic_slice_in_dim(docs_seq, start, BLK, 0)
            key_block = lax.dynamic_slice_in_dim(padded_keys, start, WB * BLK, 0)
            value_block = lax.dynamic_slice_in_dim(padded_values, start, WB * BLK, 0)
            key_docs = lax.dynamic_slice_in_dim(docs_padded, start, WB * BLK, 0)
            query_pos = start + jnp.arange(BLK, dtype=jnp.int32)
            key_pos = start - padding_rows + jnp.arange(WB * BLK, dtype=jnp.int32)
            allowed = (key_pos[None, :] >= 0) & (key_pos[None, :] <= query_pos[:, None])
            allowed = allowed & (query_pos[:, None] // BLK - key_pos[None, :] // BLK < WB)
            allowed = allowed & (query_docs[:, None] == key_docs[None, :])
            scores = jnp.einsum('qgnd,kgd->gnqk', query_block, key_block) * score_scale
            scores = jnp.where(allowed[None, None], scores, -jnp.inf)
            row_max = lax.optimization_barrier(jnp.max(scores, axis=-1, keepdims=True))
            log_total = row_max + jnp.log(lax.optimization_barrier(jnp.sum(jnp.exp(scores - row_max), axis=-1, keepdims=True)))
            attend = jnp.exp(scores - log_total)
            attended = jnp.einsum('gnqk,kgd->qgnd', attend, value_block).astype(jnp.bfloat16)
            row_dot = jnp.einsum('qgnd,qgnd->gnq', grad_block, attended.astype(jnp.float32))
            grad_prob = jnp.einsum('qgnd,kgd->gnqk', grad_block, value_block)
            grad_score = lax.optimization_barrier((attend * (grad_prob - row_dot[..., None])).astype(jnp.bfloat16)).astype(jnp.float32)
            query_grad = jnp.einsum('gnqk,kgd->qgnd', grad_score, key_block) * score_scale
            key_grad = jnp.einsum('gnqk,qgnd->kgd', grad_score, query_block) * score_scale
            weight_bf = lax.optimization_barrier(attend.astype(jnp.bfloat16)).astype(jnp.float32)
            value_grad = jnp.einsum('gnqk,qgnd->kgd', weight_bf, grad_block)
            key_accumulator = lax.dynamic_update_slice_in_dim(key_accumulator, lax.dynamic_slice_in_dim(key_accumulator, start, WB * BLK, 0) + key_grad, start, 0)
            value_accumulator = lax.dynamic_update_slice_in_dim(value_accumulator, lax.dynamic_slice_in_dim(value_accumulator, start, WB * BLK, 0) + value_grad, start, 0)
            return ((key_accumulator, value_accumulator), (attended, query_grad))
        zero_filled = jnp.zeros((padding_rows + SEQUENCE_LENGTH, KEY_VALUE_HEADS, HEAD_SIZE), jnp.float32)
        (key_accumulator, value_accumulator), (attended_blocks, query_blocks) = lax.scan(block_step, (zero_filled, zero_filled), jnp.arange(block_count, dtype=jnp.int32))
        attended = attended_blocks.reshape(SEQUENCE_LENGTH, QUERY_HEADS * HEAD_SIZE)
        query_grad = query_blocks.reshape(SEQUENCE_LENGTH, QUERY_HEADS * HEAD_SIZE)
        key_gradient = key_accumulator[padding_rows:].reshape(SEQUENCE_LENGTH, KEY_VALUE_HEADS * HEAD_SIZE).astype(jnp.bfloat16)
        value_gradient = value_accumulator[padding_rows:].reshape(SEQUENCE_LENGTH, KEY_VALUE_HEADS * HEAD_SIZE).astype(jnp.bfloat16)
        return (attended, query_grad.astype(jnp.bfloat16), key_gradient, value_gradient, lax.optimization_barrier(jnp.sum(query_grad, axis=0)))
    results = lax.map(one_sequence, (query_in, key_in, value_input, output_gradient, doc_ids))
    grad_bias = lax.optimization_barrier(jnp.sum(results[4], axis=0))
    return (results[0], results[1], results[2], results[3], grad_bias)
```

```python
import functools
import math

import jax
import jax.numpy as jnp
from jax import lax
from jax.experimental import pallas as pl
from jax.experimental.pallas import tpu as pltpu
from jax.sharding import PartitionSpec as P

QUERY_HEADS = 14
KEY_VALUE_HEADS = 2
HEAD_SIZE = 128
GROUP_SIZE = 7
BLK = 128
WB = 16
DOC_ROWS = 16
PAIR = 2
SCALE = 1.0 / math.sqrt(HEAD_SIZE)
SCALE_LOG2 = SCALE * math.log2(math.e)
LOW = -1e30

NT = (((1,), (1,)), ((), ()))


def fold(value, op):
    keys, lanes = value.shape
    return op(value.reshape(keys // 8, 8, lanes), axis=0)


def kernel(
    rank_ref, q_ref, bias_ref, do_ref, kv_ref,
    att_ref, dq_ref, part_ref, gb_ref,
    q_st, do_t, do_st, s_buf, p_buf, m_buf, l_buf, acc, dq_acc,
):
    rows = q_ref.shape[0]
    chunk = PAIR * rows
    lanes = GROUP_SIZE * rows
    tiles = [(at, min(at + chunk, lanes)) for at in range(0, lanes, chunk)]
    rank = rank_ref[0]
    counts = kv_ref[:, rows:rows + DOC_ROWS, 0:128].astype(jnp.float32)
    boundary = jnp.sum(counts) * (1.0 / (DOC_ROWS * 128))
    boundary = (boundary + 0.5).astype(jnp.int32)
    q_first = rank * rows
    q_last = q_first + rows - 1
    low_block = jnp.maximum(rank - (WB - 1), 0)
    low_block = jnp.where(q_first >= boundary, jnp.maximum(low_block, boundary // rows), low_block)
    low = low_block // PAIR
    high = rank // PAIR + 1

    part_ref[...] = jnp.zeros_like(part_ref)

    def keys_of(c, column):
        return jnp.concatenate(
            [kv_ref[PAIR * c + i, 0:rows, column:column + HEAD_SIZE] for i in range(PAIR)], axis=0
        )

    for g in range(KEY_VALUE_HEADS):
        for n in range(GROUP_SIZE):
            columns = slice((g * GROUP_SIZE + n) * HEAD_SIZE, (g * GROUP_SIZE + n + 1) * HEAD_SIZE)
            at = slice(n * rows, (n + 1) * rows)
            q_st[at, :] = (q_ref[:, columns].astype(jnp.float32) + bias_ref[:, columns]).astype(
                jnp.bfloat16
            )
            do_t[:, at] = do_ref[:, columns].astype(jnp.float32).T
        m_buf[...] = jnp.full_like(m_buf, LOW)
        l_buf[...] = jnp.zeros_like(l_buf)
        acc[...] = jnp.zeros_like(acc)
        dq_acc[...] = jnp.zeros_like(dq_acc)

        @pl.loop(low, high)
        def _(c):
            key_first = c * chunk
            k_c = keys_of(c, g * HEAD_SIZE)
            clear = (key_first + chunk <= q_first) & (rank - PAIR * c < WB)
            clear = clear & ((boundary <= key_first) | (boundary > q_last))

            def scores(masked):
                if masked:
                    key_pos = key_first + lax.broadcasted_iota(jnp.int32, (chunk, rows), 0)
                    query_pos = q_first + lax.broadcasted_iota(jnp.int32, (chunk, rows), 1)
                    allowed = (key_pos <= query_pos) & (query_pos // BLK - key_pos // BLK < WB)
                    allowed = allowed & ((key_pos >= boundary) == (query_pos >= boundary))
                    bias = jnp.where(allowed, 0.0, LOW)
                for a, b in tiles:
                    s = lax.dot_general(
                        k_c, q_st[a:b, :], NT, preferred_element_type=jnp.float32
                    )
                    if masked:
                        s = s + jnp.concatenate([bias] * ((b - a) // rows), axis=1)
                    s_buf[c - low, :, a:b] = s
                    m_buf[:, a:b] = jnp.maximum(m_buf[:, a:b], fold(s, jnp.max))

            @pl.when(clear)
            def _():
                scores(False)

            @pl.when(jnp.logical_not(clear))
            def _():
                scores(True)

        row_max = jnp.max(m_buf[...], axis=0, keepdims=True) * SCALE_LOG2

        @pl.loop(low, high)
        def _(c):
            v_t = keys_of(c, (KEY_VALUE_HEADS + g) * HEAD_SIZE).T
            for a, b in tiles:
                p = jnp.exp2(s_buf[c - low, :, a:b] * SCALE_LOG2 - row_max[:, a:b])
                l_buf[:, a:b] += fold(p, jnp.sum)
                p_bf = p.astype(jnp.bfloat16)
                p_buf[c - low, :, a:b] = p_bf
                acc[:, a:b] += jnp.dot(v_t, p_bf, preferred_element_type=jnp.float32)

        inverse = 1.0 / jnp.sum(l_buf[...], axis=0, keepdims=True)
        for n in range(GROUP_SIZE):
            columns = slice((g * GROUP_SIZE + n) * HEAD_SIZE, (g * GROUP_SIZE + n + 1) * HEAD_SIZE)
            at = slice(n * rows, (n + 1) * rows)
            att = (acc[:, at] * inverse[:, at]).T.astype(jnp.bfloat16)
            att_ref[:, columns] = att
            do_n = do_t[:, at]
            dot_n = jnp.sum(do_n * att.astype(jnp.float32).T, axis=0, keepdims=True)
            m_buf[0:1, at] = dot_n * inverse[:, at]
            do_n = do_n * inverse[:, at]
            do_t[:, at] = do_n
            do_st[at, :] = do_n.T.astype(jnp.bfloat16)
        row_dot = m_buf[0:1, :]

        @pl.loop(low, high)
        def _(c):
            k_c = keys_of(c, g * HEAD_SIZE)
            v_c = keys_of(c, (KEY_VALUE_HEADS + g) * HEAD_SIZE)
            k_t = k_c.T
            d_key = jnp.zeros((chunk, HEAD_SIZE), jnp.float32)
            d_value = jnp.zeros((chunk, HEAD_SIZE), jnp.float32)
            for a, b in tiles:
                p_bf = p_buf[c - low, :, a:b]
                d_p = jnp.dot(
                    v_c, do_t[:, a:b].astype(jnp.bfloat16), preferred_element_type=jnp.float32
                )
                d_s = (p_bf.astype(jnp.float32) * (d_p - row_dot[:, a:b])).astype(jnp.bfloat16)
                d_value = d_value + jnp.dot(p_bf, do_st[a:b, :], preferred_element_type=jnp.float32)
                d_key = d_key + jnp.dot(d_s, q_st[a:b, :], preferred_element_type=jnp.float32)
                dq_acc[:, a:b] += jnp.dot(k_t, d_s, preferred_element_type=jnp.float32)
            at = pl.ds(pl.multiple_of(c * chunk, chunk), chunk)
            key_columns = slice(g * HEAD_SIZE, (g + 1) * HEAD_SIZE)
            value_columns = slice((KEY_VALUE_HEADS + g) * HEAD_SIZE, (KEY_VALUE_HEADS + g + 1) * HEAD_SIZE)
            part_ref[at, key_columns] = (d_key * SCALE).astype(part_ref.dtype)
            part_ref[at, value_columns] = d_value.astype(part_ref.dtype)

        for n in range(GROUP_SIZE):
            columns = slice((g * GROUP_SIZE + n) * HEAD_SIZE, (g * GROUP_SIZE + n + 1) * HEAD_SIZE)
            d_q = (dq_acc[:, n * rows:(n + 1) * rows] * SCALE).T
            gb_ref[:, columns] = jnp.sum(d_q, axis=0, keepdims=True)
            dq_ref[:, columns] = d_q.astype(jnp.bfloat16)


def attention(rank, query_in, query_bias, output_gradient, kv_all):
    rows, width = query_in.shape
    shards = kv_all.shape[0]
    lanes = GROUP_SIZE * rows
    chunk = PAIR * rows
    slots = min(shards // PAIR, WB // PAIR + 1)
    vmem = pl.BlockSpec(memory_space=pltpu.VMEM)
    return pl.pallas_call(
        kernel,
        out_shape=(
            jax.ShapeDtypeStruct((rows, width), jnp.bfloat16),
            jax.ShapeDtypeStruct((rows, width), jnp.bfloat16),
            jax.ShapeDtypeStruct((shards * rows, 2 * KEY_VALUE_HEADS * HEAD_SIZE), jnp.bfloat16),
            jax.ShapeDtypeStruct((1, width), jnp.float32),
        ),
        in_specs=[pl.BlockSpec(memory_space=pltpu.SMEM)] + [vmem] * 4,
        out_specs=(vmem,) * 4,
        scratch_shapes=[
            pltpu.VMEM((lanes, HEAD_SIZE), jnp.bfloat16),
            pltpu.VMEM((HEAD_SIZE, lanes), jnp.float32),
            pltpu.VMEM((lanes, HEAD_SIZE), jnp.bfloat16),
            pltpu.VMEM((slots, chunk, lanes), jnp.float32),
            pltpu.VMEM((slots, chunk, lanes), jnp.bfloat16),
            pltpu.VMEM((8, lanes), jnp.float32),
            pltpu.VMEM((8, lanes), jnp.float32),
            pltpu.VMEM((HEAD_SIZE, lanes), jnp.float32),
            pltpu.VMEM((HEAD_SIZE, lanes), jnp.float32),
        ],
        compiler_params=pltpu.CompilerParams(vmem_limit_bytes=56 * 1024 * 1024),
        name="attention",
    )(rank, query_in, query_bias, output_gradient, kv_all)


def local(query_in, key_in, value_input, output_gradient, doc_ids, query_bias):
    rows = query_in.shape[1]
    rank = lax.axis_index("ctx")
    count = jnp.sum((doc_ids[0] == 0).astype(jnp.float32)).astype(jnp.bfloat16)
    packed = jnp.concatenate([key_in[0], value_input[0]], axis=1)
    packed = jnp.concatenate(
        [packed, jnp.broadcast_to(count, (DOC_ROWS, packed.shape[1]))], axis=0
    )
    kv_all = lax.all_gather(packed, "ctx", axis=0, tiled=False)
    attended, grad_query, partials, bias_part = attention(
        rank.astype(jnp.int32).reshape(1), query_in[0], query_bias[None], output_gradient[0], kv_all
    )
    grad_bias = jnp.sum(lax.all_gather(bias_part[0], ("dp", "ctx"), axis=0, tiled=False), axis=0)
    summed = lax.psum_scatter(partials, "ctx", scatter_dimension=0, tiled=True)
    half = KEY_VALUE_HEADS * HEAD_SIZE
    return (
        attended[None],
        grad_query[None],
        summed[:, :half][None],
        summed[:, half:][None],
        grad_bias,
    )


def solution(mesh):
    placed = (
        P("dp", "ctx", None),
        P("dp", "ctx", None),
        P("dp", "ctx", None),
        P("dp", "ctx", None),
        P("dp", "ctx"),
        P(),
    )
    return jax.shard_map(
        local,
        mesh=mesh,
        in_specs=placed,
        out_specs=(
            P("dp", "ctx", None),
            P("dp", "ctx", None),
            P("dp", "ctx", None),
            P("dp", "ctx", None),
            P(),
        ),
        check_vma=False,
    )
```

```python
import math

import jax
import jax.numpy as jnp
from jax import lax
from jax.experimental import pallas as pl
from jax.experimental.pallas import tpu as pltpu
from jax.sharding import PartitionSpec as P

QUERY_HEADS = 14
KEY_VALUE_HEADS = 2
HEAD_SIZE = 128
GROUP_SIZE = 7
BLK = 128
WB = 16
DOC_ROWS = 16
PAIR = 2
LEVEL = 4
KV_WIDTH = 2 * KEY_VALUE_HEADS * HEAD_SIZE
SCALE = 1.0 / math.sqrt(HEAD_SIZE)
SCALE_LOG2 = SCALE * math.log2(math.e)
LOW = -1e30

NT = (((1,), (1,)), ((), ()))


def fold(value, op):
    keys, lanes = value.shape
    return op(value.reshape(keys // 8, 8, lanes), axis=0)


def window_levels(shards):
    levels = max(shards // LEVEL, 1)
    return min((WB - 2 + LEVEL) // LEVEL, max(3 * levels // 4 - 1, 0) if levels % 4 == 0 else levels - 1)


def kernel(
    rank_ref, q_ref, bias_ref, do_ref, own_ref, up_ref, x_own_ref, x_up_ref, core_ref,
    att_ref, dq_ref, keep_ref, send_ref, gb_ref,
    kv_buf, q_st, do_t, do_st, s_buf, p_buf, m_buf, l_buf, acc, dq_acc,
):
    rows = q_ref.shape[0]
    packed = own_ref.shape[0]
    depth = up_ref.shape[0] // packed
    chunk = PAIR * rows
    lanes = GROUP_SIZE * rows
    tiles = [(at, min(at + chunk, lanes)) for at in range(0, lanes, chunk)]
    rank = rank_ref[0]
    inner = rank % LEVEL
    my_core = inner % 2
    my_x = inner // 2
    window = (rank // LEVEL - depth) * LEVEL

    for level in range(depth + 1):
        at = level * packed
        below = LEVEL * (depth - level)
        own = own_ref[...] if level == 0 else up_ref[at - packed:at, :]
        x_side = x_own_ref[...] if level == 0 else x_up_ref[at - packed:at, :]
        other = (depth + 1) * packed
        kv_buf[below + 2 * my_x + my_core] = own
        kv_buf[below + 2 * (1 - my_x) + my_core] = x_side
        kv_buf[below + 2 * my_x + 1 - my_core] = core_ref[at:at + packed, :]
        kv_buf[below + 2 * (1 - my_x) + 1 - my_core] = core_ref[other + at:other + at + packed, :]

    counts = kv_buf[:, rows:rows + DOC_ROWS, 0:128].astype(jnp.float32)
    boundary = jnp.sum(counts) * (1.0 / (DOC_ROWS * 128))
    boundary = (boundary + 0.5).astype(jnp.int32) + jnp.maximum(window, 0) * rows
    q_first = rank * rows
    q_last = q_first + rows - 1
    low_block = jnp.maximum(rank - (WB - 1), 0)
    low_block = jnp.where(q_first >= boundary, jnp.maximum(low_block, boundary // rows), low_block)
    low = jnp.maximum(low_block - window, 0) // PAIR
    high = (rank - window) // PAIR + 1

    keep_ref[...] = jnp.zeros_like(keep_ref)
    send_ref[...] = jnp.zeros_like(send_ref)

    def keys_of(c, column):
        return jnp.concatenate(
            [kv_buf[PAIR * c + i, 0:rows, column:column + HEAD_SIZE] for i in range(PAIR)], axis=0
        )

    for g in range(KEY_VALUE_HEADS):
        for n in range(GROUP_SIZE):
            columns = slice((g * GROUP_SIZE + n) * HEAD_SIZE, (g * GROUP_SIZE + n + 1) * HEAD_SIZE)
            at = slice(n * rows, (n + 1) * rows)
            q_st[at, :] = (q_ref[:, columns].astype(jnp.float32) + bias_ref[:, columns]).astype(
                jnp.bfloat16
            )
            do_t[:, at] = do_ref[:, columns].astype(jnp.float32).T
        m_buf[...] = jnp.full_like(m_buf, LOW)
        l_buf[...] = jnp.zeros_like(l_buf)
        acc[...] = jnp.zeros_like(acc)
        dq_acc[...] = jnp.zeros_like(dq_acc)

        @pl.loop(low, high)
        def _(c):
            key_first = window * rows + c * chunk
            k_c = keys_of(c, g * HEAD_SIZE)
            clear = (key_first + chunk <= q_first) & (rank - window - PAIR * c < WB)
            clear = clear & ((boundary <= key_first) | (boundary > q_last))

            def scores(masked):
                if masked:
                    key_pos = key_first + lax.broadcasted_iota(jnp.int32, (chunk, rows), 0)
                    query_pos = q_first + lax.broadcasted_iota(jnp.int32, (chunk, rows), 1)
                    allowed = (key_pos <= query_pos) & (query_pos // BLK - key_pos // BLK < WB)
                    allowed = allowed & ((key_pos >= boundary) == (query_pos >= boundary))
                    bias = jnp.where(allowed, 0.0, LOW)
                for a, b in tiles:
                    s = lax.dot_general(
                        k_c, q_st[a:b, :], NT, preferred_element_type=jnp.float32
                    )
                    if masked:
                        s = s + jnp.concatenate([bias] * ((b - a) // rows), axis=1)
                    s_buf[c - low, :, a:b] = s
                    m_buf[:, a:b] = jnp.maximum(m_buf[:, a:b], fold(s, jnp.max))

            @pl.when(clear)
            def _():
                scores(False)

            @pl.when(jnp.logical_not(clear))
            def _():
                scores(True)

        row_max = jnp.max(m_buf[...], axis=0, keepdims=True) * SCALE_LOG2

        @pl.loop(low, high)
        def _(c):
            v_t = keys_of(c, (KEY_VALUE_HEADS + g) * HEAD_SIZE).T
            for a, b in tiles:
                p = jnp.exp2(s_buf[c - low, :, a:b] * SCALE_LOG2 - row_max[:, a:b])
                l_buf[:, a:b] += fold(p, jnp.sum)
                p_bf = p.astype(jnp.bfloat16)
                p_buf[c - low, :, a:b] = p_bf
                acc[:, a:b] += jnp.dot(v_t, p_bf, preferred_element_type=jnp.float32)

        inverse = 1.0 / jnp.sum(l_buf[...], axis=0, keepdims=True)
        for n in range(GROUP_SIZE):
            columns = slice((g * GROUP_SIZE + n) * HEAD_SIZE, (g * GROUP_SIZE + n + 1) * HEAD_SIZE)
            at = slice(n * rows, (n + 1) * rows)
            att = (acc[:, at] * inverse[:, at]).T.astype(jnp.bfloat16)
            att_ref[:, columns] = att
            do_n = do_t[:, at]
            dot_n = jnp.sum(do_n * att.astype(jnp.float32).T, axis=0, keepdims=True)
            m_buf[0:1, at] = dot_n * inverse[:, at]
            do_n = do_n * inverse[:, at]
            do_t[:, at] = do_n
            do_st[at, :] = do_n.T.astype(jnp.bfloat16)
        row_dot = m_buf[0:1, :]

        @pl.loop(low, high)
        def _(c):
            k_c = keys_of(c, g * HEAD_SIZE)
            v_c = keys_of(c, (KEY_VALUE_HEADS + g) * HEAD_SIZE)
            k_t = k_c.T
            d_key = jnp.zeros((chunk, HEAD_SIZE), jnp.float32)
            d_value = jnp.zeros((chunk, HEAD_SIZE), jnp.float32)
            for a, b in tiles:
                p_bf = p_buf[c - low, :, a:b]
                d_p = jnp.dot(
                    v_c, do_t[:, a:b].astype(jnp.bfloat16), preferred_element_type=jnp.float32
                )
                d_s = (p_bf.astype(jnp.float32) * (d_p - row_dot[:, a:b])).astype(jnp.bfloat16)
                d_value = d_value + jnp.dot(p_bf, do_st[a:b, :], preferred_element_type=jnp.float32)
                d_key = d_key + jnp.dot(d_s, q_st[a:b, :], preferred_element_type=jnp.float32)
                dq_acc[:, a:b] += jnp.dot(k_t, d_s, preferred_element_type=jnp.float32)
            place = 2 * (depth - c // 2) + (c % 2 + my_x) % 2
            at = pl.ds(pl.multiple_of(place * rows, rows), rows)
            for value, column in (
                (d_key * SCALE, g * HEAD_SIZE), (d_value, (KEY_VALUE_HEADS + g) * HEAD_SIZE)
            ):
                first, second = value[:rows], value[rows:]
                columns = slice(column, column + HEAD_SIZE)
                keep_ref[at, columns] = jnp.where(my_core == 0, first, second)
                send_ref[at, columns] = jnp.where(my_core == 0, second, first).astype(jnp.bfloat16)

        for n in range(GROUP_SIZE):
            columns = slice((g * GROUP_SIZE + n) * HEAD_SIZE, (g * GROUP_SIZE + n + 1) * HEAD_SIZE)
            d_q = (dq_acc[:, n * rows:(n + 1) * rows] * SCALE).T
            gb_ref[:, columns] = jnp.sum(d_q, axis=0, keepdims=True)
            dq_ref[:, columns] = d_q.astype(jnp.bfloat16)


def attention(rank, query_in, query_bias, output_gradient, own, up, x_own, x_up, core_all):
    rows, width = query_in.shape
    packed = own.shape[0]
    depth = up.shape[0] // packed
    kv_width = own.shape[1]
    lanes = GROUP_SIZE * rows
    chunk = PAIR * rows
    slots = (depth + 1) * LEVEL // PAIR
    kept = (depth + 1) * 2 * rows
    vmem = pl.BlockSpec(memory_space=pltpu.VMEM)
    return pl.pallas_call(
        kernel,
        out_shape=(
            jax.ShapeDtypeStruct((rows, width), jnp.bfloat16),
            jax.ShapeDtypeStruct((rows, width), jnp.bfloat16),
            jax.ShapeDtypeStruct((kept, kv_width), jnp.float32),
            jax.ShapeDtypeStruct((kept, kv_width), jnp.bfloat16),
            jax.ShapeDtypeStruct((1, width), jnp.float32),
        ),
        in_specs=[pl.BlockSpec(memory_space=pltpu.SMEM)] + [vmem] * 8,
        out_specs=(vmem,) * 5,
        scratch_shapes=[
            pltpu.VMEM(((depth + 1) * LEVEL, packed, kv_width), jnp.bfloat16),
            pltpu.VMEM((lanes, HEAD_SIZE), jnp.bfloat16),
            pltpu.VMEM((HEAD_SIZE, lanes), jnp.float32),
            pltpu.VMEM((lanes, HEAD_SIZE), jnp.bfloat16),
            pltpu.VMEM((slots, chunk, lanes), jnp.float32),
            pltpu.VMEM((slots, chunk, lanes), jnp.bfloat16),
            pltpu.VMEM((8, lanes), jnp.float32),
            pltpu.VMEM((8, lanes), jnp.float32),
            pltpu.VMEM((HEAD_SIZE, lanes), jnp.float32),
            pltpu.VMEM((HEAD_SIZE, lanes), jnp.float32),
        ],
        compiler_params=pltpu.CompilerParams(vmem_limit_bytes=48 * 1024 * 1024),
        name="attention",
    )(rank, query_in, query_bias, output_gradient, own, up, x_own, x_up, core_all)


def shifted(value, steps):
    count = lax.axis_size("ctx")
    first, last = max(0, -steps), min(count, count - steps)
    return lax.ppermute(value, "ctx", [(at, at + steps) for at in range(first, last)])


def swapped(value, bit, axis="ctx"):
    return lax.ppermute(value, axis, [(at, at ^ bit) for at in range(lax.axis_size(axis))])


def bias_rows(vector):
    vector = jnp.pad(vector, (0, -vector.shape[0] % KV_WIDTH))
    high = lax.reduce_precision(vector, 8, 7)
    both = jnp.concatenate([high, vector - high]).astype(jnp.bfloat16).reshape(-1, KV_WIDTH)
    return jnp.pad(both, ((0, -both.shape[0] % 16), (0, 0)))


def bias_sum(rows, length):
    half = -(-length // KV_WIDTH)
    flat = rows[:2 * half].astype(jnp.float32).reshape(2, half * KV_WIDTH)
    return (flat[0] + flat[1])[:length]


def local(query_in, key_in, value_input, output_gradient, doc_ids, query_bias):
    rows = query_in.shape[1]
    width = query_in.shape[2]
    shards = lax.axis_size("ctx")
    depth = window_levels(shards)
    rank = lax.axis_index("ctx").astype(jnp.int32)
    count = jnp.sum((doc_ids[0] == 0).astype(jnp.float32)).astype(jnp.bfloat16)
    own = jnp.concatenate([key_in[0], value_input[0]], axis=1)
    own = jnp.concatenate([own, jnp.broadcast_to(count, (DOC_ROWS, KV_WIDTH))], axis=0)

    ups = [shifted(own, LEVEL * step) for step in range(depth, 0, -1)][::-1]
    x_own = swapped(own, 2)
    up = jnp.concatenate(ups, axis=0)
    x_up = swapped(up, 2)
    core_all = swapped(jnp.concatenate([own, up, x_own, x_up], axis=0), 1)

    attended, grad_query, keep, send, bias_part = attention(
        rank.reshape(1), query_in[0], query_bias[None], output_gradient[0],
        own, up, x_own, x_up, core_all,
    )
    bias_total = bias_part[0]

    got = swapped(jnp.concatenate([send, bias_rows(bias_total)], axis=0), 1)
    kept = keep.shape[0]
    bias_total = bias_total + bias_sum(got[kept:], width)
    both = (keep + got[:kept].astype(jnp.float32)).reshape(depth + 1, 2, rows, KV_WIDTH)
    send = both[:, 1].astype(jnp.bfloat16).reshape((depth + 1) * rows, KV_WIDTH)
    got = swapped(jnp.concatenate([send, bias_rows(bias_total)], axis=0), 2)
    kept = send.shape[0]
    bias_total = bias_total + bias_sum(got[kept:], width)
    summed = both[:, 0] + got[:kept].astype(jnp.float32).reshape(depth + 1, rows, KV_WIDTH)
    total = summed[0]
    down = [shifted(summed[step].astype(jnp.bfloat16), -LEVEL * step) for step in range(depth, 0, -1)]
    for part in down:
        total = total + part.astype(jnp.float32)
    total = total.astype(jnp.bfloat16)

    bit = 1
    while bit < lax.axis_size("dp"):
        bias_total = bias_total + swapped(bias_total, bit, "dp")
        bit *= 2
    bit = LEVEL
    while bit < shards:
        bias_total = bias_total + swapped(bias_total, bit)
        bit *= 2
    half = KEY_VALUE_HEADS * HEAD_SIZE
    return (
        attended[None],
        grad_query[None],
        total[:, :half][None],
        total[:, half:][None],
        bias_total,
    )


def solution(mesh):
    placed = (
        P("dp", "ctx", None),
        P("dp", "ctx", None),
        P("dp", "ctx", None),
        P("dp", "ctx", None),
        P("dp", "ctx"),
        P(),
    )
    return jax.shard_map(
        local,
        mesh=mesh,
        in_specs=placed,
        out_specs=(
            P("dp", "ctx", None),
            P("dp", "ctx", None),
            P("dp", "ctx", None),
            P("dp", "ctx", None),
            P(),
        ),
        check_vma=False,
    )
```

```python
import math

import jax
import jax.numpy as jnp
from jax import lax
from jax.experimental import pallas as pl
from jax.experimental.pallas import tpu as pltpu
from jax.sharding import PartitionSpec as P

QUERY_HEADS = 14
KEY_VALUE_HEADS = 2
HEAD_SIZE = 128
GROUP_SIZE = 7
BLK = 128
WB = 16
DOC_ROWS = 16
PAIR = 2
LEVEL = 4
KV_WIDTH = 2 * KEY_VALUE_HEADS * HEAD_SIZE
SCALE = 1.0 / math.sqrt(HEAD_SIZE)
SCALE_LOG2 = SCALE * math.log2(math.e)
LOW = -1e30

NT = (((1,), (1,)), ((), ()))


def fold(value, op):
    keys, lanes = value.shape
    return op(value.reshape(keys // 8, 8, lanes), axis=0)


def window_levels(shards):
    levels = max(shards // LEVEL, 1)
    return min((WB - 2 + LEVEL) // LEVEL, max(3 * levels // 4 - 1, 0) if levels % 4 == 0 else levels - 1)


def pack_kernel(key_hbm, value_hbm, docs_hbm, own_ref, docs, sems):
    rows = key_hbm.shape[0]
    half = key_hbm.shape[1]
    copies = [
        pltpu.make_async_copy(docs_hbm, docs, sems.at[0]),
        pltpu.make_async_copy(key_hbm, own_ref.at[0:rows, 0:half], sems.at[1]),
        pltpu.make_async_copy(value_hbm, own_ref.at[0:rows, half:2 * half], sems.at[2]),
    ]
    for copy in copies:
        copy.start()
    copies[0].wait()
    count = jnp.sum((docs[...] == 0).astype(jnp.float32), axis=1, keepdims=True)
    own_ref[rows:rows + DOC_ROWS, :] = jnp.broadcast_to(count, (DOC_ROWS, 2 * half)).astype(
        jnp.bfloat16
    )
    copies[1].wait()
    copies[2].wait()


def pack(key_in, value_input, doc_ids):
    rows, half = key_in.shape
    return pl.pallas_call(
        pack_kernel,
        out_shape=jax.ShapeDtypeStruct((rows + DOC_ROWS, 2 * half), jnp.bfloat16),
        in_specs=[pl.BlockSpec(memory_space=pltpu.HBM)] * 3,
        out_specs=pl.BlockSpec(memory_space=pltpu.VMEM),
        scratch_shapes=[pltpu.VMEM((1, rows), jnp.int32), pltpu.SemaphoreType.DMA((3,))],
        compiler_params=pltpu.CompilerParams(vmem_limit_bytes=8 * 1024 * 1024),
        name="pack",
    )(key_in, value_input, doc_ids)


def head_columns(g, n):
    head = g * GROUP_SIZE + n
    return slice(head * HEAD_SIZE, (head + 1) * HEAD_SIZE)


def prepare_kernel(q_hbm, bias_ref, do_hbm, q_st, do_t, q_buf, do_buf, sems):
    rows = q_buf.shape[0]
    first = pltpu.make_async_copy(q_hbm, q_buf, sems.at[0])
    second = pltpu.make_async_copy(do_hbm, do_buf, sems.at[1])
    first.start()
    second.start()
    first.wait()
    for g in range(KEY_VALUE_HEADS):
        for n in range(GROUP_SIZE):
            columns = head_columns(g, n)
            q_st[g, n * rows:(n + 1) * rows, :] = (
                q_buf[:, columns].astype(jnp.float32) + bias_ref[:, columns]
            ).astype(jnp.bfloat16)
    second.wait()
    for g in range(KEY_VALUE_HEADS):
        for n in range(GROUP_SIZE):
            do_t[g, :, n * rows:(n + 1) * rows] = do_buf[:, head_columns(g, n)].T


def prepare(query_in, query_bias, output_gradient):
    rows, width = query_in.shape
    lanes = GROUP_SIZE * rows
    anywhere = pl.BlockSpec(memory_space=pltpu.HBM)
    vmem = pl.BlockSpec(memory_space=pltpu.VMEM)
    return pl.pallas_call(
        prepare_kernel,
        out_shape=(
            jax.ShapeDtypeStruct((KEY_VALUE_HEADS, lanes, HEAD_SIZE), jnp.bfloat16),
            jax.ShapeDtypeStruct((KEY_VALUE_HEADS, HEAD_SIZE, lanes), jnp.bfloat16),
        ),
        in_specs=[anywhere, vmem, anywhere],
        out_specs=(vmem, vmem),
        scratch_shapes=[
            pltpu.VMEM((rows, width), jnp.bfloat16),
            pltpu.VMEM((rows, width), jnp.bfloat16),
            pltpu.SemaphoreType.DMA((2,)),
        ],
        compiler_params=pltpu.CompilerParams(vmem_limit_bytes=8 * 1024 * 1024),
        cost_estimate=pl.CostEstimate(
            flops=4 * rows * width, bytes_accessed=8 * rows * width, transcendentals=0
        ),
        name="prepare",
    )(query_in, query_bias, output_gradient)


def kernel(
    rank_ref, q_all, do_all, own_ref, up_ref, x_own_ref, x_up_ref, core_ref,
    att_ref, dq_ref, keep_ref, send_ref, gb_ref,
    kv_buf, do_t, do_st, s_buf, p_buf, m_buf, l_buf, acc, dq_acc,
):
    rows = att_ref.shape[0]
    packed = own_ref.shape[0]
    depth = up_ref.shape[0] // packed
    chunk = PAIR * rows
    lanes = GROUP_SIZE * rows
    tiles = [(at, min(at + chunk, lanes)) for at in range(0, lanes, chunk)]
    rank = rank_ref[0]
    inner = rank % LEVEL
    my_core = inner % 2
    my_x = inner // 2
    window = (rank // LEVEL - depth) * LEVEL

    for level in range(depth + 1):
        at = level * packed
        below = LEVEL * (depth - level)
        own = own_ref[...] if level == 0 else up_ref[at - packed:at, :]
        x_side = x_own_ref[...] if level == 0 else x_up_ref[at - packed:at, :]
        other = (depth + 1) * packed
        kv_buf[below + 2 * my_x + my_core] = own
        kv_buf[below + 2 * (1 - my_x) + my_core] = x_side
        kv_buf[below + 2 * my_x + 1 - my_core] = core_ref[at:at + packed, :]
        kv_buf[below + 2 * (1 - my_x) + 1 - my_core] = core_ref[other + at:other + at + packed, :]

    counts = kv_buf[:, rows:rows + DOC_ROWS, 0:128].astype(jnp.float32)
    boundary = jnp.sum(counts) * (1.0 / (DOC_ROWS * 128))
    boundary = (boundary + 0.5).astype(jnp.int32) + jnp.maximum(window, 0) * rows
    q_first = rank * rows
    q_last = q_first + rows - 1
    low_block = jnp.maximum(rank - (WB - 1), 0)
    low_block = jnp.where(q_first >= boundary, jnp.maximum(low_block, boundary // rows), low_block)
    low = jnp.maximum(low_block - window, 0) // PAIR
    high = (rank - window) // PAIR + 1

    keep_ref[...] = jnp.zeros_like(keep_ref)
    send_ref[...] = jnp.zeros_like(send_ref)

    def keys_of(c, column):
        return jnp.concatenate(
            [kv_buf[PAIR * c + i, 0:rows, column:column + HEAD_SIZE] for i in range(PAIR)], axis=0
        )

    for g in range(KEY_VALUE_HEADS):
        q_st = q_all.at[g]
        m_buf[...] = jnp.full_like(m_buf, LOW)
        l_buf[...] = jnp.zeros_like(l_buf)
        acc[...] = jnp.zeros_like(acc)
        dq_acc[...] = jnp.zeros_like(dq_acc)

        @pl.loop(low, high)
        def _(c):
            key_first = window * rows + c * chunk
            k_c = keys_of(c, g * HEAD_SIZE)
            clear = (key_first + chunk <= q_first) & (rank - window - PAIR * c < WB)
            clear = clear & ((boundary <= key_first) | (boundary > q_last))

            def scores(masked):
                if masked:
                    key_pos = key_first + lax.broadcasted_iota(jnp.int32, (chunk, rows), 0)
                    query_pos = q_first + lax.broadcasted_iota(jnp.int32, (chunk, rows), 1)
                    allowed = (key_pos <= query_pos) & (query_pos // BLK - key_pos // BLK < WB)
                    allowed = allowed & ((key_pos >= boundary) == (query_pos >= boundary))
                    bias = jnp.where(allowed, 0.0, LOW)
                for a, b in tiles:
                    s = lax.dot_general(
                        k_c, q_st[a:b, :], NT, preferred_element_type=jnp.float32
                    )
                    if masked:
                        s = s + jnp.concatenate([bias] * ((b - a) // rows), axis=1)
                    s_buf[c - low, :, a:b] = s
                    m_buf[:, a:b] = jnp.maximum(m_buf[:, a:b], fold(s, jnp.max))

            @pl.when(clear)
            def _():
                scores(False)

            @pl.when(jnp.logical_not(clear))
            def _():
                scores(True)

        row_max = jnp.max(m_buf[...], axis=0, keepdims=True) * SCALE_LOG2

        @pl.loop(low, high)
        def _(c):
            v_t = keys_of(c, (KEY_VALUE_HEADS + g) * HEAD_SIZE).T
            for a, b in tiles:
                p = jnp.exp2(s_buf[c - low, :, a:b] * SCALE_LOG2 - row_max[:, a:b])
                l_buf[:, a:b] += fold(p, jnp.sum)
                p_bf = p.astype(jnp.bfloat16)
                p_buf[c - low, :, a:b] = p_bf
                acc[:, a:b] += jnp.dot(v_t, p_bf, preferred_element_type=jnp.float32)

        inverse = 1.0 / jnp.sum(l_buf[...], axis=0, keepdims=True)
        for n in range(GROUP_SIZE):
            columns = head_columns(g, n)
            at = slice(n * rows, (n + 1) * rows)
            att = (acc[:, at] * inverse[:, at]).T.astype(jnp.bfloat16)
            att_ref[:, columns] = att
            do_n = do_all[g, :, at].astype(jnp.float32)
            dot_n = jnp.sum(do_n * att.astype(jnp.float32).T, axis=0, keepdims=True)
            m_buf[0:1, at] = dot_n * inverse[:, at]
            do_n = (do_n * inverse[:, at]).astype(jnp.bfloat16)
            do_t[:, at] = do_n
            do_st[at, :] = do_n.T
        row_dot = m_buf[0:1, :]

        @pl.loop(low, high)
        def _(c):
            k_c = keys_of(c, g * HEAD_SIZE)
            v_c = keys_of(c, (KEY_VALUE_HEADS + g) * HEAD_SIZE)
            k_t = k_c.T
            d_key = jnp.zeros((chunk, HEAD_SIZE), jnp.float32)
            d_value = jnp.zeros((chunk, HEAD_SIZE), jnp.float32)
            for a, b in tiles:
                p_bf = p_buf[c - low, :, a:b]
                d_p = jnp.dot(
                    v_c, do_t[:, a:b], preferred_element_type=jnp.float32
                )
                d_s = (p_bf.astype(jnp.float32) * (d_p - row_dot[:, a:b])).astype(jnp.bfloat16)
                d_value = d_value + jnp.dot(p_bf, do_st[a:b, :], preferred_element_type=jnp.float32)
                d_key = d_key + jnp.dot(d_s, q_st[a:b, :], preferred_element_type=jnp.float32)
                dq_acc[:, a:b] += jnp.dot(k_t, d_s, preferred_element_type=jnp.float32)
            place = 2 * (depth - c // 2) + (c % 2 + my_x) % 2
            at = pl.ds(pl.multiple_of(place * rows, rows), rows)
            for value, column in (
                (d_key * SCALE, g * HEAD_SIZE), (d_value, (KEY_VALUE_HEADS + g) * HEAD_SIZE)
            ):
                first, second = value[:rows], value[rows:]
                columns = slice(column, column + HEAD_SIZE)
                keep_ref[at, columns] = jnp.where(my_core == 0, first, second)
                send_ref[at, columns] = jnp.where(my_core == 0, second, first).astype(jnp.bfloat16)

        for n in range(GROUP_SIZE):
            columns = head_columns(g, n)
            d_q = (dq_acc[:, n * rows:(n + 1) * rows] * SCALE).T
            gb_ref[:, columns] = jnp.sum(d_q, axis=0, keepdims=True)
            dq_ref[:, columns] = d_q.astype(jnp.bfloat16)


def attention(rank, q_all, do_all, own, up, x_own, x_up, core_all):
    rows = q_all.shape[1] // GROUP_SIZE
    width = QUERY_HEADS * HEAD_SIZE
    packed = own.shape[0]
    depth = up.shape[0] // packed
    kv_width = own.shape[1]
    lanes = GROUP_SIZE * rows
    chunk = PAIR * rows
    slots = (depth + 1) * LEVEL // PAIR
    kept = (depth + 1) * 2 * rows
    vmem = pl.BlockSpec(memory_space=pltpu.VMEM)
    return pl.pallas_call(
        kernel,
        out_shape=(
            jax.ShapeDtypeStruct((rows, width), jnp.bfloat16),
            jax.ShapeDtypeStruct((rows, width), jnp.bfloat16),
            jax.ShapeDtypeStruct((kept, kv_width), jnp.float32),
            jax.ShapeDtypeStruct((kept, kv_width), jnp.bfloat16),
            jax.ShapeDtypeStruct((1, width), jnp.float32),
        ),
        in_specs=[pl.BlockSpec(memory_space=pltpu.SMEM)] + [vmem] * 7,
        out_specs=(vmem,) * 5,
        scratch_shapes=[
            pltpu.VMEM(((depth + 1) * LEVEL, packed, kv_width), jnp.bfloat16),
            pltpu.VMEM((HEAD_SIZE, lanes), jnp.bfloat16),
            pltpu.VMEM((lanes, HEAD_SIZE), jnp.bfloat16),
            pltpu.VMEM((slots, chunk, lanes), jnp.float32),
            pltpu.VMEM((slots, chunk, lanes), jnp.bfloat16),
            pltpu.VMEM((8, lanes), jnp.float32),
            pltpu.VMEM((8, lanes), jnp.float32),
            pltpu.VMEM((HEAD_SIZE, lanes), jnp.float32),
            pltpu.VMEM((HEAD_SIZE, lanes), jnp.float32),
        ],
        compiler_params=pltpu.CompilerParams(vmem_limit_bytes=32 * 1024 * 1024),
        name="attention",
    )(rank, q_all, do_all, own, up, x_own, x_up, core_all)


def shifted(value, steps):
    count = lax.axis_size("ctx")
    first, last = max(0, -steps), min(count, count - steps)
    return lax.ppermute(value, "ctx", [(at, at + steps) for at in range(first, last)])


def swapped(value, bit, axis="ctx"):
    return lax.ppermute(value, axis, [(at, at ^ bit) for at in range(lax.axis_size(axis))])


def local(query_in, key_in, value_input, output_gradient, doc_ids, query_bias):
    rows = query_in.shape[1]
    shards = lax.axis_size("ctx")
    depth = window_levels(shards)
    rank = lax.axis_index("ctx").astype(jnp.int32)
    own = pack(key_in[0], value_input[0], doc_ids)

    ups = [shifted(own, LEVEL * step) for step in range(depth, 0, -1)][::-1]
    x_own = swapped(own, 2)
    q_all, do_all = prepare(query_in[0], query_bias[None], output_gradient[0])
    up = jnp.concatenate(ups, axis=0)
    up, x_own, q_all, do_all = lax.optimization_barrier((up, x_own, q_all, do_all))
    x_up = swapped(up, 2)
    core_all = swapped(jnp.concatenate([own, up, x_own, x_up], axis=0), 1)

    attended, grad_query, keep, send, bias_part = attention(
        rank.reshape(1), q_all, do_all, own, up, x_own, x_up, core_all
    )
    bias_total = bias_part[0]
    bits = [("ctx", LEVEL << at) for at in reversed(range((shards // LEVEL - 1).bit_length()))]
    bits += [("dp", 1 << at) for at in range((lax.axis_size("dp") - 1).bit_length())]
    bits += [("ctx", 2), ("ctx", 1)]

    def bias_steps(value, steps):
        for axis, bit in steps:
            value = value + swapped(value, bit, axis)
        return value

    got = swapped(send, 1)
    bias_total = bias_steps(bias_total, bits[:1])
    got, bias_total = lax.optimization_barrier((got, bias_total))
    both = (keep + got.astype(jnp.float32)).reshape(depth + 1, 2, rows, KV_WIDTH)
    across = [swapped(both[step, 1].astype(jnp.bfloat16), 2) for step in range(depth, -1, -1)][::-1]
    bias_total = bias_steps(bias_total, bits[1:-2])
    parts = [None] * (depth + 1)
    down = [None] * (depth + 1)
    tied = bias_total
    for step in range(depth, -1, -1):
        got, tied = lax.optimization_barrier((across[step], tied))
        if step == depth:
            bias_total = tied
        parts[step] = both[step, 0] + got.astype(jnp.float32)
        if step:
            tied = parts[step].astype(jnp.bfloat16)
            down[step] = shifted(tied, -LEVEL * step)
    bias_total = bias_steps(bias_total, bits[-2:])
    total = parts[0]
    for step in range(depth, 0, -1):
        total = total + down[step].astype(jnp.float32)
    total = total.astype(jnp.bfloat16)
    half = KEY_VALUE_HEADS * HEAD_SIZE
    return (
        attended[None],
        grad_query[None],
        total[:, :half][None],
        total[:, half:][None],
        bias_total,
    )


def solution(mesh):
    placed = (
        P("dp", "ctx", None),
        P("dp", "ctx", None),
        P("dp", "ctx", None),
        P("dp", "ctx", None),
        P("dp", "ctx"),
        P(),
    )
    return jax.shard_map(
        local,
        mesh=mesh,
        in_specs=placed,
        out_specs=(
            P("dp", "ctx", None),
            P("dp", "ctx", None),
            P("dp", "ctx", None),
            P("dp", "ctx", None),
            P(),
        ),
        check_vma=False,
    )
```

```python
import functools
import math

import jax
import jax.numpy as jnp
from jax import lax
from jax.experimental import pallas as pl
from jax.experimental.pallas import tpu as pltpu
from jax.sharding import PartitionSpec as P

QUERY_HEADS = 14
KEY_VALUE_HEADS = 2
HEAD_SIZE = 128
GROUP_SIZE = 7
BLK = 128
WB = 16
DOC_ROWS = 16
PAIR = 2
LEVEL = 4
KV_WIDTH = 2 * KEY_VALUE_HEADS * HEAD_SIZE
SCALE = 1.0 / math.sqrt(HEAD_SIZE)
SCALE_LOG2 = SCALE * math.log2(math.e)
LOW = -1e30

NT = (((1,), (1,)), ((), ()))


def fold(value, op):
    keys, lanes = value.shape
    return op(value.reshape(keys // 8, 8, lanes), axis=0)


def window_levels(shards):
    levels = max(shards // LEVEL, 1)
    return min((WB - 2 + LEVEL) // LEVEL, max(3 * levels // 4 - 1, 0) if levels % 4 == 0 else levels - 1)


def pack_kernel(key_hbm, value_hbm, docs_hbm, own_ref, docs, sems):
    rows = key_hbm.shape[0]
    half = key_hbm.shape[1]
    copies = [
        pltpu.make_async_copy(docs_hbm, docs, sems.at[0]),
        pltpu.make_async_copy(key_hbm, own_ref.at[0:rows, 0:half], sems.at[1]),
        pltpu.make_async_copy(value_hbm, own_ref.at[0:rows, half:2 * half], sems.at[2]),
    ]
    for copy in copies:
        copy.start()
    copies[0].wait()
    count = jnp.sum((docs[...] == 0).astype(jnp.float32), axis=1, keepdims=True)
    own_ref[rows:rows + DOC_ROWS, :] = jnp.broadcast_to(count, (DOC_ROWS, 2 * half)).astype(
        jnp.bfloat16
    )
    copies[1].wait()
    copies[2].wait()


def pack(key_in, value_input, doc_ids):
    rows, half = key_in.shape
    return pl.pallas_call(
        pack_kernel,
        out_shape=jax.ShapeDtypeStruct((rows + DOC_ROWS, 2 * half), jnp.bfloat16),
        in_specs=[pl.BlockSpec(memory_space=pltpu.HBM)] * 3,
        out_specs=pl.BlockSpec(memory_space=pltpu.VMEM),
        scratch_shapes=[pltpu.VMEM((1, rows), jnp.int32), pltpu.SemaphoreType.DMA((3,))],
        compiler_params=pltpu.CompilerParams(vmem_limit_bytes=8 * 1024 * 1024),
        name="pack",
    )(key_in, value_input, doc_ids)


def head_columns(g, n):
    head = g * GROUP_SIZE + n
    return slice(head * HEAD_SIZE, (head + 1) * HEAD_SIZE)


def prepare_kernel(q_hbm, bias_ref, do_hbm, q_st, do_t, q_buf, do_buf, sems):
    rows = q_buf.shape[0]
    first = pltpu.make_async_copy(q_hbm, q_buf, sems.at[0])
    second = pltpu.make_async_copy(do_hbm, do_buf, sems.at[1])
    first.start()
    second.start()
    first.wait()
    for g in range(KEY_VALUE_HEADS):
        for n in range(GROUP_SIZE):
            columns = head_columns(g, n)
            q_st[g, n * rows:(n + 1) * rows, :] = (
                q_buf[:, columns].astype(jnp.float32) + bias_ref[:, columns]
            ).astype(jnp.bfloat16)
    second.wait()
    for g in range(KEY_VALUE_HEADS):
        for n in range(GROUP_SIZE):
            do_t[g, :, n * rows:(n + 1) * rows] = do_buf[:, head_columns(g, n)].T


def prepare(query_in, query_bias, output_gradient):
    rows, width = query_in.shape
    lanes = GROUP_SIZE * rows
    anywhere = pl.BlockSpec(memory_space=pltpu.HBM)
    vmem = pl.BlockSpec(memory_space=pltpu.VMEM)
    return pl.pallas_call(
        prepare_kernel,
        out_shape=(
            jax.ShapeDtypeStruct((KEY_VALUE_HEADS, lanes, HEAD_SIZE), jnp.bfloat16),
            jax.ShapeDtypeStruct((KEY_VALUE_HEADS, HEAD_SIZE, lanes), jnp.bfloat16),
        ),
        in_specs=[anywhere, vmem, anywhere],
        out_specs=(vmem, vmem),
        scratch_shapes=[
            pltpu.VMEM((rows, width), jnp.bfloat16),
            pltpu.VMEM((rows, width), jnp.bfloat16),
            pltpu.SemaphoreType.DMA((2,)),
        ],
        compiler_params=pltpu.CompilerParams(vmem_limit_bytes=8 * 1024 * 1024),
        cost_estimate=pl.CostEstimate(
            flops=4 * rows * width, bytes_accessed=8 * rows * width, transcendentals=0
        ),
        name="prepare",
    )(query_in, query_bias, output_gradient)


def kernel(
    rank_ref, q_all, do_all, column_ref, core_ref,
    att_ref, dq_ref, p_buf, ds_buf, do_t, gb_ref, span_ref,
    kv_buf, s_buf, m_buf, l_buf, acc, dq_acc,
):
    rows = att_ref.shape[0]
    slots = p_buf.shape[0]
    packed = kv_buf.shape[1]
    depth = slots * PAIR // LEVEL - 1
    chunk = PAIR * rows
    lanes = GROUP_SIZE * rows
    tiles = [(at, min(at + chunk, lanes)) for at in range(0, lanes, chunk)]
    rank = rank_ref[0]
    inner = rank % LEVEL
    my_core = inner % 2
    my_x = inner // 2
    window = (rank // LEVEL - depth) * LEVEL

    for level in range(depth + 1):
        below = LEVEL * (depth - level)
        for x_at in range(2):
            at = (x_at * (depth + 1) + level) * packed
            place = below + 2 * (my_x + x_at - 2 * my_x * x_at)
            kv_buf[place + my_core] = column_ref[at:at + packed, :]
            kv_buf[place + 1 - my_core] = core_ref[at:at + packed, :]

    counts = kv_buf[:, rows:rows + DOC_ROWS, 0:128].astype(jnp.float32)
    boundary = jnp.sum(counts) * (1.0 / (DOC_ROWS * 128))
    boundary = (boundary + 0.5).astype(jnp.int32) + jnp.maximum(window, 0) * rows
    q_first = rank * rows
    low_block = jnp.maximum(rank - (WB - 1), 0)
    low_block = jnp.where(q_first >= boundary, jnp.maximum(low_block, boundary // rows), low_block)
    low = jnp.maximum(low_block - window, 0) // PAIR
    high = (rank - window) // PAIR + 1
    span_ref[0] = low
    span_ref[1] = high

    m_buf[...] = jnp.full_like(m_buf, LOW)
    l_buf[...] = jnp.zeros_like(l_buf)
    acc[...] = jnp.zeros_like(acc)
    dq_acc[...] = jnp.zeros_like(dq_acc)

    def keys_of(c, column):
        return jnp.concatenate(
            [kv_buf[PAIR * c + i, 0:rows, column:column + HEAD_SIZE] for i in range(PAIR)], axis=0
        )

    def score_steps(c, g):
        key_first = window * rows + c * chunk
        key_pos = key_first + lax.broadcasted_iota(jnp.int32, (chunk, rows), 0)
        query_pos = q_first + lax.broadcasted_iota(jnp.int32, (chunk, rows), 1)
        allowed = (key_pos <= query_pos) & (query_pos // BLK - key_pos // BLK < WB)
        allowed = allowed & ((key_pos >= boundary) == (query_pos >= boundary))
        bias = jnp.where(allowed, 0.0, LOW)
        k_c = keys_of(c, g * HEAD_SIZE)

        def step(a, b):
            s = lax.dot_general(k_c, q_all[g, a:b, :], NT, preferred_element_type=jnp.float32)
            s = s + jnp.concatenate([bias] * ((b - a) // rows), axis=1)
            s_buf[c, :, a:b] = s
            m_buf[g, :, a:b] = jnp.maximum(m_buf[g, :, a:b], fold(s, jnp.max))

        return step

    def weight_steps(c, g, row_max):
        v_t = keys_of(c, (KEY_VALUE_HEADS + g) * HEAD_SIZE).T

        def step(a, b):
            p = jnp.exp2(s_buf[c, :, a:b] * SCALE_LOG2 - row_max[:, a:b])
            l_buf[g, :, a:b] += fold(p, jnp.sum)
            p_bf = p.astype(jnp.bfloat16)
            p_buf[c, :, g * lanes + a:g * lanes + b] = p_bf
            acc[g, :, a:b] += jnp.dot(v_t, p_bf, preferred_element_type=jnp.float32)

        return step

    def gradient_steps(c, g, row_dot):
        v_c = keys_of(c, (KEY_VALUE_HEADS + g) * HEAD_SIZE)
        k_t = keys_of(c, g * HEAD_SIZE).T

        def step(a, b):
            d_p = jnp.dot(v_c, do_t[g, :, a:b], preferred_element_type=jnp.float32)
            p = p_buf[c, :, g * lanes + a:g * lanes + b].astype(jnp.float32)
            d_s = (p * (d_p - row_dot[:, a:b])).astype(jnp.bfloat16)
            ds_buf[c, :, g * lanes + a:g * lanes + b] = d_s
            dq_acc[g, :, a:b] += jnp.dot(k_t, d_s, preferred_element_type=jnp.float32)

        return step

    def row_maximum(g):
        return jnp.max(m_buf[g], axis=0, keepdims=True) * SCALE_LOG2

    def finish_rows(g):
        inverse = 1.0 / jnp.sum(l_buf[g], axis=0, keepdims=True)
        for n in range(GROUP_SIZE):
            at = slice(n * rows, (n + 1) * rows)
            att = (acc[g, :, at] * inverse[:, at]).astype(jnp.bfloat16)
            att_ref[:, head_columns(g, n)] = att.T
            do_n = do_all[g, :, at].astype(jnp.float32)
            dot_n = jnp.sum(do_n * att.astype(jnp.float32), axis=0, keepdims=True)
            m_buf[g, 0:1, at] = dot_n * inverse[:, at]
            do_t[g, :, at] = (do_n * inverse[:, at]).astype(jnp.bfloat16)

    def over_chunks(*makers):
        @pl.loop(low, high)
        def _(c):
            steps = [make(c) for make in makers]
            for a, b in tiles:
                for step in steps:
                    step(a, b)

    over_chunks(lambda c: score_steps(c, 0))
    for g in range(KEY_VALUE_HEADS):
        row_max = row_maximum(g)
        makers = [lambda c: weight_steps(c, g, row_max)]
        if g:
            row_dot = m_buf[g - 1, 0:1, :]
            makers.append(lambda c: gradient_steps(c, g - 1, row_dot))
        if g + 1 < KEY_VALUE_HEADS:
            makers.append(lambda c: score_steps(c, g + 1))
        over_chunks(*makers)
        finish_rows(g)
    row_dot = m_buf[KEY_VALUE_HEADS - 1, 0:1, :]
    over_chunks(lambda c: gradient_steps(c, KEY_VALUE_HEADS - 1, row_dot))

    gb_ref[...] = jnp.zeros_like(gb_ref)
    for g in range(KEY_VALUE_HEADS):
        for n in range(GROUP_SIZE):
            columns = head_columns(g, n)
            d_q = (dq_acc[g, :, n * rows:(n + 1) * rows] * SCALE).astype(jnp.bfloat16).T
            row, at = divmod(columns.start, KV_WIDTH)
            gb_ref[row:row + 1, at:at + HEAD_SIZE] = jnp.sum(
                d_q.astype(jnp.float32), axis=0, keepdims=True
            )
            dq_ref[:, columns] = d_q


def attention(rank, q_all, do_all, column, core_column, depth):
    rows = q_all.shape[1] // GROUP_SIZE
    width = QUERY_HEADS * HEAD_SIZE
    packed = rows + DOC_ROWS
    lanes = GROUP_SIZE * rows
    chunk = PAIR * rows
    slots = (depth + 1) * LEVEL // PAIR
    vmem = pl.BlockSpec(memory_space=pltpu.VMEM)
    smem = pl.BlockSpec(memory_space=pltpu.SMEM)
    products = 5 * 2 * width * HEAD_SIZE * slots * chunk
    return pl.pallas_call(
        kernel,
        out_shape=(
            jax.ShapeDtypeStruct((rows, width), jnp.bfloat16),
            jax.ShapeDtypeStruct((rows, width), jnp.bfloat16),
            jax.ShapeDtypeStruct((slots, chunk, KEY_VALUE_HEADS * lanes), jnp.bfloat16),
            jax.ShapeDtypeStruct((slots, chunk, KEY_VALUE_HEADS * lanes), jnp.bfloat16),
            jax.ShapeDtypeStruct((KEY_VALUE_HEADS, HEAD_SIZE, lanes), jnp.bfloat16),
            jax.ShapeDtypeStruct((-(-width // KV_WIDTH), KV_WIDTH), jnp.float32),
            jax.ShapeDtypeStruct((2,), jnp.int32),
        ),
        in_specs=[smem] + [vmem] * 4,
        out_specs=(vmem,) * 6 + (smem,),
        scratch_shapes=[
            pltpu.VMEM(((depth + 1) * LEVEL, packed, KV_WIDTH), jnp.bfloat16),
            pltpu.VMEM((slots, chunk, lanes), jnp.float32),
            pltpu.VMEM((KEY_VALUE_HEADS, 8, lanes), jnp.float32),
            pltpu.VMEM((KEY_VALUE_HEADS, 8, lanes), jnp.float32),
            pltpu.VMEM((KEY_VALUE_HEADS, HEAD_SIZE, lanes), jnp.float32),
            pltpu.VMEM((KEY_VALUE_HEADS, HEAD_SIZE, lanes), jnp.float32),
        ],
        compiler_params=pltpu.CompilerParams(vmem_limit_bytes=36 * 1024 * 1024),
        cost_estimate=pl.CostEstimate(
            flops=products, bytes_accessed=8 * rows * width, transcendentals=0
        ),
        name="attention",
    )(rank, q_all, do_all, column, core_column)


def level_kernel(level, rank_ref, span_ref, p_buf, ds_buf, q_all, do_t, keep_ref, send_ref):
    chunk = p_buf.shape[1]
    rows = chunk // PAIR
    lanes = GROUP_SIZE * rows
    inner = rank_ref[0] % LEVEL
    my_core = inner % 2
    my_x = inner // 2
    for pair in range(LEVEL // PAIR):
        c = level * (LEVEL // PAIR) + pair
        place = (pair + my_x) % 2
        at = pl.ds(pl.multiple_of(place * rows, rows), rows)
        active = (c >= span_ref[0]) & (c < span_ref[1])

        @pl.when(active)
        def _():
            for g in range(KEY_VALUE_HEADS):
                where = slice(g * lanes, (g + 1) * lanes)
                d_key = jnp.dot(
                    ds_buf[c, :, where], q_all[g], preferred_element_type=jnp.float32
                ) * SCALE
                d_value = lax.dot_general(
                    p_buf[c, :, where], do_t[g], NT, preferred_element_type=jnp.float32
                )
                for value, column in ((d_key, g), (d_value, KEY_VALUE_HEADS + g)):
                    first, second = value[:rows], value[rows:]
                    columns = slice(column * HEAD_SIZE, (column + 1) * HEAD_SIZE)
                    keep_ref[at, columns] = jnp.where(my_core == 0, first, second)
                    send_ref[at, columns] = jnp.where(my_core == 0, second, first).astype(
                        jnp.bfloat16
                    )

        @pl.when(jnp.logical_not(active))
        def _():
            keep_ref[at, :] = jnp.zeros((rows, KV_WIDTH), jnp.float32)
            send_ref[at, :] = jnp.zeros((rows, KV_WIDTH), jnp.bfloat16)


def level_gradients(level, rank, span, p_all, ds_all, q_all, do_t):
    chunk, width = p_all.shape[1:]
    rows = chunk // PAIR
    vmem = pl.BlockSpec(memory_space=pltpu.VMEM)
    smem = pl.BlockSpec(memory_space=pltpu.SMEM)
    return pl.pallas_call(
        functools.partial(level_kernel, level),
        out_shape=(
            jax.ShapeDtypeStruct((2 * rows, KV_WIDTH), jnp.float32),
            jax.ShapeDtypeStruct((2 * rows, KV_WIDTH), jnp.bfloat16),
        ),
        in_specs=[smem, smem] + [vmem] * 4,
        out_specs=(vmem, vmem),
        compiler_params=pltpu.CompilerParams(vmem_limit_bytes=36 * 1024 * 1024),
        cost_estimate=pl.CostEstimate(
            flops=2 * 2 * LEVEL * rows * width * HEAD_SIZE,
            bytes_accessed=4 * LEVEL * rows * width,
            transcendentals=0,
        ),
        name="level_gradients",
    )(rank, span, p_all, ds_all, q_all, do_t)


def shifted(value, steps):
    count = lax.axis_size("ctx")
    first, last = max(0, -steps), min(count, count - steps)
    return lax.ppermute(value, "ctx", [(at, at + steps) for at in range(first, last)])


def rotated(value, steps):
    count = lax.axis_size("ctx")
    return lax.ppermute(value, "ctx", [(at, (at + steps) % count) for at in range(count)])


def swapped(value, bit, axis="ctx"):
    return lax.ppermute(value, axis, [(at, at ^ bit) for at in range(lax.axis_size(axis))])


def bias_rows(rows):
    high = lax.reduce_precision(rows, 8, 7)
    both = jnp.concatenate([high, rows - high]).astype(jnp.bfloat16)
    return jnp.pad(both, ((0, -both.shape[0] % 16), (0, 0)))


def local(query_in, key_in, value_input, output_gradient, doc_ids, query_bias):
    rows = query_in.shape[1]
    shards = lax.axis_size("ctx")
    depth = window_levels(shards)
    rank = lax.axis_index("ctx").astype(jnp.int32)
    own = pack(key_in[0], value_input[0], doc_ids)

    ups = [shifted(own, LEVEL * step) for step in range(depth, 0, -1)][::-1]
    x_own = swapped(own, 2)
    q_all, do_all = prepare(query_in[0], query_bias[None], output_gradient[0])
    up = jnp.concatenate(ups, axis=0)
    up, x_own, q_all, do_all = lax.optimization_barrier((up, x_own, q_all, do_all))
    x_up = swapped(up, 2)
    column = jnp.concatenate([own, up, x_own, x_up], axis=0)
    core_column = swapped(column, 1)

    rank = rank.reshape(1)
    attended, grad_query, p_all, ds_all, do_t, bias_part, span = attention(
        rank, q_all, do_all, column, core_column, depth
    )

    levels = shards // LEVEL
    carried = levels == 4 and depth == 2
    bit = 1
    while bit < lax.axis_size("dp"):
        bias_part = bias_part + swapped(bias_part, bit, "dp")
        bit *= 2
    bias_total = bias_part

    def joined(value):
        return jnp.concatenate([value, bias_rows(bias_total)], axis=0) if carried else value

    def bias_of(got):
        return got[rows:rows + half_rows].astype(jnp.float32) + got[
            rows + half_rows:rows + 2 * half_rows
        ].astype(jnp.float32)

    half_rows = bias_part.shape[0]
    parts = [None] * (depth + 1)
    down = [None] * (depth + 1)
    across = [None] * (depth + 1)
    keeps = [None] * (depth + 1)

    def products(step):
        nonlocal bias_total
        keep, send = level_gradients(depth - step, rank, span, p_all, ds_all, q_all, do_t)
        if step == depth and carried:
            got = swapped(jnp.concatenate([send, bias_rows(bias_total)], axis=0), 1)
            bias_total = bias_total + bias_of(got[rows:])
            got = got[:2 * rows]
        else:
            got = swapped(send, 1)
        both = keep + got.astype(jnp.float32)
        keeps[step] = both[:rows]
        away = both[rows:].astype(jnp.bfloat16)
        across[step] = swapped(joined(away) if step == depth else away, 2)

    def collected(step):
        nonlocal bias_total
        if step == depth and carried:
            bias_total = bias_total + bias_of(across[step])
        parts[step] = keeps[step] + across[step][:rows].astype(jnp.float32)
        if step == 0:
            return
        sent = parts[step].astype(jnp.bfloat16)
        if carried:
            sent = joined(sent)
            down[step] = rotated(sent, -LEVEL * step)
        else:
            down[step] = shifted(sent, -LEVEL * step)
        if step > 1:
            across[step - 1], _ = lax.optimization_barrier((across[step - 1], sent))

    for step in range(depth, -1, -1):
        if step + 2 <= depth:
            across[step + 2], p_all = lax.optimization_barrier((across[step + 2], p_all))
        products(step)
    for step in range(depth, -1, -1):
        collected(step)
    if carried:
        bias_total = (
            bias_total + rotated(bias_total, LEVEL) + bias_of(down[1]) + bias_of(down[2])
        )
    else:
        bit = 1
        while bit < shards:
            bias_total = bias_total + swapped(bias_total, bit)
            bit *= 2
    bias_total = bias_total.reshape(-1)[:query_bias.shape[0]]
    down = [None if part is None else part[:rows] for part in down]
    total = parts[0]
    for step in range(depth, 0, -1):
        total = total + down[step].astype(jnp.float32)
    total = total.astype(jnp.bfloat16)
    half = KEY_VALUE_HEADS * HEAD_SIZE
    return (
        attended[None],
        grad_query[None],
        total[:, :half][None],
        total[:, half:][None],
        bias_total,
    )


def solution(mesh):
    placed = (
        P("dp", "ctx", None),
        P("dp", "ctx", None),
        P("dp", "ctx", None),
        P("dp", "ctx", None),
        P("dp", "ctx"),
        P(),
    )
    return jax.shard_map(
        local,
        mesh=mesh,
        in_specs=placed,
        out_specs=(
            P("dp", "ctx", None),
            P("dp", "ctx", None),
            P("dp", "ctx", None),
            P("dp", "ctx", None),
            P(),
        ),
        check_vma=False,
    )
```

```python
import functools
import math

import jax
import jax.numpy as jnp
from jax import lax
from jax.experimental import pallas as pl
from jax.experimental.pallas import tpu as pltpu
from jax.sharding import PartitionSpec as P

QUERY_HEADS = 14
KEY_VALUE_HEADS = 2
HEAD_SIZE = 128
GROUP_SIZE = 7
BLK = 128
WB = 16
DOC_ROWS = 16
PAIR = 4
LEVEL = 4
LANE_TILE = 256
KV_WIDTH = 2 * KEY_VALUE_HEADS * HEAD_SIZE
SCALE = 1.0 / math.sqrt(HEAD_SIZE)
SCALE_LOG2 = SCALE * math.log2(math.e)
LOW = -1e30

NT = (((1,), (1,)), ((), ()))


def fold(value, op):
    keys, lanes = value.shape
    return op(value.reshape(keys // 8, 8, lanes), axis=0)


def window_levels(shards):
    levels = max(shards // LEVEL, 1)
    return min((WB - 2 + LEVEL) // LEVEL, max(3 * levels // 4 - 1, 0) if levels % 4 == 0 else levels - 1)


def pack_kernel(key_hbm, value_hbm, docs_hbm, own_ref, docs, sems):
    rows = key_hbm.shape[0]
    half = key_hbm.shape[1]
    copies = [
        pltpu.make_async_copy(docs_hbm, docs, sems.at[0]),
        pltpu.make_async_copy(key_hbm, own_ref.at[0:rows, 0:half], sems.at[1]),
        pltpu.make_async_copy(value_hbm, own_ref.at[0:rows, half:2 * half], sems.at[2]),
    ]
    for copy in copies:
        copy.start()
    copies[0].wait()
    count = jnp.sum((docs[...] == 0).astype(jnp.float32), axis=1, keepdims=True)
    own_ref[rows:rows + DOC_ROWS, :] = jnp.broadcast_to(count, (DOC_ROWS, 2 * half)).astype(
        jnp.bfloat16
    )
    copies[1].wait()
    copies[2].wait()


def pack(key_in, value_input, doc_ids):
    rows, half = key_in.shape
    return pl.pallas_call(
        pack_kernel,
        out_shape=jax.ShapeDtypeStruct((rows + DOC_ROWS, 2 * half), jnp.bfloat16),
        in_specs=[pl.BlockSpec(memory_space=pltpu.HBM)] * 3,
        out_specs=pl.BlockSpec(memory_space=pltpu.VMEM),
        scratch_shapes=[pltpu.VMEM((1, rows), jnp.int32), pltpu.SemaphoreType.DMA((3,))],
        compiler_params=pltpu.CompilerParams(vmem_limit_bytes=8 * 1024 * 1024),
        name="pack",
    )(key_in, value_input, doc_ids)


def head_columns(g, n):
    head = g * GROUP_SIZE + n
    return slice(head * HEAD_SIZE, (head + 1) * HEAD_SIZE)


def prepare_kernel(q_hbm, bias_ref, do_hbm, q_st, do_t, q_buf, do_buf, sems):
    rows = q_buf.shape[0]
    first = pltpu.make_async_copy(q_hbm, q_buf, sems.at[0])
    second = pltpu.make_async_copy(do_hbm, do_buf, sems.at[1])
    first.start()
    second.start()
    first.wait()
    for g in range(KEY_VALUE_HEADS):
        for n in range(GROUP_SIZE):
            columns = head_columns(g, n)
            q_st[g, n * rows:(n + 1) * rows, :] = (
                q_buf[:, columns].astype(jnp.float32) + bias_ref[:, columns]
            ).astype(jnp.bfloat16)
    second.wait()
    for g in range(KEY_VALUE_HEADS):
        for n in range(GROUP_SIZE):
            do_t[g, :, n * rows:(n + 1) * rows] = do_buf[:, head_columns(g, n)].T


def prepare(query_in, query_bias, output_gradient):
    rows, width = query_in.shape
    lanes = GROUP_SIZE * rows
    anywhere = pl.BlockSpec(memory_space=pltpu.HBM)
    vmem = pl.BlockSpec(memory_space=pltpu.VMEM)
    return pl.pallas_call(
        prepare_kernel,
        out_shape=(
            jax.ShapeDtypeStruct((KEY_VALUE_HEADS, lanes, HEAD_SIZE), jnp.bfloat16),
            jax.ShapeDtypeStruct((KEY_VALUE_HEADS, HEAD_SIZE, lanes), jnp.bfloat16),
        ),
        in_specs=[anywhere, vmem, anywhere],
        out_specs=(vmem, vmem),
        scratch_shapes=[
            pltpu.VMEM((rows, width), jnp.bfloat16),
            pltpu.VMEM((rows, width), jnp.bfloat16),
            pltpu.SemaphoreType.DMA((2,)),
        ],
        compiler_params=pltpu.CompilerParams(vmem_limit_bytes=8 * 1024 * 1024),
        cost_estimate=pl.CostEstimate(
            flops=4 * rows * width, bytes_accessed=8 * rows * width, transcendentals=0
        ),
        name="prepare",
    )(query_in, query_bias, output_gradient)


def kernel(
    rank_ref, q_all, do_all, column_ref, core_ref,
    att_ref, dq_ref, p_buf, ds_buf, do_t, gb_ref, span_ref,
    kv_buf, s_buf, m_buf, l_buf, acc, dq_acc,
):
    rows = att_ref.shape[0]
    slots = p_buf.shape[0]
    packed = kv_buf.shape[1]
    depth = slots * PAIR // LEVEL - 1
    chunk = PAIR * rows
    lanes = GROUP_SIZE * rows
    tiles = [(at, min(at + LANE_TILE, lanes)) for at in range(0, lanes, LANE_TILE)]
    rank = rank_ref[0]
    inner = rank % LEVEL
    my_core = inner % 2
    my_x = inner // 2
    window = (rank // LEVEL - depth) * LEVEL

    for level in range(depth + 1):
        below = LEVEL * (depth - level)
        for x_at in range(2):
            at = (x_at * (depth + 1) + level) * packed
            place = below + 2 * (my_x + x_at - 2 * my_x * x_at)
            kv_buf[place + my_core] = column_ref[at:at + packed, :]
            kv_buf[place + 1 - my_core] = core_ref[at:at + packed, :]

    counts = kv_buf[:, rows:rows + DOC_ROWS, 0:128].astype(jnp.float32)
    boundary = jnp.sum(counts) * (1.0 / (DOC_ROWS * 128))
    boundary = (boundary + 0.5).astype(jnp.int32) + jnp.maximum(window, 0) * rows
    q_first = rank * rows
    low_block = jnp.maximum(rank - (WB - 1), 0)
    low_block = jnp.where(q_first >= boundary, jnp.maximum(low_block, boundary // rows), low_block)
    low = jnp.maximum(low_block - window, 0) // PAIR
    high = (rank - window) // PAIR + 1
    span_ref[0] = low
    span_ref[1] = high

    m_buf[...] = jnp.full_like(m_buf, LOW)
    l_buf[...] = jnp.zeros_like(l_buf)
    acc[...] = jnp.zeros_like(acc)
    dq_acc[...] = jnp.zeros_like(dq_acc)

    def keys_of(c, column):
        return jnp.concatenate(
            [kv_buf[PAIR * c + i, 0:rows, column:column + HEAD_SIZE] for i in range(PAIR)], axis=0
        )

    def score_steps(c, g):
        key_first = window * rows + c * chunk
        key_pos = key_first + lax.broadcasted_iota(jnp.int32, (chunk, rows), 0)
        query_pos = q_first + lax.broadcasted_iota(jnp.int32, (chunk, rows), 1)
        allowed = (key_pos <= query_pos) & (query_pos // BLK - key_pos // BLK < WB)
        allowed = allowed & ((key_pos >= boundary) == (query_pos >= boundary))
        bias = jnp.where(allowed, 0.0, LOW)
        k_c = keys_of(c, g * HEAD_SIZE)

        def step(a, b):
            s = lax.dot_general(k_c, q_all[g, a:b, :], NT, preferred_element_type=jnp.float32)
            s = s + jnp.concatenate([bias] * ((b - a) // rows), axis=1)
            s_buf[c, :, a:b] = s
            m_buf[g, :, a:b] = jnp.maximum(m_buf[g, :, a:b], fold(s, jnp.max))

        return step

    def weight_steps(c, g, row_max):
        v_t = keys_of(c, (KEY_VALUE_HEADS + g) * HEAD_SIZE).T

        def step(a, b):
            p = jnp.exp2(s_buf[c, :, a:b] * SCALE_LOG2 - row_max[:, a:b])
            l_buf[g, :, a:b] += fold(p, jnp.sum)
            p_bf = p.astype(jnp.bfloat16)
            p_buf[c, :, g * lanes + a:g * lanes + b] = p_bf
            acc[g, :, a:b] += jnp.dot(v_t, p_bf, preferred_element_type=jnp.float32)

        return step

    def gradient_steps(c, g, row_dot):
        v_c = keys_of(c, (KEY_VALUE_HEADS + g) * HEAD_SIZE)
        k_t = keys_of(c, g * HEAD_SIZE).T

        def step(a, b):
            d_p = jnp.dot(v_c, do_t[g, :, a:b], preferred_element_type=jnp.float32)
            p = p_buf[c, :, g * lanes + a:g * lanes + b].astype(jnp.float32)
            d_s = (p * (d_p - row_dot[:, a:b])).astype(jnp.bfloat16)
            ds_buf[c, :, g * lanes + a:g * lanes + b] = d_s
            dq_acc[g, :, a:b] += jnp.dot(k_t, d_s, preferred_element_type=jnp.float32)

        return step

    def row_maximum(g):
        return jnp.max(m_buf[g], axis=0, keepdims=True) * SCALE_LOG2

    def finish_rows(g):
        inverse = 1.0 / jnp.sum(l_buf[g], axis=0, keepdims=True)
        for n in range(GROUP_SIZE):
            at = slice(n * rows, (n + 1) * rows)
            att = (acc[g, :, at] * inverse[:, at]).astype(jnp.bfloat16)
            att_ref[:, head_columns(g, n)] = att.T
            do_n = do_all[g, :, at].astype(jnp.float32)
            dot_n = jnp.sum(do_n * att.astype(jnp.float32), axis=0, keepdims=True)
            m_buf[g, 0:1, at] = dot_n * inverse[:, at]
            do_t[g, :, at] = (do_n * inverse[:, at]).astype(jnp.bfloat16)

    def over_chunks(*makers):
        @pl.loop(low, high)
        def _(c):
            steps = [make(c) for make in makers]
            for a, b in tiles:
                for step in steps:
                    step(a, b)

    over_chunks(lambda c: score_steps(c, 0))
    for g in range(KEY_VALUE_HEADS):
        row_max = row_maximum(g)
        makers = [lambda c: weight_steps(c, g, row_max)]
        if g:
            row_dot = m_buf[g - 1, 0:1, :]
            makers.append(lambda c: gradient_steps(c, g - 1, row_dot))
        if g + 1 < KEY_VALUE_HEADS:
            makers.append(lambda c: score_steps(c, g + 1))
        over_chunks(*makers)
        finish_rows(g)
    row_dot = m_buf[KEY_VALUE_HEADS - 1, 0:1, :]
    over_chunks(lambda c: gradient_steps(c, KEY_VALUE_HEADS - 1, row_dot))

    gb_ref[...] = jnp.zeros_like(gb_ref)
    for g in range(KEY_VALUE_HEADS):
        for n in range(GROUP_SIZE):
            columns = head_columns(g, n)
            d_q = (dq_acc[g, :, n * rows:(n + 1) * rows] * SCALE).astype(jnp.bfloat16).T
            row, at = divmod(columns.start, KV_WIDTH)
            gb_ref[row:row + 1, at:at + HEAD_SIZE] = jnp.sum(
                d_q.astype(jnp.float32), axis=0, keepdims=True
            )
            dq_ref[:, columns] = d_q


def attention(rank, q_all, do_all, column, core_column, depth):
    rows = q_all.shape[1] // GROUP_SIZE
    width = QUERY_HEADS * HEAD_SIZE
    packed = rows + DOC_ROWS
    lanes = GROUP_SIZE * rows
    chunk = PAIR * rows
    slots = (depth + 1) * LEVEL // PAIR
    vmem = pl.BlockSpec(memory_space=pltpu.VMEM)
    smem = pl.BlockSpec(memory_space=pltpu.SMEM)
    products = 5 * 2 * width * HEAD_SIZE * slots * chunk
    return pl.pallas_call(
        kernel,
        out_shape=(
            jax.ShapeDtypeStruct((rows, width), jnp.bfloat16),
            jax.ShapeDtypeStruct((rows, width), jnp.bfloat16),
            jax.ShapeDtypeStruct((slots, chunk, KEY_VALUE_HEADS * lanes), jnp.bfloat16),
            jax.ShapeDtypeStruct((slots, chunk, KEY_VALUE_HEADS * lanes), jnp.bfloat16),
            jax.ShapeDtypeStruct((KEY_VALUE_HEADS, HEAD_SIZE, lanes), jnp.bfloat16),
            jax.ShapeDtypeStruct((-(-width // KV_WIDTH), KV_WIDTH), jnp.float32),
            jax.ShapeDtypeStruct((2,), jnp.int32),
        ),
        in_specs=[smem] + [vmem] * 4,
        out_specs=(vmem,) * 6 + (smem,),
        scratch_shapes=[
            pltpu.VMEM(((depth + 1) * LEVEL, packed, KV_WIDTH), jnp.bfloat16),
            pltpu.VMEM((slots, chunk, lanes), jnp.float32),
            pltpu.VMEM((KEY_VALUE_HEADS, 8, lanes), jnp.float32),
            pltpu.VMEM((KEY_VALUE_HEADS, 8, lanes), jnp.float32),
            pltpu.VMEM((KEY_VALUE_HEADS, HEAD_SIZE, lanes), jnp.float32),
            pltpu.VMEM((KEY_VALUE_HEADS, HEAD_SIZE, lanes), jnp.float32),
        ],
        compiler_params=pltpu.CompilerParams(vmem_limit_bytes=36 * 1024 * 1024),
        cost_estimate=pl.CostEstimate(
            flops=products, bytes_accessed=8 * rows * width, transcendentals=0
        ),
        name="attention",
    )(rank, q_all, do_all, column, core_column)


def level_kernel(level, rank_ref, span_ref, p_buf, ds_buf, q_all, do_t, keep_ref, send_ref):
    chunk = p_buf.shape[1]
    rows = chunk // PAIR
    lanes = GROUP_SIZE * rows
    inner = rank_ref[0] % LEVEL
    my_core = inner % 2
    my_x = inner // 2
    active = (level >= span_ref[0]) & (level < span_ref[1])

    @pl.when(active)
    def _():
        for g in range(KEY_VALUE_HEADS):
            where = slice(g * lanes, (g + 1) * lanes)
            d_key = jnp.dot(
                ds_buf[level, :, where], q_all[g], preferred_element_type=jnp.float32
            ) * SCALE
            d_value = lax.dot_general(
                p_buf[level, :, where], do_t[g], NT, preferred_element_type=jnp.float32
            )
            for value, column in ((d_key, g), (d_value, KEY_VALUE_HEADS + g)):
                columns = slice(column * HEAD_SIZE, (column + 1) * HEAD_SIZE)
                for x_at in range(2):
                    first = value[2 * x_at * rows:(2 * x_at + 1) * rows]
                    second = value[(2 * x_at + 1) * rows:(2 * x_at + 2) * rows]
                    place = (x_at + my_x) % 2
                    at = pl.ds(pl.multiple_of(place * rows, rows), rows)
                    keep_ref[at, columns] = jnp.where(my_core == 0, first, second)
                    send_ref[at, columns] = jnp.where(my_core == 0, second, first).astype(
                        jnp.bfloat16
                    )

    @pl.when(jnp.logical_not(active))
    def _():
        keep_ref[...] = jnp.zeros_like(keep_ref)
        send_ref[...] = jnp.zeros_like(send_ref)


def level_gradients(level, rank, span, p_all, ds_all, q_all, do_t):
    chunk, width = p_all.shape[1:]
    rows = chunk // PAIR
    vmem = pl.BlockSpec(memory_space=pltpu.VMEM)
    smem = pl.BlockSpec(memory_space=pltpu.SMEM)
    return pl.pallas_call(
        functools.partial(level_kernel, level),
        out_shape=(
            jax.ShapeDtypeStruct((2 * rows, KV_WIDTH), jnp.float32),
            jax.ShapeDtypeStruct((2 * rows, KV_WIDTH), jnp.bfloat16),
        ),
        in_specs=[smem, smem] + [vmem] * 4,
        out_specs=(vmem, vmem),
        compiler_params=pltpu.CompilerParams(vmem_limit_bytes=36 * 1024 * 1024),
        cost_estimate=pl.CostEstimate(
            flops=2 * 2 * LEVEL * rows * width * HEAD_SIZE,
            bytes_accessed=4 * LEVEL * rows * width,
            transcendentals=0,
        ),
        name="level_gradients",
    )(rank, span, p_all, ds_all, q_all, do_t)


def shifted(value, steps):
    count = lax.axis_size("ctx")
    first, last = max(0, -steps), min(count, count - steps)
    return lax.ppermute(value, "ctx", [(at, at + steps) for at in range(first, last)])


def rotated(value, steps):
    count = lax.axis_size("ctx")
    return lax.ppermute(value, "ctx", [(at, (at + steps) % count) for at in range(count)])


def swapped(value, bit, axis="ctx"):
    return lax.ppermute(value, axis, [(at, at ^ bit) for at in range(lax.axis_size(axis))])


def bias_rows(rows):
    high = lax.reduce_precision(rows, 8, 7)
    both = jnp.concatenate([high, rows - high]).astype(jnp.bfloat16)
    return jnp.pad(both, ((0, -both.shape[0] % 16), (0, 0)))


def local(query_in, key_in, value_input, output_gradient, doc_ids, query_bias):
    rows = query_in.shape[1]
    shards = lax.axis_size("ctx")
    depth = window_levels(shards)
    rank = lax.axis_index("ctx").astype(jnp.int32)
    own = pack(key_in[0], value_input[0], doc_ids)

    ups = [shifted(own, LEVEL * step) for step in range(depth, 0, -1)][::-1]
    x_own = swapped(own, 2)
    q_all, do_all = prepare(query_in[0], query_bias[None], output_gradient[0])
    up = jnp.concatenate(ups, axis=0)
    up, x_own, q_all, do_all = lax.optimization_barrier((up, x_own, q_all, do_all))
    x_up = swapped(up, 2)
    column = jnp.concatenate([own, up, x_own, x_up], axis=0)
    core_column = swapped(column, 1)

    rank = rank.reshape(1)
    attended, grad_query, p_all, ds_all, do_t, bias_part, span = attention(
        rank, q_all, do_all, column, core_column, depth
    )

    levels = shards // LEVEL
    carried = levels == 4 and depth == 2
    bit = 1
    while bit < lax.axis_size("dp"):
        bias_part = bias_part + swapped(bias_part, bit, "dp")
        bit *= 2
    bias_total = bias_part

    def joined(value):
        return jnp.concatenate([value, bias_rows(bias_total)], axis=0) if carried else value

    def bias_of(got):
        return got[rows:rows + half_rows].astype(jnp.float32) + got[
            rows + half_rows:rows + 2 * half_rows
        ].astype(jnp.float32)

    half_rows = bias_part.shape[0]
    parts = [None] * (depth + 1)
    down = [None] * (depth + 1)
    across = [None] * (depth + 1)
    keeps = [None] * (depth + 1)

    def products(step):
        nonlocal bias_total
        keep, send = level_gradients(depth - step, rank, span, p_all, ds_all, q_all, do_t)
        if step == depth and carried:
            got = swapped(jnp.concatenate([send, bias_rows(bias_total)], axis=0), 1)
            bias_total = bias_total + bias_of(got[rows:])
            got = got[:2 * rows]
        else:
            got = swapped(send, 1)
        both = keep + got.astype(jnp.float32)
        keeps[step] = both[:rows]
        away = both[rows:].astype(jnp.bfloat16)
        across[step] = swapped(joined(away) if step == depth else away, 2)

    def collected(step):
        nonlocal bias_total
        if step == depth and carried:
            bias_total = bias_total + bias_of(across[step])
        parts[step] = keeps[step] + across[step][:rows].astype(jnp.float32)
        if step == 0:
            return
        sent = parts[step].astype(jnp.bfloat16)
        if carried:
            sent = joined(sent)
            down[step] = rotated(sent, -LEVEL * step)
        else:
            down[step] = shifted(sent, -LEVEL * step)
        if step > 1:
            across[step - 1], _ = lax.optimization_barrier((across[step - 1], sent))

    for step in range(depth, -1, -1):
        if step + 2 <= depth:
            across[step + 2], p_all = lax.optimization_barrier((across[step + 2], p_all))
        products(step)
    for step in range(depth, -1, -1):
        collected(step)
    if carried:
        bias_total = (
            bias_total + rotated(bias_total, LEVEL) + bias_of(down[1]) + bias_of(down[2])
        )
    else:
        bit = 1
        while bit < shards:
            bias_total = bias_total + swapped(bias_total, bit)
            bit *= 2
    bias_total = bias_total.reshape(-1)[:query_bias.shape[0]]
    down = [None if part is None else part[:rows] for part in down]
    total = parts[0]
    for step in range(depth, 0, -1):
        total = total + down[step].astype(jnp.float32)
    total = total.astype(jnp.bfloat16)
    half = KEY_VALUE_HEADS * HEAD_SIZE
    return (
        attended[None],
        grad_query[None],
        total[:, :half][None],
        total[:, half:][None],
        bias_total,
    )


def solution(mesh):
    placed = (
        P("dp", "ctx", None),
        P("dp", "ctx", None),
        P("dp", "ctx", None),
        P("dp", "ctx", None),
        P("dp", "ctx"),
        P(),
    )
    return jax.shard_map(
        local,
        mesh=mesh,
        in_specs=placed,
        out_specs=(
            P("dp", "ctx", None),
            P("dp", "ctx", None),
            P("dp", "ctx", None),
            P("dp", "ctx", None),
            P(),
        ),
        check_vma=False,
    )
```

```python
import functools
import math

import jax
import jax.numpy as jnp
from jax import lax
from jax.experimental import pallas as pl
from jax.experimental.pallas import tpu as pltpu
from jax.sharding import PartitionSpec as P

QUERY_HEADS = 14
KEY_VALUE_HEADS = 2
HEAD_SIZE = 128
GROUP_SIZE = 7
BLK = 128
WB = 16
DOC_ROWS = 16
PAIR = 4
LEVEL = 4
LANE_TILE = 256
KV_WIDTH = 2 * KEY_VALUE_HEADS * HEAD_SIZE
SCALE = 1.0 / math.sqrt(HEAD_SIZE)
SCALE_LOG2 = SCALE * math.log2(math.e)
LOW = -1e30

NT = (((1,), (1,)), ((), ()))


def fold(value, op):
    keys, lanes = value.shape
    return op(value.reshape(keys // 8, 8, lanes), axis=0)


def window_levels(shards):
    levels = max(shards // LEVEL, 1)
    return min((WB - 2 + LEVEL) // LEVEL, max(3 * levels // 4 - 1, 0) if levels % 4 == 0 else levels - 1)


def head_columns(g, n):
    head = g * GROUP_SIZE + n
    return slice(head * HEAD_SIZE, (head + 1) * HEAD_SIZE)


def prepare_kernel(q_hbm, bias_ref, do_hbm, q_st, do_t, q_buf, do_buf, sems):
    rows = q_buf.shape[0]
    first = pltpu.make_async_copy(q_hbm, q_buf, sems.at[0])
    second = pltpu.make_async_copy(do_hbm, do_buf, sems.at[1])
    first.start()
    second.start()
    first.wait()
    for g in range(KEY_VALUE_HEADS):
        for n in range(GROUP_SIZE):
            columns = head_columns(g, n)
            q_st[g, n * rows:(n + 1) * rows, :] = (
                q_buf[:, columns].astype(jnp.float32) + bias_ref[:, columns]
            ).astype(jnp.bfloat16)
    second.wait()
    for g in range(KEY_VALUE_HEADS):
        for n in range(GROUP_SIZE):
            do_t[g, :, n * rows:(n + 1) * rows] = do_buf[:, head_columns(g, n)].T


def prepare(query_in, query_bias, output_gradient):
    rows, width = query_in.shape
    lanes = GROUP_SIZE * rows
    anywhere = pl.BlockSpec(memory_space=pltpu.HBM)
    vmem = pl.BlockSpec(memory_space=pltpu.VMEM)
    return pl.pallas_call(
        prepare_kernel,
        out_shape=(
            jax.ShapeDtypeStruct((KEY_VALUE_HEADS, lanes, HEAD_SIZE), jnp.bfloat16),
            jax.ShapeDtypeStruct((KEY_VALUE_HEADS, HEAD_SIZE, lanes), jnp.bfloat16),
        ),
        in_specs=[anywhere, vmem, anywhere],
        out_specs=(vmem, vmem),
        scratch_shapes=[
            pltpu.VMEM((rows, width), jnp.bfloat16),
            pltpu.VMEM((rows, width), jnp.bfloat16),
            pltpu.SemaphoreType.DMA((2,)),
        ],
        compiler_params=pltpu.CompilerParams(vmem_limit_bytes=8 * 1024 * 1024),
        cost_estimate=pl.CostEstimate(
            flops=4 * rows * width, bytes_accessed=8 * rows * width, transcendentals=0
        ),
        name="prepare",
    )(query_in, query_bias, output_gradient)


def kernel(
    rank_ref, q_all, do_all, near_ref, near_core_ref, far_ref, far_core_ref,
    att_ref, dq_ref, p_buf, ds_buf, do_t, gb_ref, span_ref,
    kv_buf, s_buf, m_buf, l_buf, acc, dq_acc,
):
    rows = att_ref.shape[0]
    slots = p_buf.shape[0]
    packed = kv_buf.shape[1]
    depth = slots * PAIR // LEVEL - 1
    chunk = PAIR * rows
    lanes = GROUP_SIZE * rows
    tiles = [(at, min(at + LANE_TILE, lanes)) for at in range(0, lanes, LANE_TILE)]
    rank = rank_ref[0]
    inner = rank % LEVEL
    my_core = inner % 2
    my_x = inner // 2
    window = (rank // LEVEL - depth) * LEVEL

    for level in range(depth + 1):
        below = LEVEL * (depth - level)
        here, there = (near_ref, near_core_ref) if level < depth else (far_ref, far_core_ref)
        for x_at in range(2):
            at = (2 * (level % depth) + x_at) * packed
            place = below + 2 * (my_x + x_at - 2 * my_x * x_at)
            kv_buf[place + my_core] = here[at:at + packed, :]
            kv_buf[place + 1 - my_core] = there[at:at + packed, :]

    counts = kv_buf[:, rows:rows + DOC_ROWS, 0:128].astype(jnp.float32)
    boundary = jnp.sum(counts) * (1.0 / (DOC_ROWS * 128))
    boundary = (boundary + 0.5).astype(jnp.int32) + jnp.maximum(window, 0) * rows
    q_first = rank * rows
    low_block = jnp.maximum(rank - (WB - 1), 0)
    low_block = jnp.where(q_first >= boundary, jnp.maximum(low_block, boundary // rows), low_block)
    low = jnp.maximum(low_block - window, 0) // PAIR
    high = (rank - window) // PAIR + 1
    span_ref[0] = low
    span_ref[1] = high

    m_buf[...] = jnp.full_like(m_buf, LOW)
    l_buf[...] = jnp.zeros_like(l_buf)
    acc[...] = jnp.zeros_like(acc)
    dq_acc[...] = jnp.zeros_like(dq_acc)

    def keys_of(c, column):
        return jnp.concatenate(
            [kv_buf[PAIR * c + i, 0:rows, column:column + HEAD_SIZE] for i in range(PAIR)], axis=0
        )

    def score_steps(c, g):
        key_first = window * rows + c * chunk
        key_pos = key_first + lax.broadcasted_iota(jnp.int32, (chunk, rows), 0)
        query_pos = q_first + lax.broadcasted_iota(jnp.int32, (chunk, rows), 1)
        allowed = (key_pos <= query_pos) & (query_pos // BLK - key_pos // BLK < WB)
        allowed = allowed & ((key_pos >= boundary) == (query_pos >= boundary))
        bias = jnp.where(allowed, 0.0, LOW)
        k_c = keys_of(c, g * HEAD_SIZE)

        def step(a, b):
            s = lax.dot_general(k_c, q_all[g, a:b, :], NT, preferred_element_type=jnp.float32)
            s = s + jnp.concatenate([bias] * ((b - a) // rows), axis=1)
            s_buf[c, :, a:b] = s
            m_buf[g, :, a:b] = jnp.maximum(m_buf[g, :, a:b], fold(s, jnp.max))

        return step

    def weight_steps(c, g, row_max):
        v_t = keys_of(c, (KEY_VALUE_HEADS + g) * HEAD_SIZE).T

        def step(a, b):
            p = jnp.exp2(s_buf[c, :, a:b] * SCALE_LOG2 - row_max[:, a:b])
            l_buf[g, :, a:b] += fold(p, jnp.sum)
            p_bf = p.astype(jnp.bfloat16)
            p_buf[c, :, g * lanes + a:g * lanes + b] = p_bf
            acc[g, :, a:b] += jnp.dot(v_t, p_bf, preferred_element_type=jnp.float32)

        return step

    def gradient_steps(c, g, row_dot):
        v_c = keys_of(c, (KEY_VALUE_HEADS + g) * HEAD_SIZE)
        k_t = keys_of(c, g * HEAD_SIZE).T

        def step(a, b):
            d_p = jnp.dot(v_c, do_t[g, :, a:b], preferred_element_type=jnp.float32)
            p = p_buf[c, :, g * lanes + a:g * lanes + b].astype(jnp.float32)
            d_s = (p * (d_p - row_dot[:, a:b])).astype(jnp.bfloat16)
            ds_buf[c, :, g * lanes + a:g * lanes + b] = d_s
            dq_acc[g, :, a:b] += jnp.dot(k_t, d_s, preferred_element_type=jnp.float32)

        return step

    def row_maximum(g):
        return jnp.max(m_buf[g], axis=0, keepdims=True) * SCALE_LOG2

    def finish_rows(g):
        inverse = 1.0 / jnp.sum(l_buf[g], axis=0, keepdims=True)
        for n in range(GROUP_SIZE):
            at = slice(n * rows, (n + 1) * rows)
            att = (acc[g, :, at] * inverse[:, at]).astype(jnp.bfloat16)
            att_ref[:, head_columns(g, n)] = att.T
            do_n = do_all[g, :, at].astype(jnp.float32)
            dot_n = jnp.sum(do_n * att.astype(jnp.float32), axis=0, keepdims=True)
            m_buf[g, 0:1, at] = dot_n * inverse[:, at]
            do_t[g, :, at] = (do_n * inverse[:, at]).astype(jnp.bfloat16)

    def over_chunks(*makers):
        @pl.loop(low, high)
        def _(c):
            steps = [make(c) for make in makers]
            for a, b in tiles:
                for step in steps:
                    step(a, b)

    over_chunks(lambda c: score_steps(c, 0))
    for g in range(KEY_VALUE_HEADS):
        row_max = row_maximum(g)
        makers = [lambda c: weight_steps(c, g, row_max)]
        if g:
            row_dot = m_buf[g - 1, 0:1, :]
            makers.append(lambda c: gradient_steps(c, g - 1, row_dot))
        if g + 1 < KEY_VALUE_HEADS:
            makers.append(lambda c: score_steps(c, g + 1))
        over_chunks(*makers)
        finish_rows(g)
    row_dot = m_buf[KEY_VALUE_HEADS - 1, 0:1, :]
    over_chunks(lambda c: gradient_steps(c, KEY_VALUE_HEADS - 1, row_dot))

    gb_ref[...] = jnp.zeros_like(gb_ref)
    for g in range(KEY_VALUE_HEADS):
        for n in range(GROUP_SIZE):
            columns = head_columns(g, n)
            d_q = (dq_acc[g, :, n * rows:(n + 1) * rows] * SCALE).astype(jnp.bfloat16).T
            row, at = divmod(columns.start, KV_WIDTH)
            gb_ref[row:row + 1, at:at + HEAD_SIZE] = jnp.sum(
                d_q.astype(jnp.float32), axis=0, keepdims=True
            )
            dq_ref[:, columns] = d_q


def attention(rank, q_all, do_all, near, near_core, far, far_core, depth):
    rows = q_all.shape[1] // GROUP_SIZE
    width = QUERY_HEADS * HEAD_SIZE
    packed = rows + DOC_ROWS
    lanes = GROUP_SIZE * rows
    chunk = PAIR * rows
    slots = (depth + 1) * LEVEL // PAIR
    vmem = pl.BlockSpec(memory_space=pltpu.VMEM)
    smem = pl.BlockSpec(memory_space=pltpu.SMEM)
    products = 5 * 2 * width * HEAD_SIZE * slots * chunk
    return pl.pallas_call(
        kernel,
        out_shape=(
            jax.ShapeDtypeStruct((rows, width), jnp.bfloat16),
            jax.ShapeDtypeStruct((rows, width), jnp.bfloat16),
            jax.ShapeDtypeStruct((slots, chunk, KEY_VALUE_HEADS * lanes), jnp.bfloat16),
            jax.ShapeDtypeStruct((slots, chunk, KEY_VALUE_HEADS * lanes), jnp.bfloat16),
            jax.ShapeDtypeStruct((KEY_VALUE_HEADS, HEAD_SIZE, lanes), jnp.bfloat16),
            jax.ShapeDtypeStruct((-(-width // KV_WIDTH), KV_WIDTH), jnp.float32),
            jax.ShapeDtypeStruct((2,), jnp.int32),
        ),
        in_specs=[smem] + [vmem] * 6,
        out_specs=(vmem,) * 6 + (smem,),
        scratch_shapes=[
            pltpu.VMEM(((depth + 1) * LEVEL, packed, KV_WIDTH), jnp.bfloat16),
            pltpu.VMEM((slots, chunk, lanes), jnp.float32),
            pltpu.VMEM((KEY_VALUE_HEADS, 8, lanes), jnp.float32),
            pltpu.VMEM((KEY_VALUE_HEADS, 8, lanes), jnp.float32),
            pltpu.VMEM((KEY_VALUE_HEADS, HEAD_SIZE, lanes), jnp.float32),
            pltpu.VMEM((KEY_VALUE_HEADS, HEAD_SIZE, lanes), jnp.float32),
        ],
        compiler_params=pltpu.CompilerParams(vmem_limit_bytes=36 * 1024 * 1024),
        cost_estimate=pl.CostEstimate(
            flops=products, bytes_accessed=8 * rows * width, transcendentals=0
        ),
        name="attention",
    )(rank, q_all, do_all, near, near_core, far, far_core)


def level_kernel(level, rank_ref, span_ref, p_buf, ds_buf, q_all, do_t, keep_ref, send_ref):
    chunk = p_buf.shape[1]
    rows = chunk // PAIR
    lanes = GROUP_SIZE * rows
    inner = rank_ref[0] % LEVEL
    my_core = inner % 2
    my_x = inner // 2
    active = (level >= span_ref[0]) & (level < span_ref[1])

    @pl.when(active)
    def _():
        for g in range(KEY_VALUE_HEADS):
            where = slice(g * lanes, (g + 1) * lanes)
            d_key = jnp.dot(
                ds_buf[level, :, where], q_all[g], preferred_element_type=jnp.float32
            ) * SCALE
            d_value = lax.dot_general(
                p_buf[level, :, where], do_t[g], NT, preferred_element_type=jnp.float32
            )
            for value, column in ((d_key, g), (d_value, KEY_VALUE_HEADS + g)):
                columns = slice(column * HEAD_SIZE, (column + 1) * HEAD_SIZE)
                for x_at in range(2):
                    first = value[2 * x_at * rows:(2 * x_at + 1) * rows]
                    second = value[(2 * x_at + 1) * rows:(2 * x_at + 2) * rows]
                    place = (x_at + my_x) % 2
                    at = pl.ds(pl.multiple_of(place * rows, rows), rows)
                    keep_ref[at, columns] = jnp.where(my_core == 0, first, second)
                    send_ref[at, columns] = jnp.where(my_core == 0, second, first).astype(
                        jnp.bfloat16
                    )

    @pl.when(jnp.logical_not(active))
    def _():
        keep_ref[...] = jnp.zeros_like(keep_ref)
        send_ref[...] = jnp.zeros_like(send_ref)


def level_gradients(level, rank, span, p_all, ds_all, q_all, do_t):
    chunk, width = p_all.shape[1:]
    rows = chunk // PAIR
    vmem = pl.BlockSpec(memory_space=pltpu.VMEM)
    smem = pl.BlockSpec(memory_space=pltpu.SMEM)
    return pl.pallas_call(
        functools.partial(level_kernel, level),
        out_shape=(
            jax.ShapeDtypeStruct((2 * rows, KV_WIDTH), jnp.float32),
            jax.ShapeDtypeStruct((2 * rows, KV_WIDTH), jnp.bfloat16),
        ),
        in_specs=[smem, smem] + [vmem] * 4,
        out_specs=(vmem, vmem),
        compiler_params=pltpu.CompilerParams(vmem_limit_bytes=36 * 1024 * 1024),
        cost_estimate=pl.CostEstimate(
            flops=2 * 2 * LEVEL * rows * width * HEAD_SIZE,
            bytes_accessed=4 * LEVEL * rows * width,
            transcendentals=0,
        ),
        name="level_gradients",
    )(rank, span, p_all, ds_all, q_all, do_t)


def shifted(value, steps):
    count = lax.axis_size("ctx")
    first, last = max(0, -steps), min(count, count - steps)
    return lax.ppermute(value, "ctx", [(at, at + steps) for at in range(first, last)])


def rotated(value, steps):
    count = lax.axis_size("ctx")
    return lax.ppermute(value, "ctx", [(at, (at + steps) % count) for at in range(count)])


def swapped(value, bit, axis="ctx"):
    return lax.ppermute(value, axis, [(at, at ^ bit) for at in range(lax.axis_size(axis))])


def bias_rows(rows):
    high = lax.reduce_precision(rows, 8, 7)
    both = jnp.concatenate([high, rows - high]).astype(jnp.bfloat16)
    return jnp.pad(both, ((0, -both.shape[0] % 16), (0, 0)))


def local(query_in, key_in, value_input, output_gradient, doc_ids, query_bias):
    rows = query_in.shape[1]
    shards = lax.axis_size("ctx")
    depth = window_levels(shards)
    rank = lax.axis_index("ctx").astype(jnp.int32)
    count = jnp.sum((doc_ids == 0).astype(jnp.float32)).astype(jnp.bfloat16)
    own = (key_in[0], value_input[0], jnp.broadcast_to(count, (DOC_ROWS, KV_WIDTH)))

    def packed(shard):
        keys, values, counts = shard
        return jnp.concatenate([jnp.concatenate([keys, values], axis=1), counts], axis=0)

    up = packed([shifted(part, LEVEL) for part in own])
    x_own = packed([swapped(part, 2) for part in own])
    up, query_in, output_gradient = lax.optimization_barrier((up, query_in, output_gradient))
    near = [packed(own), x_own]
    for _ in range(depth - 1):
        near += [up, swapped(up, 2)]
        up = shifted(up, LEVEL)
    q_all, do_all = prepare(query_in[0], query_bias[None], output_gradient[0])
    up, q_all, do_all = lax.optimization_barrier((up, q_all, do_all))
    far = jnp.concatenate([up, swapped(up, 2)], axis=0)
    near = jnp.concatenate(near, axis=0)
    near_core = swapped(near, 1)
    far_core = swapped(far, 1)

    rank = rank.reshape(1)
    attended, grad_query, p_all, ds_all, do_t, bias_part, span = attention(
        rank, q_all, do_all, near, near_core, far, far_core, depth
    )

    levels = shards // LEVEL
    carried = levels == 4 and depth == 2
    bit = 1
    while bit < lax.axis_size("dp"):
        bias_part = bias_part + swapped(bias_part, bit, "dp")
        bit *= 2
    bias_total = bias_part

    def joined(value):
        return jnp.concatenate([value, bias_rows(bias_total)], axis=0) if carried else value

    def bias_of(got):
        return got[rows:rows + half_rows].astype(jnp.float32) + got[
            rows + half_rows:rows + 2 * half_rows
        ].astype(jnp.float32)

    half_rows = bias_part.shape[0]
    parts = [None] * (depth + 1)
    down = [None] * (depth + 1)
    across = [None] * (depth + 1)
    keeps = [None] * (depth + 1)
    aways = [None] * (depth + 1)

    def products(step):
        nonlocal bias_total, p_all
        keep, send = level_gradients(depth - step, rank, span, p_all, ds_all, q_all, do_t)
        if step:
            send, p_all = lax.optimization_barrier((send, p_all))
        if step == depth - 1:
            send, first_away = lax.optimization_barrier((send, aways[depth]))
            across[depth] = swapped(first_away, 2)
        if step == depth - 1 and carried:
            got = swapped(jnp.concatenate([send, bias_rows(bias_total)], axis=0), 1)
            bias_total = bias_total + bias_of(got[rows:])
            got = got[:2 * rows]
        else:
            got = swapped(send, 1)
        both = keep + got.astype(jnp.float32)
        keeps[step] = both[:rows]
        aways[step] = both[rows:].astype(jnp.bfloat16)
        if step < depth:
            across[step] = swapped(joined(aways[step]) if step == depth - 1 else aways[step], 2)

    def collected(step):
        nonlocal bias_total, p_all
        if step == depth - 1 and carried:
            bias_total = bias_total + bias_of(across[step])
        parts[step] = keeps[step] + across[step][:rows].astype(jnp.float32)
        if step == 0:
            return
        sent = parts[step].astype(jnp.bfloat16)
        if step == depth:
            sent, p_all = lax.optimization_barrier((sent, p_all))
        if step == depth - 1 and carried:
            sent = joined(sent)
            down[step] = rotated(sent, -LEVEL * step)
        else:
            down[step] = shifted(sent, -LEVEL * step)

    for step in range(depth, -1, -1):
        products(step)
        if step < depth:
            collected(step + 1)
    collected(0)
    if carried:
        bias_total = (
            bias_total
            + rotated(bias_total, LEVEL)
            + rotated(bias_total, 2 * LEVEL)
            + bias_of(down[1])
        )
    else:
        bit = 1
        while bit < shards:
            bias_total = bias_total + swapped(bias_total, bit)
            bit *= 2
    bias_total = bias_total.reshape(-1)[:query_bias.shape[0]]
    down = [None if part is None else part[:rows] for part in down]
    total = parts[0]
    for step in range(depth, 0, -1):
        total = total + down[step].astype(jnp.float32)
    total = total.astype(jnp.bfloat16)
    half = KEY_VALUE_HEADS * HEAD_SIZE
    return (
        attended[None],
        grad_query[None],
        total[:, :half][None],
        total[:, half:][None],
        bias_total,
    )


def solution(mesh):
    placed = (
        P("dp", "ctx", None),
        P("dp", "ctx", None),
        P("dp", "ctx", None),
        P("dp", "ctx", None),
        P("dp", "ctx"),
        P(),
    )
    return jax.shard_map(
        local,
        mesh=mesh,
        in_specs=placed,
        out_specs=(
            P("dp", "ctx", None),
            P("dp", "ctx", None),
            P("dp", "ctx", None),
            P("dp", "ctx", None),
            P(),
        ),
        check_vma=False,
    )
```

```python
import functools
import math

import jax
import jax.numpy as jnp
from jax import lax
from jax.experimental import pallas as pl
from jax.experimental.pallas import tpu as pltpu
from jax.sharding import PartitionSpec as P

QUERY_HEADS = 14
KEY_VALUE_HEADS = 2
HEAD_SIZE = 128
GROUP_SIZE = 7
BLK = 128
WB = 16
DOC_ROWS = 16
PAIR = 4
LEVEL = 4
LANE_TILE = 256
KV_WIDTH = 2 * KEY_VALUE_HEADS * HEAD_SIZE
SCALE = 1.0 / math.sqrt(HEAD_SIZE)
SCALE_LOG2 = SCALE * math.log2(math.e)
LOW = -1e30

NT = (((1,), (1,)), ((), ()))


def fold(value, op):
    keys, lanes = value.shape
    return op(value.reshape(keys // 8, 8, lanes), axis=0)


def window_levels(shards):
    levels = max(shards // LEVEL, 1)
    return min((WB - 2 + LEVEL) // LEVEL, max(3 * levels // 4 - 1, 0) if levels % 4 == 0 else levels - 1)


def pack_kernel(key_hbm, value_hbm, docs_hbm, own_ref, docs, sems):
    rows = key_hbm.shape[0]
    half = key_hbm.shape[1]
    copies = [
        pltpu.make_async_copy(docs_hbm, docs, sems.at[0]),
        pltpu.make_async_copy(key_hbm, own_ref.at[0:rows, 0:half], sems.at[1]),
        pltpu.make_async_copy(value_hbm, own_ref.at[0:rows, half:2 * half], sems.at[2]),
    ]
    for copy in copies:
        copy.start()
    copies[0].wait()
    count = jnp.sum((docs[...] == 0).astype(jnp.float32), axis=1, keepdims=True)
    own_ref[rows:rows + DOC_ROWS, :] = jnp.broadcast_to(count, (DOC_ROWS, 2 * half)).astype(
        jnp.bfloat16
    )
    copies[1].wait()
    copies[2].wait()


def pack(key_in, value_input, doc_ids):
    rows, half = key_in.shape
    return pl.pallas_call(
        pack_kernel,
        out_shape=jax.ShapeDtypeStruct((rows + DOC_ROWS, 2 * half), jnp.bfloat16),
        in_specs=[pl.BlockSpec(memory_space=pltpu.HBM)] * 3,
        out_specs=pl.BlockSpec(memory_space=pltpu.VMEM),
        scratch_shapes=[pltpu.VMEM((1, rows), jnp.int32), pltpu.SemaphoreType.DMA((3,))],
        compiler_params=pltpu.CompilerParams(vmem_limit_bytes=8 * 1024 * 1024),
        name="pack",
    )(key_in, value_input, doc_ids)


def head_columns(g, n):
    head = g * GROUP_SIZE + n
    return slice(head * HEAD_SIZE, (head + 1) * HEAD_SIZE)


def prepare_kernel(q_hbm, bias_ref, do_hbm, q_st, do_t, q_buf, do_buf, sems):
    rows = q_buf.shape[0]
    first = pltpu.make_async_copy(q_hbm, q_buf, sems.at[0])
    second = pltpu.make_async_copy(do_hbm, do_buf, sems.at[1])
    first.start()
    second.start()
    first.wait()
    for g in range(KEY_VALUE_HEADS):
        for n in range(GROUP_SIZE):
            columns = head_columns(g, n)
            q_st[g, n * rows:(n + 1) * rows, :] = (
                q_buf[:, columns].astype(jnp.float32) + bias_ref[:, columns]
            ).astype(jnp.bfloat16)
    second.wait()
    for g in range(KEY_VALUE_HEADS):
        for n in range(GROUP_SIZE):
            do_t[g, :, n * rows:(n + 1) * rows] = do_buf[:, head_columns(g, n)].T


def prepare(query_in, query_bias, output_gradient):
    rows, width = query_in.shape
    lanes = GROUP_SIZE * rows
    anywhere = pl.BlockSpec(memory_space=pltpu.HBM)
    vmem = pl.BlockSpec(memory_space=pltpu.VMEM)
    return pl.pallas_call(
        prepare_kernel,
        out_shape=(
            jax.ShapeDtypeStruct((KEY_VALUE_HEADS, lanes, HEAD_SIZE), jnp.bfloat16),
            jax.ShapeDtypeStruct((KEY_VALUE_HEADS, HEAD_SIZE, lanes), jnp.bfloat16),
        ),
        in_specs=[anywhere, vmem, anywhere],
        out_specs=(vmem, vmem),
        scratch_shapes=[
            pltpu.VMEM((rows, width), jnp.bfloat16),
            pltpu.VMEM((rows, width), jnp.bfloat16),
            pltpu.SemaphoreType.DMA((2,)),
        ],
        compiler_params=pltpu.CompilerParams(vmem_limit_bytes=8 * 1024 * 1024),
        cost_estimate=pl.CostEstimate(
            flops=4 * rows * width, bytes_accessed=8 * rows * width, transcendentals=0
        ),
        name="prepare",
    )(query_in, query_bias, output_gradient)


def kernel(
    rank_ref, q_all, do_all, column_ref, core_ref,
    att_ref, dq_ref, p_buf, ds_buf, do_t, gb_ref, span_ref,
    kv_buf, s_buf, m_buf, l_buf, acc, dq_acc,
):
    rows = att_ref.shape[0]
    slots = p_buf.shape[0]
    packed = kv_buf.shape[1]
    depth = slots * PAIR // LEVEL - 1
    chunk = PAIR * rows
    lanes = GROUP_SIZE * rows
    tiles = [(at, min(at + LANE_TILE, lanes)) for at in range(0, lanes, LANE_TILE)]
    rank = rank_ref[0]
    inner = rank % LEVEL
    my_core = inner % 2
    my_x = inner // 2
    window = (rank // LEVEL - depth) * LEVEL

    for level in range(depth + 1):
        below = LEVEL * (depth - level)
        for x_at in range(2):
            at = (x_at * (depth + 1) + level) * packed
            place = below + 2 * (my_x + x_at - 2 * my_x * x_at)
            kv_buf[place + my_core] = column_ref[at:at + packed, :]
            kv_buf[place + 1 - my_core] = core_ref[at:at + packed, :]

    counts = kv_buf[:, rows:rows + DOC_ROWS, 0:128].astype(jnp.float32)
    boundary = jnp.sum(counts) * (1.0 / (DOC_ROWS * 128))
    boundary = (boundary + 0.5).astype(jnp.int32) + jnp.maximum(window, 0) * rows
    q_first = rank * rows
    low_block = jnp.maximum(rank - (WB - 1), 0)
    low_block = jnp.where(q_first >= boundary, jnp.maximum(low_block, boundary // rows), low_block)
    low = jnp.maximum(low_block - window, 0) // PAIR
    high = (rank - window) // PAIR + 1
    span_ref[0] = low
    span_ref[1] = high

    m_buf[...] = jnp.full_like(m_buf, LOW)
    l_buf[...] = jnp.zeros_like(l_buf)
    acc[...] = jnp.zeros_like(acc)
    dq_acc[...] = jnp.zeros_like(dq_acc)

    def keys_of(c, column):
        return jnp.concatenate(
            [kv_buf[PAIR * c + i, 0:rows, column:column + HEAD_SIZE] for i in range(PAIR)], axis=0
        )

    def score_steps(c, g):
        key_first = window * rows + c * chunk
        key_pos = key_first + lax.broadcasted_iota(jnp.int32, (chunk, rows), 0)
        query_pos = q_first + lax.broadcasted_iota(jnp.int32, (chunk, rows), 1)
        allowed = (key_pos <= query_pos) & (query_pos // BLK - key_pos // BLK < WB)
        allowed = allowed & ((key_pos >= boundary) == (query_pos >= boundary))
        bias = jnp.where(allowed, 0.0, LOW)
        k_c = keys_of(c, g * HEAD_SIZE)

        def step(a, b):
            s = lax.dot_general(k_c, q_all[g, a:b, :], NT, preferred_element_type=jnp.float32)
            s = s + jnp.concatenate([bias] * ((b - a) // rows), axis=1)
            s_buf[c, :, a:b] = s
            m_buf[g, :, a:b] = jnp.maximum(m_buf[g, :, a:b], fold(s, jnp.max))

        return step

    def weight_steps(c, g, row_max):
        v_t = keys_of(c, (KEY_VALUE_HEADS + g) * HEAD_SIZE).T

        def step(a, b):
            p = jnp.exp2(s_buf[c, :, a:b] * SCALE_LOG2 - row_max[:, a:b])
            l_buf[g, :, a:b] += fold(p, jnp.sum)
            p_bf = p.astype(jnp.bfloat16)
            p_buf[c, :, g * lanes + a:g * lanes + b] = p_bf
            acc[g, :, a:b] += jnp.dot(v_t, p_bf, preferred_element_type=jnp.float32)

        return step

    def gradient_steps(c, g, row_dot):
        v_c = keys_of(c, (KEY_VALUE_HEADS + g) * HEAD_SIZE)
        k_t = keys_of(c, g * HEAD_SIZE).T

        def step(a, b):
            d_p = jnp.dot(v_c, do_t[g, :, a:b], preferred_element_type=jnp.float32)
            p = p_buf[c, :, g * lanes + a:g * lanes + b].astype(jnp.float32)
            d_s = (p * (d_p - row_dot[:, a:b])).astype(jnp.bfloat16)
            ds_buf[c, :, g * lanes + a:g * lanes + b] = d_s
            dq_acc[g, :, a:b] += jnp.dot(k_t, d_s, preferred_element_type=jnp.float32)

        return step

    def row_maximum(g):
        return jnp.max(m_buf[g], axis=0, keepdims=True) * SCALE_LOG2

    def finish_rows(g):
        inverse = 1.0 / jnp.sum(l_buf[g], axis=0, keepdims=True)
        for n in range(GROUP_SIZE):
            at = slice(n * rows, (n + 1) * rows)
            att = (acc[g, :, at] * inverse[:, at]).astype(jnp.bfloat16)
            att_ref[:, head_columns(g, n)] = att.T
            do_n = do_all[g, :, at].astype(jnp.float32)
            dot_n = jnp.sum(do_n * att.astype(jnp.float32), axis=0, keepdims=True)
            m_buf[g, 0:1, at] = dot_n * inverse[:, at]
            do_t[g, :, at] = (do_n * inverse[:, at]).astype(jnp.bfloat16)

    def over_chunks(*makers):
        @pl.loop(low, high)
        def _(c):
            steps = [make(c) for make in makers]
            for a, b in tiles:
                for step in steps:
                    step(a, b)

    over_chunks(lambda c: score_steps(c, 0))
    for g in range(KEY_VALUE_HEADS):
        row_max = row_maximum(g)
        makers = [lambda c: weight_steps(c, g, row_max)]
        if g:
            row_dot = m_buf[g - 1, 0:1, :]
            makers.append(lambda c: gradient_steps(c, g - 1, row_dot))
        if g + 1 < KEY_VALUE_HEADS:
            makers.append(lambda c: score_steps(c, g + 1))
        over_chunks(*makers)
        finish_rows(g)
    row_dot = m_buf[KEY_VALUE_HEADS - 1, 0:1, :]
    over_chunks(lambda c: gradient_steps(c, KEY_VALUE_HEADS - 1, row_dot))

    gb_ref[...] = jnp.zeros_like(gb_ref)
    for g in range(KEY_VALUE_HEADS):
        for n in range(GROUP_SIZE):
            columns = head_columns(g, n)
            d_q = (dq_acc[g, :, n * rows:(n + 1) * rows] * SCALE).astype(jnp.bfloat16).T
            row, at = divmod(columns.start, KV_WIDTH)
            gb_ref[row:row + 1, at:at + HEAD_SIZE] = jnp.sum(
                d_q.astype(jnp.float32), axis=0, keepdims=True
            )
            dq_ref[:, columns] = d_q


def attention(rank, q_all, do_all, column, core_column, depth):
    rows = q_all.shape[1] // GROUP_SIZE
    width = QUERY_HEADS * HEAD_SIZE
    packed = rows + DOC_ROWS
    lanes = GROUP_SIZE * rows
    chunk = PAIR * rows
    slots = (depth + 1) * LEVEL // PAIR
    vmem = pl.BlockSpec(memory_space=pltpu.VMEM)
    smem = pl.BlockSpec(memory_space=pltpu.SMEM)
    products = 5 * 2 * width * HEAD_SIZE * slots * chunk
    return pl.pallas_call(
        kernel,
        out_shape=(
            jax.ShapeDtypeStruct((rows, width), jnp.bfloat16),
            jax.ShapeDtypeStruct((rows, width), jnp.bfloat16),
            jax.ShapeDtypeStruct((slots, chunk, KEY_VALUE_HEADS * lanes), jnp.bfloat16),
            jax.ShapeDtypeStruct((slots, chunk, KEY_VALUE_HEADS * lanes), jnp.bfloat16),
            jax.ShapeDtypeStruct((KEY_VALUE_HEADS, HEAD_SIZE, lanes), jnp.bfloat16),
            jax.ShapeDtypeStruct((-(-width // KV_WIDTH), KV_WIDTH), jnp.float32),
            jax.ShapeDtypeStruct((2,), jnp.int32),
        ),
        in_specs=[smem] + [vmem] * 4,
        out_specs=(vmem,) * 6 + (smem,),
        scratch_shapes=[
            pltpu.VMEM(((depth + 1) * LEVEL, packed, KV_WIDTH), jnp.bfloat16),
            pltpu.VMEM((slots, chunk, lanes), jnp.float32),
            pltpu.VMEM((KEY_VALUE_HEADS, 8, lanes), jnp.float32),
            pltpu.VMEM((KEY_VALUE_HEADS, 8, lanes), jnp.float32),
            pltpu.VMEM((KEY_VALUE_HEADS, HEAD_SIZE, lanes), jnp.float32),
            pltpu.VMEM((KEY_VALUE_HEADS, HEAD_SIZE, lanes), jnp.float32),
        ],
        compiler_params=pltpu.CompilerParams(vmem_limit_bytes=36 * 1024 * 1024),
        cost_estimate=pl.CostEstimate(
            flops=products, bytes_accessed=8 * rows * width, transcendentals=0
        ),
        name="attention",
    )(rank, q_all, do_all, column, core_column)


def level_kernel(level, rank_ref, span_ref, p_buf, ds_buf, q_all, do_t, keep_ref, send_ref):
    chunk = p_buf.shape[1]
    rows = chunk // PAIR
    lanes = GROUP_SIZE * rows
    inner = rank_ref[0] % LEVEL
    my_core = inner % 2
    my_x = inner // 2
    active = (level >= span_ref[0]) & (level < span_ref[1])

    @pl.when(active)
    def _():
        for g in range(KEY_VALUE_HEADS):
            where = slice(g * lanes, (g + 1) * lanes)
            d_key = jnp.dot(
                ds_buf[level, :, where], q_all[g], preferred_element_type=jnp.float32
            ) * SCALE
            d_value = lax.dot_general(
                p_buf[level, :, where], do_t[g], NT, preferred_element_type=jnp.float32
            )
            for value, column in ((d_key, g), (d_value, KEY_VALUE_HEADS + g)):
                columns = slice(column * HEAD_SIZE, (column + 1) * HEAD_SIZE)
                for x_at in range(2):
                    first = value[2 * x_at * rows:(2 * x_at + 1) * rows]
                    second = value[(2 * x_at + 1) * rows:(2 * x_at + 2) * rows]
                    place = (x_at + my_x) % 2
                    at = pl.ds(pl.multiple_of(place * rows, rows), rows)
                    keep_ref[at, columns] = jnp.where(my_core == 0, first, second)
                    send_ref[at, columns] = jnp.where(my_core == 0, second, first).astype(
                        jnp.bfloat16
                    )

    @pl.when(jnp.logical_not(active))
    def _():
        keep_ref[...] = jnp.zeros_like(keep_ref)
        send_ref[...] = jnp.zeros_like(send_ref)


def level_gradients(level, rank, span, p_all, ds_all, q_all, do_t):
    chunk, width = p_all.shape[1:]
    rows = chunk // PAIR
    vmem = pl.BlockSpec(memory_space=pltpu.VMEM)
    smem = pl.BlockSpec(memory_space=pltpu.SMEM)
    return pl.pallas_call(
        functools.partial(level_kernel, level),
        out_shape=(
            jax.ShapeDtypeStruct((2 * rows, KV_WIDTH), jnp.float32),
            jax.ShapeDtypeStruct((2 * rows, KV_WIDTH), jnp.bfloat16),
        ),
        in_specs=[smem, smem] + [vmem] * 4,
        out_specs=(vmem, vmem),
        compiler_params=pltpu.CompilerParams(vmem_limit_bytes=36 * 1024 * 1024),
        cost_estimate=pl.CostEstimate(
            flops=2 * 2 * LEVEL * rows * width * HEAD_SIZE,
            bytes_accessed=4 * LEVEL * rows * width,
            transcendentals=0,
        ),
        name="level_gradients",
    )(rank, span, p_all, ds_all, q_all, do_t)


def shifted(value, steps, bit=0):
    count = lax.axis_size("ctx")
    first, last = max(0, -steps), min(count, count - steps)
    return lax.ppermute(value, "ctx", [(at, (at + steps) ^ bit) for at in range(first, last)])


def rotated(value, steps):
    count = lax.axis_size("ctx")
    return lax.ppermute(value, "ctx", [(at, (at + steps) % count) for at in range(count)])


def swapped(value, bit, axis="ctx"):
    return lax.ppermute(value, axis, [(at, at ^ bit) for at in range(lax.axis_size(axis))])


def bias_rows(rows):
    high = lax.reduce_precision(rows, 8, 7)
    both = jnp.concatenate([high, rows - high]).astype(jnp.bfloat16)
    return jnp.pad(both, ((0, -both.shape[0] % 16), (0, 0)))


def local(query_in, key_in, value_input, output_gradient, doc_ids, query_bias):
    rows = query_in.shape[1]
    shards = lax.axis_size("ctx")
    depth = window_levels(shards)
    rank = lax.axis_index("ctx").astype(jnp.int32)
    own = pack(key_in[0], value_input[0], doc_ids)

    ups = [shifted(own, LEVEL * step) for step in range(depth, 0, -1)][::-1]
    crossed = [shifted(own, LEVEL * step, 2) for step in range(depth, 0, -1)][::-1]
    x_own = swapped(own, 2)
    q_all, do_all = prepare(query_in[0], query_bias[None], output_gradient[0])
    column = jnp.concatenate([own] + ups + [x_own] + crossed, axis=0)
    column, q_all, do_all = lax.optimization_barrier((column, q_all, do_all))
    core_column = swapped(column, 1)

    rank = rank.reshape(1)
    attended, grad_query, p_all, ds_all, do_t, bias_part, span = attention(
        rank, q_all, do_all, column, core_column, depth
    )

    levels = shards // LEVEL
    carried = levels == 4 and depth == 2

    def joined(value):
        return jnp.concatenate([value, bias_rows(bias_total)], axis=0) if carried else value

    def bias_of(got):
        return got[rows:rows + half_rows].astype(jnp.float32) + got[
            rows + half_rows:rows + 2 * half_rows
        ].astype(jnp.float32)

    half_rows = bias_part.shape[0]
    bias_total = bias_part
    parts = [None] * (depth + 1)
    down = [None] * (depth + 1)
    across = [None] * (depth + 1)
    keeps = [None] * (depth + 1)
    aways = [None] * (depth + 1)

    def products(step):
        nonlocal bias_total, p_all
        keep, send = level_gradients(depth - step, rank, span, p_all, ds_all, q_all, do_t)
        if step:
            send, p_all = lax.optimization_barrier((send, p_all))
        if step == depth:
            send, bias_total = lax.optimization_barrier((send, bias_part))
            bit = 1
            while bit < lax.axis_size("dp"):
                bias_total = bias_total + swapped(bias_total, bit, "dp")
                bit *= 2
        if step == depth - 1:
            send, first_away = lax.optimization_barrier((send, aways[depth]))
            across[depth] = swapped(first_away, 2)
        if step == depth - 1 and carried:
            got = swapped(jnp.concatenate([send, bias_rows(bias_total)], axis=0), 1)
            bias_total = bias_total + bias_of(got[rows:])
            got = got[:2 * rows]
        else:
            got = swapped(send, 1)
        both = keep + got.astype(jnp.float32)
        keeps[step] = both[:rows]
        aways[step] = both[rows:].astype(jnp.bfloat16)
        if 0 < step < depth:
            across[step] = swapped(joined(aways[step]) if step == depth - 1 else aways[step], 2)

    def collected(step):
        nonlocal bias_total, p_all
        if step == depth - 1 and carried:
            bias_total = bias_total + bias_of(across[step])
        parts[step] = keeps[step] + across[step][:rows].astype(jnp.float32)
        if step == 0:
            return
        sent = parts[step].astype(jnp.bfloat16)
        if step == depth:
            sent, p_all = lax.optimization_barrier((sent, p_all))
        if step == depth - 1 and carried:
            sent = joined(sent)
            down[step] = rotated(sent, -LEVEL * step)
        else:
            down[step] = shifted(sent, -LEVEL * step)

    for step in range(depth, -1, -1):
        products(step)
        if step < depth:
            collected(step + 1)
    aways[0], bias_total = lax.optimization_barrier((aways[0], bias_total))
    across[0] = swapped(aways[0], 2)
    collected(0)
    if carried:
        bias_total = (
            bias_total
            + rotated(bias_total, LEVEL)
            + rotated(bias_total, 2 * LEVEL)
            + bias_of(down[1])
        )
    else:
        bit = 1
        while bit < shards:
            bias_total = bias_total + swapped(bias_total, bit)
            bit *= 2
    bias_total = bias_total.reshape(-1)[:query_bias.shape[0]]
    total = parts[0]
    for step in range(depth, 0, -1):
        total = total + down[step][:rows].astype(jnp.float32)
    total = total.astype(jnp.bfloat16)
    half = KEY_VALUE_HEADS * HEAD_SIZE
    return (
        attended[None],
        grad_query[None],
        total[:, :half][None],
        total[:, half:][None],
        bias_total,
    )


def solution(mesh):
    placed = (
        P("dp", "ctx", None),
        P("dp", "ctx", None),
        P("dp", "ctx", None),
        P("dp", "ctx", None),
        P("dp", "ctx"),
        P(),
    )
    return jax.shard_map(
        local,
        mesh=mesh,
        in_specs=placed,
        out_specs=(
            P("dp", "ctx", None),
            P("dp", "ctx", None),
            P("dp", "ctx", None),
            P("dp", "ctx", None),
            P(),
        ),
        check_vma=False,
    )
```

```python
import functools
import math

import jax
import jax.numpy as jnp
from jax import lax
from jax.experimental import pallas as pl
from jax.experimental.pallas import tpu as pltpu
from jax.sharding import PartitionSpec as P

QUERY_HEADS = 14
KEY_VALUE_HEADS = 2
HEAD_SIZE = 128
GROUP_SIZE = 7
BLK = 128
WB = 16
DOC_ROWS = 16
PAIR = 4
LEVEL = 4
LANE_TILE = 256
KV_WIDTH = 2 * KEY_VALUE_HEADS * HEAD_SIZE
SCALE = 1.0 / math.sqrt(HEAD_SIZE)
SCALE_LOG2 = SCALE * math.log2(math.e)
LOW = -1e30

NT = (((1,), (1,)), ((), ()))


def fold(value, op):
    keys, lanes = value.shape
    return op(value.reshape(keys // 8, 8, lanes), axis=0)


def window_levels(shards):
    levels = max(shards // LEVEL, 1)
    return min((WB - 2 + LEVEL) // LEVEL, max(3 * levels // 4 - 1, 0) if levels % 4 == 0 else levels - 1)


def pack_kernel(key_hbm, value_hbm, docs_hbm, own_hbm, docs, counts, sems):
    rows, half = key_hbm.shape
    copies = [
        pltpu.make_async_copy(docs_hbm, docs, sems.at[0]),
        pltpu.make_async_copy(key_hbm, own_hbm.at[0:rows, 0:half], sems.at[1]),
        pltpu.make_async_copy(value_hbm, own_hbm.at[0:rows, half:2 * half], sems.at[2]),
    ]
    for copy in copies:
        copy.start()
    copies[0].wait()
    count = jnp.sum((docs[...] == 0).astype(jnp.float32), axis=1, keepdims=True)
    counts[...] = jnp.broadcast_to(count, counts.shape).astype(jnp.bfloat16)
    last = pltpu.make_async_copy(counts, own_hbm.at[rows:rows + DOC_ROWS, :], sems.at[3])
    last.start()
    copies[1].wait()
    copies[2].wait()
    last.wait()


def pack(key_in, value_input, doc_ids):
    rows, half = key_in.shape
    anywhere = pl.BlockSpec(memory_space=pltpu.HBM)
    return pl.pallas_call(
        pack_kernel,
        out_shape=jax.ShapeDtypeStruct((rows + DOC_ROWS, 2 * half), jnp.bfloat16),
        in_specs=[anywhere] * 3,
        out_specs=anywhere,
        scratch_shapes=[
            pltpu.VMEM((1, rows), jnp.int32),
            pltpu.VMEM((DOC_ROWS, 2 * half), jnp.bfloat16),
            pltpu.SemaphoreType.DMA((4,)),
        ],
        compiler_params=pltpu.CompilerParams(vmem_limit_bytes=60 * 1024 * 1024),
        name="pack",
    )(key_in, value_input, doc_ids)


def head_columns(g, n):
    head = g * GROUP_SIZE + n
    return slice(head * HEAD_SIZE, (head + 1) * HEAD_SIZE)


def prepare_kernel(q_hbm, bias_ref, do_hbm, q_st, do_t, q_buf, do_buf, sems):
    rows = q_buf.shape[0]
    first = pltpu.make_async_copy(q_hbm, q_buf, sems.at[0])
    second = pltpu.make_async_copy(do_hbm, do_buf, sems.at[1])
    first.start()
    second.start()
    first.wait()
    for g in range(KEY_VALUE_HEADS):
        for n in range(GROUP_SIZE):
            columns = head_columns(g, n)
            q_st[g, n * rows:(n + 1) * rows, :] = (
                q_buf[:, columns].astype(jnp.float32) + bias_ref[:, columns]
            ).astype(jnp.bfloat16)
    second.wait()
    for g in range(KEY_VALUE_HEADS):
        for n in range(GROUP_SIZE):
            do_t[g, :, n * rows:(n + 1) * rows] = do_buf[:, head_columns(g, n)].T


def prepare(query_in, query_bias, output_gradient):
    rows, width = query_in.shape
    lanes = GROUP_SIZE * rows
    anywhere = pl.BlockSpec(memory_space=pltpu.HBM)
    vmem = pl.BlockSpec(memory_space=pltpu.VMEM)
    return pl.pallas_call(
        prepare_kernel,
        out_shape=(
            jax.ShapeDtypeStruct((KEY_VALUE_HEADS, lanes, HEAD_SIZE), jnp.bfloat16),
            jax.ShapeDtypeStruct((KEY_VALUE_HEADS, HEAD_SIZE, lanes), jnp.bfloat16),
        ),
        in_specs=[anywhere, vmem, anywhere],
        out_specs=(vmem, vmem),
        scratch_shapes=[
            pltpu.VMEM((rows, width), jnp.bfloat16),
            pltpu.VMEM((rows, width), jnp.bfloat16),
            pltpu.SemaphoreType.DMA((2,)),
        ],
        compiler_params=pltpu.CompilerParams(vmem_limit_bytes=8 * 1024 * 1024),
        cost_estimate=pl.CostEstimate(
            flops=4 * rows * width, bytes_accessed=8 * rows * width, transcendentals=0
        ),
        name="prepare",
    )(query_in, query_bias, output_gradient)


def kernel(
    rank_ref, q_all, do_all, near_ref, near_core_ref, far_ref, far_core_ref,
    att_ref, dq_ref, p_buf, ds_buf, do_t, gb_ref, span_ref,
    kv_buf, s_buf, m_buf, l_buf, acc, dq_acc,
):
    rows = att_ref.shape[0]
    slots = p_buf.shape[0]
    packed = kv_buf.shape[1]
    depth = slots * PAIR // LEVEL - 1
    chunk = PAIR * rows
    lanes = GROUP_SIZE * rows
    tiles = [(at, min(at + LANE_TILE, lanes)) for at in range(0, lanes, LANE_TILE)]
    rank = rank_ref[0]
    inner = rank % LEVEL
    my_core = inner % 2
    my_x = inner // 2
    window = (rank // LEVEL - depth) * LEVEL

    for level in range(depth + 1):
        below = LEVEL * (depth - level)
        here, there = (near_ref, near_core_ref) if level < depth else (far_ref, far_core_ref)
        for x_at in range(2):
            at = (2 * (level % depth) + x_at) * packed
            place = below + 2 * (my_x + x_at - 2 * my_x * x_at)
            kv_buf[place + my_core] = here[at:at + packed, :]
            kv_buf[place + 1 - my_core] = there[at:at + packed, :]

    counts = kv_buf[:, rows:rows + DOC_ROWS, 0:128].astype(jnp.float32)
    boundary = jnp.sum(counts) * (1.0 / (DOC_ROWS * 128))
    boundary = (boundary + 0.5).astype(jnp.int32) + jnp.maximum(window, 0) * rows
    q_first = rank * rows
    low_block = jnp.maximum(rank - (WB - 1), 0)
    low_block = jnp.where(q_first >= boundary, jnp.maximum(low_block, boundary // rows), low_block)
    low = jnp.maximum(low_block - window, 0) // PAIR
    high = (rank - window) // PAIR + 1
    span_ref[0] = low
    span_ref[1] = high

    m_buf[...] = jnp.full_like(m_buf, LOW)
    l_buf[...] = jnp.zeros_like(l_buf)
    acc[...] = jnp.zeros_like(acc)
    dq_acc[...] = jnp.zeros_like(dq_acc)

    def keys_of(c, column):
        return jnp.concatenate(
            [kv_buf[PAIR * c + i, 0:rows, column:column + HEAD_SIZE] for i in range(PAIR)], axis=0
        )

    def score_steps(c, g):
        key_first = window * rows + c * chunk
        key_pos = key_first + lax.broadcasted_iota(jnp.int32, (chunk, rows), 0)
        query_pos = q_first + lax.broadcasted_iota(jnp.int32, (chunk, rows), 1)
        allowed = (key_pos <= query_pos) & (query_pos // BLK - key_pos // BLK < WB)
        allowed = allowed & ((key_pos >= boundary) == (query_pos >= boundary))
        bias = jnp.where(allowed, 0.0, LOW)
        k_c = keys_of(c, g * HEAD_SIZE)

        def step(a, b):
            s = lax.dot_general(k_c, q_all[g, a:b, :], NT, preferred_element_type=jnp.float32)
            s = s + jnp.concatenate([bias] * ((b - a) // rows), axis=1)
            s_buf[c, :, a:b] = s
            m_buf[g, :, a:b] = jnp.maximum(m_buf[g, :, a:b], fold(s, jnp.max))

        return step

    def weight_steps(c, g, row_max):
        v_t = keys_of(c, (KEY_VALUE_HEADS + g) * HEAD_SIZE).T

        def step(a, b):
            p = jnp.exp2(s_buf[c, :, a:b] * SCALE_LOG2 - row_max[:, a:b])
            l_buf[g, :, a:b] += fold(p, jnp.sum)
            p_bf = p.astype(jnp.bfloat16)
            p_buf[c, :, g * lanes + a:g * lanes + b] = p_bf
            acc[g, :, a:b] += jnp.dot(v_t, p_bf, preferred_element_type=jnp.float32)

        return step

    def gradient_steps(c, g, row_dot):
        v_c = keys_of(c, (KEY_VALUE_HEADS + g) * HEAD_SIZE)
        k_t = keys_of(c, g * HEAD_SIZE).T

        def step(a, b):
            d_p = jnp.dot(v_c, do_t[g, :, a:b], preferred_element_type=jnp.float32)
            p = p_buf[c, :, g * lanes + a:g * lanes + b].astype(jnp.float32)
            d_s = (p * (d_p - row_dot[:, a:b])).astype(jnp.bfloat16)
            ds_buf[c, :, g * lanes + a:g * lanes + b] = d_s
            dq_acc[g, :, a:b] += jnp.dot(k_t, d_s, preferred_element_type=jnp.float32)

        return step

    def row_maximum(g):
        return jnp.max(m_buf[g], axis=0, keepdims=True) * SCALE_LOG2

    def finish_rows(g):
        inverse = 1.0 / jnp.sum(l_buf[g], axis=0, keepdims=True)
        for n in range(GROUP_SIZE):
            at = slice(n * rows, (n + 1) * rows)
            att = (acc[g, :, at] * inverse[:, at]).astype(jnp.bfloat16)
            att_ref[:, head_columns(g, n)] = att.T
            do_n = do_all[g, :, at].astype(jnp.float32)
            dot_n = jnp.sum(do_n * att.astype(jnp.float32), axis=0, keepdims=True)
            m_buf[g, 0:1, at] = dot_n * inverse[:, at]
            do_t[g, :, at] = (do_n * inverse[:, at]).astype(jnp.bfloat16)

    def over_chunks(*makers):
        @pl.loop(low, high)
        def _(c):
            steps = [make(c) for make in makers]
            for a, b in tiles:
                for step in steps:
                    step(a, b)

    over_chunks(lambda c: score_steps(c, 0))
    for g in range(KEY_VALUE_HEADS):
        row_max = row_maximum(g)
        makers = [lambda c: weight_steps(c, g, row_max)]
        if g:
            row_dot = m_buf[g - 1, 0:1, :]
            makers.append(lambda c: gradient_steps(c, g - 1, row_dot))
        if g + 1 < KEY_VALUE_HEADS:
            makers.append(lambda c: score_steps(c, g + 1))
        over_chunks(*makers)
        finish_rows(g)
    row_dot = m_buf[KEY_VALUE_HEADS - 1, 0:1, :]
    over_chunks(lambda c: gradient_steps(c, KEY_VALUE_HEADS - 1, row_dot))

    gb_ref[...] = jnp.zeros_like(gb_ref)
    for g in range(KEY_VALUE_HEADS):
        for n in range(GROUP_SIZE):
            columns = head_columns(g, n)
            d_q = (dq_acc[g, :, n * rows:(n + 1) * rows] * SCALE).astype(jnp.bfloat16).T
            row, at = divmod(columns.start, KV_WIDTH)
            gb_ref[row:row + 1, at:at + HEAD_SIZE] = jnp.sum(
                d_q.astype(jnp.float32), axis=0, keepdims=True
            )
            dq_ref[:, columns] = d_q


def attention(rank, q_all, do_all, near, near_core, far, far_core, depth):
    rows = q_all.shape[1] // GROUP_SIZE
    width = QUERY_HEADS * HEAD_SIZE
    packed = rows + DOC_ROWS
    lanes = GROUP_SIZE * rows
    chunk = PAIR * rows
    slots = (depth + 1) * LEVEL // PAIR
    vmem = pl.BlockSpec(memory_space=pltpu.VMEM)
    smem = pl.BlockSpec(memory_space=pltpu.SMEM)
    products = 5 * 2 * width * HEAD_SIZE * slots * chunk
    return pl.pallas_call(
        kernel,
        out_shape=(
            jax.ShapeDtypeStruct((rows, width), jnp.bfloat16),
            jax.ShapeDtypeStruct((rows, width), jnp.bfloat16),
            jax.ShapeDtypeStruct((slots, chunk, KEY_VALUE_HEADS * lanes), jnp.bfloat16),
            jax.ShapeDtypeStruct((slots, chunk, KEY_VALUE_HEADS * lanes), jnp.bfloat16),
            jax.ShapeDtypeStruct((KEY_VALUE_HEADS, HEAD_SIZE, lanes), jnp.bfloat16),
            jax.ShapeDtypeStruct((-(-width // KV_WIDTH), KV_WIDTH), jnp.float32),
            jax.ShapeDtypeStruct((2,), jnp.int32),
        ),
        in_specs=[smem] + [vmem] * 6,
        out_specs=(vmem,) * 6 + (smem,),
        scratch_shapes=[
            pltpu.VMEM(((depth + 1) * LEVEL, packed, KV_WIDTH), jnp.bfloat16),
            pltpu.VMEM((slots, chunk, lanes), jnp.float32),
            pltpu.VMEM((KEY_VALUE_HEADS, 8, lanes), jnp.float32),
            pltpu.VMEM((KEY_VALUE_HEADS, 8, lanes), jnp.float32),
            pltpu.VMEM((KEY_VALUE_HEADS, HEAD_SIZE, lanes), jnp.float32),
            pltpu.VMEM((KEY_VALUE_HEADS, HEAD_SIZE, lanes), jnp.float32),
        ],
        compiler_params=pltpu.CompilerParams(vmem_limit_bytes=36 * 1024 * 1024),
        cost_estimate=pl.CostEstimate(
            flops=products, bytes_accessed=8 * rows * width, transcendentals=0
        ),
        name="attention",
    )(rank, q_all, do_all, near, near_core, far, far_core)


def level_kernel(level, rank_ref, span_ref, p_buf, ds_buf, q_all, do_t, keep_ref, send_ref):
    chunk = p_buf.shape[1]
    rows = chunk // PAIR
    lanes = GROUP_SIZE * rows
    inner = rank_ref[0] % LEVEL
    my_core = inner % 2
    my_x = inner // 2
    active = (level >= span_ref[0]) & (level < span_ref[1])

    @pl.when(active)
    def _():
        for g in range(KEY_VALUE_HEADS):
            where = slice(g * lanes, (g + 1) * lanes)
            d_key = jnp.dot(
                ds_buf[level, :, where], q_all[g], preferred_element_type=jnp.float32
            ) * SCALE
            d_value = lax.dot_general(
                p_buf[level, :, where], do_t[g], NT, preferred_element_type=jnp.float32
            )
            for value, column in ((d_key, g), (d_value, KEY_VALUE_HEADS + g)):
                columns = slice(column * HEAD_SIZE, (column + 1) * HEAD_SIZE)
                for x_at in range(2):
                    first = value[2 * x_at * rows:(2 * x_at + 1) * rows]
                    second = value[(2 * x_at + 1) * rows:(2 * x_at + 2) * rows]
                    place = (x_at + my_x) % 2
                    at = pl.ds(pl.multiple_of(place * rows, rows), rows)
                    keep_ref[at, columns] = jnp.where(my_core == 0, first, second)
                    send_ref[at, columns] = jnp.where(my_core == 0, second, first).astype(
                        jnp.bfloat16
                    )

    @pl.when(jnp.logical_not(active))
    def _():
        keep_ref[...] = jnp.zeros_like(keep_ref)
        send_ref[...] = jnp.zeros_like(send_ref)


def level_gradients(level, rank, span, p_all, ds_all, q_all, do_t):
    chunk, width = p_all.shape[1:]
    rows = chunk // PAIR
    vmem = pl.BlockSpec(memory_space=pltpu.VMEM)
    smem = pl.BlockSpec(memory_space=pltpu.SMEM)
    return pl.pallas_call(
        functools.partial(level_kernel, level),
        out_shape=(
            jax.ShapeDtypeStruct((2 * rows, KV_WIDTH), jnp.float32),
            jax.ShapeDtypeStruct((2 * rows, KV_WIDTH), jnp.bfloat16),
        ),
        in_specs=[smem, smem] + [vmem] * 4,
        out_specs=(vmem, vmem),
        compiler_params=pltpu.CompilerParams(vmem_limit_bytes=36 * 1024 * 1024),
        cost_estimate=pl.CostEstimate(
            flops=2 * 2 * LEVEL * rows * width * HEAD_SIZE,
            bytes_accessed=4 * LEVEL * rows * width,
            transcendentals=0,
        ),
        name="level_gradients",
    )(rank, span, p_all, ds_all, q_all, do_t)


def shifted(value, steps, bit=0):
    count = lax.axis_size("ctx")
    first, last = max(0, -steps), min(count, count - steps)
    return lax.ppermute(value, "ctx", [(at, (at + steps) ^ bit) for at in range(first, last)])


def rotated(value, steps):
    count = lax.axis_size("ctx")
    return lax.ppermute(value, "ctx", [(at, (at + steps) % count) for at in range(count)])


def swapped(value, bit, axis="ctx"):
    return lax.ppermute(value, axis, [(at, at ^ bit) for at in range(lax.axis_size(axis))])


def bias_rows(rows):
    high = lax.reduce_precision(rows, 8, 7)
    both = jnp.concatenate([high, rows - high]).astype(jnp.bfloat16)
    return jnp.pad(both, ((0, -both.shape[0] % 16), (0, 0)))


def local(query_in, key_in, value_input, output_gradient, doc_ids, query_bias):
    rows = query_in.shape[1]
    shards = lax.axis_size("ctx")
    depth = window_levels(shards)
    rank = lax.axis_index("ctx").astype(jnp.int32)
    own = pack(key_in[0], value_input[0], doc_ids)

    up = shifted(own, LEVEL)
    x_own = swapped(own, 2)
    q_all, do_all = prepare(query_in[0], query_bias[None], output_gradient[0])
    up, x_own, q_all, do_all = lax.optimization_barrier((up, x_own, q_all, do_all))
    near = [own, x_own]
    for _ in range(depth - 1):
        near += [up, swapped(up, 2)]
        up = shifted(up, LEVEL)
    up, near = lax.optimization_barrier((up, near))
    far = jnp.concatenate([up, swapped(up, 2)], axis=0)
    near = jnp.concatenate(near, axis=0)
    near_core = swapped(near, 1)
    far_core = swapped(far, 1)

    rank = rank.reshape(1)
    attended, grad_query, p_all, ds_all, do_t, bias_part, span = attention(
        rank, q_all, do_all, near, near_core, far, far_core, depth
    )

    levels = shards // LEVEL
    carried = levels == 4 and depth == 2

    def joined(value):
        return jnp.concatenate([value, bias_rows(bias_total)], axis=0) if carried else value

    def bias_of(got):
        return got[rows:rows + half_rows].astype(jnp.float32) + got[
            rows + half_rows:rows + 2 * half_rows
        ].astype(jnp.float32)

    half_rows = bias_part.shape[0]
    bias_total = bias_part
    parts = [None] * (depth + 1)
    down = [None] * (depth + 1)
    across = [None] * (depth + 1)
    keeps = [None] * (depth + 1)
    aways = [None] * (depth + 1)

    def products(step):
        nonlocal bias_total, p_all
        keep, send = level_gradients(depth - step, rank, span, p_all, ds_all, q_all, do_t)
        if step:
            send, p_all = lax.optimization_barrier((send, p_all))
        if step == depth:
            send, bias_total = lax.optimization_barrier((send, bias_part))
            bit = 1
            while bit < lax.axis_size("dp"):
                bias_total = bias_total + swapped(bias_total, bit, "dp")
                bit *= 2
        if step == depth - 1:
            send, first_away = lax.optimization_barrier((send, aways[depth]))
            across[depth] = swapped(first_away, 2)
        if step == depth - 1 and carried:
            got = swapped(jnp.concatenate([send, bias_rows(bias_total)], axis=0), 1)
            bias_total = bias_total + bias_of(got[rows:])
            got = got[:2 * rows]
        else:
            got = swapped(send, 1)
        both = keep + got.astype(jnp.float32)
        keeps[step] = both[:rows]
        aways[step] = both[rows:].astype(jnp.bfloat16)
        if step < depth:
            across[step] = swapped(joined(aways[step]) if step == depth - 1 else aways[step], 2)

    def collected(step):
        nonlocal bias_total, p_all
        if step == depth - 1 and carried:
            bias_total = bias_total + bias_of(across[step])
        parts[step] = keeps[step] + across[step][:rows].astype(jnp.float32)
        if step == 0:
            return
        sent = parts[step].astype(jnp.bfloat16)
        if step == depth:
            sent, p_all = lax.optimization_barrier((sent, p_all))
        if step == depth - 1 and carried:
            sent = joined(sent)
            down[step] = rotated(sent, -LEVEL * step)
        else:
            down[step] = shifted(sent, -LEVEL * step)

    for step in range(depth, -1, -1):
        products(step)
        if step < depth:
            collected(step + 1)
    collected(0)
    if carried:
        bias_total = (
            bias_total
            + rotated(bias_total, LEVEL)
            + rotated(bias_total, 2 * LEVEL)
            + bias_of(down[1])
        )
    else:
        bit = 1
        while bit < shards:
            bias_total = bias_total + swapped(bias_total, bit)
            bit *= 2
    bias_total = bias_total.reshape(-1)[:query_bias.shape[0]]
    total = parts[0]
    for step in range(depth, 0, -1):
        total = total + down[step][:rows].astype(jnp.float32)
    total = total.astype(jnp.bfloat16)
    half = KEY_VALUE_HEADS * HEAD_SIZE
    return (
        attended[None],
        grad_query[None],
        total[:, :half][None],
        total[:, half:][None],
        bias_total,
    )


def solution(mesh):
    placed = (
        P("dp", "ctx", None),
        P("dp", "ctx", None),
        P("dp", "ctx", None),
        P("dp", "ctx", None),
        P("dp", "ctx"),
        P(),
    )
    return jax.shard_map(
        local,
        mesh=mesh,
        in_specs=placed,
        out_specs=(
            P("dp", "ctx", None),
            P("dp", "ctx", None),
            P("dp", "ctx", None),
            P("dp", "ctx", None),
            P(),
        ),
        check_vma=False,
    )
```

```python
import functools
import math

import jax
import jax.numpy as jnp
from jax import lax
from jax.experimental import pallas as pl
from jax.experimental.pallas import tpu as pltpu
from jax.sharding import PartitionSpec as P

QUERY_HEADS = 14
KEY_VALUE_HEADS = 2
HEAD_SIZE = 128
GROUP_SIZE = 7
BLK = 128
WB = 16
DOC_ROWS = 16
PAIR = 4
LEVEL = 4
LANE_TILE = 256
KV_WIDTH = 2 * KEY_VALUE_HEADS * HEAD_SIZE
SCALE = 1.0 / math.sqrt(HEAD_SIZE)
SCALE_LOG2 = SCALE * math.log2(math.e)
LOW = -1e30

NT = (((1,), (1,)), ((), ()))


def fold(value, op):
    keys, lanes = value.shape
    return op(value.reshape(keys // 8, 8, lanes), axis=0)


def window_levels(shards):
    levels = max(shards // LEVEL, 1)
    return min((WB - 2 + LEVEL) // LEVEL, max(3 * levels // 4 - 1, 0) if levels % 4 == 0 else levels - 1)


def pack_kernel(key_hbm, value_hbm, docs_hbm, own_ref, docs, sems):
    rows = key_hbm.shape[0]
    half = key_hbm.shape[1]
    copies = [
        pltpu.make_async_copy(docs_hbm, docs, sems.at[0]),
        pltpu.make_async_copy(key_hbm, own_ref.at[0:rows, 0:half], sems.at[1]),
        pltpu.make_async_copy(value_hbm, own_ref.at[0:rows, half:2 * half], sems.at[2]),
    ]
    for copy in copies:
        copy.start()
    copies[0].wait()
    count = jnp.sum((docs[...] == 0).astype(jnp.float32), axis=1, keepdims=True)
    own_ref[rows:rows + DOC_ROWS, :] = jnp.broadcast_to(count, (DOC_ROWS, 2 * half)).astype(
        jnp.bfloat16
    )
    copies[1].wait()
    copies[2].wait()


def pack(key_in, value_input, doc_ids):
    rows, half = key_in.shape
    return pl.pallas_call(
        pack_kernel,
        out_shape=jax.ShapeDtypeStruct((rows + DOC_ROWS, 2 * half), jnp.bfloat16),
        in_specs=[pl.BlockSpec(memory_space=pltpu.HBM)] * 3,
        out_specs=pl.BlockSpec(memory_space=pltpu.VMEM),
        scratch_shapes=[pltpu.VMEM((1, rows), jnp.int32), pltpu.SemaphoreType.DMA((3,))],
        compiler_params=pltpu.CompilerParams(vmem_limit_bytes=8 * 1024 * 1024),
        name="pack",
    )(key_in, value_input, doc_ids)


def head_columns(g, n):
    head = g * GROUP_SIZE + n
    return slice(head * HEAD_SIZE, (head + 1) * HEAD_SIZE)


def prepare_kernel(q_hbm, bias_ref, do_hbm, q_st, do_t, q_buf, do_buf, sems):
    rows = q_buf.shape[0]
    first = pltpu.make_async_copy(q_hbm, q_buf, sems.at[0])
    second = pltpu.make_async_copy(do_hbm, do_buf, sems.at[1])
    first.start()
    second.start()
    first.wait()
    for g in range(KEY_VALUE_HEADS):
        for n in range(GROUP_SIZE):
            columns = head_columns(g, n)
            q_st[g, n * rows:(n + 1) * rows, :] = (
                q_buf[:, columns].astype(jnp.float32) + bias_ref[:, columns]
            ).astype(jnp.bfloat16)
    second.wait()
    for g in range(KEY_VALUE_HEADS):
        for n in range(GROUP_SIZE):
            do_t[g, :, n * rows:(n + 1) * rows] = do_buf[:, head_columns(g, n)].T


def prepare(query_in, query_bias, output_gradient):
    rows, width = query_in.shape
    lanes = GROUP_SIZE * rows
    anywhere = pl.BlockSpec(memory_space=pltpu.HBM)
    vmem = pl.BlockSpec(memory_space=pltpu.VMEM)
    return pl.pallas_call(
        prepare_kernel,
        out_shape=(
            jax.ShapeDtypeStruct((KEY_VALUE_HEADS, lanes, HEAD_SIZE), jnp.bfloat16),
            jax.ShapeDtypeStruct((KEY_VALUE_HEADS, HEAD_SIZE, lanes), jnp.bfloat16),
        ),
        in_specs=[anywhere, vmem, anywhere],
        out_specs=(vmem, vmem),
        scratch_shapes=[
            pltpu.VMEM((rows, width), jnp.bfloat16),
            pltpu.VMEM((rows, width), jnp.bfloat16),
            pltpu.SemaphoreType.DMA((2,)),
        ],
        compiler_params=pltpu.CompilerParams(vmem_limit_bytes=8 * 1024 * 1024),
        cost_estimate=pl.CostEstimate(
            flops=4 * rows * width, bytes_accessed=8 * rows * width, transcendentals=0
        ),
        name="prepare",
    )(query_in, query_bias, output_gradient)


def kernel(
    rank_ref, q_all, do_all, near_ref, near_core_ref, far_ref, far_core_ref,
    att_ref, dq_ref, p_buf, ds_buf, do_t, gb_ref, span_ref,
    kv_buf, s_buf, m_buf, l_buf, acc, dq_acc,
):
    rows = att_ref.shape[0]
    slots = p_buf.shape[0]
    packed = kv_buf.shape[1]
    depth = slots * PAIR // LEVEL - 1
    chunk = PAIR * rows
    lanes = GROUP_SIZE * rows
    tiles = [(at, min(at + LANE_TILE, lanes)) for at in range(0, lanes, LANE_TILE)]
    rank = rank_ref[0]
    inner = rank % LEVEL
    my_core = inner % 2
    my_x = inner // 2
    window = (rank // LEVEL - depth) * LEVEL

    for level in range(depth + 1):
        below = LEVEL * (depth - level)
        here, there = (near_ref, near_core_ref) if level < depth else (far_ref, far_core_ref)
        for x_at in range(2):
            at = (2 * (level % depth) + x_at) * packed
            place = below + 2 * (my_x + x_at - 2 * my_x * x_at)
            kv_buf[place + my_core] = here[at:at + packed, :]
            kv_buf[place + 1 - my_core] = there[at:at + packed, :]

    counts = kv_buf[:, rows:rows + DOC_ROWS, 0:128].astype(jnp.float32)
    boundary = jnp.sum(counts) * (1.0 / (DOC_ROWS * 128))
    boundary = (boundary + 0.5).astype(jnp.int32) + jnp.maximum(window, 0) * rows
    q_first = rank * rows
    low_block = jnp.maximum(rank - (WB - 1), 0)
    low_block = jnp.where(q_first >= boundary, jnp.maximum(low_block, boundary // rows), low_block)
    low = jnp.maximum(low_block - window, 0) // PAIR
    high = (rank - window) // PAIR + 1
    span_ref[0] = low
    span_ref[1] = high

    m_buf[...] = jnp.full_like(m_buf, LOW)
    l_buf[...] = jnp.zeros_like(l_buf)
    acc[...] = jnp.zeros_like(acc)
    dq_acc[...] = jnp.zeros_like(dq_acc)

    def keys_of(c, column):
        return jnp.concatenate(
            [kv_buf[PAIR * c + i, 0:rows, column:column + HEAD_SIZE] for i in range(PAIR)], axis=0
        )

    def score_steps(c, g):
        key_first = window * rows + c * chunk
        key_pos = key_first + lax.broadcasted_iota(jnp.int32, (chunk, rows), 0)
        query_pos = q_first + lax.broadcasted_iota(jnp.int32, (chunk, rows), 1)
        allowed = (key_pos <= query_pos) & (query_pos // BLK - key_pos // BLK < WB)
        allowed = allowed & ((key_pos >= boundary) == (query_pos >= boundary))
        bias = jnp.where(allowed, 0.0, LOW)
        k_c = keys_of(c, g * HEAD_SIZE)

        def step(a, b):
            s = lax.dot_general(k_c, q_all[g, a:b, :], NT, preferred_element_type=jnp.float32)
            s = s + jnp.concatenate([bias] * ((b - a) // rows), axis=1)
            s_buf[c, :, a:b] = s
            m_buf[g, :, a:b] = jnp.maximum(m_buf[g, :, a:b], fold(s, jnp.max))

        return step

    def weight_steps(c, g, row_max):
        v_t = keys_of(c, (KEY_VALUE_HEADS + g) * HEAD_SIZE).T

        def step(a, b):
            p = jnp.exp2(s_buf[c, :, a:b] * SCALE_LOG2 - row_max[:, a:b])
            l_buf[g, :, a:b] += fold(p, jnp.sum)
            p_bf = p.astype(jnp.bfloat16)
            p_buf[c, :, g * lanes + a:g * lanes + b] = p_bf
            acc[g, :, a:b] += jnp.dot(v_t, p_bf, preferred_element_type=jnp.float32)

        return step

    def gradient_steps(c, g, row_dot):
        v_c = keys_of(c, (KEY_VALUE_HEADS + g) * HEAD_SIZE)
        k_t = keys_of(c, g * HEAD_SIZE).T

        def step(a, b):
            d_p = jnp.dot(v_c, do_t[g, :, a:b], preferred_element_type=jnp.float32)
            p = p_buf[c, :, g * lanes + a:g * lanes + b].astype(jnp.float32)
            d_s = (p * (d_p - row_dot[:, a:b])).astype(jnp.bfloat16)
            ds_buf[c, :, g * lanes + a:g * lanes + b] = d_s
            dq_acc[g, :, a:b] += jnp.dot(k_t, d_s, preferred_element_type=jnp.float32)

        return step

    def row_maximum(g):
        return jnp.max(m_buf[g], axis=0, keepdims=True) * SCALE_LOG2

    def finish_rows(g):
        inverse = 1.0 / jnp.sum(l_buf[g], axis=0, keepdims=True)
        for n in range(GROUP_SIZE):
            at = slice(n * rows, (n + 1) * rows)
            att = (acc[g, :, at] * inverse[:, at]).astype(jnp.bfloat16)
            att_ref[:, head_columns(g, n)] = att.T
            do_n = do_all[g, :, at].astype(jnp.float32)
            dot_n = jnp.sum(do_n * att.astype(jnp.float32), axis=0, keepdims=True)
            m_buf[g, 0:1, at] = dot_n * inverse[:, at]
            do_t[g, :, at] = (do_n * inverse[:, at]).astype(jnp.bfloat16)

    def over_chunks(*makers):
        @pl.loop(low, high)
        def _(c):
            steps = [make(c) for make in makers]
            for a, b in tiles:
                for step in steps:
                    step(a, b)

    over_chunks(lambda c: score_steps(c, 0))
    for g in range(KEY_VALUE_HEADS):
        row_max = row_maximum(g)
        makers = [lambda c: weight_steps(c, g, row_max)]
        if g:
            row_dot = m_buf[g - 1, 0:1, :]
            makers.append(lambda c: gradient_steps(c, g - 1, row_dot))
        if g + 1 < KEY_VALUE_HEADS:
            makers.append(lambda c: score_steps(c, g + 1))
        over_chunks(*makers)
        finish_rows(g)
    row_dot = m_buf[KEY_VALUE_HEADS - 1, 0:1, :]
    over_chunks(lambda c: gradient_steps(c, KEY_VALUE_HEADS - 1, row_dot))

    gb_ref[...] = jnp.zeros_like(gb_ref)
    for g in range(KEY_VALUE_HEADS):
        for n in range(GROUP_SIZE):
            columns = head_columns(g, n)
            d_q = (dq_acc[g, :, n * rows:(n + 1) * rows] * SCALE).astype(jnp.bfloat16).T
            row, at = divmod(columns.start, KV_WIDTH)
            gb_ref[row:row + 1, at:at + HEAD_SIZE] = jnp.sum(
                d_q.astype(jnp.float32), axis=0, keepdims=True
            )
            dq_ref[:, columns] = d_q


def attention(rank, q_all, do_all, near, near_core, far, far_core, depth):
    rows = q_all.shape[1] // GROUP_SIZE
    width = QUERY_HEADS * HEAD_SIZE
    packed = rows + DOC_ROWS
    lanes = GROUP_SIZE * rows
    chunk = PAIR * rows
    slots = (depth + 1) * LEVEL // PAIR
    vmem = pl.BlockSpec(memory_space=pltpu.VMEM)
    smem = pl.BlockSpec(memory_space=pltpu.SMEM)
    products = 5 * 2 * width * HEAD_SIZE * slots * chunk
    return pl.pallas_call(
        kernel,
        out_shape=(
            jax.ShapeDtypeStruct((rows, width), jnp.bfloat16),
            jax.ShapeDtypeStruct((rows, width), jnp.bfloat16),
            jax.ShapeDtypeStruct((slots, chunk, KEY_VALUE_HEADS * lanes), jnp.bfloat16),
            jax.ShapeDtypeStruct((slots, chunk, KEY_VALUE_HEADS * lanes), jnp.bfloat16),
            jax.ShapeDtypeStruct((KEY_VALUE_HEADS, HEAD_SIZE, lanes), jnp.bfloat16),
            jax.ShapeDtypeStruct((-(-width // KV_WIDTH), KV_WIDTH), jnp.float32),
            jax.ShapeDtypeStruct((2,), jnp.int32),
        ),
        in_specs=[smem] + [vmem] * 6,
        out_specs=(vmem,) * 6 + (smem,),
        scratch_shapes=[
            pltpu.VMEM(((depth + 1) * LEVEL, packed, KV_WIDTH), jnp.bfloat16),
            pltpu.VMEM((slots, chunk, lanes), jnp.float32),
            pltpu.VMEM((KEY_VALUE_HEADS, 8, lanes), jnp.float32),
            pltpu.VMEM((KEY_VALUE_HEADS, 8, lanes), jnp.float32),
            pltpu.VMEM((KEY_VALUE_HEADS, HEAD_SIZE, lanes), jnp.float32),
            pltpu.VMEM((KEY_VALUE_HEADS, HEAD_SIZE, lanes), jnp.float32),
        ],
        compiler_params=pltpu.CompilerParams(vmem_limit_bytes=36 * 1024 * 1024),
        cost_estimate=pl.CostEstimate(
            flops=products, bytes_accessed=8 * rows * width, transcendentals=0
        ),
        name="attention",
    )(rank, q_all, do_all, near, near_core, far, far_core)


def level_kernel(level, rank_ref, span_ref, p_buf, ds_buf, q_all, do_t, keep_ref, send_ref):
    chunk = p_buf.shape[1]
    rows = chunk // PAIR
    lanes = GROUP_SIZE * rows
    inner = rank_ref[0] % LEVEL
    my_core = inner % 2
    my_x = inner // 2
    active = (level >= span_ref[0]) & (level < span_ref[1])

    @pl.when(active)
    def _():
        for g in range(KEY_VALUE_HEADS):
            where = slice(g * lanes, (g + 1) * lanes)
            d_key = jnp.dot(
                ds_buf[level, :, where], q_all[g], preferred_element_type=jnp.float32
            ) * SCALE
            d_value = lax.dot_general(
                p_buf[level, :, where], do_t[g], NT, preferred_element_type=jnp.float32
            )
            for value, column in ((d_key, g), (d_value, KEY_VALUE_HEADS + g)):
                columns = slice(column * HEAD_SIZE, (column + 1) * HEAD_SIZE)
                for x_at in range(2):
                    first = value[2 * x_at * rows:(2 * x_at + 1) * rows]
                    second = value[(2 * x_at + 1) * rows:(2 * x_at + 2) * rows]
                    place = (x_at + my_x) % 2
                    at = pl.ds(pl.multiple_of(place * rows, rows), rows)
                    keep_ref[at, columns] = jnp.where(my_core == 0, first, second)
                    send_ref[at, columns] = jnp.where(my_core == 0, second, first).astype(
                        jnp.bfloat16
                    )

    @pl.when(jnp.logical_not(active))
    def _():
        keep_ref[...] = jnp.zeros_like(keep_ref)
        send_ref[...] = jnp.zeros_like(send_ref)


def level_gradients(level, rank, span, p_all, ds_all, q_all, do_t):
    chunk, width = p_all.shape[1:]
    rows = chunk // PAIR
    vmem = pl.BlockSpec(memory_space=pltpu.VMEM)
    smem = pl.BlockSpec(memory_space=pltpu.SMEM)
    return pl.pallas_call(
        functools.partial(level_kernel, level),
        out_shape=(
            jax.ShapeDtypeStruct((2 * rows, KV_WIDTH), jnp.float32),
            jax.ShapeDtypeStruct((2 * rows, KV_WIDTH), jnp.bfloat16),
        ),
        in_specs=[smem, smem] + [vmem] * 4,
        out_specs=(vmem, vmem),
        compiler_params=pltpu.CompilerParams(vmem_limit_bytes=36 * 1024 * 1024),
        cost_estimate=pl.CostEstimate(
            flops=2 * 2 * LEVEL * rows * width * HEAD_SIZE,
            bytes_accessed=4 * LEVEL * rows * width,
            transcendentals=0,
        ),
        name="level_gradients",
    )(rank, span, p_all, ds_all, q_all, do_t)


def shifted(value, steps):
    count = lax.axis_size("ctx")
    first, last = max(0, -steps), min(count, count - steps)
    return lax.ppermute(value, "ctx", [(at, at + steps) for at in range(first, last)])


def rotated(value, steps):
    count = lax.axis_size("ctx")
    return lax.ppermute(value, "ctx", [(at, (at + steps) % count) for at in range(count)])


def swapped(value, bit, axis="ctx"):
    return lax.ppermute(value, axis, [(at, at ^ bit) for at in range(lax.axis_size(axis))])


def bias_rows(rows):
    high = lax.reduce_precision(rows, 8, 7)
    both = jnp.concatenate([high, rows - high]).astype(jnp.bfloat16)
    return jnp.pad(both, ((0, -both.shape[0] % 16), (0, 0)))


def local(query_in, key_in, value_input, output_gradient, doc_ids, query_bias):
    rows = query_in.shape[1]
    shards = lax.axis_size("ctx")
    depth = window_levels(shards)
    rank = lax.axis_index("ctx").astype(jnp.int32)
    own = pack(key_in[0], value_input[0], doc_ids)

    ups = [shifted(own, LEVEL * step) for step in range(1, depth + 1)]
    x_own = swapped(own, 2)
    q_all, do_all = prepare(query_in[0], query_bias[None], output_gradient[0])
    ups[0], x_own, q_all, do_all = lax.optimization_barrier((ups[0], x_own, q_all, do_all))
    near = [own, x_own]
    for up in ups[:-1]:
        near += [up, swapped(up, 2)]
    far = [ups[-1], swapped(ups[-1], 2)]
    far[0], near = lax.optimization_barrier((far[0], near))
    near = jnp.concatenate(near, axis=0)
    near_core = swapped(near, 1)
    far = jnp.concatenate(far, axis=0)
    far_core = swapped(far, 1)

    rank = rank.reshape(1)
    attended, grad_query, p_all, ds_all, do_t, bias_part, span = attention(
        rank, q_all, do_all, near, near_core, far, far_core, depth
    )

    levels = shards // LEVEL
    carried = levels == 4 and depth == 2
    bit = 1
    while bit < lax.axis_size("dp"):
        bias_part = bias_part + swapped(bias_part, bit, "dp")
        bit *= 2
    bias_total = bias_part

    def joined(value):
        return jnp.concatenate([value, bias_rows(bias_total)], axis=0) if carried else value

    def bias_of(got):
        return got[rows:rows + half_rows].astype(jnp.float32) + got[
            rows + half_rows:rows + 2 * half_rows
        ].astype(jnp.float32)

    half_rows = bias_part.shape[0]
    parts = [None] * (depth + 1)
    down = [None] * (depth + 1)
    across = [None] * (depth + 1)
    keeps = [None] * (depth + 1)

    def products(step):
        nonlocal bias_total
        keep, send = level_gradients(depth - step, rank, span, p_all, ds_all, q_all, do_t)
        if step == depth and carried:
            got = swapped(jnp.concatenate([send, bias_rows(bias_total)], axis=0), 1)
            bias_total = bias_total + bias_of(got[rows:])
            got = got[:2 * rows]
        else:
            got = swapped(send, 1)
        both = keep + got.astype(jnp.float32)
        keeps[step] = both[:rows]
        away = both[rows:].astype(jnp.bfloat16)
        across[step] = swapped(joined(away) if step == depth else away, 2)

    def collected(step):
        nonlocal bias_total
        if step == depth and carried:
            bias_total = bias_total + bias_of(across[step])
        parts[step] = keeps[step] + across[step][:rows].astype(jnp.float32)
        if step == 0:
            return
        sent = parts[step].astype(jnp.bfloat16)
        if carried:
            sent = joined(sent)
            down[step] = rotated(sent, -LEVEL * step)
        else:
            down[step] = shifted(sent, -LEVEL * step)
        if step > 1:
            across[step - 1], _ = lax.optimization_barrier((across[step - 1], sent))

    for step in range(depth, -1, -1):
        if step + 2 <= depth:
            across[step + 2], p_all = lax.optimization_barrier((across[step + 2], p_all))
        products(step)
    for step in range(depth, -1, -1):
        collected(step)
    if carried:
        bias_total = (
            bias_total + rotated(bias_total, LEVEL) + bias_of(down[1]) + bias_of(down[2])
        )
    else:
        bit = 1
        while bit < shards:
            bias_total = bias_total + swapped(bias_total, bit)
            bit *= 2
    bias_total = bias_total.reshape(-1)[:query_bias.shape[0]]
    down = [None if part is None else part[:rows] for part in down]
    total = parts[0]
    for step in range(depth, 0, -1):
        total = total + down[step].astype(jnp.float32)
    total = total.astype(jnp.bfloat16)
    half = KEY_VALUE_HEADS * HEAD_SIZE
    return (
        attended[None],
        grad_query[None],
        total[:, :half][None],
        total[:, half:][None],
        bias_total,
    )


def solution(mesh):
    placed = (
        P("dp", "ctx", None),
        P("dp", "ctx", None),
        P("dp", "ctx", None),
        P("dp", "ctx", None),
        P("dp", "ctx"),
        P(),
    )
    return jax.shard_map(
        local,
        mesh=mesh,
        in_specs=placed,
        out_specs=(
            P("dp", "ctx", None),
            P("dp", "ctx", None),
            P("dp", "ctx", None),
            P("dp", "ctx", None),
            P(),
        ),
        check_vma=False,
    )
```

```python
import functools
import math

import jax
import jax.numpy as jnp
from jax import lax
from jax.experimental import pallas as pl
from jax.experimental.pallas import tpu as pltpu
from jax.sharding import PartitionSpec as P

QUERY_HEADS = 14
KEY_VALUE_HEADS = 2
HEAD_SIZE = 128
GROUP_SIZE = 7
BLK = 128
WB = 16
DOC_ROWS = 16
PAIR = 4
LEVEL = 4
LANE_TILE = 256
KV_WIDTH = 2 * KEY_VALUE_HEADS * HEAD_SIZE
SCALE = 1.0 / math.sqrt(HEAD_SIZE)
SCALE_LOG2 = SCALE * math.log2(math.e)
LOW = -1e30

NT = (((1,), (1,)), ((), ()))


def fold(value, op):
    keys, lanes = value.shape
    return op(value.reshape(keys // 8, 8, lanes), axis=0)


def window_levels(shards):
    levels = max(shards // LEVEL, 1)
    return min((WB - 2 + LEVEL) // LEVEL, max(3 * levels // 4 - 1, 0) if levels % 4 == 0 else levels - 1)


def pack_kernel(key_hbm, value_hbm, docs_hbm, own_ref, docs, sems):
    rows = key_hbm.shape[0]
    half = key_hbm.shape[1]
    copies = [
        pltpu.make_async_copy(docs_hbm, docs, sems.at[0]),
        pltpu.make_async_copy(key_hbm, own_ref.at[0:rows, 0:half], sems.at[1]),
        pltpu.make_async_copy(value_hbm, own_ref.at[0:rows, half:2 * half], sems.at[2]),
    ]
    for copy in copies:
        copy.start()
    copies[0].wait()
    count = jnp.sum((docs[...] == 0).astype(jnp.float32), axis=1, keepdims=True)
    own_ref[rows:rows + DOC_ROWS, :] = jnp.broadcast_to(count, (DOC_ROWS, 2 * half)).astype(
        jnp.bfloat16
    )
    copies[1].wait()
    copies[2].wait()


def pack(key_in, value_input, doc_ids):
    rows, half = key_in.shape
    return pl.pallas_call(
        pack_kernel,
        out_shape=jax.ShapeDtypeStruct((rows + DOC_ROWS, 2 * half), jnp.bfloat16),
        in_specs=[pl.BlockSpec(memory_space=pltpu.HBM)] * 3,
        out_specs=pl.BlockSpec(memory_space=pltpu.VMEM),
        scratch_shapes=[pltpu.VMEM((1, rows), jnp.int32), pltpu.SemaphoreType.DMA((3,))],
        compiler_params=pltpu.CompilerParams(vmem_limit_bytes=8 * 1024 * 1024),
        name="pack",
    )(key_in, value_input, doc_ids)


def head_columns(g, n):
    head = g * GROUP_SIZE + n
    return slice(head * HEAD_SIZE, (head + 1) * HEAD_SIZE)


def prepare_kernel(q_hbm, bias_ref, do_hbm, q_st, do_t, q_buf, do_buf, sems):
    rows = q_buf.shape[0]
    first = pltpu.make_async_copy(q_hbm, q_buf, sems.at[0])
    second = pltpu.make_async_copy(do_hbm, do_buf, sems.at[1])
    first.start()
    second.start()
    first.wait()
    for g in range(KEY_VALUE_HEADS):
        for n in range(GROUP_SIZE):
            columns = head_columns(g, n)
            q_st[g, n * rows:(n + 1) * rows, :] = (
                q_buf[:, columns].astype(jnp.float32) + bias_ref[:, columns]
            ).astype(jnp.bfloat16)
    second.wait()
    for g in range(KEY_VALUE_HEADS):
        for n in range(GROUP_SIZE):
            do_t[g, :, n * rows:(n + 1) * rows] = do_buf[:, head_columns(g, n)].T


def prepare(query_in, query_bias, output_gradient):
    rows, width = query_in.shape
    lanes = GROUP_SIZE * rows
    anywhere = pl.BlockSpec(memory_space=pltpu.HBM)
    vmem = pl.BlockSpec(memory_space=pltpu.VMEM)
    return pl.pallas_call(
        prepare_kernel,
        out_shape=(
            jax.ShapeDtypeStruct((KEY_VALUE_HEADS, lanes, HEAD_SIZE), jnp.bfloat16),
            jax.ShapeDtypeStruct((KEY_VALUE_HEADS, HEAD_SIZE, lanes), jnp.bfloat16),
        ),
        in_specs=[anywhere, vmem, anywhere],
        out_specs=(vmem, vmem),
        scratch_shapes=[
            pltpu.VMEM((rows, width), jnp.bfloat16),
            pltpu.VMEM((rows, width), jnp.bfloat16),
            pltpu.SemaphoreType.DMA((2,)),
        ],
        compiler_params=pltpu.CompilerParams(vmem_limit_bytes=8 * 1024 * 1024),
        cost_estimate=pl.CostEstimate(
            flops=4 * rows * width, bytes_accessed=8 * rows * width, transcendentals=0
        ),
        name="prepare",
    )(query_in, query_bias, output_gradient)


def keys_of(kv_buf, c, rows, column):
    columns = slice(column * HEAD_SIZE, (column + 1) * HEAD_SIZE)
    return jnp.concatenate([kv_buf[PAIR * c + i, 0:rows, columns] for i in range(PAIR)], axis=0)


def spread(kv_buf, level, slot, here, there, inner):
    packed = kv_buf.shape[1]
    core = inner % 2
    x = inner // 2
    for x_at in range(2):
        at = (2 * level + x_at) * packed
        place = slot * LEVEL + 2 * (x + x_at - 2 * x * x_at)
        kv_buf[place + core] = here[at:at + packed, :]
        kv_buf[place + 1 - core] = there[at:at + packed, :]


def doc_count(kv_buf, rows):
    counts = kv_buf[:, rows:rows + DOC_ROWS, 0:128].astype(jnp.float32)
    return jnp.sum(counts) * (1.0 / (DOC_ROWS * 128))


def window_start(rank, rows, first, count):
    boundary = (count + 0.5).astype(jnp.int32) + jnp.maximum(first, 0) * rows
    low_block = jnp.maximum(rank - (WB - 1), 0)
    in_second = rank * rows >= boundary
    return boundary, jnp.where(in_second, jnp.maximum(low_block, boundary // rows), low_block)


def mask_bias(key_first, q_first, boundary, chunk, rows):
    key_pos = key_first + lax.broadcasted_iota(jnp.int32, (chunk, rows), 0)
    query_pos = q_first + lax.broadcasted_iota(jnp.int32, (chunk, rows), 1)
    allowed = (key_pos <= query_pos) & (query_pos // BLK - key_pos // BLK < WB)
    allowed = allowed & ((key_pos >= boundary) == (query_pos >= boundary))
    return jnp.where(allowed, 0.0, LOW)


def lane_tiles(lanes):
    return [(at, min(at + LANE_TILE, lanes)) for at in range(0, lanes, LANE_TILE)]


def near_kernel(
    rank_ref, q_all, near_ref, near_core_ref,
    kv_buf, p_buf, stats_ref, acc,
    s_buf,
):
    depth, chunk = p_buf.shape[:2]
    rows = chunk // PAIR
    lanes = q_all.shape[1]
    tiles = lane_tiles(lanes)
    rank = rank_ref[0]
    first = (rank // LEVEL - (depth - 1)) * LEVEL
    for level in range(depth):
        spread(kv_buf, level, depth - 1 - level, near_ref, near_core_ref, rank % LEVEL)
    boundary, low_block = window_start(rank, rows, first, doc_count(kv_buf, rows))
    low = jnp.maximum(low_block - first, 0) // PAIR

    for g in range(KEY_VALUE_HEADS):
        stats_ref[g, 0:8, :] = jnp.full((8, lanes), LOW, jnp.float32)
        stats_ref[g, 8:16, :] = jnp.zeros((8, lanes), jnp.float32)
    acc[...] = jnp.zeros_like(acc)

    def score_steps(c, g):
        bias = mask_bias((first + PAIR * c) * rows, rank * rows, boundary, chunk, rows)
        k_c = keys_of(kv_buf, c, rows, g)

        def step(a, b):
            s = lax.dot_general(k_c, q_all[g, a:b, :], NT, preferred_element_type=jnp.float32)
            s = s + jnp.concatenate([bias] * ((b - a) // rows), axis=1)
            s_buf[c, :, a:b] = s
            stats_ref[g, 0:8, a:b] = jnp.maximum(stats_ref[g, 0:8, a:b], fold(s, jnp.max))

        return step

    def weight_steps(c, g, row_max):
        v_t = keys_of(kv_buf, c, rows, KEY_VALUE_HEADS + g).T

        def step(a, b):
            p = jnp.exp2(s_buf[c, :, a:b] * SCALE_LOG2 - row_max[:, a:b])
            stats_ref[g, 8:16, a:b] += fold(p, jnp.sum)
            p_bf = p.astype(jnp.bfloat16)
            p_buf[c, :, g * lanes + a:g * lanes + b] = p_bf
            acc[g, :, a:b] += jnp.dot(v_t, p_bf, preferred_element_type=jnp.float32)

        return step

    def over_chunks(*makers):
        @pl.loop(low, depth)
        def _(c):
            steps = [make(c) for make in makers]
            for a, b in tiles:
                for step in steps:
                    step(a, b)

    over_chunks(lambda c: score_steps(c, 0))
    for g in range(KEY_VALUE_HEADS):
        row_max = jnp.max(stats_ref[g, 0:8, :], axis=0, keepdims=True) * SCALE_LOG2
        makers = [lambda c: weight_steps(c, g, row_max)]
        if g + 1 < KEY_VALUE_HEADS:
            makers.append(lambda c: score_steps(c, g + 1))
        over_chunks(*makers)
        stats_ref[g, 0:1, :] = row_max
        stats_ref[g, 8:9, :] = jnp.sum(stats_ref[g, 8:16, :], axis=0, keepdims=True)


def near_attention(rank, q_all, near, near_core, depth):
    lanes = q_all.shape[1]
    rows = lanes // GROUP_SIZE
    packed = rows + DOC_ROWS
    chunk = PAIR * rows
    vmem = pl.BlockSpec(memory_space=pltpu.VMEM)
    smem = pl.BlockSpec(memory_space=pltpu.SMEM)
    heads = KEY_VALUE_HEADS
    return pl.pallas_call(
        near_kernel,
        out_shape=(
            jax.ShapeDtypeStruct((depth * LEVEL, packed, KV_WIDTH), jnp.bfloat16),
            jax.ShapeDtypeStruct((depth, chunk, heads * lanes), jnp.bfloat16),
            jax.ShapeDtypeStruct((heads, 16, lanes), jnp.float32),
            jax.ShapeDtypeStruct((heads, HEAD_SIZE, lanes), jnp.float32),
        ),
        in_specs=[smem] + [vmem] * 3,
        out_specs=(vmem,) * 4,
        scratch_shapes=[pltpu.VMEM((depth, chunk, lanes), jnp.float32)],
        compiler_params=pltpu.CompilerParams(vmem_limit_bytes=28 * 1024 * 1024),
        cost_estimate=pl.CostEstimate(
            flops=2 * 2 * heads * lanes * HEAD_SIZE * depth * chunk,
            bytes_accessed=4 * heads * lanes * HEAD_SIZE,
            transcendentals=heads * lanes * depth * chunk,
        ),
        name="near_attention",
    )(rank, q_all, near, near_core)


def kernel(
    rank_ref, q_all, do_all, kv_near, p_near, stats_ref, acc_near, far_ref, far_core_ref,
    att_ref, dq_ref, p_far, ds_buf, do_near, do_far, gb_ref, span_ref,
    kv_far, s_buf, sum_buf, factor_buf, dot_buf, acc, dq_acc,
):
    rows = att_ref.shape[0]
    depth, chunk = p_near.shape[:2]
    lanes = GROUP_SIZE * rows
    tiles = lane_tiles(lanes)
    rank = rank_ref[0]
    first = (rank // LEVEL - depth) * LEVEL
    spread(kv_far, 0, 0, far_ref, far_core_ref, rank % LEVEL)
    count = doc_count(kv_far, rows) + doc_count(kv_near, rows)
    boundary, low_block = window_start(rank, rows, first, count)
    low = jnp.maximum(low_block - first, 0) // PAIR
    span_ref[0] = low
    with_far = low == 0

    dq_acc[...] = jnp.zeros_like(dq_acc)

    @pl.when(with_far)
    def _():
        bias = mask_bias(first * rows, rank * rows, boundary, chunk, rows)
        for g in range(KEY_VALUE_HEADS):
            k_c = keys_of(kv_far, 0, rows, g)
            v_t = keys_of(kv_far, 0, rows, KEY_VALUE_HEADS + g).T
            for a, b in tiles:
                s = lax.dot_general(k_c, q_all[g, a:b, :], NT, preferred_element_type=jnp.float32)
                s = (s + jnp.concatenate([bias] * ((b - a) // rows), axis=1)) * SCALE_LOG2
                s_buf[g, :, a:b] = s
                near_max = stats_ref[g, 0:1, a:b]
                top = jnp.maximum(near_max, jnp.max(fold(s, jnp.max), axis=0, keepdims=True))
                factor = jnp.exp2(near_max - top)
                p = jnp.exp2(s_buf[g, :, a:b] - top)
                p_bf = p.astype(jnp.bfloat16)
                p_far[0, :, g * lanes + a:g * lanes + b] = p_bf
                total = jnp.sum(fold(p, jnp.sum), axis=0, keepdims=True)
                sum_buf[g, 0:1, a:b] = stats_ref[g, 8:9, a:b] * factor + total
                factor_buf[g, 0:1, a:b] = factor
                acc[g, :, a:b] = acc_near[g, :, a:b] * factor + jnp.dot(
                    v_t, p_bf, preferred_element_type=jnp.float32
                )

    @pl.when(jnp.logical_not(with_far))
    def _():
        sum_buf[:, 0:1, :] = stats_ref[:, 8:9, :]
        factor_buf[:, 0:1, :] = jnp.ones((KEY_VALUE_HEADS, 1, lanes), jnp.float32)
        acc[...] = acc_near[...]

    for g in range(KEY_VALUE_HEADS):
        inverse = 1.0 / sum_buf[g, 0:1, :]
        factor = factor_buf[g, 0:1, :]
        for n in range(GROUP_SIZE):
            at = slice(n * rows, (n + 1) * rows)
            att = (acc[g, :, at] * inverse[:, at]).astype(jnp.bfloat16)
            att_ref[:, head_columns(g, n)] = att.T
            do_n = do_all[g, :, at].astype(jnp.float32)
            dot_n = jnp.sum(do_n * att.astype(jnp.float32), axis=0, keepdims=True) * inverse[:, at]
            do_n = do_n * inverse[:, at]
            dot_buf[g, 0:1, at] = dot_n
            dot_buf[g, 1:2, at] = dot_n * factor[:, at]
            do_far[g, :, at] = do_n.astype(jnp.bfloat16)
            do_near[g, :, at] = (do_n * factor[:, at]).astype(jnp.bfloat16)

    def gradient_steps(g, c, kv_buf, at, p_buf, do_t, row):
        v_c = keys_of(kv_buf, at, rows, KEY_VALUE_HEADS + g)
        k_t = keys_of(kv_buf, at, rows, g).T

        def step(a, b):
            where = slice(g * lanes + a, g * lanes + b)
            d_p = jnp.dot(v_c, do_t[g, :, a:b], preferred_element_type=jnp.float32)
            p = p_buf[at, :, where].astype(jnp.float32)
            d_s = (p * (d_p - dot_buf[g, row:row + 1, a:b])).astype(jnp.bfloat16)
            ds_buf[c, :, where] = d_s
            dq_acc[g, :, a:b] += jnp.dot(k_t, d_s, preferred_element_type=jnp.float32)

        return step

    def gradients(c, kv_buf, at, p_buf, do_t, row):
        steps = [
            gradient_steps(g, c, kv_buf, at, p_buf, do_t, row) for g in range(KEY_VALUE_HEADS)
        ]
        for a, b in tiles:
            for step in steps:
                step(a, b)

    @pl.when(with_far)
    def _():
        gradients(0, kv_far, 0, p_far, do_far, 0)

    @pl.loop(jnp.maximum(low, 1), depth + 1)
    def _(c):
        gradients(c, kv_near, c - 1, p_near, do_near, 1)

    gb_ref[...] = jnp.zeros_like(gb_ref)
    for g in range(KEY_VALUE_HEADS):
        for n in range(GROUP_SIZE):
            columns = head_columns(g, n)
            d_q = (dq_acc[g, :, n * rows:(n + 1) * rows] * SCALE).astype(jnp.bfloat16).T
            row, at = divmod(columns.start, KV_WIDTH)
            gb_ref[row:row + 1, at:at + HEAD_SIZE] = jnp.sum(
                d_q.astype(jnp.float32), axis=0, keepdims=True
            )
            dq_ref[:, columns] = d_q


def attention(rank, q_all, do_all, kv_near, p_near, stats, acc_near, far, far_core):
    lanes = q_all.shape[1]
    rows = lanes // GROUP_SIZE
    width = QUERY_HEADS * HEAD_SIZE
    packed = rows + DOC_ROWS
    depth, chunk = p_near.shape[:2]
    vmem = pl.BlockSpec(memory_space=pltpu.VMEM)
    smem = pl.BlockSpec(memory_space=pltpu.SMEM)
    heads = KEY_VALUE_HEADS
    return pl.pallas_call(
        kernel,
        out_shape=(
            jax.ShapeDtypeStruct((rows, width), jnp.bfloat16),
            jax.ShapeDtypeStruct((rows, width), jnp.bfloat16),
            jax.ShapeDtypeStruct((1, chunk, heads * lanes), jnp.bfloat16),
            jax.ShapeDtypeStruct((depth + 1, chunk, heads * lanes), jnp.bfloat16),
            jax.ShapeDtypeStruct((heads, HEAD_SIZE, lanes), jnp.bfloat16),
            jax.ShapeDtypeStruct((heads, HEAD_SIZE, lanes), jnp.bfloat16),
            jax.ShapeDtypeStruct((-(-width // KV_WIDTH), KV_WIDTH), jnp.float32),
            jax.ShapeDtypeStruct((1,), jnp.int32),
        ),
        in_specs=[smem] + [vmem] * 8,
        out_specs=(vmem,) * 7 + (smem,),
        scratch_shapes=[
            pltpu.VMEM((LEVEL, packed, KV_WIDTH), jnp.bfloat16),
            pltpu.VMEM((heads, chunk, lanes), jnp.float32),
            pltpu.VMEM((heads, 8, lanes), jnp.float32),
            pltpu.VMEM((heads, 8, lanes), jnp.float32),
            pltpu.VMEM((heads, 8, lanes), jnp.float32),
            pltpu.VMEM((heads, HEAD_SIZE, lanes), jnp.float32),
            pltpu.VMEM((heads, HEAD_SIZE, lanes), jnp.float32),
        ],
        compiler_params=pltpu.CompilerParams(vmem_limit_bytes=28 * 1024 * 1024),
        cost_estimate=pl.CostEstimate(
            flops=2 * 2 * width * HEAD_SIZE * (depth + 2) * chunk,
            bytes_accessed=8 * rows * width,
            transcendentals=0,
        ),
        name="attention",
    )(rank, q_all, do_all, kv_near, p_near, stats, acc_near, far, far_core)


def level_kernel(
    level, p_at, rank_ref, span_ref, p_buf, ds_buf, q_all, do_t, keep_ref, send_ref
):
    chunk = p_buf.shape[1]
    rows = chunk // PAIR
    lanes = GROUP_SIZE * rows
    inner = rank_ref[0] % LEVEL
    my_core = inner % 2
    my_x = inner // 2
    active = level >= span_ref[0]

    @pl.when(active)
    def _():
        for g in range(KEY_VALUE_HEADS):
            where = slice(g * lanes, (g + 1) * lanes)
            d_key = jnp.dot(
                ds_buf[level, :, where], q_all[g], preferred_element_type=jnp.float32
            ) * SCALE
            d_value = lax.dot_general(
                p_buf[p_at, :, where], do_t[g], NT, preferred_element_type=jnp.float32
            )
            for value, column in ((d_key, g), (d_value, KEY_VALUE_HEADS + g)):
                columns = slice(column * HEAD_SIZE, (column + 1) * HEAD_SIZE)
                for x_at in range(2):
                    one = value[2 * x_at * rows:(2 * x_at + 1) * rows]
                    two = value[(2 * x_at + 1) * rows:(2 * x_at + 2) * rows]
                    place = (x_at + my_x) % 2
                    at = pl.ds(pl.multiple_of(place * rows, rows), rows)
                    keep_ref[at, columns] = jnp.where(my_core == 0, one, two)
                    send_ref[at, columns] = jnp.where(my_core == 0, two, one).astype(jnp.bfloat16)

    @pl.when(jnp.logical_not(active))
    def _():
        keep_ref[...] = jnp.zeros_like(keep_ref)
        send_ref[...] = jnp.zeros_like(send_ref)


def level_gradients(level, p_at, rank, span, p_all, ds_all, q_all, do_t):
    chunk, width = p_all.shape[1:]
    rows = chunk // PAIR
    vmem = pl.BlockSpec(memory_space=pltpu.VMEM)
    smem = pl.BlockSpec(memory_space=pltpu.SMEM)
    return pl.pallas_call(
        functools.partial(level_kernel, level, p_at),
        out_shape=(
            jax.ShapeDtypeStruct((2 * rows, KV_WIDTH), jnp.float32),
            jax.ShapeDtypeStruct((2 * rows, KV_WIDTH), jnp.bfloat16),
        ),
        in_specs=[smem, smem] + [vmem] * 4,
        out_specs=(vmem, vmem),
        compiler_params=pltpu.CompilerParams(vmem_limit_bytes=28 * 1024 * 1024),
        cost_estimate=pl.CostEstimate(
            flops=2 * 2 * LEVEL * rows * width * HEAD_SIZE,
            bytes_accessed=4 * LEVEL * rows * width,
            transcendentals=0,
        ),
        name="level_gradients",
    )(rank, span, p_all, ds_all, q_all, do_t)


def shifted(value, steps):
    count = lax.axis_size("ctx")
    first, last = max(0, -steps), min(count, count - steps)
    return lax.ppermute(value, "ctx", [(at, at + steps) for at in range(first, last)])


def rotated(value, steps):
    count = lax.axis_size("ctx")
    return lax.ppermute(value, "ctx", [(at, (at + steps) % count) for at in range(count)])


def swapped(value, bit, axis="ctx"):
    return lax.ppermute(value, axis, [(at, at ^ bit) for at in range(lax.axis_size(axis))])


def bias_rows(rows):
    high = lax.reduce_precision(rows, 8, 7)
    both = jnp.concatenate([high, rows - high]).astype(jnp.bfloat16)
    return jnp.pad(both, ((0, -both.shape[0] % 16), (0, 0)))


def local(query_in, key_in, value_input, output_gradient, doc_ids, query_bias):
    rows = query_in.shape[1]
    shards = lax.axis_size("ctx")
    depth = window_levels(shards)
    rank = lax.axis_index("ctx").astype(jnp.int32)
    own = pack(key_in[0], value_input[0], doc_ids)

    ups = [shifted(own, LEVEL * step) for step in range(1, depth + 1)]
    x_own = swapped(own, 2)
    q_all, do_all = prepare(query_in[0], query_bias[None], output_gradient[0])
    ups[0], x_own, q_all, do_all = lax.optimization_barrier((ups[0], x_own, q_all, do_all))
    near = [own, x_own]
    for up in ups[:-1]:
        near += [up, swapped(up, 2)]
    x_far = swapped(ups[-1], 2)
    far, near = lax.optimization_barrier((ups[-1], near))
    near = jnp.concatenate(near, axis=0)
    near_core = swapped(near, 1)
    rank = rank.reshape(1)
    kv_near, p_near, stats, acc_near = near_attention(rank, q_all, near, near_core, depth)
    x_far, p_near = lax.optimization_barrier((x_far, p_near))
    far = jnp.concatenate([far, x_far], axis=0)
    far_core = swapped(far, 1)
    attended, grad_query, p_far, ds_all, do_near, do_far, bias_part, span = attention(
        rank, q_all, do_all, kv_near, p_near, stats, acc_near, far, far_core
    )

    levels = shards // LEVEL
    carried = levels == 4 and depth == 2
    bit = 1
    while bit < lax.axis_size("dp"):
        bias_part = bias_part + swapped(bias_part, bit, "dp")
        bit *= 2
    bias_total = bias_part

    def joined(value):
        return jnp.concatenate([value, bias_rows(bias_total)], axis=0) if carried else value

    def bias_of(got):
        return got[rows:rows + half_rows].astype(jnp.float32) + got[
            rows + half_rows:rows + 2 * half_rows
        ].astype(jnp.float32)

    half_rows = bias_part.shape[0]
    parts = [None] * (depth + 1)
    down = [None] * (depth + 1)
    across = [None] * (depth + 1)
    keeps = [None] * (depth + 1)

    def products(step):
        nonlocal bias_total
        if step == depth:
            keep, send = level_gradients(0, 0, rank, span, p_far, ds_all, q_all, do_far)
        else:
            level = depth - step
            keep, send = level_gradients(
                level, level - 1, rank, span, p_near, ds_all, q_all, do_near
            )
        if step == depth and carried:
            got = swapped(jnp.concatenate([send, bias_rows(bias_total)], axis=0), 1)
            bias_total = bias_total + bias_of(got[rows:])
            got = got[:2 * rows]
        else:
            got = swapped(send, 1)
        both = keep + got.astype(jnp.float32)
        keeps[step] = both[:rows]
        away = both[rows:].astype(jnp.bfloat16)
        across[step] = swapped(joined(away) if step == depth else away, 2)

    def collected(step):
        nonlocal bias_total
        if step == depth and carried:
            bias_total = bias_total + bias_of(across[step])
        parts[step] = keeps[step] + across[step][:rows].astype(jnp.float32)
        if step == 0:
            return
        sent = parts[step].astype(jnp.bfloat16)
        if carried:
            sent = joined(sent)
            down[step] = rotated(sent, -LEVEL * step)
        else:
            down[step] = shifted(sent, -LEVEL * step)
        if step > 1:
            across[step - 1], _ = lax.optimization_barrier((across[step - 1], sent))

    for step in range(depth, -1, -1):
        if step + 2 <= depth:
            across[step + 2], ds_all = lax.optimization_barrier((across[step + 2], ds_all))
        products(step)
    for step in range(depth, -1, -1):
        collected(step)
    if carried:
        bias_total = (
            bias_total + rotated(bias_total, LEVEL) + bias_of(down[1]) + bias_of(down[2])
        )
    else:
        bit = 1
        while bit < shards:
            bias_total = bias_total + swapped(bias_total, bit)
            bit *= 2
    bias_total = bias_total.reshape(-1)[:query_bias.shape[0]]
    down = [None if part is None else part[:rows] for part in down]
    total = parts[0]
    for step in range(depth, 0, -1):
        total = total + down[step].astype(jnp.float32)
    total = total.astype(jnp.bfloat16)
    half = KEY_VALUE_HEADS * HEAD_SIZE
    return (
        attended[None],
        grad_query[None],
        total[:, :half][None],
        total[:, half:][None],
        bias_total,
    )


def solution(mesh):
    placed = (
        P("dp", "ctx", None),
        P("dp", "ctx", None),
        P("dp", "ctx", None),
        P("dp", "ctx", None),
        P("dp", "ctx"),
        P(),
    )
    return jax.shard_map(
        local,
        mesh=mesh,
        in_specs=placed,
        out_specs=(
            P("dp", "ctx", None),
            P("dp", "ctx", None),
            P("dp", "ctx", None),
            P("dp", "ctx", None),
            P(),
        ),
        check_vma=False,
    )
```

```python
import functools
import math

import jax
import jax.numpy as jnp
from jax import lax
from jax.experimental import pallas as pl
from jax.experimental.pallas import tpu as pltpu
from jax.sharding import PartitionSpec as P

QUERY_HEADS = 14
KEY_VALUE_HEADS = 2
HEAD_SIZE = 128
GROUP_SIZE = 7
BLK = 128
WB = 16
DOC_ROWS = 16
PAIR = 4
LEVEL = 4
LANE_TILE = 256
KV_WIDTH = 2 * KEY_VALUE_HEADS * HEAD_SIZE
SCALE = 1.0 / math.sqrt(HEAD_SIZE)
SCALE_LOG2 = SCALE * math.log2(math.e)
LOW = -1e30

NT = (((1,), (1,)), ((), ()))


def fold(value, op):
    keys, lanes = value.shape
    return op(value.reshape(keys // 8, 8, lanes), axis=0)


def window_levels(shards):
    levels = max(shards // LEVEL, 1)
    return min((WB - 2 + LEVEL) // LEVEL, max(3 * levels // 4 - 1, 0) if levels % 4 == 0 else levels - 1)


def pack_kernel(key_hbm, value_hbm, docs_hbm, own_ref, docs, sems):
    rows = key_hbm.shape[0]
    half = key_hbm.shape[1]
    copies = [
        pltpu.make_async_copy(docs_hbm, docs, sems.at[0]),
        pltpu.make_async_copy(key_hbm, own_ref.at[0:rows, 0:half], sems.at[1]),
        pltpu.make_async_copy(value_hbm, own_ref.at[0:rows, half:2 * half], sems.at[2]),
    ]
    for copy in copies:
        copy.start()
    copies[0].wait()
    count = jnp.sum((docs[...] == 0).astype(jnp.float32), axis=1, keepdims=True)
    own_ref[rows:rows + DOC_ROWS, :] = jnp.broadcast_to(count, (DOC_ROWS, 2 * half)).astype(
        jnp.bfloat16
    )
    copies[1].wait()
    copies[2].wait()


def pack(key_in, value_input, doc_ids):
    rows, half = key_in.shape
    return pl.pallas_call(
        pack_kernel,
        out_shape=jax.ShapeDtypeStruct((rows + DOC_ROWS, 2 * half), jnp.bfloat16),
        in_specs=[pl.BlockSpec(memory_space=pltpu.HBM)] * 3,
        out_specs=pl.BlockSpec(memory_space=pltpu.VMEM),
        scratch_shapes=[pltpu.VMEM((1, rows), jnp.int32), pltpu.SemaphoreType.DMA((3,))],
        compiler_params=pltpu.CompilerParams(vmem_limit_bytes=8 * 1024 * 1024),
        name="pack",
    )(key_in, value_input, doc_ids)


def head_columns(g, n):
    head = g * GROUP_SIZE + n
    return slice(head * HEAD_SIZE, (head + 1) * HEAD_SIZE)


def prepare_kernel(q_hbm, bias_ref, do_hbm, q_st, do_t, q_buf, do_buf, sems):
    rows = q_buf.shape[0]
    first = pltpu.make_async_copy(q_hbm, q_buf, sems.at[0])
    second = pltpu.make_async_copy(do_hbm, do_buf, sems.at[1])
    first.start()
    second.start()
    first.wait()
    for g in range(KEY_VALUE_HEADS):
        for n in range(GROUP_SIZE):
            columns = head_columns(g, n)
            q_st[g, n * rows:(n + 1) * rows, :] = (
                q_buf[:, columns].astype(jnp.float32) + bias_ref[:, columns]
            ).astype(jnp.bfloat16)
    second.wait()
    for g in range(KEY_VALUE_HEADS):
        for n in range(GROUP_SIZE):
            do_t[g, :, n * rows:(n + 1) * rows] = do_buf[:, head_columns(g, n)].T


def prepare(query_in, query_bias, output_gradient):
    rows, width = query_in.shape
    lanes = GROUP_SIZE * rows
    anywhere = pl.BlockSpec(memory_space=pltpu.HBM)
    vmem = pl.BlockSpec(memory_space=pltpu.VMEM)
    return pl.pallas_call(
        prepare_kernel,
        out_shape=(
            jax.ShapeDtypeStruct((KEY_VALUE_HEADS, lanes, HEAD_SIZE), jnp.bfloat16),
            jax.ShapeDtypeStruct((KEY_VALUE_HEADS, HEAD_SIZE, lanes), jnp.bfloat16),
        ),
        in_specs=[anywhere, vmem, anywhere],
        out_specs=(vmem, vmem),
        scratch_shapes=[
            pltpu.VMEM((rows, width), jnp.bfloat16),
            pltpu.VMEM((rows, width), jnp.bfloat16),
            pltpu.SemaphoreType.DMA((2,)),
        ],
        compiler_params=pltpu.CompilerParams(vmem_limit_bytes=8 * 1024 * 1024),
        cost_estimate=pl.CostEstimate(
            flops=4 * rows * width, bytes_accessed=8 * rows * width, transcendentals=0
        ),
        name="prepare",
    )(query_in, query_bias, output_gradient)


def keys_of(kv_buf, c, rows, column):
    columns = slice(column * HEAD_SIZE, (column + 1) * HEAD_SIZE)
    return jnp.concatenate([kv_buf[PAIR * c + i, 0:rows, columns] for i in range(PAIR)], axis=0)


def spread(kv_buf, level, slot, here, there, inner):
    packed = kv_buf.shape[1]
    core = inner % 2
    x = inner // 2
    for x_at in range(2):
        at = (2 * level + x_at) * packed
        place = slot * LEVEL + 2 * (x + x_at - 2 * x * x_at)
        kv_buf[place + core] = here[at:at + packed, :]
        kv_buf[place + 1 - core] = there[at:at + packed, :]


def doc_count(kv_buf, rows):
    counts = kv_buf[:, rows:rows + DOC_ROWS, 0:128].astype(jnp.float32)
    return jnp.sum(counts) * (1.0 / (DOC_ROWS * 128))


def window_start(rank, rows, first, count):
    boundary = (count + 0.5).astype(jnp.int32) + jnp.maximum(first, 0) * rows
    low_block = jnp.maximum(rank - (WB - 1), 0)
    in_second = rank * rows >= boundary
    return boundary, jnp.where(in_second, jnp.maximum(low_block, boundary // rows), low_block)


def mask_bias(key_first, q_first, boundary, chunk, rows):
    key_pos = key_first + lax.broadcasted_iota(jnp.int32, (chunk, rows), 0)
    query_pos = q_first + lax.broadcasted_iota(jnp.int32, (chunk, rows), 1)
    allowed = (key_pos <= query_pos) & (query_pos // BLK - key_pos // BLK < WB)
    allowed = allowed & ((key_pos >= boundary) == (query_pos >= boundary))
    return jnp.where(allowed, 0.0, LOW)


def lane_tiles(lanes):
    return [(at, min(at + LANE_TILE, lanes)) for at in range(0, lanes, LANE_TILE)]


def near_kernel(
    rank_ref, q_all, near_ref, near_core_ref,
    kv_buf, p_buf, stats_ref, acc,
    s_buf,
):
    depth, chunk = p_buf.shape[:2]
    rows = chunk // PAIR
    lanes = q_all.shape[1]
    tiles = lane_tiles(lanes)
    rank = rank_ref[0]
    first = (rank // LEVEL - (depth - 1)) * LEVEL
    for level in range(depth):
        spread(kv_buf, level, depth - 1 - level, near_ref, near_core_ref, rank % LEVEL)
    boundary, low_block = window_start(rank, rows, first, doc_count(kv_buf, rows))
    low = jnp.maximum(low_block - first, 0) // PAIR

    for g in range(KEY_VALUE_HEADS):
        stats_ref[g, 0:8, :] = jnp.full((8, lanes), LOW, jnp.float32)
        stats_ref[g, 8:16, :] = jnp.zeros((8, lanes), jnp.float32)
    acc[...] = jnp.zeros_like(acc)

    def score_steps(c, g):
        bias = mask_bias((first + PAIR * c) * rows, rank * rows, boundary, chunk, rows)
        k_c = keys_of(kv_buf, c, rows, g)

        def step(a, b):
            s = lax.dot_general(k_c, q_all[g, a:b, :], NT, preferred_element_type=jnp.float32)
            s = s + jnp.concatenate([bias] * ((b - a) // rows), axis=1)
            s_buf[c, :, a:b] = s
            stats_ref[g, 0:8, a:b] = jnp.maximum(stats_ref[g, 0:8, a:b], fold(s, jnp.max))

        return step

    def weight_steps(c, g, row_max):
        v_t = keys_of(kv_buf, c, rows, KEY_VALUE_HEADS + g).T

        def step(a, b):
            p = jnp.exp2(s_buf[c, :, a:b] * SCALE_LOG2 - row_max[:, a:b])
            stats_ref[g, 8:16, a:b] += fold(p, jnp.sum)
            p_bf = p.astype(jnp.bfloat16)
            p_buf[c, :, g * lanes + a:g * lanes + b] = p_bf
            acc[g, :, a:b] += jnp.dot(v_t, p_bf, preferred_element_type=jnp.float32)

        return step

    def over_chunks(*makers):
        @pl.loop(low, depth)
        def _(c):
            steps = [make(c) for make in makers]
            for a, b in tiles:
                for step in steps:
                    step(a, b)

    over_chunks(lambda c: score_steps(c, 0))
    for g in range(KEY_VALUE_HEADS):
        row_max = jnp.max(stats_ref[g, 0:8, :], axis=0, keepdims=True) * SCALE_LOG2
        makers = [lambda c: weight_steps(c, g, row_max)]
        if g + 1 < KEY_VALUE_HEADS:
            makers.append(lambda c: score_steps(c, g + 1))
        over_chunks(*makers)
        stats_ref[g, 0:1, :] = row_max
        stats_ref[g, 8:9, :] = jnp.sum(stats_ref[g, 8:16, :], axis=0, keepdims=True)


def near_attention(rank, q_all, near, near_core, depth):
    lanes = q_all.shape[1]
    rows = lanes // GROUP_SIZE
    packed = rows + DOC_ROWS
    chunk = PAIR * rows
    vmem = pl.BlockSpec(memory_space=pltpu.VMEM)
    smem = pl.BlockSpec(memory_space=pltpu.SMEM)
    heads = KEY_VALUE_HEADS
    return pl.pallas_call(
        near_kernel,
        out_shape=(
            jax.ShapeDtypeStruct((depth * LEVEL, packed, KV_WIDTH), jnp.bfloat16),
            jax.ShapeDtypeStruct((depth, chunk, heads * lanes), jnp.bfloat16),
            jax.ShapeDtypeStruct((heads, 16, lanes), jnp.float32),
            jax.ShapeDtypeStruct((heads, HEAD_SIZE, lanes), jnp.float32),
        ),
        in_specs=[smem] + [vmem] * 3,
        out_specs=(vmem,) * 4,
        scratch_shapes=[pltpu.VMEM((depth, chunk, lanes), jnp.float32)],
        compiler_params=pltpu.CompilerParams(vmem_limit_bytes=28 * 1024 * 1024),
        cost_estimate=pl.CostEstimate(
            flops=2 * 2 * heads * lanes * HEAD_SIZE * depth * chunk,
            bytes_accessed=4 * heads * lanes * HEAD_SIZE,
            transcendentals=heads * lanes * depth * chunk,
        ),
        name="near_attention",
    )(rank, q_all, near, near_core)


def kernel(
    rank_ref, q_all, do_all, kv_near, p_near, stats_ref, acc_near, far_ref, far_core_ref,
    att_ref, dq_ref, p_far, ds_buf, do_near, do_far, gb_ref, span_ref,
    kv_far, s_buf, sum_buf, factor_buf, dot_buf, acc, dq_acc,
):
    rows = att_ref.shape[0]
    depth, chunk = p_near.shape[:2]
    lanes = GROUP_SIZE * rows
    tiles = lane_tiles(lanes)
    rank = rank_ref[0]
    first = (rank // LEVEL - depth) * LEVEL
    spread(kv_far, 0, 0, far_ref, far_core_ref, rank % LEVEL)
    count = doc_count(kv_far, rows) + doc_count(kv_near, rows)
    boundary, low_block = window_start(rank, rows, first, count)
    low = jnp.maximum(low_block - first, 0) // PAIR
    span_ref[0] = low
    with_far = low == 0

    dq_acc[...] = jnp.zeros_like(dq_acc)

    @pl.when(with_far)
    def _():
        bias = mask_bias(first * rows, rank * rows, boundary, chunk, rows)

        def score(g, a, b):
            k_c = keys_of(kv_far, 0, rows, g)
            s = lax.dot_general(k_c, q_all[g, a:b, :], NT, preferred_element_type=jnp.float32)
            s = s + jnp.concatenate([bias] * ((b - a) // rows), axis=1)
            s_buf[g, :, a:b] = s
            far_max = jnp.max(fold(s, jnp.max), axis=0, keepdims=True) * SCALE_LOG2
            factor_buf[g, 0:1, a:b] = jnp.maximum(stats_ref[g, 0:1, a:b], far_max)

        def weight(g, a, b):
            v_t = keys_of(kv_far, 0, rows, KEY_VALUE_HEADS + g).T
            top = factor_buf[g, 0:1, a:b]
            factor = jnp.exp2(stats_ref[g, 0:1, a:b] - top)
            p = jnp.exp2(s_buf[g, :, a:b] * SCALE_LOG2 - top)
            p_bf = p.astype(jnp.bfloat16)
            p_far[0, :, g * lanes + a:g * lanes + b] = p_bf
            total = jnp.sum(fold(p, jnp.sum), axis=0, keepdims=True)
            sum_buf[g, 0:1, a:b] = stats_ref[g, 8:9, a:b] * factor + total
            factor_buf[g, 0:1, a:b] = factor
            acc[g, :, a:b] = acc_near[g, :, a:b] * factor + jnp.dot(
                v_t, p_bf, preferred_element_type=jnp.float32
            )

        for a, b in tiles:
            score(0, a, b)
        for g in range(KEY_VALUE_HEADS):
            for a, b in tiles:
                weight(g, a, b)
                if g + 1 < KEY_VALUE_HEADS:
                    score(g + 1, a, b)

    @pl.when(jnp.logical_not(with_far))
    def _():
        sum_buf[:, 0:1, :] = stats_ref[:, 8:9, :]
        factor_buf[:, 0:1, :] = jnp.ones((KEY_VALUE_HEADS, 1, lanes), jnp.float32)
        acc[...] = acc_near[...]

    for g in range(KEY_VALUE_HEADS):
        inverse = 1.0 / sum_buf[g, 0:1, :]
        factor = factor_buf[g, 0:1, :]
        for n in range(GROUP_SIZE):
            at = slice(n * rows, (n + 1) * rows)
            att = (acc[g, :, at] * inverse[:, at]).astype(jnp.bfloat16)
            att_ref[:, head_columns(g, n)] = att.T
            do_n = do_all[g, :, at].astype(jnp.float32)
            dot_n = jnp.sum(do_n * att.astype(jnp.float32), axis=0, keepdims=True) * inverse[:, at]
            do_n = do_n * inverse[:, at]
            dot_buf[g, 0:1, at] = dot_n
            dot_buf[g, 1:2, at] = dot_n * factor[:, at]
            do_far[g, :, at] = do_n.astype(jnp.bfloat16)
            do_near[g, :, at] = (do_n * factor[:, at]).astype(jnp.bfloat16)

    def gradient_steps(g, c, kv_buf, at, p_buf, do_t, row):
        v_c = keys_of(kv_buf, at, rows, KEY_VALUE_HEADS + g)
        k_t = keys_of(kv_buf, at, rows, g).T

        def step(a, b):
            where = slice(g * lanes + a, g * lanes + b)
            d_p = jnp.dot(v_c, do_t[g, :, a:b], preferred_element_type=jnp.float32)
            p = p_buf[at, :, where].astype(jnp.float32)
            d_s = (p * (d_p - dot_buf[g, row:row + 1, a:b])).astype(jnp.bfloat16)
            ds_buf[c, :, where] = d_s
            dq_acc[g, :, a:b] += jnp.dot(k_t, d_s, preferred_element_type=jnp.float32)

        return step

    def gradients(c, kv_buf, at, p_buf, do_t, row):
        steps = [
            gradient_steps(g, c, kv_buf, at, p_buf, do_t, row) for g in range(KEY_VALUE_HEADS)
        ]
        for a, b in tiles:
            for step in steps:
                step(a, b)

    @pl.when(with_far)
    def _():
        gradients(0, kv_far, 0, p_far, do_far, 0)

    @pl.loop(jnp.maximum(low, 1), depth + 1)
    def _(c):
        gradients(c, kv_near, c - 1, p_near, do_near, 1)

    gb_ref[...] = jnp.zeros_like(gb_ref)
    for g in range(KEY_VALUE_HEADS):
        for n in range(GROUP_SIZE):
            columns = head_columns(g, n)
            d_q = (dq_acc[g, :, n * rows:(n + 1) * rows] * SCALE).astype(jnp.bfloat16).T
            row, at = divmod(columns.start, KV_WIDTH)
            gb_ref[row:row + 1, at:at + HEAD_SIZE] = jnp.sum(
                d_q.astype(jnp.float32), axis=0, keepdims=True
            )
            dq_ref[:, columns] = d_q


def attention(rank, q_all, do_all, kv_near, p_near, stats, acc_near, far, far_core):
    lanes = q_all.shape[1]
    rows = lanes // GROUP_SIZE
    width = QUERY_HEADS * HEAD_SIZE
    packed = rows + DOC_ROWS
    depth, chunk = p_near.shape[:2]
    vmem = pl.BlockSpec(memory_space=pltpu.VMEM)
    smem = pl.BlockSpec(memory_space=pltpu.SMEM)
    heads = KEY_VALUE_HEADS
    return pl.pallas_call(
        kernel,
        out_shape=(
            jax.ShapeDtypeStruct((rows, width), jnp.bfloat16),
            jax.ShapeDtypeStruct((rows, width), jnp.bfloat16),
            jax.ShapeDtypeStruct((1, chunk, heads * lanes), jnp.bfloat16),
            jax.ShapeDtypeStruct((depth + 1, chunk, heads * lanes), jnp.bfloat16),
            jax.ShapeDtypeStruct((heads, HEAD_SIZE, lanes), jnp.bfloat16),
            jax.ShapeDtypeStruct((heads, HEAD_SIZE, lanes), jnp.bfloat16),
            jax.ShapeDtypeStruct((-(-width // KV_WIDTH), KV_WIDTH), jnp.float32),
            jax.ShapeDtypeStruct((1,), jnp.int32),
        ),
        in_specs=[smem] + [vmem] * 8,
        out_specs=(vmem,) * 7 + (smem,),
        scratch_shapes=[
            pltpu.VMEM((LEVEL, packed, KV_WIDTH), jnp.bfloat16),
            pltpu.VMEM((heads, chunk, lanes), jnp.float32),
            pltpu.VMEM((heads, 8, lanes), jnp.float32),
            pltpu.VMEM((heads, 8, lanes), jnp.float32),
            pltpu.VMEM((heads, 8, lanes), jnp.float32),
            pltpu.VMEM((heads, HEAD_SIZE, lanes), jnp.float32),
            pltpu.VMEM((heads, HEAD_SIZE, lanes), jnp.float32),
        ],
        compiler_params=pltpu.CompilerParams(vmem_limit_bytes=28 * 1024 * 1024),
        cost_estimate=pl.CostEstimate(
            flops=2 * 2 * width * HEAD_SIZE * (depth + 2) * chunk,
            bytes_accessed=8 * rows * width,
            transcendentals=0,
        ),
        name="attention",
    )(rank, q_all, do_all, kv_near, p_near, stats, acc_near, far, far_core)


def level_kernel(
    level, p_at, rank_ref, span_ref, p_buf, ds_buf, q_all, do_t, keep_ref, send_ref
):
    chunk = p_buf.shape[1]
    rows = chunk // PAIR
    lanes = GROUP_SIZE * rows
    inner = rank_ref[0] % LEVEL
    my_core = inner % 2
    my_x = inner // 2
    active = level >= span_ref[0]

    @pl.when(active)
    def _():
        for g in range(KEY_VALUE_HEADS):
            where = slice(g * lanes, (g + 1) * lanes)
            d_key = jnp.dot(
                ds_buf[level, :, where], q_all[g], preferred_element_type=jnp.float32
            ) * SCALE
            d_value = lax.dot_general(
                p_buf[p_at, :, where], do_t[g], NT, preferred_element_type=jnp.float32
            )
            for value, column in ((d_key, g), (d_value, KEY_VALUE_HEADS + g)):
                columns = slice(column * HEAD_SIZE, (column + 1) * HEAD_SIZE)
                for x_at in range(2):
                    one = value[2 * x_at * rows:(2 * x_at + 1) * rows]
                    two = value[(2 * x_at + 1) * rows:(2 * x_at + 2) * rows]
                    place = (x_at + my_x) % 2
                    at = pl.ds(pl.multiple_of(place * rows, rows), rows)
                    keep_ref[at, columns] = jnp.where(my_core == 0, one, two)
                    send_ref[at, columns] = jnp.where(my_core == 0, two, one).astype(jnp.bfloat16)

    @pl.when(jnp.logical_not(active))
    def _():
        keep_ref[...] = jnp.zeros_like(keep_ref)
        send_ref[...] = jnp.zeros_like(send_ref)


def level_gradients(level, p_at, rank, span, p_all, ds_all, q_all, do_t):
    chunk, width = p_all.shape[1:]
    rows = chunk // PAIR
    vmem = pl.BlockSpec(memory_space=pltpu.VMEM)
    smem = pl.BlockSpec(memory_space=pltpu.SMEM)
    return pl.pallas_call(
        functools.partial(level_kernel, level, p_at),
        out_shape=(
            jax.ShapeDtypeStruct((2 * rows, KV_WIDTH), jnp.float32),
            jax.ShapeDtypeStruct((2 * rows, KV_WIDTH), jnp.bfloat16),
        ),
        in_specs=[smem, smem] + [vmem] * 4,
        out_specs=(vmem, vmem),
        compiler_params=pltpu.CompilerParams(vmem_limit_bytes=28 * 1024 * 1024),
        cost_estimate=pl.CostEstimate(
            flops=2 * 2 * LEVEL * rows * width * HEAD_SIZE,
            bytes_accessed=4 * LEVEL * rows * width,
            transcendentals=0,
        ),
        name="level_gradients",
    )(rank, span, p_all, ds_all, q_all, do_t)


def shifted(value, steps):
    count = lax.axis_size("ctx")
    first, last = max(0, -steps), min(count, count - steps)
    return lax.ppermute(value, "ctx", [(at, at + steps) for at in range(first, last)])


def rotated(value, steps):
    count = lax.axis_size("ctx")
    return lax.ppermute(value, "ctx", [(at, (at + steps) % count) for at in range(count)])


def swapped(value, bit, axis="ctx"):
    return lax.ppermute(value, axis, [(at, at ^ bit) for at in range(lax.axis_size(axis))])


def bias_rows(rows):
    high = lax.reduce_precision(rows, 8, 7)
    both = jnp.concatenate([high, rows - high]).astype(jnp.bfloat16)
    return jnp.pad(both, ((0, -both.shape[0] % 16), (0, 0)))


def local(query_in, key_in, value_input, output_gradient, doc_ids, query_bias):
    rows = query_in.shape[1]
    shards = lax.axis_size("ctx")
    depth = window_levels(shards)
    rank = lax.axis_index("ctx").astype(jnp.int32)
    own = pack(key_in[0], value_input[0], doc_ids)

    ups = [shifted(own, LEVEL * step) for step in range(1, depth + 1)]
    x_own = swapped(own, 2)
    q_all, do_all = prepare(query_in[0], query_bias[None], output_gradient[0])
    ups[0], x_own, q_all, do_all = lax.optimization_barrier((ups[0], x_own, q_all, do_all))
    near = [own, x_own]
    for up in ups[:-1]:
        near += [up, swapped(up, 2)]
    x_far = swapped(ups[-1], 2)
    far, near = lax.optimization_barrier((ups[-1], near))
    near = jnp.concatenate(near, axis=0)
    near_core = swapped(near, 1)
    rank = rank.reshape(1)
    kv_near, p_near, stats, acc_near = near_attention(rank, q_all, near, near_core, depth)
    x_far, p_near = lax.optimization_barrier((x_far, p_near))
    far = jnp.concatenate([far, x_far], axis=0)
    far_core = swapped(far, 1)
    attended, grad_query, p_far, ds_all, do_near, do_far, bias_part, span = attention(
        rank, q_all, do_all, kv_near, p_near, stats, acc_near, far, far_core
    )

    levels = shards // LEVEL
    carried = levels == 4 and depth == 2
    bit = 1
    while bit < lax.axis_size("dp"):
        bias_part = bias_part + swapped(bias_part, bit, "dp")
        bit *= 2
    bias_total = bias_part

    def joined(value):
        return jnp.concatenate([value, bias_rows(bias_total)], axis=0) if carried else value

    def bias_of(got):
        return got[rows:rows + half_rows].astype(jnp.float32) + got[
            rows + half_rows:rows + 2 * half_rows
        ].astype(jnp.float32)

    half_rows = bias_part.shape[0]
    sends = [None] * (depth + 1)
    keeps = [None] * (depth + 1)
    for step in range(depth, -1, -1):
        if step == depth:
            keep, send = level_gradients(0, 0, rank, span, p_far, ds_all, q_all, do_far)
        else:
            level = depth - step
            keep, send = level_gradients(
                level, level - 1, rank, span, p_near, ds_all, q_all, do_near
            )
        send, ds_all = lax.optimization_barrier((send, ds_all))
        if step == max(depth - 1, 0) and carried:
            got = swapped(jnp.concatenate([send, bias_rows(bias_total)], axis=0), 1)
            bias_total = bias_total + bias_of(got[rows:])
            got = got[:2 * rows]
        else:
            got = swapped(send, 1)
        keeps[step] = keep + got.astype(jnp.float32)
        sends[step] = send

    across = [None] * (depth + 1)
    for step in range(depth, -1, -1):
        away = keeps[step][rows:].astype(jnp.bfloat16)
        if step == depth:
            away, ds_all = lax.optimization_barrier((away, ds_all))
            away = joined(away)
        across[step] = swapped(away, 2)
    down = [None] * (depth + 1)
    total = None
    for step in range(depth, -1, -1):
        if step == depth and carried:
            bias_total = bias_total + bias_of(across[step])
        total = keeps[step][:rows] + across[step][:rows].astype(jnp.float32)
        if step:
            sent = joined(total.astype(jnp.bfloat16))
            down[step] = (rotated if carried else shifted)(sent, -LEVEL * step)
            across[step - 1], _ = lax.optimization_barrier((across[step - 1], sent))
    if carried:
        bias_total = (
            bias_total + rotated(bias_total, LEVEL) + bias_of(down[1]) + bias_of(down[2])
        )
    else:
        bit = 1
        while bit < shards:
            bias_total = bias_total + swapped(bias_total, bit)
            bit *= 2
    bias_total = bias_total.reshape(-1)[:query_bias.shape[0]]
    down = [None if part is None else part[:rows] for part in down]
    for step in range(depth, 0, -1):
        total = total + down[step].astype(jnp.float32)
    total = total.astype(jnp.bfloat16)
    half = KEY_VALUE_HEADS * HEAD_SIZE
    return (
        attended[None],
        grad_query[None],
        total[:, :half][None],
        total[:, half:][None],
        bias_total,
    )


def solution(mesh):
    placed = (
        P("dp", "ctx", None),
        P("dp", "ctx", None),
        P("dp", "ctx", None),
        P("dp", "ctx", None),
        P("dp", "ctx"),
        P(),
    )
    return jax.shard_map(
        local,
        mesh=mesh,
        in_specs=placed,
        out_specs=(
            P("dp", "ctx", None),
            P("dp", "ctx", None),
            P("dp", "ctx", None),
            P("dp", "ctx", None),
            P(),
        ),
        check_vma=False,
    )
```

```python
import functools
import math

import jax
import jax.numpy as jnp
from jax import lax
from jax.experimental import pallas as pl
from jax.experimental.pallas import tpu as pltpu
from jax.sharding import PartitionSpec as P

QUERY_HEADS = 14
KEY_VALUE_HEADS = 2
HEAD_SIZE = 128
GROUP_SIZE = 7
BLK = 128
WB = 16
DOC_ROWS = 16
PAIR = 4
LEVEL = 4
LANE_TILE = 256
KV_WIDTH = 2 * KEY_VALUE_HEADS * HEAD_SIZE
SCALE = 1.0 / math.sqrt(HEAD_SIZE)
SCALE_LOG2 = SCALE * math.log2(math.e)
LOW = -1e30

NT = (((1,), (1,)), ((), ()))


def fold(value, op):
    keys, lanes = value.shape
    return op(value.reshape(keys // 8, 8, lanes), axis=0)


def window_levels(shards):
    levels = max(shards // LEVEL, 1)
    return min((WB - 2 + LEVEL) // LEVEL, max(3 * levels // 4 - 1, 0) if levels % 4 == 0 else levels - 1)


def pack_kernel(key_hbm, value_hbm, docs_hbm, own_ref, docs, sems):
    rows = key_hbm.shape[0]
    half = key_hbm.shape[1]
    copies = [
        pltpu.make_async_copy(docs_hbm, docs, sems.at[0]),
        pltpu.make_async_copy(key_hbm, own_ref.at[0:rows, 0:half], sems.at[1]),
        pltpu.make_async_copy(value_hbm, own_ref.at[0:rows, half:2 * half], sems.at[2]),
    ]
    for copy in copies:
        copy.start()
    copies[0].wait()
    count = jnp.sum((docs[...] == 0).astype(jnp.float32), axis=1, keepdims=True)
    own_ref[rows:rows + DOC_ROWS, :] = jnp.broadcast_to(count, (DOC_ROWS, 2 * half)).astype(
        jnp.bfloat16
    )
    copies[1].wait()
    copies[2].wait()


def pack(key_in, value_input, doc_ids):
    rows, half = key_in.shape
    return pl.pallas_call(
        pack_kernel,
        out_shape=jax.ShapeDtypeStruct((rows + DOC_ROWS, 2 * half), jnp.bfloat16),
        in_specs=[pl.BlockSpec(memory_space=pltpu.HBM)] * 3,
        out_specs=pl.BlockSpec(memory_space=pltpu.VMEM),
        scratch_shapes=[pltpu.VMEM((1, rows), jnp.int32), pltpu.SemaphoreType.DMA((3,))],
        compiler_params=pltpu.CompilerParams(vmem_limit_bytes=8 * 1024 * 1024),
        name="pack",
    )(key_in, value_input, doc_ids)


def head_columns(g, n):
    head = g * GROUP_SIZE + n
    return slice(head * HEAD_SIZE, (head + 1) * HEAD_SIZE)


def prepare_kernel(q_hbm, bias_ref, do_hbm, q_st, do_t, q_buf, do_buf, sems):
    rows = q_buf.shape[0]
    first = pltpu.make_async_copy(q_hbm, q_buf, sems.at[0])
    second = pltpu.make_async_copy(do_hbm, do_buf, sems.at[1])
    first.start()
    second.start()
    first.wait()
    for g in range(KEY_VALUE_HEADS):
        for n in range(GROUP_SIZE):
            columns = head_columns(g, n)
            q_st[g, n * rows:(n + 1) * rows, :] = (
                q_buf[:, columns].astype(jnp.float32) + bias_ref[:, columns]
            ).astype(jnp.bfloat16)
    second.wait()
    for g in range(KEY_VALUE_HEADS):
        for n in range(GROUP_SIZE):
            do_t[g, :, n * rows:(n + 1) * rows] = do_buf[:, head_columns(g, n)].T


def prepare(query_in, query_bias, output_gradient):
    rows, width = query_in.shape
    lanes = GROUP_SIZE * rows
    anywhere = pl.BlockSpec(memory_space=pltpu.HBM)
    vmem = pl.BlockSpec(memory_space=pltpu.VMEM)
    return pl.pallas_call(
        prepare_kernel,
        out_shape=(
            jax.ShapeDtypeStruct((KEY_VALUE_HEADS, lanes, HEAD_SIZE), jnp.bfloat16),
            jax.ShapeDtypeStruct((KEY_VALUE_HEADS, HEAD_SIZE, lanes), jnp.bfloat16),
        ),
        in_specs=[anywhere, vmem, anywhere],
        out_specs=(vmem, vmem),
        scratch_shapes=[
            pltpu.VMEM((rows, width), jnp.bfloat16),
            pltpu.VMEM((rows, width), jnp.bfloat16),
            pltpu.SemaphoreType.DMA((2,)),
        ],
        compiler_params=pltpu.CompilerParams(vmem_limit_bytes=8 * 1024 * 1024),
        cost_estimate=pl.CostEstimate(
            flops=4 * rows * width, bytes_accessed=8 * rows * width, transcendentals=0
        ),
        name="prepare",
    )(query_in, query_bias, output_gradient)


def keys_of(kv_buf, c, rows, column):
    columns = slice(column * HEAD_SIZE, (column + 1) * HEAD_SIZE)
    return jnp.concatenate([kv_buf[PAIR * c + i, 0:rows, columns] for i in range(PAIR)], axis=0)


def spread(kv_buf, level, slot, here, there, inner):
    packed = kv_buf.shape[1]
    core = inner % 2
    x = inner // 2
    for x_at in range(2):
        at = (2 * level + x_at) * packed
        place = slot * LEVEL + 2 * (x + x_at - 2 * x * x_at)
        kv_buf[place + core] = here[at:at + packed, :]
        kv_buf[place + 1 - core] = there[at:at + packed, :]


def doc_count(kv_buf, rows):
    counts = kv_buf[:, rows:rows + DOC_ROWS, 0:128].astype(jnp.float32)
    return jnp.sum(counts) * (1.0 / (DOC_ROWS * 128))


def window_start(rank, rows, first, count):
    boundary = (count + 0.5).astype(jnp.int32) + jnp.maximum(first, 0) * rows
    low_block = jnp.maximum(rank - (WB - 1), 0)
    in_second = rank * rows >= boundary
    return boundary, jnp.where(in_second, jnp.maximum(low_block, boundary // rows), low_block)


def mask_bias(key_first, q_first, boundary, chunk, rows):
    key_pos = key_first + lax.broadcasted_iota(jnp.int32, (chunk, rows), 0)
    query_pos = q_first + lax.broadcasted_iota(jnp.int32, (chunk, rows), 1)
    allowed = (key_pos <= query_pos) & (query_pos // BLK - key_pos // BLK < WB)
    allowed = allowed & ((key_pos >= boundary) == (query_pos >= boundary))
    return jnp.where(allowed, 0.0, LOW)


def lane_tiles(lanes):
    return [(at, min(at + LANE_TILE, lanes)) for at in range(0, lanes, LANE_TILE)]


def near_kernel(
    rank_ref, q_all, near_ref, near_core_ref,
    kv_buf, p_buf, stats_ref, acc,
    s_buf,
):
    depth, chunk = p_buf.shape[:2]
    rows = chunk // PAIR
    lanes = q_all.shape[1]
    tiles = lane_tiles(lanes)
    rank = rank_ref[0]
    first = (rank // LEVEL - (depth - 1)) * LEVEL
    for level in range(depth):
        spread(kv_buf, level, depth - 1 - level, near_ref, near_core_ref, rank % LEVEL)
    boundary, low_block = window_start(rank, rows, first, doc_count(kv_buf, rows))
    low = jnp.maximum(low_block - first, 0) // PAIR

    for g in range(KEY_VALUE_HEADS):
        stats_ref[g, 0:8, :] = jnp.full((8, lanes), LOW, jnp.float32)
        stats_ref[g, 8:16, :] = jnp.zeros((8, lanes), jnp.float32)
    acc[...] = jnp.zeros_like(acc)

    def score_steps(c, g):
        bias = mask_bias((first + PAIR * c) * rows, rank * rows, boundary, chunk, rows)
        k_c = keys_of(kv_buf, c, rows, g)

        def step(a, b):
            s = lax.dot_general(k_c, q_all[g, a:b, :], NT, preferred_element_type=jnp.float32)
            s = s + jnp.concatenate([bias] * ((b - a) // rows), axis=1)
            s_buf[c, :, a:b] = s
            stats_ref[g, 0:8, a:b] = jnp.maximum(stats_ref[g, 0:8, a:b], fold(s, jnp.max))

        return step

    def weight_steps(c, g, row_max):
        v_t = keys_of(kv_buf, c, rows, KEY_VALUE_HEADS + g).T

        def step(a, b):
            p = jnp.exp2(s_buf[c, :, a:b] * SCALE_LOG2 - row_max[:, a:b])
            stats_ref[g, 8:16, a:b] += fold(p, jnp.sum)
            p_bf = p.astype(jnp.bfloat16)
            p_buf[c, :, g * lanes + a:g * lanes + b] = p_bf
            acc[g, :, a:b] += jnp.dot(v_t, p_bf, preferred_element_type=jnp.float32)

        return step

    def over_chunks(*makers):
        @pl.loop(low, depth)
        def _(c):
            steps = [make(c) for make in makers]
            for a, b in tiles:
                for step in steps:
                    step(a, b)

    over_chunks(lambda c: score_steps(c, 0))
    for g in range(KEY_VALUE_HEADS):
        row_max = jnp.max(stats_ref[g, 0:8, :], axis=0, keepdims=True) * SCALE_LOG2
        makers = [lambda c: weight_steps(c, g, row_max)]
        if g + 1 < KEY_VALUE_HEADS:
            makers.append(lambda c: score_steps(c, g + 1))
        over_chunks(*makers)
        stats_ref[g, 0:1, :] = row_max
        stats_ref[g, 8:9, :] = jnp.sum(stats_ref[g, 8:16, :], axis=0, keepdims=True)


def near_attention(rank, q_all, near, near_core, depth):
    lanes = q_all.shape[1]
    rows = lanes // GROUP_SIZE
    packed = rows + DOC_ROWS
    chunk = PAIR * rows
    vmem = pl.BlockSpec(memory_space=pltpu.VMEM)
    smem = pl.BlockSpec(memory_space=pltpu.SMEM)
    heads = KEY_VALUE_HEADS
    return pl.pallas_call(
        near_kernel,
        out_shape=(
            jax.ShapeDtypeStruct((depth * LEVEL, packed, KV_WIDTH), jnp.bfloat16),
            jax.ShapeDtypeStruct((depth, chunk, heads * lanes), jnp.bfloat16),
            jax.ShapeDtypeStruct((heads, 16, lanes), jnp.float32),
            jax.ShapeDtypeStruct((heads, HEAD_SIZE, lanes), jnp.float32),
        ),
        in_specs=[smem] + [vmem] * 3,
        out_specs=(vmem,) * 4,
        scratch_shapes=[pltpu.VMEM((depth, chunk, lanes), jnp.float32)],
        compiler_params=pltpu.CompilerParams(vmem_limit_bytes=28 * 1024 * 1024),
        cost_estimate=pl.CostEstimate(
            flops=2 * 2 * heads * lanes * HEAD_SIZE * depth * chunk,
            bytes_accessed=4 * heads * lanes * HEAD_SIZE,
            transcendentals=heads * lanes * depth * chunk,
        ),
        name="near_attention",
    )(rank, q_all, near, near_core)


def kernel(
    rank_ref, q_all, do_all, kv_near, p_near, stats_ref, acc_near, far_ref, far_core_ref,
    att_ref, dq_ref, p_far, ds_buf, do_near, do_far, gb_ref, span_ref,
    kv_far, s_buf, sum_buf, factor_buf, dot_buf, acc, dq_acc,
):
    rows = att_ref.shape[0]
    depth, chunk = p_near.shape[:2]
    lanes = GROUP_SIZE * rows
    tiles = lane_tiles(lanes)
    rank = rank_ref[0]
    first = (rank // LEVEL - depth) * LEVEL
    spread(kv_far, 0, 0, far_ref, far_core_ref, rank % LEVEL)
    count = doc_count(kv_far, rows) + doc_count(kv_near, rows)
    boundary, low_block = window_start(rank, rows, first, count)
    low = jnp.maximum(low_block - first, 0) // PAIR
    span_ref[0] = low
    with_far = low == 0

    dq_acc[...] = jnp.zeros_like(dq_acc)

    @pl.when(with_far)
    def _():
        bias = mask_bias(first * rows, rank * rows, boundary, chunk, rows)

        def score(g, a, b):
            k_c = keys_of(kv_far, 0, rows, g)
            s = lax.dot_general(k_c, q_all[g, a:b, :], NT, preferred_element_type=jnp.float32)
            s = s + jnp.concatenate([bias] * ((b - a) // rows), axis=1)
            s_buf[g, :, a:b] = s
            far_max = jnp.max(fold(s, jnp.max), axis=0, keepdims=True) * SCALE_LOG2
            factor_buf[g, 0:1, a:b] = jnp.maximum(stats_ref[g, 0:1, a:b], far_max)

        def weight(g, a, b):
            v_t = keys_of(kv_far, 0, rows, KEY_VALUE_HEADS + g).T
            top = factor_buf[g, 0:1, a:b]
            factor = jnp.exp2(stats_ref[g, 0:1, a:b] - top)
            p = jnp.exp2(s_buf[g, :, a:b] * SCALE_LOG2 - top)
            p_bf = p.astype(jnp.bfloat16)
            p_far[0, :, g * lanes + a:g * lanes + b] = p_bf
            total = jnp.sum(fold(p, jnp.sum), axis=0, keepdims=True)
            sum_buf[g, 0:1, a:b] = stats_ref[g, 8:9, a:b] * factor + total
            factor_buf[g, 0:1, a:b] = factor
            acc[g, :, a:b] = acc_near[g, :, a:b] * factor + jnp.dot(
                v_t, p_bf, preferred_element_type=jnp.float32
            )

        for a, b in tiles:
            score(0, a, b)
        for g in range(KEY_VALUE_HEADS):
            for a, b in tiles:
                weight(g, a, b)
                if g + 1 < KEY_VALUE_HEADS:
                    score(g + 1, a, b)

    @pl.when(jnp.logical_not(with_far))
    def _():
        sum_buf[:, 0:1, :] = stats_ref[:, 8:9, :]
        factor_buf[:, 0:1, :] = jnp.ones((KEY_VALUE_HEADS, 1, lanes), jnp.float32)
        acc[...] = acc_near[...]

    for g in range(KEY_VALUE_HEADS):
        inverse = 1.0 / sum_buf[g, 0:1, :]
        factor = factor_buf[g, 0:1, :]
        for n in range(GROUP_SIZE):
            at = slice(n * rows, (n + 1) * rows)
            att = (acc[g, :, at] * inverse[:, at]).astype(jnp.bfloat16)
            att_ref[:, head_columns(g, n)] = att.T
            do_n = do_all[g, :, at].astype(jnp.float32)
            dot_n = jnp.sum(do_n * att.astype(jnp.float32), axis=0, keepdims=True) * inverse[:, at]
            do_n = do_n * inverse[:, at]
            dot_buf[g, 0:1, at] = dot_n
            dot_buf[g, 1:2, at] = dot_n * factor[:, at]
            do_far[g, :, at] = do_n.astype(jnp.bfloat16)
            do_near[g, :, at] = (do_n * factor[:, at]).astype(jnp.bfloat16)

    def gradient_steps(g, c, kv_buf, at, p_buf, do_t, row):
        v_c = keys_of(kv_buf, at, rows, KEY_VALUE_HEADS + g)
        k_t = keys_of(kv_buf, at, rows, g).T

        def step(a, b):
            where = slice(g * lanes + a, g * lanes + b)
            d_p = jnp.dot(v_c, do_t[g, :, a:b], preferred_element_type=jnp.float32)
            p = p_buf[at, :, where].astype(jnp.float32)
            d_s = (p * (d_p - dot_buf[g, row:row + 1, a:b])).astype(jnp.bfloat16)
            ds_buf[c, :, where] = d_s
            dq_acc[g, :, a:b] += jnp.dot(k_t, d_s, preferred_element_type=jnp.float32)

        return step

    def gradients(c, kv_buf, at, p_buf, do_t, row):
        steps = [
            gradient_steps(g, c, kv_buf, at, p_buf, do_t, row) for g in range(KEY_VALUE_HEADS)
        ]
        for a, b in tiles:
            for step in steps:
                step(a, b)

    @pl.when(with_far)
    def _():
        gradients(0, kv_far, 0, p_far, do_far, 0)

    @pl.loop(jnp.maximum(low, 1), depth + 1)
    def _(c):
        gradients(c, kv_near, c - 1, p_near, do_near, 1)

    gb_ref[...] = jnp.zeros_like(gb_ref)
    for g in range(KEY_VALUE_HEADS):
        for n in range(GROUP_SIZE):
            columns = head_columns(g, n)
            d_q = (dq_acc[g, :, n * rows:(n + 1) * rows] * SCALE).astype(jnp.bfloat16).T
            row, at = divmod(columns.start, KV_WIDTH)
            gb_ref[row:row + 1, at:at + HEAD_SIZE] = jnp.sum(
                d_q.astype(jnp.float32), axis=0, keepdims=True
            )
            dq_ref[:, columns] = d_q


def attention(rank, q_all, do_all, kv_near, p_near, stats, acc_near, far, far_core):
    lanes = q_all.shape[1]
    rows = lanes // GROUP_SIZE
    width = QUERY_HEADS * HEAD_SIZE
    packed = rows + DOC_ROWS
    depth, chunk = p_near.shape[:2]
    vmem = pl.BlockSpec(memory_space=pltpu.VMEM)
    smem = pl.BlockSpec(memory_space=pltpu.SMEM)
    heads = KEY_VALUE_HEADS
    return pl.pallas_call(
        kernel,
        out_shape=(
            jax.ShapeDtypeStruct((rows, width), jnp.bfloat16),
            jax.ShapeDtypeStruct((rows, width), jnp.bfloat16),
            jax.ShapeDtypeStruct((1, chunk, heads * lanes), jnp.bfloat16),
            jax.ShapeDtypeStruct((depth + 1, chunk, heads * lanes), jnp.bfloat16),
            jax.ShapeDtypeStruct((heads, HEAD_SIZE, lanes), jnp.bfloat16),
            jax.ShapeDtypeStruct((heads, HEAD_SIZE, lanes), jnp.bfloat16),
            jax.ShapeDtypeStruct((-(-width // KV_WIDTH), KV_WIDTH), jnp.float32),
            jax.ShapeDtypeStruct((1,), jnp.int32),
        ),
        in_specs=[smem] + [vmem] * 8,
        out_specs=(vmem,) * 7 + (smem,),
        scratch_shapes=[
            pltpu.VMEM((LEVEL, packed, KV_WIDTH), jnp.bfloat16),
            pltpu.VMEM((heads, chunk, lanes), jnp.float32),
            pltpu.VMEM((heads, 8, lanes), jnp.float32),
            pltpu.VMEM((heads, 8, lanes), jnp.float32),
            pltpu.VMEM((heads, 8, lanes), jnp.float32),
            pltpu.VMEM((heads, HEAD_SIZE, lanes), jnp.float32),
            pltpu.VMEM((heads, HEAD_SIZE, lanes), jnp.float32),
        ],
        compiler_params=pltpu.CompilerParams(vmem_limit_bytes=28 * 1024 * 1024),
        cost_estimate=pl.CostEstimate(
            flops=2 * 2 * width * HEAD_SIZE * (depth + 2) * chunk,
            bytes_accessed=8 * rows * width,
            transcendentals=0,
        ),
        name="attention",
    )(rank, q_all, do_all, kv_near, p_near, stats, acc_near, far, far_core)


def level_kernel(
    level, p_at, rank_ref, span_ref, p_buf, ds_buf, q_all, do_t, keep_ref, send_ref
):
    chunk = p_buf.shape[1]
    rows = chunk // PAIR
    lanes = GROUP_SIZE * rows
    inner = rank_ref[0] % LEVEL
    my_core = inner % 2
    my_x = inner // 2
    active = level >= span_ref[0]

    @pl.when(active)
    def _():
        for g in range(KEY_VALUE_HEADS):
            where = slice(g * lanes, (g + 1) * lanes)
            d_key = jnp.dot(
                ds_buf[level, :, where], q_all[g], preferred_element_type=jnp.float32
            ) * SCALE
            d_value = lax.dot_general(
                p_buf[p_at, :, where], do_t[g], NT, preferred_element_type=jnp.float32
            )
            for value, column in ((d_key, g), (d_value, KEY_VALUE_HEADS + g)):
                columns = slice(column * HEAD_SIZE, (column + 1) * HEAD_SIZE)
                for x_at in range(2):
                    one = value[2 * x_at * rows:(2 * x_at + 1) * rows]
                    two = value[(2 * x_at + 1) * rows:(2 * x_at + 2) * rows]
                    place = (x_at + my_x) % 2
                    at = pl.ds(pl.multiple_of(place * rows, rows), rows)
                    keep_ref[at, columns] = jnp.where(my_core == 0, one, two)
                    send_ref[at, columns] = jnp.where(my_core == 0, two, one).astype(jnp.bfloat16)

    @pl.when(jnp.logical_not(active))
    def _():
        keep_ref[...] = jnp.zeros_like(keep_ref)
        send_ref[...] = jnp.zeros_like(send_ref)


def level_gradients(level, p_at, rank, span, p_all, ds_all, q_all, do_t):
    chunk, width = p_all.shape[1:]
    rows = chunk // PAIR
    vmem = pl.BlockSpec(memory_space=pltpu.VMEM)
    smem = pl.BlockSpec(memory_space=pltpu.SMEM)
    return pl.pallas_call(
        functools.partial(level_kernel, level, p_at),
        out_shape=(
            jax.ShapeDtypeStruct((2 * rows, KV_WIDTH), jnp.float32),
            jax.ShapeDtypeStruct((2 * rows, KV_WIDTH), jnp.bfloat16),
        ),
        in_specs=[smem, smem] + [vmem] * 4,
        out_specs=(vmem, vmem),
        compiler_params=pltpu.CompilerParams(vmem_limit_bytes=28 * 1024 * 1024),
        cost_estimate=pl.CostEstimate(
            flops=2 * 2 * LEVEL * rows * width * HEAD_SIZE,
            bytes_accessed=4 * LEVEL * rows * width,
            transcendentals=0,
        ),
        name="level_gradients",
    )(rank, span, p_all, ds_all, q_all, do_t)


def shifted(value, steps, bit=0):
    count = lax.axis_size("ctx")
    first, last = max(0, -steps), min(count, count - steps)
    return lax.ppermute(value, "ctx", [(at, (at + steps) ^ bit) for at in range(first, last)])


def rotated(value, steps, bit=0):
    count = lax.axis_size("ctx")
    return lax.ppermute(value, "ctx", [(at, (at + steps) % count ^ bit) for at in range(count)])


def swapped(value, bit, axis="ctx"):
    return lax.ppermute(value, axis, [(at, at ^ bit) for at in range(lax.axis_size(axis))])


def bias_rows(rows):
    high = lax.reduce_precision(rows, 8, 7)
    both = jnp.concatenate([high, rows - high]).astype(jnp.bfloat16)
    return jnp.pad(both, ((0, -both.shape[0] % 16), (0, 0)))


def local(query_in, key_in, value_input, output_gradient, doc_ids, query_bias):
    rows = query_in.shape[1]
    shards = lax.axis_size("ctx")
    depth = window_levels(shards)
    rank = lax.axis_index("ctx").astype(jnp.int32)
    own = pack(key_in[0], value_input[0], doc_ids)

    ups = [shifted(own, LEVEL * step) for step in range(1, depth + 1)]
    x_own = swapped(own, 2)
    q_all, do_all = prepare(query_in[0], query_bias[None], output_gradient[0])
    ups[0], x_own, q_all, do_all = lax.optimization_barrier((ups[0], x_own, q_all, do_all))
    near = [own, x_own]
    for up in ups[:-1]:
        near += [up, swapped(up, 2)]
    x_far = swapped(ups[-1], 2)
    far, near = lax.optimization_barrier((ups[-1], near))
    near = jnp.concatenate(near, axis=0)
    near_core = swapped(near, 1)
    rank = rank.reshape(1)
    kv_near, p_near, stats, acc_near = near_attention(rank, q_all, near, near_core, depth)
    x_far, p_near = lax.optimization_barrier((x_far, p_near))
    far = jnp.concatenate([far, x_far], axis=0)
    far_core = swapped(far, 1)
    attended, grad_query, p_far, ds_all, do_near, do_far, bias_part, span = attention(
        rank, q_all, do_all, kv_near, p_near, stats, acc_near, far, far_core
    )

    levels = shards // LEVEL
    carried = levels == 4 and depth == 2
    bit = 1
    while bit < lax.axis_size("dp"):
        bias_part = bias_part + swapped(bias_part, bit, "dp")
        bit *= 2
    bias_total = bias_part

    def joined(value):
        return jnp.concatenate([value, bias_rows(bias_total)], axis=0) if carried else value

    def bias_of(got):
        return got[rows:rows + half_rows].astype(jnp.float32) + got[
            rows + half_rows:rows + 2 * half_rows
        ].astype(jnp.float32)

    half_rows = bias_part.shape[0]
    sends = [None] * (depth + 1)
    keeps = [None] * (depth + 1)
    for step in range(depth, -1, -1):
        if step == depth:
            keep, send = level_gradients(0, 0, rank, span, p_far, ds_all, q_all, do_far)
        else:
            level = depth - step
            keep, send = level_gradients(
                level, level - 1, rank, span, p_near, ds_all, q_all, do_near
            )
        send, ds_all = lax.optimization_barrier((send, ds_all))
        if step == max(depth - 1, 0) and carried:
            got = swapped(jnp.concatenate([send, bias_rows(bias_total)], axis=0), 1)
            bias_total = bias_total + bias_of(got[rows:])
            got = got[:2 * rows]
        else:
            got = swapped(send, 1)
        keeps[step] = keep + got.astype(jnp.float32)
        sends[step] = send

    def lowered(value, step, bit=0):
        if carried:
            return rotated(joined(value), -LEVEL * step, bit)
        return shifted(value, -LEVEL * step, bit)

    keeps, ds_all = lax.optimization_barrier((keeps, ds_all))
    down = []
    for step in range(depth, 1, -1):
        down.append(lowered(keeps[step][:rows].astype(jnp.bfloat16), step))
        down.append(lowered(keeps[step][rows:].astype(jnp.bfloat16), step, 2))
    across = [swapped(keeps[0][rows:].astype(jnp.bfloat16), 2)]
    if depth:
        across.append(swapped(joined(keeps[1][rows:].astype(jnp.bfloat16)), 2))
        across = lax.optimization_barrier(across)
        if carried:
            bias_total = bias_total + bias_of(across[1])
        near_sum = keeps[1][:rows] + across[1][:rows].astype(jnp.float32)
        down.append(lowered(near_sum.astype(jnp.bfloat16), 1))
    total = keeps[0][:rows] + across[0].astype(jnp.float32)
    for got in down:
        total = total + got[:rows].astype(jnp.float32)
    if carried:
        bias_total = (
            bias_total + rotated(bias_total, LEVEL) + sum(bias_of(got) for got in down)
        )
    else:
        bit = 1
        while bit < shards:
            bias_total = bias_total + swapped(bias_total, bit)
            bit *= 2
    bias_total = bias_total.reshape(-1)[:query_bias.shape[0]]
    total = total.astype(jnp.bfloat16)
    half = KEY_VALUE_HEADS * HEAD_SIZE
    return (
        attended[None],
        grad_query[None],
        total[:, :half][None],
        total[:, half:][None],
        bias_total,
    )


def solution(mesh):
    placed = (
        P("dp", "ctx", None),
        P("dp", "ctx", None),
        P("dp", "ctx", None),
        P("dp", "ctx", None),
        P("dp", "ctx"),
        P(),
    )
    return jax.shard_map(
        local,
        mesh=mesh,
        in_specs=placed,
        out_specs=(
            P("dp", "ctx", None),
            P("dp", "ctx", None),
            P("dp", "ctx", None),
            P("dp", "ctx", None),
            P(),
        ),
        check_vma=False,
    )
```

```python
import functools
import math

import jax
import jax.numpy as jnp
from jax import lax
from jax.experimental import pallas as pl
from jax.experimental.pallas import tpu as pltpu
from jax.sharding import PartitionSpec as P

QUERY_HEADS = 14
KEY_VALUE_HEADS = 2
HEAD_SIZE = 128
GROUP_SIZE = 7
BLK = 128
WB = 16
DOC_ROWS = 16
PAIR = 4
LEVEL = 4
LANE_TILE = 256
KV_WIDTH = 2 * KEY_VALUE_HEADS * HEAD_SIZE
SCALE = 1.0 / math.sqrt(HEAD_SIZE)
SCALE_LOG2 = SCALE * math.log2(math.e)
LOW = -1e30

NT = (((1,), (1,)), ((), ()))


def fold(value, op):
    keys, lanes = value.shape
    return op(value.reshape(keys // 8, 8, lanes), axis=0)


def window_levels(shards):
    levels = max(shards // LEVEL, 1)
    return min((WB - 2 + LEVEL) // LEVEL, max(3 * levels // 4 - 1, 0) if levels % 4 == 0 else levels - 1)


def pack_kernel(key_hbm, value_hbm, docs_hbm, own_ref, docs, sems):
    rows = key_hbm.shape[0]
    half = key_hbm.shape[1]
    copies = [
        pltpu.make_async_copy(docs_hbm, docs, sems.at[0]),
        pltpu.make_async_copy(key_hbm, own_ref.at[0:rows, 0:half], sems.at[1]),
        pltpu.make_async_copy(value_hbm, own_ref.at[0:rows, half:2 * half], sems.at[2]),
    ]
    for copy in copies:
        copy.start()
    copies[0].wait()
    count = jnp.sum((docs[...] == 0).astype(jnp.float32), axis=1, keepdims=True)
    own_ref[rows:rows + DOC_ROWS, :] = jnp.broadcast_to(count, (DOC_ROWS, 2 * half)).astype(
        jnp.bfloat16
    )
    copies[1].wait()
    copies[2].wait()


def pack(key_in, value_input, doc_ids):
    rows, half = key_in.shape
    return pl.pallas_call(
        pack_kernel,
        out_shape=jax.ShapeDtypeStruct((rows + DOC_ROWS, 2 * half), jnp.bfloat16),
        in_specs=[pl.BlockSpec(memory_space=pltpu.HBM)] * 3,
        out_specs=pl.BlockSpec(memory_space=pltpu.VMEM),
        scratch_shapes=[pltpu.VMEM((1, rows), jnp.int32), pltpu.SemaphoreType.DMA((3,))],
        compiler_params=pltpu.CompilerParams(vmem_limit_bytes=8 * 1024 * 1024),
        name="pack",
    )(key_in, value_input, doc_ids)


def head_columns(g, n):
    head = g * GROUP_SIZE + n
    return slice(head * HEAD_SIZE, (head + 1) * HEAD_SIZE)


def prepare_kernel(q_hbm, bias_ref, do_hbm, q_st, do_t, q_buf, do_buf, sems):
    rows = q_buf.shape[0]
    first = pltpu.make_async_copy(q_hbm, q_buf, sems.at[0])
    second = pltpu.make_async_copy(do_hbm, do_buf, sems.at[1])
    first.start()
    second.start()
    first.wait()
    for g in range(KEY_VALUE_HEADS):
        for n in range(GROUP_SIZE):
            columns = head_columns(g, n)
            q_st[g, n * rows:(n + 1) * rows, :] = (
                q_buf[:, columns].astype(jnp.float32) + bias_ref[:, columns]
            ).astype(jnp.bfloat16)
    second.wait()
    for g in range(KEY_VALUE_HEADS):
        for n in range(GROUP_SIZE):
            do_t[g, :, n * rows:(n + 1) * rows] = do_buf[:, head_columns(g, n)].T


def prepare(query_in, query_bias, output_gradient):
    rows, width = query_in.shape
    lanes = GROUP_SIZE * rows
    anywhere = pl.BlockSpec(memory_space=pltpu.HBM)
    vmem = pl.BlockSpec(memory_space=pltpu.VMEM)
    return pl.pallas_call(
        prepare_kernel,
        out_shape=(
            jax.ShapeDtypeStruct((KEY_VALUE_HEADS, lanes, HEAD_SIZE), jnp.bfloat16),
            jax.ShapeDtypeStruct((KEY_VALUE_HEADS, HEAD_SIZE, lanes), jnp.bfloat16),
        ),
        in_specs=[anywhere, vmem, anywhere],
        out_specs=(vmem, vmem),
        scratch_shapes=[
            pltpu.VMEM((rows, width), jnp.bfloat16),
            pltpu.VMEM((rows, width), jnp.bfloat16),
            pltpu.SemaphoreType.DMA((2,)),
        ],
        compiler_params=pltpu.CompilerParams(vmem_limit_bytes=8 * 1024 * 1024),
        cost_estimate=pl.CostEstimate(
            flops=4 * rows * width, bytes_accessed=8 * rows * width, transcendentals=0
        ),
        name="prepare",
    )(query_in, query_bias, output_gradient)


def keys_of(kv_buf, c, rows, column):
    columns = slice(column * HEAD_SIZE, (column + 1) * HEAD_SIZE)
    return jnp.concatenate([kv_buf[PAIR * c + i, 0:rows, columns] for i in range(PAIR)], axis=0)


def spread(kv_buf, level, slot, here, there, inner):
    packed = kv_buf.shape[1]
    core = inner % 2
    x = inner // 2
    for x_at in range(2):
        at = (2 * level + x_at) * packed
        place = slot * LEVEL + 2 * (x + x_at - 2 * x * x_at)
        kv_buf[place + core] = here[at:at + packed, :]
        kv_buf[place + 1 - core] = there[at:at + packed, :]


def doc_count(kv_buf, rows):
    counts = kv_buf[:, rows:rows + DOC_ROWS, 0:128].astype(jnp.float32)
    return jnp.sum(counts) * (1.0 / (DOC_ROWS * 128))


def window_start(rank, rows, first, count):
    boundary = (count + 0.5).astype(jnp.int32) + jnp.maximum(first, 0) * rows
    low_block = jnp.maximum(rank - (WB - 1), 0)
    in_second = rank * rows >= boundary
    return boundary, jnp.where(in_second, jnp.maximum(low_block, boundary // rows), low_block)


def mask_bias(key_first, q_first, boundary, chunk, rows):
    key_pos = key_first + lax.broadcasted_iota(jnp.int32, (chunk, rows), 0)
    query_pos = q_first + lax.broadcasted_iota(jnp.int32, (chunk, rows), 1)
    allowed = (key_pos <= query_pos) & (query_pos // BLK - key_pos // BLK < WB)
    allowed = allowed & ((key_pos >= boundary) == (query_pos >= boundary))
    return jnp.where(allowed, 0.0, LOW)


def lane_tiles(lanes):
    return [(at, min(at + LANE_TILE, lanes)) for at in range(0, lanes, LANE_TILE)]


def near_kernel(
    rank_ref, q_all, near_ref, near_core_ref,
    kv_buf, p_buf, stats_ref, acc,
    s_buf,
):
    depth, chunk = p_buf.shape[:2]
    rows = chunk // PAIR
    lanes = q_all.shape[1]
    tiles = lane_tiles(lanes)
    rank = rank_ref[0]
    first = (rank // LEVEL - (depth - 1)) * LEVEL
    for level in range(depth):
        spread(kv_buf, level, depth - 1 - level, near_ref, near_core_ref, rank % LEVEL)
    boundary, low_block = window_start(rank, rows, first, doc_count(kv_buf, rows))
    low = jnp.maximum(low_block - first, 0) // PAIR

    for g in range(KEY_VALUE_HEADS):
        stats_ref[g, 0:8, :] = jnp.full((8, lanes), LOW, jnp.float32)
        stats_ref[g, 8:16, :] = jnp.zeros((8, lanes), jnp.float32)
    acc[...] = jnp.zeros_like(acc)

    def score_steps(c, g):
        bias = mask_bias((first + PAIR * c) * rows, rank * rows, boundary, chunk, rows)
        k_c = keys_of(kv_buf, c, rows, g)

        def step(a, b):
            s = lax.dot_general(k_c, q_all[g, a:b, :], NT, preferred_element_type=jnp.float32)
            s = s + jnp.concatenate([bias] * ((b - a) // rows), axis=1)
            s_buf[c, :, a:b] = s
            stats_ref[g, 0:8, a:b] = jnp.maximum(stats_ref[g, 0:8, a:b], fold(s, jnp.max))

        return step

    def weight_steps(c, g, row_max):
        v_t = keys_of(kv_buf, c, rows, KEY_VALUE_HEADS + g).T

        def step(a, b):
            p = jnp.exp2(s_buf[c, :, a:b] * SCALE_LOG2 - row_max[:, a:b])
            stats_ref[g, 8:16, a:b] += fold(p, jnp.sum)
            p_bf = p.astype(jnp.bfloat16)
            p_buf[c, :, g * lanes + a:g * lanes + b] = p_bf
            acc[g, :, a:b] += jnp.dot(v_t, p_bf, preferred_element_type=jnp.float32)

        return step

    def over_chunks(*makers):
        @pl.loop(low, depth)
        def _(c):
            steps = [make(c) for make in makers]
            for a, b in tiles:
                for step in steps:
                    step(a, b)

    over_chunks(lambda c: score_steps(c, 0))
    for g in range(KEY_VALUE_HEADS):
        row_max = jnp.max(stats_ref[g, 0:8, :], axis=0, keepdims=True) * SCALE_LOG2
        makers = [lambda c: weight_steps(c, g, row_max)]
        if g + 1 < KEY_VALUE_HEADS:
            makers.append(lambda c: score_steps(c, g + 1))
        over_chunks(*makers)
        stats_ref[g, 0:1, :] = row_max
        stats_ref[g, 8:9, :] = jnp.sum(stats_ref[g, 8:16, :], axis=0, keepdims=True)


def near_attention(rank, q_all, near, near_core, depth):
    lanes = q_all.shape[1]
    rows = lanes // GROUP_SIZE
    packed = rows + DOC_ROWS
    chunk = PAIR * rows
    vmem = pl.BlockSpec(memory_space=pltpu.VMEM)
    smem = pl.BlockSpec(memory_space=pltpu.SMEM)
    heads = KEY_VALUE_HEADS
    return pl.pallas_call(
        near_kernel,
        out_shape=(
            jax.ShapeDtypeStruct((depth * LEVEL, packed, KV_WIDTH), jnp.bfloat16),
            jax.ShapeDtypeStruct((depth, chunk, heads * lanes), jnp.bfloat16),
            jax.ShapeDtypeStruct((heads, 16, lanes), jnp.float32),
            jax.ShapeDtypeStruct((heads, HEAD_SIZE, lanes), jnp.float32),
        ),
        in_specs=[smem] + [vmem] * 3,
        out_specs=(vmem,) * 4,
        scratch_shapes=[pltpu.VMEM((depth, chunk, lanes), jnp.float32)],
        compiler_params=pltpu.CompilerParams(vmem_limit_bytes=28 * 1024 * 1024),
        cost_estimate=pl.CostEstimate(
            flops=2 * 2 * heads * lanes * HEAD_SIZE * depth * chunk,
            bytes_accessed=4 * heads * lanes * HEAD_SIZE,
            transcendentals=heads * lanes * depth * chunk,
        ),
        name="near_attention",
    )(rank, q_all, near, near_core)


def kernel(
    rank_ref, q_all, do_all, kv_near, p_near, stats_ref, acc_near, far_ref, far_core_ref,
    att_t, dq_t, p_far, ds_buf, do_near, do_far, gb_ref, span_ref,
    kv_far, s_buf, sum_buf, factor_buf, dot_buf, acc, dq_acc,
):
    depth, chunk = p_near.shape[:2]
    rows = chunk // PAIR
    lanes = GROUP_SIZE * rows
    tiles = lane_tiles(lanes)
    rank = rank_ref[0]
    first = (rank // LEVEL - depth) * LEVEL
    spread(kv_far, 0, 0, far_ref, far_core_ref, rank % LEVEL)
    count = doc_count(kv_far, rows) + doc_count(kv_near, rows)
    boundary, low_block = window_start(rank, rows, first, count)
    low = jnp.maximum(low_block - first, 0) // PAIR
    span_ref[0] = low
    with_far = low == 0

    dq_acc[...] = jnp.zeros_like(dq_acc)

    @pl.when(with_far)
    def _():
        bias = mask_bias(first * rows, rank * rows, boundary, chunk, rows)

        def score(g, a, b):
            k_c = keys_of(kv_far, 0, rows, g)
            s = lax.dot_general(k_c, q_all[g, a:b, :], NT, preferred_element_type=jnp.float32)
            s = s + jnp.concatenate([bias] * ((b - a) // rows), axis=1)
            s_buf[g, :, a:b] = s
            far_max = jnp.max(fold(s, jnp.max), axis=0, keepdims=True) * SCALE_LOG2
            factor_buf[g, 0:1, a:b] = jnp.maximum(stats_ref[g, 0:1, a:b], far_max)

        def weight(g, a, b):
            v_t = keys_of(kv_far, 0, rows, KEY_VALUE_HEADS + g).T
            top = factor_buf[g, 0:1, a:b]
            factor = jnp.exp2(stats_ref[g, 0:1, a:b] - top)
            p = jnp.exp2(s_buf[g, :, a:b] * SCALE_LOG2 - top)
            p_bf = p.astype(jnp.bfloat16)
            p_far[0, :, g * lanes + a:g * lanes + b] = p_bf
            total = jnp.sum(fold(p, jnp.sum), axis=0, keepdims=True)
            sum_buf[g, 0:1, a:b] = stats_ref[g, 8:9, a:b] * factor + total
            factor_buf[g, 0:1, a:b] = factor
            acc[g, :, a:b] = acc_near[g, :, a:b] * factor + jnp.dot(
                v_t, p_bf, preferred_element_type=jnp.float32
            )

        for a, b in tiles:
            score(0, a, b)
        for g in range(KEY_VALUE_HEADS):
            for a, b in tiles:
                weight(g, a, b)
                if g + 1 < KEY_VALUE_HEADS:
                    score(g + 1, a, b)

    @pl.when(jnp.logical_not(with_far))
    def _():
        sum_buf[:, 0:1, :] = stats_ref[:, 8:9, :]
        factor_buf[:, 0:1, :] = jnp.ones((KEY_VALUE_HEADS, 1, lanes), jnp.float32)
        acc[...] = acc_near[...]

    for g in range(KEY_VALUE_HEADS):
        inverse = 1.0 / sum_buf[g, 0:1, :]
        factor = factor_buf[g, 0:1, :]
        for n in range(GROUP_SIZE):
            at = slice(n * rows, (n + 1) * rows)
            att = (acc[g, :, at] * inverse[:, at]).astype(jnp.bfloat16)
            att_t[g, :, at] = att
            do_n = do_all[g, :, at].astype(jnp.float32)
            dot_n = jnp.sum(do_n * att.astype(jnp.float32), axis=0, keepdims=True) * inverse[:, at]
            do_n = do_n * inverse[:, at]
            dot_buf[g, 0:1, at] = dot_n
            dot_buf[g, 1:2, at] = dot_n * factor[:, at]
            do_far[g, :, at] = do_n.astype(jnp.bfloat16)
            do_near[g, :, at] = (do_n * factor[:, at]).astype(jnp.bfloat16)

    def gradient_steps(g, c, kv_buf, at, p_buf, do_t, row):
        v_c = keys_of(kv_buf, at, rows, KEY_VALUE_HEADS + g)
        k_t = keys_of(kv_buf, at, rows, g).T

        def step(a, b):
            where = slice(g * lanes + a, g * lanes + b)
            d_p = jnp.dot(v_c, do_t[g, :, a:b], preferred_element_type=jnp.float32)
            p = p_buf[at, :, where].astype(jnp.float32)
            d_s = (p * (d_p - dot_buf[g, row:row + 1, a:b])).astype(jnp.bfloat16)
            ds_buf[c, :, where] = d_s
            dq_acc[g, :, a:b] += jnp.dot(k_t, d_s, preferred_element_type=jnp.float32)

        return step

    def gradients(c, kv_buf, at, p_buf, do_t, row):
        steps = [
            gradient_steps(g, c, kv_buf, at, p_buf, do_t, row) for g in range(KEY_VALUE_HEADS)
        ]
        for a, b in tiles:
            for step in steps:
                step(a, b)

    @pl.when(with_far)
    def _():
        gradients(0, kv_far, 0, p_far, do_far, 0)

    @pl.loop(jnp.maximum(low, 1), depth + 1)
    def _(c):
        gradients(c, kv_near, c - 1, p_near, do_near, 1)

    gb_ref[...] = jnp.zeros_like(gb_ref)
    ones = jnp.ones((8, rows), jnp.bfloat16)
    for g in range(KEY_VALUE_HEADS):
        for n in range(GROUP_SIZE):
            columns = slice(n * rows, (n + 1) * rows)
            d_q = (dq_acc[g, :, columns] * SCALE).astype(jnp.bfloat16)
            dq_t[g, :, columns] = d_q
            row, at = divmod(head_columns(g, n).start, KV_WIDTH)
            sums = lax.dot_general(ones, d_q, NT, preferred_element_type=jnp.float32)
            gb_ref[row:row + 1, at:at + HEAD_SIZE] = sums[0:1]


def rows_kernel(att_t, dq_t, att_ref, dq_ref):
    rows = att_ref.shape[0]
    for g in range(KEY_VALUE_HEADS):
        for n in range(GROUP_SIZE):
            at = slice(n * rows, (n + 1) * rows)
            att_ref[:, head_columns(g, n)] = att_t[g, :, at].T
            dq_ref[:, head_columns(g, n)] = dq_t[g, :, at].T


def row_results(att_t, dq_t):
    rows = att_t.shape[2] // GROUP_SIZE
    width = QUERY_HEADS * HEAD_SIZE
    vmem = pl.BlockSpec(memory_space=pltpu.VMEM)
    return pl.pallas_call(
        rows_kernel,
        out_shape=(jax.ShapeDtypeStruct((rows, width), jnp.bfloat16),) * 2,
        in_specs=[vmem] * 2,
        out_specs=(vmem,) * 2,
        compiler_params=pltpu.CompilerParams(vmem_limit_bytes=8 * 1024 * 1024),
        cost_estimate=pl.CostEstimate(
            flops=2 * rows * width, bytes_accessed=8 * rows * width, transcendentals=0
        ),
        name="row_results",
    )(att_t, dq_t)


def attention(rank, q_all, do_all, kv_near, p_near, stats, acc_near, far, far_core):
    lanes = q_all.shape[1]
    rows = lanes // GROUP_SIZE
    width = QUERY_HEADS * HEAD_SIZE
    packed = rows + DOC_ROWS
    depth, chunk = p_near.shape[:2]
    vmem = pl.BlockSpec(memory_space=pltpu.VMEM)
    smem = pl.BlockSpec(memory_space=pltpu.SMEM)
    heads = KEY_VALUE_HEADS
    return pl.pallas_call(
        kernel,
        out_shape=(
            jax.ShapeDtypeStruct((heads, HEAD_SIZE, lanes), jnp.bfloat16),
            jax.ShapeDtypeStruct((heads, HEAD_SIZE, lanes), jnp.bfloat16),
            jax.ShapeDtypeStruct((1, chunk, heads * lanes), jnp.bfloat16),
            jax.ShapeDtypeStruct((depth + 1, chunk, heads * lanes), jnp.bfloat16),
            jax.ShapeDtypeStruct((heads, HEAD_SIZE, lanes), jnp.bfloat16),
            jax.ShapeDtypeStruct((heads, HEAD_SIZE, lanes), jnp.bfloat16),
            jax.ShapeDtypeStruct((-(-width // KV_WIDTH), KV_WIDTH), jnp.float32),
            jax.ShapeDtypeStruct((1,), jnp.int32),
        ),
        in_specs=[smem] + [vmem] * 8,
        out_specs=(vmem,) * 7 + (smem,),
        scratch_shapes=[
            pltpu.VMEM((LEVEL, packed, KV_WIDTH), jnp.bfloat16),
            pltpu.VMEM((heads, chunk, lanes), jnp.float32),
            pltpu.VMEM((heads, 8, lanes), jnp.float32),
            pltpu.VMEM((heads, 8, lanes), jnp.float32),
            pltpu.VMEM((heads, 8, lanes), jnp.float32),
            pltpu.VMEM((heads, HEAD_SIZE, lanes), jnp.float32),
            pltpu.VMEM((heads, HEAD_SIZE, lanes), jnp.float32),
        ],
        compiler_params=pltpu.CompilerParams(vmem_limit_bytes=28 * 1024 * 1024),
        cost_estimate=pl.CostEstimate(
            flops=2 * 2 * width * HEAD_SIZE * (depth + 2) * chunk,
            bytes_accessed=8 * rows * width,
            transcendentals=0,
        ),
        name="attention",
    )(rank, q_all, do_all, kv_near, p_near, stats, acc_near, far, far_core)


def level_kernel(
    level, p_at, rank_ref, span_ref, p_buf, ds_buf, q_all, do_t, keep_ref, send_ref
):
    chunk = p_buf.shape[1]
    rows = chunk // PAIR
    lanes = GROUP_SIZE * rows
    inner = rank_ref[0] % LEVEL
    my_core = inner % 2
    my_x = inner // 2
    active = level >= span_ref[0]

    @pl.when(active)
    def _():
        for g in range(KEY_VALUE_HEADS):
            where = slice(g * lanes, (g + 1) * lanes)
            d_key = jnp.dot(
                ds_buf[level, :, where], q_all[g], preferred_element_type=jnp.float32
            ) * SCALE
            d_value = lax.dot_general(
                p_buf[p_at, :, where], do_t[g], NT, preferred_element_type=jnp.float32
            )
            for value, column in ((d_key, g), (d_value, KEY_VALUE_HEADS + g)):
                columns = slice(column * HEAD_SIZE, (column + 1) * HEAD_SIZE)
                for x_at in range(2):
                    one = value[2 * x_at * rows:(2 * x_at + 1) * rows]
                    two = value[(2 * x_at + 1) * rows:(2 * x_at + 2) * rows]
                    place = (x_at + my_x) % 2
                    at = pl.ds(pl.multiple_of(place * rows, rows), rows)
                    keep_ref[at, columns] = jnp.where(my_core == 0, one, two)
                    send_ref[at, columns] = jnp.where(my_core == 0, two, one).astype(jnp.bfloat16)

    @pl.when(jnp.logical_not(active))
    def _():
        keep_ref[...] = jnp.zeros_like(keep_ref)
        send_ref[...] = jnp.zeros_like(send_ref)


def level_gradients(level, p_at, rank, span, p_all, ds_all, q_all, do_t):
    chunk, width = p_all.shape[1:]
    rows = chunk // PAIR
    vmem = pl.BlockSpec(memory_space=pltpu.VMEM)
    smem = pl.BlockSpec(memory_space=pltpu.SMEM)
    return pl.pallas_call(
        functools.partial(level_kernel, level, p_at),
        out_shape=(
            jax.ShapeDtypeStruct((2 * rows, KV_WIDTH), jnp.float32),
            jax.ShapeDtypeStruct((2 * rows, KV_WIDTH), jnp.bfloat16),
        ),
        in_specs=[smem, smem] + [vmem] * 4,
        out_specs=(vmem, vmem),
        compiler_params=pltpu.CompilerParams(vmem_limit_bytes=28 * 1024 * 1024),
        cost_estimate=pl.CostEstimate(
            flops=LEVEL * rows * width * HEAD_SIZE // 4,
            bytes_accessed=LEVEL * rows * width // 4,
            transcendentals=0,
        ),
        name="level_gradients",
    )(rank, span, p_all, ds_all, q_all, do_t)


def shifted(value, steps):
    count = lax.axis_size("ctx")
    first, last = max(0, -steps), min(count, count - steps)
    return lax.ppermute(value, "ctx", [(at, at + steps) for at in range(first, last)])


def rotated(value, steps):
    count = lax.axis_size("ctx")
    return lax.ppermute(value, "ctx", [(at, (at + steps) % count) for at in range(count)])


def swapped(value, bit, axis="ctx"):
    return lax.ppermute(value, axis, [(at, at ^ bit) for at in range(lax.axis_size(axis))])


def bias_rows(rows):
    high = lax.reduce_precision(rows, 8, 7)
    both = jnp.concatenate([high, rows - high]).astype(jnp.bfloat16)
    return jnp.pad(both, ((0, -both.shape[0] % 16), (0, 0)))


def local(query_in, key_in, value_input, output_gradient, doc_ids, query_bias):
    rows = query_in.shape[1]
    shards = lax.axis_size("ctx")
    depth = window_levels(shards)
    rank = lax.axis_index("ctx").astype(jnp.int32)
    own = pack(key_in[0], value_input[0], doc_ids)

    ups = [shifted(own, LEVEL * step) for step in range(1, depth + 1)]
    x_own = swapped(own, 2)
    q_all, do_all = prepare(query_in[0], query_bias[None], output_gradient[0])
    ups[0], x_own, q_all, do_all = lax.optimization_barrier((ups[0], x_own, q_all, do_all))
    near = [own, x_own]
    for up in ups[:-1]:
        near += [up, swapped(up, 2)]
    x_far = swapped(ups[-1], 2)
    far, near = lax.optimization_barrier((ups[-1], near))
    near = jnp.concatenate(near, axis=0)
    near_core = swapped(near, 1)
    rank = rank.reshape(1)
    kv_near, p_near, stats, acc_near = near_attention(rank, q_all, near, near_core, depth)
    x_far, p_near = lax.optimization_barrier((x_far, p_near))
    far = jnp.concatenate([far, x_far], axis=0)
    far_core = swapped(far, 1)
    att_t, dq_t, p_far, ds_all, do_near, do_far, bias_part, span = attention(
        rank, q_all, do_all, kv_near, p_near, stats, acc_near, far, far_core
    )

    levels = shards // LEVEL
    carried = levels == 4 and depth == 2
    bit = 1
    while bit < lax.axis_size("dp"):
        bias_part = bias_part + swapped(bias_part, bit, "dp")
        bit *= 2
    bias_total = bias_part

    def joined(value):
        return jnp.concatenate([value, bias_rows(bias_total)], axis=0) if carried else value

    def bias_of(got):
        return got[rows:rows + half_rows].astype(jnp.float32) + got[
            rows + half_rows:rows + 2 * half_rows
        ].astype(jnp.float32)

    half_rows = bias_part.shape[0]
    sends = [None] * (depth + 1)
    keeps = [None] * (depth + 1)
    for step in range(depth, -1, -1):
        if step == depth:
            keep, send = level_gradients(0, 0, rank, span, p_far, ds_all, q_all, do_far)
        else:
            level = depth - step
            keep, send = level_gradients(
                level, level - 1, rank, span, p_near, ds_all, q_all, do_near
            )
        send, ds_all = lax.optimization_barrier((send, ds_all))
        if step == max(depth - 1, 0) and carried:
            got = swapped(jnp.concatenate([send, bias_rows(bias_total)], axis=0), 1)
            bias_total = bias_total + bias_of(got[rows:])
            got = got[:2 * rows]
        else:
            got = swapped(send, 1)
        keeps[step] = keep + got.astype(jnp.float32)
        sends[step] = send

    across = [None] * (depth + 1)
    for step in range(depth, -1, -1):
        away = keeps[step][rows:].astype(jnp.bfloat16)
        if step == depth:
            away, att_t = lax.optimization_barrier((away, att_t))
            away = joined(away)
        across[step] = swapped(away, 2)
    attended, grad_query = row_results(att_t, dq_t)
    down = [None] * (depth + 1)
    total = None
    for step in range(depth, -1, -1):
        if step == depth and carried:
            bias_total = bias_total + bias_of(across[step])
        total = keeps[step][:rows] + across[step][:rows].astype(jnp.float32)
        if step:
            sent = joined(total.astype(jnp.bfloat16))
            down[step] = (rotated if carried else shifted)(sent, -LEVEL * step)
            across[step - 1], _ = lax.optimization_barrier((across[step - 1], sent))
    if carried:
        bias_total = (
            bias_total + rotated(bias_total, LEVEL) + bias_of(down[1]) + bias_of(down[2])
        )
    else:
        bit = 1
        while bit < shards:
            bias_total = bias_total + swapped(bias_total, bit)
            bit *= 2
    bias_total = bias_total.reshape(-1)[:query_bias.shape[0]]
    down = [None if part is None else part[:rows] for part in down]
    for step in range(depth, 0, -1):
        total = total + down[step].astype(jnp.float32)
    total = total.astype(jnp.bfloat16)
    half = KEY_VALUE_HEADS * HEAD_SIZE
    return (
        attended[None],
        grad_query[None],
        total[:, :half][None],
        total[:, half:][None],
        bias_total,
    )


def solution(mesh):
    placed = (
        P("dp", "ctx", None),
        P("dp", "ctx", None),
        P("dp", "ctx", None),
        P("dp", "ctx", None),
        P("dp", "ctx"),
        P(),
    )
    return jax.shard_map(
        local,
        mesh=mesh,
        in_specs=placed,
        out_specs=(
            P("dp", "ctx", None),
            P("dp", "ctx", None),
            P("dp", "ctx", None),
            P("dp", "ctx", None),
            P(),
        ),
        check_vma=False,
    )
```

```python
import functools
import math

import jax
import jax.numpy as jnp
from jax import lax
from jax.experimental import pallas as pl
from jax.experimental.pallas import tpu as pltpu
from jax.sharding import PartitionSpec as P

QUERY_HEADS = 14
KEY_VALUE_HEADS = 2
HEAD_SIZE = 128
GROUP_SIZE = 7
BLK = 128
WB = 16
DOC_ROWS = 16
PAIR = 4
LEVEL = 4
LANE_TILE = 256
KV_WIDTH = 2 * KEY_VALUE_HEADS * HEAD_SIZE
SCALE = 1.0 / math.sqrt(HEAD_SIZE)
SCALE_LOG2 = SCALE * math.log2(math.e)
LOW = -1e30

NT = (((1,), (1,)), ((), ()))


def fold(value, op):
    keys, lanes = value.shape
    return op(value.reshape(keys // 8, 8, lanes), axis=0)


def window_levels(shards):
    levels = max(shards // LEVEL, 1)
    return min((WB - 2 + LEVEL) // LEVEL, max(3 * levels // 4 - 1, 0) if levels % 4 == 0 else levels - 1)


def pack_kernel(key_hbm, value_hbm, docs_hbm, own_ref, docs, sems):
    rows, half = key_hbm.shape
    copies = [
        pltpu.make_async_copy(docs_hbm, docs, sems.at[0]),
        pltpu.make_async_copy(key_hbm, own_ref.at[0:rows, 0:half], sems.at[1]),
        pltpu.make_async_copy(value_hbm, own_ref.at[0:rows, half:2 * half], sems.at[2]),
    ]
    for copy in copies:
        copy.start()
    copies[0].wait()
    count = jnp.sum((docs[...] == 0).astype(jnp.float32), axis=1, keepdims=True)
    own_ref[rows:rows + DOC_ROWS, :] = jnp.broadcast_to(count, (DOC_ROWS, 2 * half)).astype(
        jnp.bfloat16
    )
    copies[1].wait()
    copies[2].wait()


def pack(key_in, value_input, doc_ids):
    rows, half = key_in.shape
    return pl.pallas_call(
        pack_kernel,
        out_shape=jax.ShapeDtypeStruct((rows + DOC_ROWS, 2 * half), jnp.bfloat16),
        in_specs=[pl.BlockSpec(memory_space=pltpu.HBM)] * 3,
        out_specs=pl.BlockSpec(memory_space=pltpu.VMEM),
        scratch_shapes=[pltpu.VMEM((1, rows), jnp.int32), pltpu.SemaphoreType.DMA((3,))],
        compiler_params=pltpu.CompilerParams(vmem_limit_bytes=60 * 1024 * 1024),
        name="pack",
    )(key_in, value_input, doc_ids)


def head_columns(g, n):
    head = g * GROUP_SIZE + n
    return slice(head * HEAD_SIZE, (head + 1) * HEAD_SIZE)


def prepare_kernel(q_hbm, bias_ref, do_hbm, q_st, do_t, q_buf, do_buf, sems):
    rows = q_buf.shape[0]
    first = pltpu.make_async_copy(q_hbm, q_buf, sems.at[0])
    second = pltpu.make_async_copy(do_hbm, do_buf, sems.at[1])
    first.start()
    second.start()
    first.wait()
    for g in range(KEY_VALUE_HEADS):
        for n in range(GROUP_SIZE):
            columns = head_columns(g, n)
            q_st[g, n * rows:(n + 1) * rows, :] = (
                q_buf[:, columns].astype(jnp.float32) + bias_ref[:, columns]
            ).astype(jnp.bfloat16)
    second.wait()
    for g in range(KEY_VALUE_HEADS):
        for n in range(GROUP_SIZE):
            do_t[g, :, n * rows:(n + 1) * rows] = do_buf[:, head_columns(g, n)].T


def prepare(query_in, query_bias, output_gradient):
    rows, width = query_in.shape
    lanes = GROUP_SIZE * rows
    anywhere = pl.BlockSpec(memory_space=pltpu.HBM)
    vmem = pl.BlockSpec(memory_space=pltpu.VMEM)
    return pl.pallas_call(
        prepare_kernel,
        out_shape=(
            jax.ShapeDtypeStruct((KEY_VALUE_HEADS, lanes, HEAD_SIZE), jnp.bfloat16),
            jax.ShapeDtypeStruct((KEY_VALUE_HEADS, HEAD_SIZE, lanes), jnp.bfloat16),
        ),
        in_specs=[anywhere, vmem, anywhere],
        out_specs=(vmem, vmem),
        scratch_shapes=[
            pltpu.VMEM((rows, width), jnp.bfloat16),
            pltpu.VMEM((rows, width), jnp.bfloat16),
            pltpu.SemaphoreType.DMA((2,)),
        ],
        compiler_params=pltpu.CompilerParams(vmem_limit_bytes=8 * 1024 * 1024),
        cost_estimate=pl.CostEstimate(
            flops=4 * rows * width, bytes_accessed=8 * rows * width, transcendentals=0
        ),
        name="prepare",
    )(query_in, query_bias, output_gradient)


def keys_of(kv_buf, c, rows, column):
    columns = slice(column * HEAD_SIZE, (column + 1) * HEAD_SIZE)
    return jnp.concatenate([kv_buf[PAIR * c + i, 0:rows, columns] for i in range(PAIR)], axis=0)


def spread(kv_buf, slot, pieces, inner):
    core = inner % 2
    x = inner // 2
    for at, piece in enumerate(pieces):
        place_x = 1 - x if at % 2 else x
        place_core = 1 - core if at // 2 else core
        kv_buf[slot * LEVEL + 2 * place_x + place_core] = piece[...]


def doc_count(kv_buf, rows):
    counts = kv_buf[:, rows:rows + DOC_ROWS, 0:128].astype(jnp.float32)
    return jnp.sum(counts) * (1.0 / (DOC_ROWS * 128))


def window_start(rank, rows, first, count):
    boundary = (count + 0.5).astype(jnp.int32) + jnp.maximum(first, 0) * rows
    low_block = jnp.maximum(rank - (WB - 1), 0)
    in_second = rank * rows >= boundary
    return boundary, jnp.where(in_second, jnp.maximum(low_block, boundary // rows), low_block)


def mask_bias(key_first, q_first, boundary, chunk, rows):
    key_pos = key_first + lax.broadcasted_iota(jnp.int32, (chunk, rows), 0)
    query_pos = q_first + lax.broadcasted_iota(jnp.int32, (chunk, rows), 1)
    allowed = (key_pos <= query_pos) & (query_pos // BLK - key_pos // BLK < WB)
    allowed = allowed & ((key_pos >= boundary) == (query_pos >= boundary))
    return jnp.where(allowed, 0.0, LOW)


def lane_tiles(lanes):
    return [(at, min(at + LANE_TILE, lanes)) for at in range(0, lanes, LANE_TILE)]


def near_kernel(rank_ref, q_all, *refs):
    pieces, (kv_buf, p_buf, stats_ref, acc, s_buf) = refs[:-5], refs[-5:]
    depth, chunk = p_buf.shape[:2]
    rows = chunk // PAIR
    lanes = q_all.shape[1]
    tiles = lane_tiles(lanes)
    rank = rank_ref[0]
    first = (rank // LEVEL - (depth - 1)) * LEVEL
    for level in range(depth):
        spread(kv_buf, depth - 1 - level, pieces[4 * level:4 * level + 4], rank % LEVEL)
    boundary, low_block = window_start(rank, rows, first, doc_count(kv_buf, rows))
    low = jnp.maximum(low_block - first, 0) // PAIR

    for g in range(KEY_VALUE_HEADS):
        stats_ref[g, 0:8, :] = jnp.full((8, lanes), LOW, jnp.float32)
        stats_ref[g, 8:16, :] = jnp.zeros((8, lanes), jnp.float32)
    acc[...] = jnp.zeros_like(acc)

    def score_steps(c, g):
        bias = mask_bias((first + PAIR * c) * rows, rank * rows, boundary, chunk, rows)
        k_c = keys_of(kv_buf, c, rows, g)

        def step(a, b):
            s = lax.dot_general(k_c, q_all[g, a:b, :], NT, preferred_element_type=jnp.float32)
            s = s + jnp.concatenate([bias] * ((b - a) // rows), axis=1)
            s_buf[c, :, a:b] = s
            stats_ref[g, 0:8, a:b] = jnp.maximum(stats_ref[g, 0:8, a:b], fold(s, jnp.max))

        return step

    def weight_steps(c, g, row_max):
        v_t = keys_of(kv_buf, c, rows, KEY_VALUE_HEADS + g).T

        def step(a, b):
            p = jnp.exp2(s_buf[c, :, a:b] * SCALE_LOG2 - row_max[:, a:b])
            stats_ref[g, 8:16, a:b] += fold(p, jnp.sum)
            p_bf = p.astype(jnp.bfloat16)
            p_buf[c, :, g * lanes + a:g * lanes + b] = p_bf
            acc[g, :, a:b] += jnp.dot(v_t, p_bf, preferred_element_type=jnp.float32)

        return step

    def over_chunks(*makers):
        @pl.loop(low, depth)
        def _(c):
            steps = [make(c) for make in makers]
            for a, b in tiles:
                for step in steps:
                    step(a, b)

    over_chunks(lambda c: score_steps(c, 0))
    for g in range(KEY_VALUE_HEADS):
        row_max = jnp.max(stats_ref[g, 0:8, :], axis=0, keepdims=True) * SCALE_LOG2
        makers = [lambda c: weight_steps(c, g, row_max)]
        if g + 1 < KEY_VALUE_HEADS:
            makers.append(lambda c: score_steps(c, g + 1))
        over_chunks(*makers)
        stats_ref[g, 0:1, :] = row_max
        stats_ref[g, 8:9, :] = jnp.sum(stats_ref[g, 8:16, :], axis=0, keepdims=True)


def near_attention(rank, q_all, pieces):
    depth = len(pieces) // 4
    lanes = q_all.shape[1]
    rows = lanes // GROUP_SIZE
    packed = rows + DOC_ROWS
    chunk = PAIR * rows
    vmem = pl.BlockSpec(memory_space=pltpu.VMEM)
    smem = pl.BlockSpec(memory_space=pltpu.SMEM)
    heads = KEY_VALUE_HEADS
    return pl.pallas_call(
        near_kernel,
        out_shape=(
            jax.ShapeDtypeStruct((depth * LEVEL, packed, KV_WIDTH), jnp.bfloat16),
            jax.ShapeDtypeStruct((depth, chunk, heads * lanes), jnp.bfloat16),
            jax.ShapeDtypeStruct((heads, 16, lanes), jnp.float32),
            jax.ShapeDtypeStruct((heads, HEAD_SIZE, lanes), jnp.float32),
        ),
        in_specs=[smem] + [vmem] * (1 + len(pieces)),
        out_specs=(vmem,) * 4,
        scratch_shapes=[pltpu.VMEM((depth, chunk, lanes), jnp.float32)],
        compiler_params=pltpu.CompilerParams(vmem_limit_bytes=28 * 1024 * 1024),
        cost_estimate=pl.CostEstimate(
            flops=2 * 2 * heads * lanes * HEAD_SIZE * depth * chunk,
            bytes_accessed=4 * heads * lanes * HEAD_SIZE,
            transcendentals=heads * lanes * depth * chunk,
        ),
        name="near_attention",
    )(rank, q_all, *pieces)


def kernel(
    rank_ref, q_all, do_all, kv_near, p_near, stats_ref, acc_near, far_0, far_1, far_2, far_3,
    att_t, dq_t, p_far, ds_buf, do_near, do_far, gb_ref, span_ref,
    kv_far, s_buf, sum_buf, factor_buf, dot_buf, acc, dq_acc,
):
    depth, chunk = p_near.shape[:2]
    rows = chunk // PAIR
    lanes = GROUP_SIZE * rows
    tiles = lane_tiles(lanes)
    rank = rank_ref[0]
    first = (rank // LEVEL - depth) * LEVEL
    spread(kv_far, 0, (far_0, far_1, far_2, far_3), rank % LEVEL)
    count = doc_count(kv_far, rows) + doc_count(kv_near, rows)
    boundary, low_block = window_start(rank, rows, first, count)
    low = jnp.maximum(low_block - first, 0) // PAIR
    span_ref[0] = low
    with_far = low == 0

    dq_acc[...] = jnp.zeros_like(dq_acc)

    @pl.when(with_far)
    def _():
        bias = mask_bias(first * rows, rank * rows, boundary, chunk, rows)

        def score(g, a, b):
            k_c = keys_of(kv_far, 0, rows, g)
            s = lax.dot_general(k_c, q_all[g, a:b, :], NT, preferred_element_type=jnp.float32)
            s = s + jnp.concatenate([bias] * ((b - a) // rows), axis=1)
            s_buf[g, :, a:b] = s
            far_max = jnp.max(fold(s, jnp.max), axis=0, keepdims=True) * SCALE_LOG2
            factor_buf[g, 0:1, a:b] = jnp.maximum(stats_ref[g, 0:1, a:b], far_max)

        def weight(g, a, b):
            v_t = keys_of(kv_far, 0, rows, KEY_VALUE_HEADS + g).T
            top = factor_buf[g, 0:1, a:b]
            factor = jnp.exp2(stats_ref[g, 0:1, a:b] - top)
            p = jnp.exp2(s_buf[g, :, a:b] * SCALE_LOG2 - top)
            p_bf = p.astype(jnp.bfloat16)
            p_far[0, :, g * lanes + a:g * lanes + b] = p_bf
            total = jnp.sum(fold(p, jnp.sum), axis=0, keepdims=True)
            sum_buf[g, 0:1, a:b] = stats_ref[g, 8:9, a:b] * factor + total
            factor_buf[g, 0:1, a:b] = factor
            acc[g, :, a:b] = acc_near[g, :, a:b] * factor + jnp.dot(
                v_t, p_bf, preferred_element_type=jnp.float32
            )

        for a, b in tiles:
            score(0, a, b)
        for g in range(KEY_VALUE_HEADS):
            for a, b in tiles:
                weight(g, a, b)
                if g + 1 < KEY_VALUE_HEADS:
                    score(g + 1, a, b)

    @pl.when(jnp.logical_not(with_far))
    def _():
        sum_buf[:, 0:1, :] = stats_ref[:, 8:9, :]
        factor_buf[:, 0:1, :] = jnp.ones((KEY_VALUE_HEADS, 1, lanes), jnp.float32)
        acc[...] = acc_near[...]

    for g in range(KEY_VALUE_HEADS):
        inverse = 1.0 / sum_buf[g, 0:1, :]
        factor = factor_buf[g, 0:1, :]
        for n in range(GROUP_SIZE):
            at = slice(n * rows, (n + 1) * rows)
            att = (acc[g, :, at] * inverse[:, at]).astype(jnp.bfloat16)
            att_t[g, :, at] = att
            do_n = do_all[g, :, at].astype(jnp.float32)
            dot_n = jnp.sum(do_n * att.astype(jnp.float32), axis=0, keepdims=True) * inverse[:, at]
            do_n = do_n * inverse[:, at]
            dot_buf[g, 0:1, at] = dot_n
            dot_buf[g, 1:2, at] = dot_n * factor[:, at]
            do_far[g, :, at] = do_n.astype(jnp.bfloat16)
            do_near[g, :, at] = (do_n * factor[:, at]).astype(jnp.bfloat16)

    def gradient_steps(g, c, kv_buf, at, p_buf, do_t, row):
        v_c = keys_of(kv_buf, at, rows, KEY_VALUE_HEADS + g)
        k_t = keys_of(kv_buf, at, rows, g).T

        def step(a, b):
            where = slice(g * lanes + a, g * lanes + b)
            d_p = jnp.dot(v_c, do_t[g, :, a:b], preferred_element_type=jnp.float32)
            p = p_buf[at, :, where].astype(jnp.float32)
            d_s = (p * (d_p - dot_buf[g, row:row + 1, a:b])).astype(jnp.bfloat16)
            ds_buf[c, :, where] = d_s
            dq_acc[g, :, a:b] += jnp.dot(k_t, d_s, preferred_element_type=jnp.float32)

        return step

    def gradients(c, kv_buf, at, p_buf, do_t, row):
        steps = [
            gradient_steps(g, c, kv_buf, at, p_buf, do_t, row) for g in range(KEY_VALUE_HEADS)
        ]
        for a, b in tiles:
            for step in steps:
                step(a, b)

    @pl.when(with_far)
    def _():
        gradients(0, kv_far, 0, p_far, do_far, 0)

    @pl.loop(jnp.maximum(low, 1), depth + 1)
    def _(c):
        gradients(c, kv_near, c - 1, p_near, do_near, 1)

    gb_ref[...] = jnp.zeros_like(gb_ref)
    ones = jnp.ones((8, rows), jnp.bfloat16)
    for g in range(KEY_VALUE_HEADS):
        for n in range(GROUP_SIZE):
            columns = slice(n * rows, (n + 1) * rows)
            d_q = (dq_acc[g, :, columns] * SCALE).astype(jnp.bfloat16)
            dq_t[g, :, columns] = d_q
            row, at = divmod(head_columns(g, n).start, KV_WIDTH)
            sums = lax.dot_general(ones, d_q, NT, preferred_element_type=jnp.float32)
            gb_ref[row:row + 1, at:at + HEAD_SIZE] = sums[0:1]


def rows_kernel(att_t, dq_t, att_ref, dq_ref):
    rows = att_ref.shape[0]
    for g in range(KEY_VALUE_HEADS):
        for n in range(GROUP_SIZE):
            at = slice(n * rows, (n + 1) * rows)
            att_ref[:, head_columns(g, n)] = att_t[g, :, at].T
            dq_ref[:, head_columns(g, n)] = dq_t[g, :, at].T


def row_results(att_t, dq_t):
    rows = att_t.shape[2] // GROUP_SIZE
    width = QUERY_HEADS * HEAD_SIZE
    vmem = pl.BlockSpec(memory_space=pltpu.VMEM)
    return pl.pallas_call(
        rows_kernel,
        out_shape=(jax.ShapeDtypeStruct((rows, width), jnp.bfloat16),) * 2,
        in_specs=[vmem] * 2,
        out_specs=(vmem,) * 2,
        compiler_params=pltpu.CompilerParams(vmem_limit_bytes=8 * 1024 * 1024),
        cost_estimate=pl.CostEstimate(
            flops=2 * rows * width, bytes_accessed=8 * rows * width, transcendentals=0
        ),
        name="row_results",
    )(att_t, dq_t)


def attention(rank, q_all, do_all, kv_near, p_near, stats, acc_near, far):
    lanes = q_all.shape[1]
    rows = lanes // GROUP_SIZE
    width = QUERY_HEADS * HEAD_SIZE
    packed = rows + DOC_ROWS
    depth, chunk = p_near.shape[:2]
    vmem = pl.BlockSpec(memory_space=pltpu.VMEM)
    smem = pl.BlockSpec(memory_space=pltpu.SMEM)
    heads = KEY_VALUE_HEADS
    return pl.pallas_call(
        kernel,
        out_shape=(
            jax.ShapeDtypeStruct((heads, HEAD_SIZE, lanes), jnp.bfloat16),
            jax.ShapeDtypeStruct((heads, HEAD_SIZE, lanes), jnp.bfloat16),
            jax.ShapeDtypeStruct((1, chunk, heads * lanes), jnp.bfloat16),
            jax.ShapeDtypeStruct((depth + 1, chunk, heads * lanes), jnp.bfloat16),
            jax.ShapeDtypeStruct((heads, HEAD_SIZE, lanes), jnp.bfloat16),
            jax.ShapeDtypeStruct((heads, HEAD_SIZE, lanes), jnp.bfloat16),
            jax.ShapeDtypeStruct((-(-width // KV_WIDTH), KV_WIDTH), jnp.float32),
            jax.ShapeDtypeStruct((1,), jnp.int32),
        ),
        in_specs=[smem] + [vmem] * (6 + len(far)),
        out_specs=(vmem,) * 7 + (smem,),
        scratch_shapes=[
            pltpu.VMEM((LEVEL, packed, KV_WIDTH), jnp.bfloat16),
            pltpu.VMEM((heads, chunk, lanes), jnp.float32),
            pltpu.VMEM((heads, 8, lanes), jnp.float32),
            pltpu.VMEM((heads, 8, lanes), jnp.float32),
            pltpu.VMEM((heads, 8, lanes), jnp.float32),
            pltpu.VMEM((heads, HEAD_SIZE, lanes), jnp.float32),
            pltpu.VMEM((heads, HEAD_SIZE, lanes), jnp.float32),
        ],
        compiler_params=pltpu.CompilerParams(vmem_limit_bytes=28 * 1024 * 1024),
        cost_estimate=pl.CostEstimate(
            flops=2 * 2 * width * HEAD_SIZE * (depth + 2) * chunk,
            bytes_accessed=8 * rows * width,
            transcendentals=0,
        ),
        name="attention",
    )(rank, q_all, do_all, kv_near, p_near, stats, acc_near, *far)


def level_kernel(
    level, p_at, rank_ref, span_ref, p_buf, ds_buf, q_all, do_t, keep_ref, send_ref
):
    chunk = p_buf.shape[1]
    rows = chunk // PAIR
    lanes = GROUP_SIZE * rows
    inner = rank_ref[0] % LEVEL
    my_core = inner % 2
    my_x = inner // 2
    active = level >= span_ref[0]

    @pl.when(active)
    def _():
        for g in range(KEY_VALUE_HEADS):
            where = slice(g * lanes, (g + 1) * lanes)
            d_key = jnp.dot(
                ds_buf[level, :, where], q_all[g], preferred_element_type=jnp.float32
            ) * SCALE
            d_value = lax.dot_general(
                p_buf[p_at, :, where], do_t[g], NT, preferred_element_type=jnp.float32
            )
            for value, column in ((d_key, g), (d_value, KEY_VALUE_HEADS + g)):
                columns = slice(column * HEAD_SIZE, (column + 1) * HEAD_SIZE)
                for x_at in range(2):
                    one = value[2 * x_at * rows:(2 * x_at + 1) * rows]
                    two = value[(2 * x_at + 1) * rows:(2 * x_at + 2) * rows]
                    place = (x_at + my_x) % 2
                    at = pl.ds(pl.multiple_of(place * rows, rows), rows)
                    keep_ref[at, columns] = jnp.where(my_core == 0, one, two)
                    send_ref[at, columns] = jnp.where(my_core == 0, two, one).astype(jnp.bfloat16)

    @pl.when(jnp.logical_not(active))
    def _():
        keep_ref[...] = jnp.zeros_like(keep_ref)
        send_ref[...] = jnp.zeros_like(send_ref)


def level_gradients(level, p_at, rank, span, p_all, ds_all, q_all, do_t):
    chunk, width = p_all.shape[1:]
    rows = chunk // PAIR
    vmem = pl.BlockSpec(memory_space=pltpu.VMEM)
    smem = pl.BlockSpec(memory_space=pltpu.SMEM)
    return pl.pallas_call(
        functools.partial(level_kernel, level, p_at),
        out_shape=(
            jax.ShapeDtypeStruct((2 * rows, KV_WIDTH), jnp.float32),
            jax.ShapeDtypeStruct((2 * rows, KV_WIDTH), jnp.bfloat16),
        ),
        in_specs=[smem, smem] + [vmem] * 4,
        out_specs=(vmem, vmem),
        compiler_params=pltpu.CompilerParams(vmem_limit_bytes=28 * 1024 * 1024),
        cost_estimate=pl.CostEstimate(
            flops=LEVEL * rows * width * HEAD_SIZE // 4,
            bytes_accessed=LEVEL * rows * width // 4,
            transcendentals=0,
        ),
        name="level_gradients",
    )(rank, span, p_all, ds_all, q_all, do_t)


def shifted(value, steps):
    count = lax.axis_size("ctx")
    first, last = max(0, -steps), min(count, count - steps)
    return lax.ppermute(value, "ctx", [(at, at + steps) for at in range(first, last)])


def rotated(value, steps):
    count = lax.axis_size("ctx")
    return lax.ppermute(value, "ctx", [(at, (at + steps) % count) for at in range(count)])


def swapped(value, bit, axis="ctx"):
    return lax.ppermute(value, axis, [(at, at ^ bit) for at in range(lax.axis_size(axis))])


def bias_rows(rows):
    high = lax.reduce_precision(rows, 8, 7)
    both = jnp.concatenate([high, rows - high]).astype(jnp.bfloat16)
    return jnp.pad(both, ((0, -both.shape[0] % 16), (0, 0)))


def local(query_in, key_in, value_input, output_gradient, doc_ids, query_bias):
    rows = query_in.shape[1]
    shards = lax.axis_size("ctx")
    depth = window_levels(shards)
    rank = lax.axis_index("ctx").astype(jnp.int32)
    own = pack(key_in[0], value_input[0], doc_ids)

    ups = [shifted(own, LEVEL * step) for step in range(1, depth + 1)]
    x_own = swapped(own, 2)
    q_all, do_all = prepare(query_in[0], query_bias[None], output_gradient[0])
    ups[0], x_own, q_all, do_all = lax.optimization_barrier((ups[0], x_own, q_all, do_all))
    pairs = [(own, x_own)] + [(up, swapped(up, 2)) for up in ups[:-1]]
    x_far = swapped(ups[-1], 2)
    far_up, pairs = lax.optimization_barrier((ups[-1], pairs))
    pieces = []
    for shard, x_shard in pairs:
        pieces += [shard, x_shard, swapped(shard, 1), swapped(x_shard, 1)]
    rank = rank.reshape(1)
    kv_near, p_near, stats, acc_near = near_attention(rank, q_all, pieces)
    core_far = swapped(far_up, 1)
    x_far, p_near = lax.optimization_barrier((x_far, p_near))
    far = [far_up, x_far, core_far, swapped(x_far, 1)]
    att_t, dq_t, p_far, ds_all, do_near, do_far, bias_part, span = attention(
        rank, q_all, do_all, kv_near, p_near, stats, acc_near, far
    )

    levels = shards // LEVEL
    carried = levels == 4 and depth == 2
    bit = 1
    while bit < lax.axis_size("dp"):
        bias_part = bias_part + swapped(bias_part, bit, "dp")
        bit *= 2
    bias_total = bias_part

    def joined(value):
        return jnp.concatenate([value, bias_rows(bias_total)], axis=0) if carried else value

    def bias_of(got):
        return got[rows:rows + half_rows].astype(jnp.float32) + got[
            rows + half_rows:rows + 2 * half_rows
        ].astype(jnp.float32)

    half_rows = bias_part.shape[0]
    sends = [None] * (depth + 1)
    keeps = [None] * (depth + 1)
    for step in range(depth, -1, -1):
        if step == depth:
            keep, send = level_gradients(0, 0, rank, span, p_far, ds_all, q_all, do_far)
        else:
            level = depth - step
            keep, send = level_gradients(
                level, level - 1, rank, span, p_near, ds_all, q_all, do_near
            )
        send, ds_all = lax.optimization_barrier((send, ds_all))
        if step == max(depth - 1, 0) and carried:
            got = swapped(jnp.concatenate([send, bias_rows(bias_total)], axis=0), 1)
            bias_total = bias_total + bias_of(got[rows:])
            got = got[:2 * rows]
        else:
            got = swapped(send, 1)
        keeps[step] = keep + got.astype(jnp.float32)
        sends[step] = send

    across = [None] * (depth + 1)
    for step in range(depth, -1, -1):
        away = keeps[step][rows:].astype(jnp.bfloat16)
        if step == depth:
            away, att_t = lax.optimization_barrier((away, att_t))
            away = joined(away)
        across[step] = swapped(away, 2)
    attended, grad_query = row_results(att_t, dq_t)
    down = [None] * (depth + 1)
    total = None
    for step in range(depth, -1, -1):
        if step == depth and carried:
            bias_total = bias_total + bias_of(across[step])
        total = keeps[step][:rows] + across[step][:rows].astype(jnp.float32)
        if step:
            sent = joined(total.astype(jnp.bfloat16))
            down[step] = (rotated if carried else shifted)(sent, -LEVEL * step)
            across[step - 1], _ = lax.optimization_barrier((across[step - 1], sent))
    if carried:
        bias_total = (
            bias_total + rotated(bias_total, LEVEL) + bias_of(down[1]) + bias_of(down[2])
        )
    else:
        bit = 1
        while bit < shards:
            bias_total = bias_total + swapped(bias_total, bit)
            bit *= 2
    bias_total = bias_total.reshape(-1)[:query_bias.shape[0]]
    down = [None if part is None else part[:rows] for part in down]
    for step in range(depth, 0, -1):
        total = total + down[step].astype(jnp.float32)
    total = total.astype(jnp.bfloat16)
    half = KEY_VALUE_HEADS * HEAD_SIZE
    return (
        attended[None],
        grad_query[None],
        total[:, :half][None],
        total[:, half:][None],
        bias_total,
    )


def solution(mesh):
    placed = (
        P("dp", "ctx", None),
        P("dp", "ctx", None),
        P("dp", "ctx", None),
        P("dp", "ctx", None),
        P("dp", "ctx"),
        P(),
    )
    return jax.shard_map(
        local,
        mesh=mesh,
        in_specs=placed,
        out_specs=(
            P("dp", "ctx", None),
            P("dp", "ctx", None),
            P("dp", "ctx", None),
            P("dp", "ctx", None),
            P(),
        ),
        check_vma=False,
    )
```

```python
import functools
import math

import jax
import jax.numpy as jnp
from jax import lax
from jax.experimental import pallas as pl
from jax.experimental.pallas import tpu as pltpu
from jax.sharding import PartitionSpec as P

QUERY_HEADS = 14
KEY_VALUE_HEADS = 2
HEAD_SIZE = 128
GROUP_SIZE = 7
BLK = 128
WB = 16
DOC_ROWS = 16
PAIR = 4
LEVEL = 4
LANE_TILE = 256
KV_WIDTH = 2 * KEY_VALUE_HEADS * HEAD_SIZE
SCALE = 1.0 / math.sqrt(HEAD_SIZE)
SCALE_LOG2 = SCALE * math.log2(math.e)
LOW = -1e30

NT = (((1,), (1,)), ((), ()))


def fold(value, op):
    keys, lanes = value.shape
    return op(value.reshape(keys // 8, 8, lanes), axis=0)


def window_levels(shards):
    levels = max(shards // LEVEL, 1)
    return min((WB - 2 + LEVEL) // LEVEL, max(3 * levels // 4 - 1, 0) if levels % 4 == 0 else levels - 1)


def pack_kernel(key_hbm, value_hbm, docs_hbm, own_ref, docs, sems):
    rows, half = key_hbm.shape
    copies = [
        pltpu.make_async_copy(docs_hbm, docs, sems.at[0]),
        pltpu.make_async_copy(key_hbm, own_ref.at[0:rows, 0:half], sems.at[1]),
        pltpu.make_async_copy(value_hbm, own_ref.at[0:rows, half:2 * half], sems.at[2]),
    ]
    for copy in copies:
        copy.start()
    copies[0].wait()
    count = jnp.sum((docs[...] == 0).astype(jnp.float32), axis=1, keepdims=True)
    own_ref[rows:rows + DOC_ROWS, :] = jnp.broadcast_to(count, (DOC_ROWS, 2 * half)).astype(
        jnp.bfloat16
    )
    copies[1].wait()
    copies[2].wait()


def pack(key_in, value_input, doc_ids):
    rows, half = key_in.shape
    return pl.pallas_call(
        pack_kernel,
        out_shape=jax.ShapeDtypeStruct((rows + DOC_ROWS, 2 * half), jnp.bfloat16),
        in_specs=[pl.BlockSpec(memory_space=pltpu.HBM)] * 3,
        out_specs=pl.BlockSpec(memory_space=pltpu.VMEM),
        scratch_shapes=[pltpu.VMEM((1, rows), jnp.int32), pltpu.SemaphoreType.DMA((3,))],
        compiler_params=pltpu.CompilerParams(vmem_limit_bytes=60 * 1024 * 1024),
        name="pack",
    )(key_in, value_input, doc_ids)


def head_columns(g, n):
    head = g * GROUP_SIZE + n
    return slice(head * HEAD_SIZE, (head + 1) * HEAD_SIZE)


def prepare_kernel(q_hbm, bias_ref, do_hbm, own_hbm, q_st, do_t, own_ref, q_buf, do_buf, sems):
    rows = q_buf.shape[0]
    first = pltpu.make_async_copy(q_hbm, q_buf, sems.at[0])
    second = pltpu.make_async_copy(do_hbm, do_buf, sems.at[1])
    third = pltpu.make_async_copy(own_hbm, own_ref, sems.at[2])
    first.start()
    second.start()
    third.start()
    first.wait()
    for g in range(KEY_VALUE_HEADS):
        for n in range(GROUP_SIZE):
            columns = head_columns(g, n)
            q_st[g, n * rows:(n + 1) * rows, :] = (
                q_buf[:, columns].astype(jnp.float32) + bias_ref[:, columns]
            ).astype(jnp.bfloat16)
    second.wait()
    for g in range(KEY_VALUE_HEADS):
        for n in range(GROUP_SIZE):
            do_t[g, :, n * rows:(n + 1) * rows] = do_buf[:, head_columns(g, n)].T
    third.wait()


def prepare(query_in, query_bias, output_gradient, own):
    rows, width = query_in.shape
    lanes = GROUP_SIZE * rows
    anywhere = pl.BlockSpec(memory_space=pltpu.HBM)
    vmem = pl.BlockSpec(memory_space=pltpu.VMEM)
    return pl.pallas_call(
        prepare_kernel,
        out_shape=(
            jax.ShapeDtypeStruct((KEY_VALUE_HEADS, lanes, HEAD_SIZE), jnp.bfloat16),
            jax.ShapeDtypeStruct((KEY_VALUE_HEADS, HEAD_SIZE, lanes), jnp.bfloat16),
            jax.ShapeDtypeStruct(own.shape, own.dtype),
        ),
        in_specs=[anywhere, vmem, anywhere, anywhere],
        out_specs=(vmem, vmem, vmem),
        scratch_shapes=[
            pltpu.VMEM((rows, width), jnp.bfloat16),
            pltpu.VMEM((rows, width), jnp.bfloat16),
            pltpu.SemaphoreType.DMA((3,)),
        ],
        compiler_params=pltpu.CompilerParams(vmem_limit_bytes=8 * 1024 * 1024),
        cost_estimate=pl.CostEstimate(
            flops=4 * rows * width, bytes_accessed=8 * rows * width, transcendentals=0
        ),
        name="prepare",
    )(query_in, query_bias, output_gradient, own)


def keys_of(kv_buf, c, rows, column):
    columns = slice(column * HEAD_SIZE, (column + 1) * HEAD_SIZE)
    return jnp.concatenate([kv_buf[PAIR * c + i, 0:rows, columns] for i in range(PAIR)], axis=0)


def spread(kv_buf, slot, pieces, inner):
    core = inner % 2
    x = inner // 2
    for at, piece in enumerate(pieces):
        place_x = 1 - x if at % 2 else x
        place_core = 1 - core if at // 2 else core
        kv_buf[slot * LEVEL + 2 * place_x + place_core] = piece[...]


def doc_count(kv_buf, rows):
    counts = kv_buf[:, rows:rows + DOC_ROWS, 0:128].astype(jnp.float32)
    return jnp.sum(counts) * (1.0 / (DOC_ROWS * 128))


def window_start(rank, rows, first, count):
    boundary = (count + 0.5).astype(jnp.int32) + jnp.maximum(first, 0) * rows
    low_block = jnp.maximum(rank - (WB - 1), 0)
    in_second = rank * rows >= boundary
    return boundary, jnp.where(in_second, jnp.maximum(low_block, boundary // rows), low_block)


def mask_bias(key_first, q_first, boundary, chunk, rows):
    key_pos = key_first + lax.broadcasted_iota(jnp.int32, (chunk, rows), 0)
    query_pos = q_first + lax.broadcasted_iota(jnp.int32, (chunk, rows), 1)
    allowed = (key_pos <= query_pos) & (query_pos // BLK - key_pos // BLK < WB)
    allowed = allowed & ((key_pos >= boundary) == (query_pos >= boundary))
    return jnp.where(allowed, 0.0, LOW)


def lane_tiles(lanes):
    return [(at, min(at + LANE_TILE, lanes)) for at in range(0, lanes, LANE_TILE)]


def near_kernel(
    rank_ref, q_all, near_ref, near_core_ref,
    kv_buf, p_buf, stats_ref, acc,
    s_buf,
):
    packed = kv_buf.shape[1]
    depth, chunk = p_buf.shape[:2]
    rows = chunk // PAIR
    lanes = q_all.shape[1]
    tiles = lane_tiles(lanes)
    rank = rank_ref[0]
    first = (rank // LEVEL - (depth - 1)) * LEVEL
    for level in range(depth):
        pieces = [
            ref.at[at * packed:(at + 1) * packed]
            for ref in (near_ref, near_core_ref) for at in (2 * level, 2 * level + 1)
        ]
        spread(kv_buf, depth - 1 - level, pieces, rank % LEVEL)
    boundary, low_block = window_start(rank, rows, first, doc_count(kv_buf, rows))
    low = jnp.maximum(low_block - first, 0) // PAIR

    for g in range(KEY_VALUE_HEADS):
        stats_ref[g, 0:8, :] = jnp.full((8, lanes), LOW, jnp.float32)
        stats_ref[g, 8:16, :] = jnp.zeros((8, lanes), jnp.float32)
    acc[...] = jnp.zeros_like(acc)

    def score_steps(c, g):
        bias = mask_bias((first + PAIR * c) * rows, rank * rows, boundary, chunk, rows)
        k_c = keys_of(kv_buf, c, rows, g)

        def step(a, b):
            s = lax.dot_general(k_c, q_all[g, a:b, :], NT, preferred_element_type=jnp.float32)
            s = s + jnp.concatenate([bias] * ((b - a) // rows), axis=1)
            s_buf[c, :, a:b] = s
            stats_ref[g, 0:8, a:b] = jnp.maximum(stats_ref[g, 0:8, a:b], fold(s, jnp.max))

        return step

    def weight_steps(c, g, row_max):
        v_t = keys_of(kv_buf, c, rows, KEY_VALUE_HEADS + g).T

        def step(a, b):
            p = jnp.exp2(s_buf[c, :, a:b] * SCALE_LOG2 - row_max[:, a:b])
            stats_ref[g, 8:16, a:b] += fold(p, jnp.sum)
            p_bf = p.astype(jnp.bfloat16)
            p_buf[c, :, g * lanes + a:g * lanes + b] = p_bf
            acc[g, :, a:b] += jnp.dot(v_t, p_bf, preferred_element_type=jnp.float32)

        return step

    def over_chunks(*makers):
        @pl.loop(low, depth)
        def _(c):
            steps = [make(c) for make in makers]
            for a, b in tiles:
                for step in steps:
                    step(a, b)

    over_chunks(lambda c: score_steps(c, 0))
    for g in range(KEY_VALUE_HEADS):
        row_max = jnp.max(stats_ref[g, 0:8, :], axis=0, keepdims=True) * SCALE_LOG2
        makers = [lambda c: weight_steps(c, g, row_max)]
        if g + 1 < KEY_VALUE_HEADS:
            makers.append(lambda c: score_steps(c, g + 1))
        over_chunks(*makers)
        stats_ref[g, 0:1, :] = row_max
        stats_ref[g, 8:9, :] = jnp.sum(stats_ref[g, 8:16, :], axis=0, keepdims=True)


def near_attention(rank, q_all, near, near_core, depth):
    lanes = q_all.shape[1]
    rows = lanes // GROUP_SIZE
    packed = rows + DOC_ROWS
    chunk = PAIR * rows
    vmem = pl.BlockSpec(memory_space=pltpu.VMEM)
    smem = pl.BlockSpec(memory_space=pltpu.SMEM)
    heads = KEY_VALUE_HEADS
    return pl.pallas_call(
        near_kernel,
        out_shape=(
            jax.ShapeDtypeStruct((depth * LEVEL, packed, KV_WIDTH), jnp.bfloat16),
            jax.ShapeDtypeStruct((depth, chunk, heads * lanes), jnp.bfloat16),
            jax.ShapeDtypeStruct((heads, 16, lanes), jnp.float32),
            jax.ShapeDtypeStruct((heads, HEAD_SIZE, lanes), jnp.float32),
        ),
        in_specs=[smem] + [vmem] * 3,
        out_specs=(vmem,) * 4,
        scratch_shapes=[pltpu.VMEM((depth, chunk, lanes), jnp.float32)],
        compiler_params=pltpu.CompilerParams(vmem_limit_bytes=28 * 1024 * 1024),
        cost_estimate=pl.CostEstimate(
            flops=2 * 2 * heads * lanes * HEAD_SIZE * depth * chunk,
            bytes_accessed=4 * heads * lanes * HEAD_SIZE,
            transcendentals=heads * lanes * depth * chunk,
        ),
        name="near_attention",
    )(rank, q_all, near, near_core)


def kernel(
    rank_ref, q_all, do_all, kv_near, p_near, stats_ref, acc_near, far_0, far_1, far_2, far_3,
    att_t, dq_t, p_far, ds_buf, do_near, do_far, gb_ref, span_ref,
    kv_far, s_buf, sum_buf, factor_buf, dot_buf, acc, dq_acc,
):
    depth, chunk = p_near.shape[:2]
    rows = chunk // PAIR
    lanes = GROUP_SIZE * rows
    tiles = lane_tiles(lanes)
    rank = rank_ref[0]
    first = (rank // LEVEL - depth) * LEVEL
    spread(kv_far, 0, (far_0, far_1, far_2, far_3), rank % LEVEL)
    count = doc_count(kv_far, rows) + doc_count(kv_near, rows)
    boundary, low_block = window_start(rank, rows, first, count)
    low = jnp.maximum(low_block - first, 0) // PAIR
    span_ref[0] = low
    with_far = low == 0

    dq_acc[...] = jnp.zeros_like(dq_acc)

    @pl.when(with_far)
    def _():
        bias = mask_bias(first * rows, rank * rows, boundary, chunk, rows)

        def score(g, a, b):
            k_c = keys_of(kv_far, 0, rows, g)
            s = lax.dot_general(k_c, q_all[g, a:b, :], NT, preferred_element_type=jnp.float32)
            s = s + jnp.concatenate([bias] * ((b - a) // rows), axis=1)
            s_buf[g, :, a:b] = s
            far_max = jnp.max(fold(s, jnp.max), axis=0, keepdims=True) * SCALE_LOG2
            factor_buf[g, 0:1, a:b] = jnp.maximum(stats_ref[g, 0:1, a:b], far_max)

        def weight(g, a, b):
            v_t = keys_of(kv_far, 0, rows, KEY_VALUE_HEADS + g).T
            top = factor_buf[g, 0:1, a:b]
            factor = jnp.exp2(stats_ref[g, 0:1, a:b] - top)
            p = jnp.exp2(s_buf[g, :, a:b] * SCALE_LOG2 - top)
            p_bf = p.astype(jnp.bfloat16)
            p_far[0, :, g * lanes + a:g * lanes + b] = p_bf
            total = jnp.sum(fold(p, jnp.sum), axis=0, keepdims=True)
            sum_buf[g, 0:1, a:b] = stats_ref[g, 8:9, a:b] * factor + total
            factor_buf[g, 0:1, a:b] = factor
            acc[g, :, a:b] = acc_near[g, :, a:b] * factor + jnp.dot(
                v_t, p_bf, preferred_element_type=jnp.float32
            )

        for a, b in tiles:
            score(0, a, b)
        for g in range(KEY_VALUE_HEADS):
            for a, b in tiles:
                weight(g, a, b)
                if g + 1 < KEY_VALUE_HEADS:
                    score(g + 1, a, b)

    @pl.when(jnp.logical_not(with_far))
    def _():
        sum_buf[:, 0:1, :] = stats_ref[:, 8:9, :]
        factor_buf[:, 0:1, :] = jnp.ones((KEY_VALUE_HEADS, 1, lanes), jnp.float32)
        acc[...] = acc_near[...]

    for g in range(KEY_VALUE_HEADS):
        inverse = 1.0 / sum_buf[g, 0:1, :]
        factor = factor_buf[g, 0:1, :]
        for n in range(GROUP_SIZE):
            at = slice(n * rows, (n + 1) * rows)
            att = (acc[g, :, at] * inverse[:, at]).astype(jnp.bfloat16)
            att_t[g, :, at] = att
            do_n = do_all[g, :, at].astype(jnp.float32)
            dot_n = jnp.sum(do_n * att.astype(jnp.float32), axis=0, keepdims=True) * inverse[:, at]
            do_n = do_n * inverse[:, at]
            dot_buf[g, 0:1, at] = dot_n
            dot_buf[g, 1:2, at] = dot_n * factor[:, at]
            do_far[g, :, at] = do_n.astype(jnp.bfloat16)
            do_near[g, :, at] = (do_n * factor[:, at]).astype(jnp.bfloat16)

    def gradient_steps(g, c, kv_buf, at, p_buf, do_t, row):
        v_c = keys_of(kv_buf, at, rows, KEY_VALUE_HEADS + g)
        k_t = keys_of(kv_buf, at, rows, g).T

        def step(a, b):
            where = slice(g * lanes + a, g * lanes + b)
            d_p = jnp.dot(v_c, do_t[g, :, a:b], preferred_element_type=jnp.float32)
            p = p_buf[at, :, where].astype(jnp.float32)
            d_s = (p * (d_p - dot_buf[g, row:row + 1, a:b])).astype(jnp.bfloat16)
            ds_buf[c, :, where] = d_s
            dq_acc[g, :, a:b] += jnp.dot(k_t, d_s, preferred_element_type=jnp.float32)

        return step

    def gradients(c, kv_buf, at, p_buf, do_t, row):
        steps = [
            gradient_steps(g, c, kv_buf, at, p_buf, do_t, row) for g in range(KEY_VALUE_HEADS)
        ]
        for a, b in tiles:
            for step in steps:
                step(a, b)

    @pl.when(with_far)
    def _():
        gradients(0, kv_far, 0, p_far, do_far, 0)

    @pl.loop(jnp.maximum(low, 1), depth + 1)
    def _(c):
        gradients(c, kv_near, c - 1, p_near, do_near, 1)

    gb_ref[...] = jnp.zeros_like(gb_ref)
    ones = jnp.ones((8, rows), jnp.bfloat16)
    for g in range(KEY_VALUE_HEADS):
        for n in range(GROUP_SIZE):
            columns = slice(n * rows, (n + 1) * rows)
            d_q = (dq_acc[g, :, columns] * SCALE).astype(jnp.bfloat16)
            dq_t[g, :, columns] = d_q
            row, at = divmod(head_columns(g, n).start, KV_WIDTH)
            sums = lax.dot_general(ones, d_q, NT, preferred_element_type=jnp.float32)
            gb_ref[row:row + 1, at:at + HEAD_SIZE] = sums[0:1]


def rows_kernel(att_t, dq_t, att_ref, dq_ref):
    rows = att_ref.shape[0]
    for g in range(KEY_VALUE_HEADS):
        for n in range(GROUP_SIZE):
            at = slice(n * rows, (n + 1) * rows)
            att_ref[:, head_columns(g, n)] = att_t[g, :, at].T
            dq_ref[:, head_columns(g, n)] = dq_t[g, :, at].T


def row_results(att_t, dq_t):
    rows = att_t.shape[2] // GROUP_SIZE
    width = QUERY_HEADS * HEAD_SIZE
    vmem = pl.BlockSpec(memory_space=pltpu.VMEM)
    return pl.pallas_call(
        rows_kernel,
        out_shape=(jax.ShapeDtypeStruct((rows, width), jnp.bfloat16),) * 2,
        in_specs=[vmem] * 2,
        out_specs=(vmem,) * 2,
        compiler_params=pltpu.CompilerParams(vmem_limit_bytes=8 * 1024 * 1024),
        cost_estimate=pl.CostEstimate(
            flops=2 * rows * width, bytes_accessed=8 * rows * width, transcendentals=0
        ),
        name="row_results",
    )(att_t, dq_t)


def attention(rank, q_all, do_all, kv_near, p_near, stats, acc_near, far):
    lanes = q_all.shape[1]
    rows = lanes // GROUP_SIZE
    width = QUERY_HEADS * HEAD_SIZE
    packed = rows + DOC_ROWS
    depth, chunk = p_near.shape[:2]
    vmem = pl.BlockSpec(memory_space=pltpu.VMEM)
    smem = pl.BlockSpec(memory_space=pltpu.SMEM)
    heads = KEY_VALUE_HEADS
    return pl.pallas_call(
        kernel,
        out_shape=(
            jax.ShapeDtypeStruct((heads, HEAD_SIZE, lanes), jnp.bfloat16),
            jax.ShapeDtypeStruct((heads, HEAD_SIZE, lanes), jnp.bfloat16),
            jax.ShapeDtypeStruct((1, chunk, heads * lanes), jnp.bfloat16),
            jax.ShapeDtypeStruct((depth + 1, chunk, heads * lanes), jnp.bfloat16),
            jax.ShapeDtypeStruct((heads, HEAD_SIZE, lanes), jnp.bfloat16),
            jax.ShapeDtypeStruct((heads, HEAD_SIZE, lanes), jnp.bfloat16),
            jax.ShapeDtypeStruct((-(-width // KV_WIDTH), KV_WIDTH), jnp.float32),
            jax.ShapeDtypeStruct((1,), jnp.int32),
        ),
        in_specs=[smem] + [vmem] * (6 + len(far)),
        out_specs=(vmem,) * 7 + (smem,),
        scratch_shapes=[
            pltpu.VMEM((LEVEL, packed, KV_WIDTH), jnp.bfloat16),
            pltpu.VMEM((heads, chunk, lanes), jnp.float32),
            pltpu.VMEM((heads, 8, lanes), jnp.float32),
            pltpu.VMEM((heads, 8, lanes), jnp.float32),
            pltpu.VMEM((heads, 8, lanes), jnp.float32),
            pltpu.VMEM((heads, HEAD_SIZE, lanes), jnp.float32),
            pltpu.VMEM((heads, HEAD_SIZE, lanes), jnp.float32),
        ],
        compiler_params=pltpu.CompilerParams(vmem_limit_bytes=28 * 1024 * 1024),
        cost_estimate=pl.CostEstimate(
            flops=2 * 2 * width * HEAD_SIZE * (depth + 2) * chunk,
            bytes_accessed=8 * rows * width,
            transcendentals=0,
        ),
        name="attention",
    )(rank, q_all, do_all, kv_near, p_near, stats, acc_near, *far)


def level_kernel(
    level, p_at, rank_ref, span_ref, p_buf, ds_buf, q_all, do_t, keep_ref, send_ref
):
    chunk = p_buf.shape[1]
    rows = chunk // PAIR
    lanes = GROUP_SIZE * rows
    inner = rank_ref[0] % LEVEL
    my_core = inner % 2
    my_x = inner // 2
    active = level >= span_ref[0]

    @pl.when(active)
    def _():
        for g in range(KEY_VALUE_HEADS):
            where = slice(g * lanes, (g + 1) * lanes)
            d_key = jnp.dot(
                ds_buf[level, :, where], q_all[g], preferred_element_type=jnp.float32
            ) * SCALE
            d_value = lax.dot_general(
                p_buf[p_at, :, where], do_t[g], NT, preferred_element_type=jnp.float32
            )
            for value, column in ((d_key, g), (d_value, KEY_VALUE_HEADS + g)):
                columns = slice(column * HEAD_SIZE, (column + 1) * HEAD_SIZE)
                for x_at in range(2):
                    one = value[2 * x_at * rows:(2 * x_at + 1) * rows]
                    two = value[(2 * x_at + 1) * rows:(2 * x_at + 2) * rows]
                    place = (x_at + my_x) % 2
                    at = pl.ds(pl.multiple_of(place * rows, rows), rows)
                    keep_ref[at, columns] = jnp.where(my_core == 0, one, two)
                    send_ref[at, columns] = jnp.where(my_core == 0, two, one).astype(jnp.bfloat16)

    @pl.when(jnp.logical_not(active))
    def _():
        keep_ref[...] = jnp.zeros_like(keep_ref)
        send_ref[...] = jnp.zeros_like(send_ref)


def level_gradients(level, p_at, rank, span, p_all, ds_all, q_all, do_t):
    chunk, width = p_all.shape[1:]
    rows = chunk // PAIR
    vmem = pl.BlockSpec(memory_space=pltpu.VMEM)
    smem = pl.BlockSpec(memory_space=pltpu.SMEM)
    return pl.pallas_call(
        functools.partial(level_kernel, level, p_at),
        out_shape=(
            jax.ShapeDtypeStruct((2 * rows, KV_WIDTH), jnp.float32),
            jax.ShapeDtypeStruct((2 * rows, KV_WIDTH), jnp.bfloat16),
        ),
        in_specs=[smem, smem] + [vmem] * 4,
        out_specs=(vmem, vmem),
        compiler_params=pltpu.CompilerParams(vmem_limit_bytes=28 * 1024 * 1024),
        cost_estimate=pl.CostEstimate(
            flops=LEVEL * rows * width * HEAD_SIZE // 4,
            bytes_accessed=LEVEL * rows * width // 4,
            transcendentals=0,
        ),
        name="level_gradients",
    )(rank, span, p_all, ds_all, q_all, do_t)


def shifted(value, steps):
    count = lax.axis_size("ctx")
    first, last = max(0, -steps), min(count, count - steps)
    return lax.ppermute(value, "ctx", [(at, at + steps) for at in range(first, last)])


def rotated(value, steps):
    count = lax.axis_size("ctx")
    return lax.ppermute(value, "ctx", [(at, (at + steps) % count) for at in range(count)])


def swapped(value, bit, axis="ctx"):
    return lax.ppermute(value, axis, [(at, at ^ bit) for at in range(lax.axis_size(axis))])


def bias_rows(rows):
    high = lax.reduce_precision(rows, 8, 7)
    both = jnp.concatenate([high, rows - high]).astype(jnp.bfloat16)
    return jnp.pad(both, ((0, -both.shape[0] % 16), (0, 0)))


def local(query_in, key_in, value_input, output_gradient, doc_ids, query_bias):
    rows = query_in.shape[1]
    shards = lax.axis_size("ctx")
    depth = window_levels(shards)
    rank = lax.axis_index("ctx").astype(jnp.int32)
    own = pack(key_in[0], value_input[0], doc_ids)

    ups = [shifted(own, LEVEL * step) for step in range(1, depth + 1)]
    x_own = swapped(own, 2)
    q_all, do_all, own = prepare(query_in[0], query_bias[None], output_gradient[0], own)
    ups[0], x_own, q_all, do_all = lax.optimization_barrier((ups[0], x_own, q_all, do_all))
    near = [own, x_own]
    for up in ups[:-1]:
        near += [up, swapped(up, 2)]
    x_far = swapped(ups[-1], 2)
    far_up, near = lax.optimization_barrier((ups[-1], near))
    near = jnp.concatenate(near, axis=0)
    near_core = swapped(near, 1)
    core_far = swapped(far_up, 1)
    rank = rank.reshape(1)
    kv_near, p_near, stats, acc_near = near_attention(rank, q_all, near, near_core, depth)
    x_far, p_near = lax.optimization_barrier((x_far, p_near))
    far = [far_up, x_far, core_far, swapped(x_far, 1)]
    att_t, dq_t, p_far, ds_all, do_near, do_far, bias_part, span = attention(
        rank, q_all, do_all, kv_near, p_near, stats, acc_near, far
    )

    levels = shards // LEVEL
    carried = levels == 4 and depth == 2
    bit = 1
    while bit < lax.axis_size("dp"):
        bias_part = bias_part + swapped(bias_part, bit, "dp")
        bit *= 2
    bias_total = bias_part

    def joined(value):
        return jnp.concatenate([value, bias_rows(bias_total)], axis=0) if carried else value

    def bias_of(got):
        return got[rows:rows + half_rows].astype(jnp.float32) + got[
            rows + half_rows:rows + 2 * half_rows
        ].astype(jnp.float32)

    half_rows = bias_part.shape[0]
    sends = [None] * (depth + 1)
    keeps = [None] * (depth + 1)
    for step in range(depth, -1, -1):
        if step == depth:
            keep, send = level_gradients(0, 0, rank, span, p_far, ds_all, q_all, do_far)
        else:
            level = depth - step
            keep, send = level_gradients(
                level, level - 1, rank, span, p_near, ds_all, q_all, do_near
            )
        send, ds_all = lax.optimization_barrier((send, ds_all))
        if step == max(depth - 1, 0) and carried:
            got = swapped(jnp.concatenate([send, bias_rows(bias_total)], axis=0), 1)
            bias_total = bias_total + bias_of(got[rows:])
            got = got[:2 * rows]
        else:
            got = swapped(send, 1)
        keeps[step] = keep + got.astype(jnp.float32)
        sends[step] = send

    across = [None] * (depth + 1)
    for step in range(depth, -1, -1):
        away = keeps[step][rows:].astype(jnp.bfloat16)
        if step == depth:
            away, att_t = lax.optimization_barrier((away, att_t))
            away = joined(away)
        across[step] = swapped(away, 2)
    attended, grad_query = row_results(att_t, dq_t)
    down = [None] * (depth + 1)
    total = None
    for step in range(depth, -1, -1):
        if step == depth and carried:
            bias_total = bias_total + bias_of(across[step])
        total = keeps[step][:rows] + across[step][:rows].astype(jnp.float32)
        if step:
            sent = joined(total.astype(jnp.bfloat16))
            down[step] = (rotated if carried else shifted)(sent, -LEVEL * step)
            across[step - 1], _ = lax.optimization_barrier((across[step - 1], sent))
    if carried:
        bias_total = (
            bias_total + rotated(bias_total, LEVEL) + bias_of(down[1]) + bias_of(down[2])
        )
    else:
        bit = 1
        while bit < shards:
            bias_total = bias_total + swapped(bias_total, bit)
            bit *= 2
    bias_total = bias_total.reshape(-1)[:query_bias.shape[0]]
    down = [None if part is None else part[:rows] for part in down]
    for step in range(depth, 0, -1):
        total = total + down[step].astype(jnp.float32)
    total = total.astype(jnp.bfloat16)
    half = KEY_VALUE_HEADS * HEAD_SIZE
    return (
        attended[None],
        grad_query[None],
        total[:, :half][None],
        total[:, half:][None],
        bias_total,
    )


def solution(mesh):
    placed = (
        P("dp", "ctx", None),
        P("dp", "ctx", None),
        P("dp", "ctx", None),
        P("dp", "ctx", None),
        P("dp", "ctx"),
        P(),
    )
    return jax.shard_map(
        local,
        mesh=mesh,
        in_specs=placed,
        out_specs=(
            P("dp", "ctx", None),
            P("dp", "ctx", None),
            P("dp", "ctx", None),
            P("dp", "ctx", None),
            P(),
        ),
        check_vma=False,
    )
```

```python
import functools
import math

import jax
import jax.numpy as jnp
from jax import lax
from jax.experimental import pallas as pl
from jax.experimental.pallas import tpu as pltpu
from jax.sharding import PartitionSpec as P

QUERY_HEADS = 14
KEY_VALUE_HEADS = 2
HEAD_SIZE = 128
GROUP_SIZE = 7
BLK = 128
WB = 16
DOC_ROWS = 16
PAIR = 4
LEVEL = 4
LANE_TILE = 256
KV_WIDTH = 2 * KEY_VALUE_HEADS * HEAD_SIZE
SCALE = 1.0 / math.sqrt(HEAD_SIZE)
SCALE_LOG2 = SCALE * math.log2(math.e)
LOW = -1e30

NT = (((1,), (1,)), ((), ()))


def fold(value, op):
    keys, lanes = value.shape
    return op(value.reshape(keys // 8, 8, lanes), axis=0)


def window_levels(shards):
    levels = max(shards // LEVEL, 1)
    return min((WB - 2 + LEVEL) // LEVEL, max(3 * levels // 4 - 1, 0) if levels % 4 == 0 else levels - 1)


def pack_kernel(key_hbm, value_hbm, docs_hbm, own_ref, docs, sems):
    rows, half = key_hbm.shape
    copies = [
        pltpu.make_async_copy(docs_hbm, docs, sems.at[0]),
        pltpu.make_async_copy(key_hbm, own_ref.at[0:rows, 0:half], sems.at[1]),
        pltpu.make_async_copy(value_hbm, own_ref.at[0:rows, half:2 * half], sems.at[2]),
    ]
    for copy in copies:
        copy.start()
    copies[0].wait()
    count = jnp.sum((docs[...] == 0).astype(jnp.float32), axis=1, keepdims=True)
    own_ref[rows:rows + DOC_ROWS, :] = jnp.broadcast_to(count, (DOC_ROWS, 2 * half)).astype(
        jnp.bfloat16
    )
    copies[1].wait()
    copies[2].wait()


def pack(key_in, value_input, doc_ids):
    rows, half = key_in.shape
    return pl.pallas_call(
        pack_kernel,
        out_shape=jax.ShapeDtypeStruct((rows + DOC_ROWS, 2 * half), jnp.bfloat16),
        in_specs=[pl.BlockSpec(memory_space=pltpu.HBM)] * 3,
        out_specs=pl.BlockSpec(memory_space=pltpu.VMEM),
        scratch_shapes=[pltpu.VMEM((1, rows), jnp.int32), pltpu.SemaphoreType.DMA((3,))],
        compiler_params=pltpu.CompilerParams(vmem_limit_bytes=60 * 1024 * 1024),
        name="pack",
    )(key_in, value_input, doc_ids)


def head_columns(g, n):
    head = g * GROUP_SIZE + n
    return slice(head * HEAD_SIZE, (head + 1) * HEAD_SIZE)


def prepare_kernel(q_hbm, bias_ref, do_hbm, own_hbm, q_st, do_t, own_ref, q_buf, do_buf, sems):
    rows = q_buf.shape[0]
    first = pltpu.make_async_copy(q_hbm, q_buf, sems.at[0])
    second = pltpu.make_async_copy(do_hbm, do_buf, sems.at[1])
    third = pltpu.make_async_copy(own_hbm, own_ref, sems.at[2])
    first.start()
    second.start()
    third.start()
    first.wait()
    for g in range(KEY_VALUE_HEADS):
        for n in range(GROUP_SIZE):
            columns = head_columns(g, n)
            q_st[g, n * rows:(n + 1) * rows, :] = (
                q_buf[:, columns].astype(jnp.float32) + bias_ref[:, columns]
            ).astype(jnp.bfloat16)
    second.wait()
    for g in range(KEY_VALUE_HEADS):
        for n in range(GROUP_SIZE):
            do_t[g, :, n * rows:(n + 1) * rows] = do_buf[:, head_columns(g, n)].T
    third.wait()


def prepare(query_in, query_bias, output_gradient, own):
    rows, width = query_in.shape
    lanes = GROUP_SIZE * rows
    anywhere = pl.BlockSpec(memory_space=pltpu.HBM)
    vmem = pl.BlockSpec(memory_space=pltpu.VMEM)
    return pl.pallas_call(
        prepare_kernel,
        out_shape=(
            jax.ShapeDtypeStruct((KEY_VALUE_HEADS, lanes, HEAD_SIZE), jnp.bfloat16),
            jax.ShapeDtypeStruct((KEY_VALUE_HEADS, HEAD_SIZE, lanes), jnp.bfloat16),
            jax.ShapeDtypeStruct(own.shape, own.dtype),
        ),
        in_specs=[anywhere, vmem, anywhere, anywhere],
        out_specs=(vmem, vmem, vmem),
        scratch_shapes=[
            pltpu.VMEM((rows, width), jnp.bfloat16),
            pltpu.VMEM((rows, width), jnp.bfloat16),
            pltpu.SemaphoreType.DMA((3,)),
        ],
        compiler_params=pltpu.CompilerParams(vmem_limit_bytes=8 * 1024 * 1024),
        cost_estimate=pl.CostEstimate(
            flops=4 * rows * width, bytes_accessed=8 * rows * width, transcendentals=0
        ),
        name="prepare",
    )(query_in, query_bias, output_gradient, own)


def keys_of(kv_buf, c, rows, column):
    columns = slice(column * HEAD_SIZE, (column + 1) * HEAD_SIZE)
    return jnp.concatenate([kv_buf[PAIR * c + i, 0:rows, columns] for i in range(PAIR)], axis=0)


def spread(kv_buf, slot, pieces, inner):
    core = inner % 2
    x = inner // 2
    for at, piece in enumerate(pieces):
        place_x = 1 - x if at % 2 else x
        place_core = 1 - core if at // 2 else core
        kv_buf[slot * LEVEL + 2 * place_x + place_core] = piece[...]


def doc_count(kv_buf, rows):
    counts = kv_buf[:, rows:rows + DOC_ROWS, 0:128].astype(jnp.float32)
    return jnp.sum(counts) * (1.0 / (DOC_ROWS * 128))


def window_start(rank, rows, first, count):
    boundary = (count + 0.5).astype(jnp.int32) + jnp.maximum(first, 0) * rows
    low_block = jnp.maximum(rank - (WB - 1), 0)
    in_second = rank * rows >= boundary
    return boundary, jnp.where(in_second, jnp.maximum(low_block, boundary // rows), low_block)


def mask_bias(key_first, q_first, boundary, chunk, rows):
    key_pos = key_first + lax.broadcasted_iota(jnp.int32, (chunk, rows), 0)
    query_pos = q_first + lax.broadcasted_iota(jnp.int32, (chunk, rows), 1)
    allowed = (key_pos <= query_pos) & (query_pos // BLK - key_pos // BLK < WB)
    allowed = allowed & ((key_pos >= boundary) == (query_pos >= boundary))
    return jnp.where(allowed, 0.0, LOW)


def lane_tiles(lanes):
    return [(at, min(at + LANE_TILE, lanes)) for at in range(0, lanes, LANE_TILE)]


def near_kernel(
    rank_ref, q_all, near_ref, near_core_ref,
    kv_buf, p_buf, stats_ref, acc,
    s_buf,
):
    packed = kv_buf.shape[1]
    depth, chunk = p_buf.shape[:2]
    rows = chunk // PAIR
    lanes = q_all.shape[1]
    tiles = lane_tiles(lanes)
    rank = rank_ref[0]
    first = (rank // LEVEL - (depth - 1)) * LEVEL
    for level in range(depth):
        pieces = [
            ref.at[at * packed:(at + 1) * packed]
            for ref in (near_ref, near_core_ref) for at in (2 * level, 2 * level + 1)
        ]
        spread(kv_buf, depth - 1 - level, pieces, rank % LEVEL)
    boundary, low_block = window_start(rank, rows, first, doc_count(kv_buf, rows))
    low = jnp.maximum(low_block - first, 0) // PAIR

    for g in range(KEY_VALUE_HEADS):
        stats_ref[g, 0:8, :] = jnp.full((8, lanes), LOW, jnp.float32)
        stats_ref[g, 8:16, :] = jnp.zeros((8, lanes), jnp.float32)
    acc[...] = jnp.zeros_like(acc)

    def score_steps(c, g):
        bias = mask_bias((first + PAIR * c) * rows, rank * rows, boundary, chunk, rows)
        k_c = keys_of(kv_buf, c, rows, g)

        def step(a, b):
            s = lax.dot_general(k_c, q_all[g, a:b, :], NT, preferred_element_type=jnp.float32)
            s = s + jnp.concatenate([bias] * ((b - a) // rows), axis=1)
            s_buf[c, :, a:b] = s
            stats_ref[g, 0:8, a:b] = jnp.maximum(stats_ref[g, 0:8, a:b], fold(s, jnp.max))

        return step

    def weight_steps(c, g, row_max):
        v_t = keys_of(kv_buf, c, rows, KEY_VALUE_HEADS + g).T

        def step(a, b):
            p = jnp.exp2(s_buf[c, :, a:b] * SCALE_LOG2 - row_max[:, a:b])
            stats_ref[g, 8:16, a:b] += fold(p, jnp.sum)
            p_bf = p.astype(jnp.bfloat16)
            p_buf[c, :, g * lanes + a:g * lanes + b] = p_bf
            acc[g, :, a:b] += jnp.dot(v_t, p_bf, preferred_element_type=jnp.float32)

        return step

    def over_chunks(*makers):
        @pl.loop(low, depth)
        def _(c):
            steps = [make(c) for make in makers]
            for a, b in tiles:
                for step in steps:
                    step(a, b)

    over_chunks(lambda c: score_steps(c, 0))
    for g in range(KEY_VALUE_HEADS):
        row_max = jnp.max(stats_ref[g, 0:8, :], axis=0, keepdims=True) * SCALE_LOG2
        makers = [lambda c: weight_steps(c, g, row_max)]
        if g + 1 < KEY_VALUE_HEADS:
            makers.append(lambda c: score_steps(c, g + 1))
        over_chunks(*makers)
        stats_ref[g, 0:1, :] = row_max
        stats_ref[g, 8:9, :] = jnp.sum(stats_ref[g, 8:16, :], axis=0, keepdims=True)


def near_attention(rank, q_all, near, near_core, depth):
    lanes = q_all.shape[1]
    rows = lanes // GROUP_SIZE
    packed = rows + DOC_ROWS
    chunk = PAIR * rows
    vmem = pl.BlockSpec(memory_space=pltpu.VMEM)
    smem = pl.BlockSpec(memory_space=pltpu.SMEM)
    heads = KEY_VALUE_HEADS
    return pl.pallas_call(
        near_kernel,
        out_shape=(
            jax.ShapeDtypeStruct((depth * LEVEL, packed, KV_WIDTH), jnp.bfloat16),
            jax.ShapeDtypeStruct((depth, chunk, heads * lanes), jnp.bfloat16),
            jax.ShapeDtypeStruct((heads, 16, lanes), jnp.float32),
            jax.ShapeDtypeStruct((heads, HEAD_SIZE, lanes), jnp.float32),
        ),
        in_specs=[smem] + [vmem] * 3,
        out_specs=(vmem,) * 4,
        scratch_shapes=[pltpu.VMEM((depth, chunk, lanes), jnp.float32)],
        compiler_params=pltpu.CompilerParams(vmem_limit_bytes=28 * 1024 * 1024),
        cost_estimate=pl.CostEstimate(
            flops=2 * 2 * heads * lanes * HEAD_SIZE * depth * chunk,
            bytes_accessed=4 * heads * lanes * HEAD_SIZE,
            transcendentals=heads * lanes * depth * chunk,
        ),
        name="near_attention",
    )(rank, q_all, near, near_core)


def kernel(
    rank_ref, q_all, do_all, kv_near, p_near, stats_ref, acc_near, far_0, far_1, far_2, far_3,
    att_t, dq_t, p_far, ds_buf, do_near, do_far, gb_ref, span_ref,
    kv_far, s_buf, sum_buf, factor_buf, dot_buf, acc, dq_acc,
):
    depth, chunk = p_near.shape[:2]
    rows = chunk // PAIR
    lanes = GROUP_SIZE * rows
    tiles = lane_tiles(lanes)
    rank = rank_ref[0]
    first = (rank // LEVEL - depth) * LEVEL
    spread(kv_far, 0, (far_0, far_1, far_2, far_3), rank % LEVEL)
    count = doc_count(kv_far, rows) + doc_count(kv_near, rows)
    boundary, low_block = window_start(rank, rows, first, count)
    low = jnp.maximum(low_block - first, 0) // PAIR
    span_ref[0] = low
    with_far = low == 0

    dq_acc[...] = jnp.zeros_like(dq_acc)

    @pl.when(with_far)
    def _():
        bias = mask_bias(first * rows, rank * rows, boundary, chunk, rows)

        def score(g, a, b):
            k_c = keys_of(kv_far, 0, rows, g)
            s = lax.dot_general(k_c, q_all[g, a:b, :], NT, preferred_element_type=jnp.float32)
            s = s + jnp.concatenate([bias] * ((b - a) // rows), axis=1)
            s_buf[g, :, a:b] = s
            far_max = jnp.max(fold(s, jnp.max), axis=0, keepdims=True) * SCALE_LOG2
            factor_buf[g, 0:1, a:b] = jnp.maximum(stats_ref[g, 0:1, a:b], far_max)

        def weight(g, a, b):
            v_t = keys_of(kv_far, 0, rows, KEY_VALUE_HEADS + g).T
            top = factor_buf[g, 0:1, a:b]
            factor = jnp.exp2(stats_ref[g, 0:1, a:b] - top)
            p = jnp.exp2(s_buf[g, :, a:b] * SCALE_LOG2 - top)
            p_bf = p.astype(jnp.bfloat16)
            p_far[0, :, g * lanes + a:g * lanes + b] = p_bf
            total = jnp.sum(fold(p, jnp.sum), axis=0, keepdims=True)
            sum_buf[g, 0:1, a:b] = stats_ref[g, 8:9, a:b] * factor + total
            factor_buf[g, 0:1, a:b] = factor
            acc[g, :, a:b] = acc_near[g, :, a:b] * factor + jnp.dot(
                v_t, p_bf, preferred_element_type=jnp.float32
            )

        for a, b in tiles:
            score(0, a, b)
        for g in range(KEY_VALUE_HEADS):
            for a, b in tiles:
                weight(g, a, b)
                if g + 1 < KEY_VALUE_HEADS:
                    score(g + 1, a, b)

    @pl.when(jnp.logical_not(with_far))
    def _():
        sum_buf[:, 0:1, :] = stats_ref[:, 8:9, :]
        factor_buf[:, 0:1, :] = jnp.ones((KEY_VALUE_HEADS, 1, lanes), jnp.float32)
        acc[...] = acc_near[...]

    for g in range(KEY_VALUE_HEADS):
        inverse = 1.0 / sum_buf[g, 0:1, :]
        factor = factor_buf[g, 0:1, :]
        for n in range(GROUP_SIZE):
            at = slice(n * rows, (n + 1) * rows)
            att = (acc[g, :, at] * inverse[:, at]).astype(jnp.bfloat16)
            att_t[g, :, at] = att
            do_n = do_all[g, :, at].astype(jnp.float32)
            dot_n = jnp.sum(do_n * att.astype(jnp.float32), axis=0, keepdims=True) * inverse[:, at]
            do_n = do_n * inverse[:, at]
            dot_buf[g, 0:1, at] = dot_n
            dot_buf[g, 1:2, at] = dot_n * factor[:, at]
            do_far[g, :, at] = do_n.astype(jnp.bfloat16)
            do_near[g, :, at] = (do_n * factor[:, at]).astype(jnp.bfloat16)

    def gradient_steps(g, c, kv_buf, at, p_buf, do_t, row):
        v_c = keys_of(kv_buf, at, rows, KEY_VALUE_HEADS + g)
        k_t = keys_of(kv_buf, at, rows, g).T

        def step(a, b):
            where = slice(g * lanes + a, g * lanes + b)
            d_p = jnp.dot(v_c, do_t[g, :, a:b], preferred_element_type=jnp.float32)
            d_s = p_buf[at, :, where] * (d_p - dot_buf[g, row:row + 1, a:b]).astype(jnp.bfloat16)
            ds_buf[c, :, where] = d_s
            dq_acc[g, :, a:b] += jnp.dot(k_t, d_s, preferred_element_type=jnp.float32)

        return step

    def gradients(c, kv_buf, at, p_buf, do_t, row):
        steps = [
            gradient_steps(g, c, kv_buf, at, p_buf, do_t, row) for g in range(KEY_VALUE_HEADS)
        ]
        for a, b in tiles:
            for step in steps:
                step(a, b)

    @pl.when(with_far)
    def _():
        gradients(0, kv_far, 0, p_far, do_far, 0)

    @pl.loop(jnp.maximum(low, 1), depth + 1)
    def _(c):
        gradients(c, kv_near, c - 1, p_near, do_near, 1)

    gb_ref[...] = jnp.zeros_like(gb_ref)
    ones = jnp.ones((8, rows), jnp.bfloat16)
    for g in range(KEY_VALUE_HEADS):
        for n in range(GROUP_SIZE):
            columns = slice(n * rows, (n + 1) * rows)
            d_q = (dq_acc[g, :, columns] * SCALE).astype(jnp.bfloat16)
            dq_t[g, :, columns] = d_q
            row, at = divmod(head_columns(g, n).start, KV_WIDTH)
            sums = lax.dot_general(ones, d_q, NT, preferred_element_type=jnp.float32)
            gb_ref[row:row + 1, at:at + HEAD_SIZE] = sums[0:1]


def rows_kernel(att_t, dq_t, att_ref, dq_ref):
    rows = att_ref.shape[0]
    for g in range(KEY_VALUE_HEADS):
        for n in range(GROUP_SIZE):
            at = slice(n * rows, (n + 1) * rows)
            att_ref[:, head_columns(g, n)] = att_t[g, :, at].T
            dq_ref[:, head_columns(g, n)] = dq_t[g, :, at].T


def row_results(att_t, dq_t):
    rows = att_t.shape[2] // GROUP_SIZE
    width = QUERY_HEADS * HEAD_SIZE
    vmem = pl.BlockSpec(memory_space=pltpu.VMEM)
    return pl.pallas_call(
        rows_kernel,
        out_shape=(jax.ShapeDtypeStruct((rows, width), jnp.bfloat16),) * 2,
        in_specs=[vmem] * 2,
        out_specs=(vmem,) * 2,
        compiler_params=pltpu.CompilerParams(vmem_limit_bytes=8 * 1024 * 1024),
        cost_estimate=pl.CostEstimate(
            flops=2 * rows * width, bytes_accessed=8 * rows * width, transcendentals=0
        ),
        name="row_results",
    )(att_t, dq_t)


def attention(rank, q_all, do_all, kv_near, p_near, stats, acc_near, far):
    lanes = q_all.shape[1]
    rows = lanes // GROUP_SIZE
    width = QUERY_HEADS * HEAD_SIZE
    packed = rows + DOC_ROWS
    depth, chunk = p_near.shape[:2]
    vmem = pl.BlockSpec(memory_space=pltpu.VMEM)
    smem = pl.BlockSpec(memory_space=pltpu.SMEM)
    heads = KEY_VALUE_HEADS
    return pl.pallas_call(
        kernel,
        out_shape=(
            jax.ShapeDtypeStruct((heads, HEAD_SIZE, lanes), jnp.bfloat16),
            jax.ShapeDtypeStruct((heads, HEAD_SIZE, lanes), jnp.bfloat16),
            jax.ShapeDtypeStruct((1, chunk, heads * lanes), jnp.bfloat16),
            jax.ShapeDtypeStruct((depth + 1, chunk, heads * lanes), jnp.bfloat16),
            jax.ShapeDtypeStruct((heads, HEAD_SIZE, lanes), jnp.bfloat16),
            jax.ShapeDtypeStruct((heads, HEAD_SIZE, lanes), jnp.bfloat16),
            jax.ShapeDtypeStruct((-(-width // KV_WIDTH), KV_WIDTH), jnp.float32),
            jax.ShapeDtypeStruct((1,), jnp.int32),
        ),
        in_specs=[smem] + [vmem] * (6 + len(far)),
        out_specs=(vmem,) * 7 + (smem,),
        scratch_shapes=[
            pltpu.VMEM((LEVEL, packed, KV_WIDTH), jnp.bfloat16),
            pltpu.VMEM((heads, chunk, lanes), jnp.float32),
            pltpu.VMEM((heads, 8, lanes), jnp.float32),
            pltpu.VMEM((heads, 8, lanes), jnp.float32),
            pltpu.VMEM((heads, 8, lanes), jnp.float32),
            pltpu.VMEM((heads, HEAD_SIZE, lanes), jnp.float32),
            pltpu.VMEM((heads, HEAD_SIZE, lanes), jnp.float32),
        ],
        compiler_params=pltpu.CompilerParams(vmem_limit_bytes=28 * 1024 * 1024),
        cost_estimate=pl.CostEstimate(
            flops=2 * 2 * width * HEAD_SIZE * (depth + 2) * chunk,
            bytes_accessed=8 * rows * width,
            transcendentals=0,
        ),
        name="attention",
    )(rank, q_all, do_all, kv_near, p_near, stats, acc_near, *far)


def level_kernel(
    level, p_at, rank_ref, span_ref, p_buf, ds_buf, q_all, do_t, keep_ref, send_ref
):
    chunk = p_buf.shape[1]
    rows = chunk // PAIR
    lanes = GROUP_SIZE * rows
    inner = rank_ref[0] % LEVEL
    my_core = inner % 2
    my_x = inner // 2
    active = level >= span_ref[0]

    @pl.when(active)
    def _():
        for g in range(KEY_VALUE_HEADS):
            where = slice(g * lanes, (g + 1) * lanes)
            d_key = jnp.dot(
                ds_buf[level, :, where], q_all[g], preferred_element_type=jnp.float32
            ) * SCALE
            d_value = lax.dot_general(
                p_buf[p_at, :, where], do_t[g], NT, preferred_element_type=jnp.float32
            )
            for value, column in ((d_key, g), (d_value, KEY_VALUE_HEADS + g)):
                columns = slice(column * HEAD_SIZE, (column + 1) * HEAD_SIZE)
                for x_at in range(2):
                    one = value[2 * x_at * rows:(2 * x_at + 1) * rows]
                    two = value[(2 * x_at + 1) * rows:(2 * x_at + 2) * rows]
                    place = (x_at + my_x) % 2
                    at = pl.ds(pl.multiple_of(place * rows, rows), rows)
                    keep_ref[at, columns] = jnp.where(my_core == 0, one, two)
                    send_ref[at, columns] = jnp.where(my_core == 0, two, one).astype(jnp.bfloat16)

    @pl.when(jnp.logical_not(active))
    def _():
        keep_ref[...] = jnp.zeros_like(keep_ref)
        send_ref[...] = jnp.zeros_like(send_ref)


def level_gradients(level, p_at, rank, span, p_all, ds_all, q_all, do_t):
    chunk, width = p_all.shape[1:]
    rows = chunk // PAIR
    vmem = pl.BlockSpec(memory_space=pltpu.VMEM)
    smem = pl.BlockSpec(memory_space=pltpu.SMEM)
    return pl.pallas_call(
        functools.partial(level_kernel, level, p_at),
        out_shape=(
            jax.ShapeDtypeStruct((2 * rows, KV_WIDTH), jnp.float32),
            jax.ShapeDtypeStruct((2 * rows, KV_WIDTH), jnp.bfloat16),
        ),
        in_specs=[smem, smem] + [vmem] * 4,
        out_specs=(vmem, vmem),
        compiler_params=pltpu.CompilerParams(vmem_limit_bytes=28 * 1024 * 1024),
        cost_estimate=pl.CostEstimate(
            flops=LEVEL * rows * width * HEAD_SIZE // 4,
            bytes_accessed=LEVEL * rows * width // 4,
            transcendentals=0,
        ),
        name="level_gradients",
    )(rank, span, p_all, ds_all, q_all, do_t)


def shifted(value, steps):
    count = lax.axis_size("ctx")
    first, last = max(0, -steps), min(count, count - steps)
    return lax.ppermute(value, "ctx", [(at, at + steps) for at in range(first, last)])


def rotated(value, steps):
    count = lax.axis_size("ctx")
    return lax.ppermute(value, "ctx", [(at, (at + steps) % count) for at in range(count)])


def swapped(value, bit, axis="ctx"):
    return lax.ppermute(value, axis, [(at, at ^ bit) for at in range(lax.axis_size(axis))])


def bias_rows(rows):
    high = lax.reduce_precision(rows, 8, 7)
    both = jnp.concatenate([high, rows - high]).astype(jnp.bfloat16)
    return jnp.pad(both, ((0, -both.shape[0] % 16), (0, 0)))


def local(query_in, key_in, value_input, output_gradient, doc_ids, query_bias):
    rows = query_in.shape[1]
    shards = lax.axis_size("ctx")
    depth = window_levels(shards)
    rank = lax.axis_index("ctx").astype(jnp.int32)
    own = pack(key_in[0], value_input[0], doc_ids)

    ups = [shifted(own, LEVEL * step) for step in range(1, depth + 1)]
    x_own = swapped(own, 2)
    q_all, do_all, own = prepare(query_in[0], query_bias[None], output_gradient[0], own)
    ups[0], x_own, q_all, do_all = lax.optimization_barrier((ups[0], x_own, q_all, do_all))
    near = [own, x_own]
    for up in ups[:-1]:
        near += [up, swapped(up, 2)]
    x_far = swapped(ups[-1], 2)
    far_up, near = lax.optimization_barrier((ups[-1], near))
    near = jnp.concatenate(near, axis=0)
    near_core = swapped(near, 1)
    core_far = swapped(far_up, 1)
    rank = rank.reshape(1)
    kv_near, p_near, stats, acc_near = near_attention(rank, q_all, near, near_core, depth)
    x_far, p_near = lax.optimization_barrier((x_far, p_near))
    far = [far_up, x_far, core_far, swapped(x_far, 1)]
    att_t, dq_t, p_far, ds_all, do_near, do_far, bias_part, span = attention(
        rank, q_all, do_all, kv_near, p_near, stats, acc_near, far
    )

    levels = shards // LEVEL
    carried = levels == 4 and depth == 2
    bit = 1
    while bit < lax.axis_size("dp"):
        bias_part = bias_part + swapped(bias_part, bit, "dp")
        bit *= 2
    bias_total = bias_part

    def joined(value):
        return jnp.concatenate([value, bias_rows(bias_total)], axis=0) if carried else value

    def bias_of(got):
        return got[rows:rows + half_rows].astype(jnp.float32) + got[
            rows + half_rows:rows + 2 * half_rows
        ].astype(jnp.float32)

    half_rows = bias_part.shape[0]
    sends = [None] * (depth + 1)
    keeps = [None] * (depth + 1)
    for step in range(depth, -1, -1):
        if step == depth:
            keep, send = level_gradients(0, 0, rank, span, p_far, ds_all, q_all, do_far)
        else:
            level = depth - step
            keep, send = level_gradients(
                level, level - 1, rank, span, p_near, ds_all, q_all, do_near
            )
        send, ds_all = lax.optimization_barrier((send, ds_all))
        if step == max(depth - 1, 0) and carried:
            got = swapped(jnp.concatenate([send, bias_rows(bias_total)], axis=0), 1)
            bias_total = bias_total + bias_of(got[rows:])
            got = got[:2 * rows]
        else:
            got = swapped(send, 1)
        keeps[step] = keep + got.astype(jnp.float32)
        sends[step] = send

    across = [None] * (depth + 1)
    for step in range(depth, -1, -1):
        away = keeps[step][rows:].astype(jnp.bfloat16)
        if step == depth:
            away, att_t = lax.optimization_barrier((away, att_t))
            away = joined(away)
        across[step] = swapped(away, 2)
    attended, grad_query = row_results(att_t, dq_t)
    down = [None] * (depth + 1)
    total = None
    for step in range(depth, -1, -1):
        if step == depth and carried:
            bias_total = bias_total + bias_of(across[step])
        total = keeps[step][:rows] + across[step][:rows].astype(jnp.float32)
        if step:
            sent = joined(total.astype(jnp.bfloat16))
            down[step] = (rotated if carried else shifted)(sent, -LEVEL * step)
            across[step - 1], _ = lax.optimization_barrier((across[step - 1], sent))
    if carried:
        bias_total = (
            bias_total + rotated(bias_total, LEVEL) + bias_of(down[1]) + bias_of(down[2])
        )
    else:
        bit = 1
        while bit < shards:
            bias_total = bias_total + swapped(bias_total, bit)
            bit *= 2
    bias_total = bias_total.reshape(-1)[:query_bias.shape[0]]
    down = [None if part is None else part[:rows] for part in down]
    for step in range(depth, 0, -1):
        total = total + down[step].astype(jnp.float32)
    total = total.astype(jnp.bfloat16)
    half = KEY_VALUE_HEADS * HEAD_SIZE
    return (
        attended[None],
        grad_query[None],
        total[:, :half][None],
        total[:, half:][None],
        bias_total,
    )


def solution(mesh):
    placed = (
        P("dp", "ctx", None),
        P("dp", "ctx", None),
        P("dp", "ctx", None),
        P("dp", "ctx", None),
        P("dp", "ctx"),
        P(),
    )
    return jax.shard_map(
        local,
        mesh=mesh,
        in_specs=placed,
        out_specs=(
            P("dp", "ctx", None),
            P("dp", "ctx", None),
            P("dp", "ctx", None),
            P("dp", "ctx", None),
            P(),
        ),
        check_vma=False,
    )
```

```python
import functools
import math

import jax
import jax.numpy as jnp
from jax import lax
from jax.experimental import pallas as pl
from jax.experimental.pallas import tpu as pltpu
from jax.sharding import PartitionSpec as P

QUERY_HEADS = 14
KEY_VALUE_HEADS = 2
HEAD_SIZE = 128
GROUP_SIZE = 7
BLK = 128
WB = 16
DOC_ROWS = 16
PAIR = 4
LEVEL = 4
LANE_TILE = 512
KV_WIDTH = 2 * KEY_VALUE_HEADS * HEAD_SIZE
SCALE = 1.0 / math.sqrt(HEAD_SIZE)
SCALE_LOG2 = SCALE * math.log2(math.e)
LOW = -1e30

NT = (((1,), (1,)), ((), ()))


def fold(value, op):
    keys, lanes = value.shape
    return op(value.reshape(keys // 8, 8, lanes), axis=0)


def window_levels(shards):
    levels = max(shards // LEVEL, 1)
    return min((WB - 2 + LEVEL) // LEVEL, max(3 * levels // 4 - 1, 0) if levels % 4 == 0 else levels - 1)


def pack_kernel(key_hbm, value_hbm, docs_hbm, own_ref, docs, sems):
    rows, half = key_hbm.shape
    copies = [
        pltpu.make_async_copy(docs_hbm, docs, sems.at[0]),
        pltpu.make_async_copy(key_hbm, own_ref.at[0:rows, 0:half], sems.at[1]),
        pltpu.make_async_copy(value_hbm, own_ref.at[0:rows, half:2 * half], sems.at[2]),
    ]
    for copy in copies:
        copy.start()
    copies[0].wait()
    count = jnp.sum((docs[...] == 0).astype(jnp.float32), axis=1, keepdims=True)
    own_ref[rows:rows + DOC_ROWS, :] = jnp.broadcast_to(count, (DOC_ROWS, 2 * half)).astype(
        jnp.bfloat16
    )
    copies[1].wait()
    copies[2].wait()


def pack(key_in, value_input, doc_ids):
    rows, half = key_in.shape
    return pl.pallas_call(
        pack_kernel,
        out_shape=jax.ShapeDtypeStruct((rows + DOC_ROWS, 2 * half), jnp.bfloat16),
        in_specs=[pl.BlockSpec(memory_space=pltpu.HBM)] * 3,
        out_specs=pl.BlockSpec(memory_space=pltpu.VMEM),
        scratch_shapes=[pltpu.VMEM((1, rows), jnp.int32), pltpu.SemaphoreType.DMA((3,))],
        compiler_params=pltpu.CompilerParams(vmem_limit_bytes=60 * 1024 * 1024),
        name="pack",
    )(key_in, value_input, doc_ids)


def head_columns(g, n):
    head = g * GROUP_SIZE + n
    return slice(head * HEAD_SIZE, (head + 1) * HEAD_SIZE)


def prepare_kernel(q_hbm, bias_ref, do_hbm, own_hbm, q_st, do_t, own_ref, q_buf, do_buf, sems):
    rows = q_buf.shape[0]
    first = pltpu.make_async_copy(q_hbm, q_buf, sems.at[0])
    second = pltpu.make_async_copy(do_hbm, do_buf, sems.at[1])
    third = pltpu.make_async_copy(own_hbm, own_ref, sems.at[2])
    first.start()
    second.start()
    third.start()
    first.wait()
    for g in range(KEY_VALUE_HEADS):
        for n in range(GROUP_SIZE):
            columns = head_columns(g, n)
            q_st[g, n * rows:(n + 1) * rows, :] = (
                q_buf[:, columns].astype(jnp.float32) + bias_ref[:, columns]
            ).astype(jnp.bfloat16)
    second.wait()
    for g in range(KEY_VALUE_HEADS):
        for n in range(GROUP_SIZE):
            do_t[g, :, n * rows:(n + 1) * rows] = do_buf[:, head_columns(g, n)].T
    third.wait()


def prepare(query_in, query_bias, output_gradient, own):
    rows, width = query_in.shape
    lanes = GROUP_SIZE * rows
    anywhere = pl.BlockSpec(memory_space=pltpu.HBM)
    vmem = pl.BlockSpec(memory_space=pltpu.VMEM)
    return pl.pallas_call(
        prepare_kernel,
        out_shape=(
            jax.ShapeDtypeStruct((KEY_VALUE_HEADS, lanes, HEAD_SIZE), jnp.bfloat16),
            jax.ShapeDtypeStruct((KEY_VALUE_HEADS, HEAD_SIZE, lanes), jnp.bfloat16),
            jax.ShapeDtypeStruct(own.shape, own.dtype),
        ),
        in_specs=[anywhere, vmem, anywhere, anywhere],
        out_specs=(vmem, vmem, vmem),
        scratch_shapes=[
            pltpu.VMEM((rows, width), jnp.bfloat16),
            pltpu.VMEM((rows, width), jnp.bfloat16),
            pltpu.SemaphoreType.DMA((3,)),
        ],
        compiler_params=pltpu.CompilerParams(vmem_limit_bytes=8 * 1024 * 1024),
        cost_estimate=pl.CostEstimate(
            flops=4 * rows * width, bytes_accessed=8 * rows * width, transcendentals=0
        ),
        name="prepare",
    )(query_in, query_bias, output_gradient, own)


def keys_of(kv_buf, c, rows, column):
    columns = slice(column * HEAD_SIZE, (column + 1) * HEAD_SIZE)
    return jnp.concatenate([kv_buf[PAIR * c + i, 0:rows, columns] for i in range(PAIR)], axis=0)


def spread(kv_buf, slot, pieces, inner):
    core = inner % 2
    x = inner // 2
    for at, piece in enumerate(pieces):
        place_x = 1 - x if at % 2 else x
        place_core = 1 - core if at // 2 else core
        kv_buf[slot * LEVEL + 2 * place_x + place_core] = piece[...]


def doc_count(kv_buf, rows):
    counts = kv_buf[:, rows:rows + DOC_ROWS, 0:128].astype(jnp.float32)
    return jnp.sum(counts) * (1.0 / (DOC_ROWS * 128))


def window_start(rank, rows, first, count):
    boundary = (count + 0.5).astype(jnp.int32) + jnp.maximum(first, 0) * rows
    low_block = jnp.maximum(rank - (WB - 1), 0)
    in_second = rank * rows >= boundary
    return boundary, jnp.where(in_second, jnp.maximum(low_block, boundary // rows), low_block)


def mask_bias(key_first, q_first, boundary, chunk, rows):
    key_pos = key_first + lax.broadcasted_iota(jnp.int32, (chunk, rows), 0)
    query_pos = q_first + lax.broadcasted_iota(jnp.int32, (chunk, rows), 1)
    allowed = (key_pos <= query_pos) & (query_pos // BLK - key_pos // BLK < WB)
    allowed = allowed & ((key_pos >= boundary) == (query_pos >= boundary))
    return jnp.where(allowed, 0.0, LOW)


def lane_tiles(lanes):
    return [(at, min(at + LANE_TILE, lanes)) for at in range(0, lanes, LANE_TILE)]


def near_kernel(
    rank_ref, q_all, near_ref, near_core_ref,
    kv_buf, p_buf, stats_ref, acc,
    s_buf,
):
    packed = kv_buf.shape[1]
    depth, chunk = p_buf.shape[:2]
    rows = chunk // PAIR
    lanes = q_all.shape[1]
    tiles = lane_tiles(lanes)
    rank = rank_ref[0]
    first = (rank // LEVEL - (depth - 1)) * LEVEL
    for level in range(depth):
        pieces = [
            ref.at[at * packed:(at + 1) * packed]
            for ref in (near_ref, near_core_ref) for at in (2 * level, 2 * level + 1)
        ]
        spread(kv_buf, depth - 1 - level, pieces, rank % LEVEL)
    boundary, low_block = window_start(rank, rows, first, doc_count(kv_buf, rows))
    low = jnp.maximum(low_block - first, 0) // PAIR

    for g in range(KEY_VALUE_HEADS):
        stats_ref[g, 0:8, :] = jnp.full((8, lanes), LOW, jnp.float32)
        stats_ref[g, 8:16, :] = jnp.zeros((8, lanes), jnp.float32)
    acc[...] = jnp.zeros_like(acc)

    def score_steps(c, g):
        bias = mask_bias((first + PAIR * c) * rows, rank * rows, boundary, chunk, rows)
        k_c = keys_of(kv_buf, c, rows, g)

        def step(a, b):
            s = lax.dot_general(k_c, q_all[g, a:b, :], NT, preferred_element_type=jnp.float32)
            s = s + jnp.concatenate([bias] * ((b - a) // rows), axis=1)
            s_buf[c, :, a:b] = s
            stats_ref[g, 0:8, a:b] = jnp.maximum(stats_ref[g, 0:8, a:b], fold(s, jnp.max))

        return step

    def weight_steps(c, g, row_max):
        v_t = keys_of(kv_buf, c, rows, KEY_VALUE_HEADS + g).T

        def step(a, b):
            p = jnp.exp2(s_buf[c, :, a:b] * SCALE_LOG2 - row_max[:, a:b])
            stats_ref[g, 8:16, a:b] += fold(p, jnp.sum)
            p_bf = p.astype(jnp.bfloat16)
            p_buf[c, :, g * lanes + a:g * lanes + b] = p_bf
            acc[g, :, a:b] += jnp.dot(v_t, p_bf, preferred_element_type=jnp.float32)

        return step

    def over_chunks(*makers):
        @pl.loop(low, depth)
        def _(c):
            steps = [make(c) for make in makers]
            for a, b in tiles:
                for step in steps:
                    step(a, b)

    over_chunks(lambda c: score_steps(c, 0))
    for g in range(KEY_VALUE_HEADS):
        row_max = jnp.max(stats_ref[g, 0:8, :], axis=0, keepdims=True) * SCALE_LOG2
        makers = [lambda c: weight_steps(c, g, row_max)]
        if g + 1 < KEY_VALUE_HEADS:
            makers.append(lambda c: score_steps(c, g + 1))
        over_chunks(*makers)
        stats_ref[g, 0:1, :] = row_max
        stats_ref[g, 8:9, :] = jnp.sum(stats_ref[g, 8:16, :], axis=0, keepdims=True)


def near_attention(rank, q_all, near, near_core, depth):
    lanes = q_all.shape[1]
    rows = lanes // GROUP_SIZE
    packed = rows + DOC_ROWS
    chunk = PAIR * rows
    vmem = pl.BlockSpec(memory_space=pltpu.VMEM)
    smem = pl.BlockSpec(memory_space=pltpu.SMEM)
    heads = KEY_VALUE_HEADS
    return pl.pallas_call(
        near_kernel,
        out_shape=(
            jax.ShapeDtypeStruct((depth * LEVEL, packed, KV_WIDTH), jnp.bfloat16),
            jax.ShapeDtypeStruct((depth, chunk, heads * lanes), jnp.bfloat16),
            jax.ShapeDtypeStruct((heads, 16, lanes), jnp.float32),
            jax.ShapeDtypeStruct((heads, HEAD_SIZE, lanes), jnp.float32),
        ),
        in_specs=[smem] + [vmem] * 3,
        out_specs=(vmem,) * 4,
        scratch_shapes=[pltpu.VMEM((depth, chunk, lanes), jnp.float32)],
        compiler_params=pltpu.CompilerParams(vmem_limit_bytes=28 * 1024 * 1024),
        cost_estimate=pl.CostEstimate(
            flops=2 * 2 * heads * lanes * HEAD_SIZE * depth * chunk,
            bytes_accessed=4 * heads * lanes * HEAD_SIZE,
            transcendentals=heads * lanes * depth * chunk,
        ),
        name="near_attention",
    )(rank, q_all, near, near_core)


def kernel(
    rank_ref, q_all, do_all, kv_near, p_near, stats_ref, acc_near, far_0, far_1, far_2, far_3,
    att_t, dq_t, p_far, ds_buf, do_near, do_far, gb_ref, span_ref,
    kv_far, s_buf, sum_buf, factor_buf, dot_buf, acc, dq_acc,
):
    depth, chunk = p_near.shape[:2]
    rows = chunk // PAIR
    lanes = GROUP_SIZE * rows
    tiles = lane_tiles(lanes)
    rank = rank_ref[0]
    first = (rank // LEVEL - depth) * LEVEL
    spread(kv_far, 0, (far_0, far_1, far_2, far_3), rank % LEVEL)
    count = doc_count(kv_far, rows) + doc_count(kv_near, rows)
    boundary, low_block = window_start(rank, rows, first, count)
    low = jnp.maximum(low_block - first, 0) // PAIR
    span_ref[0] = low
    with_far = low == 0

    dq_acc[...] = jnp.zeros_like(dq_acc)

    @pl.when(with_far)
    def _():
        bias = mask_bias(first * rows, rank * rows, boundary, chunk, rows)

        def score(g, a, b):
            k_c = keys_of(kv_far, 0, rows, g)
            s = lax.dot_general(k_c, q_all[g, a:b, :], NT, preferred_element_type=jnp.float32)
            s = s + jnp.concatenate([bias] * ((b - a) // rows), axis=1)
            s_buf[g, :, a:b] = s
            far_max = jnp.max(fold(s, jnp.max), axis=0, keepdims=True) * SCALE_LOG2
            factor_buf[g, 0:1, a:b] = jnp.maximum(stats_ref[g, 0:1, a:b], far_max)

        def weight(g, a, b):
            v_t = keys_of(kv_far, 0, rows, KEY_VALUE_HEADS + g).T
            top = factor_buf[g, 0:1, a:b]
            factor = jnp.exp2(stats_ref[g, 0:1, a:b] - top)
            p = jnp.exp2(s_buf[g, :, a:b] * SCALE_LOG2 - top)
            p_bf = p.astype(jnp.bfloat16)
            p_far[0, :, g * lanes + a:g * lanes + b] = p_bf
            total = jnp.sum(fold(p, jnp.sum), axis=0, keepdims=True)
            sum_buf[g, 0:1, a:b] = stats_ref[g, 8:9, a:b] * factor + total
            factor_buf[g, 0:1, a:b] = factor
            acc[g, :, a:b] = acc_near[g, :, a:b] * factor + jnp.dot(
                v_t, p_bf, preferred_element_type=jnp.float32
            )

        for a, b in tiles:
            score(0, a, b)
        for g in range(KEY_VALUE_HEADS):
            for a, b in tiles:
                weight(g, a, b)
                if g + 1 < KEY_VALUE_HEADS:
                    score(g + 1, a, b)

    @pl.when(jnp.logical_not(with_far))
    def _():
        sum_buf[:, 0:1, :] = stats_ref[:, 8:9, :]
        factor_buf[:, 0:1, :] = jnp.ones((KEY_VALUE_HEADS, 1, lanes), jnp.float32)
        acc[...] = acc_near[...]

    for g in range(KEY_VALUE_HEADS):
        inverse = 1.0 / sum_buf[g, 0:1, :]
        factor = factor_buf[g, 0:1, :]
        for n in range(GROUP_SIZE):
            at = slice(n * rows, (n + 1) * rows)
            att = (acc[g, :, at] * inverse[:, at]).astype(jnp.bfloat16)
            att_t[g, :, at] = att
            do_n = do_all[g, :, at].astype(jnp.float32)
            dot_n = jnp.sum(do_n * att.astype(jnp.float32), axis=0, keepdims=True) * inverse[:, at]
            do_n = do_n * inverse[:, at]
            dot_buf[g, 0:1, at] = dot_n
            dot_buf[g, 1:2, at] = dot_n * factor[:, at]
            do_far[g, :, at] = do_n.astype(jnp.bfloat16)
            do_near[g, :, at] = (do_n * factor[:, at]).astype(jnp.bfloat16)

    def gradient_steps(g, c, kv_buf, at, p_buf, do_t, row):
        v_c = keys_of(kv_buf, at, rows, KEY_VALUE_HEADS + g)
        k_t = keys_of(kv_buf, at, rows, g).T

        def step(a, b):
            where = slice(g * lanes + a, g * lanes + b)
            d_p = jnp.dot(v_c, do_t[g, :, a:b], preferred_element_type=jnp.float32)
            p = p_buf[at, :, where].astype(jnp.float32)
            d_s = (p * (d_p - dot_buf[g, row:row + 1, a:b])).astype(jnp.bfloat16)
            ds_buf[c, :, where] = d_s
            dq_acc[g, :, a:b] += jnp.dot(k_t, d_s, preferred_element_type=jnp.float32)

        return step

    def gradients(c, kv_buf, at, p_buf, do_t, row):
        steps = [
            gradient_steps(g, c, kv_buf, at, p_buf, do_t, row) for g in range(KEY_VALUE_HEADS)
        ]
        for a, b in tiles:
            for step in steps:
                step(a, b)

    @pl.when(with_far)
    def _():
        gradients(0, kv_far, 0, p_far, do_far, 0)

    @pl.loop(jnp.maximum(low, 1), depth + 1)
    def _(c):
        gradients(c, kv_near, c - 1, p_near, do_near, 1)

    gb_ref[...] = jnp.zeros_like(gb_ref)
    ones = jnp.ones((8, rows), jnp.bfloat16)
    for g in range(KEY_VALUE_HEADS):
        for n in range(GROUP_SIZE):
            columns = slice(n * rows, (n + 1) * rows)
            d_q = (dq_acc[g, :, columns] * SCALE).astype(jnp.bfloat16)
            dq_t[g, :, columns] = d_q
            row, at = divmod(head_columns(g, n).start, KV_WIDTH)
            sums = lax.dot_general(ones, d_q, NT, preferred_element_type=jnp.float32)
            gb_ref[row:row + 1, at:at + HEAD_SIZE] = sums[0:1]


def rows_kernel(att_t, dq_t, att_ref, dq_ref):
    rows = att_ref.shape[0]
    for g in range(KEY_VALUE_HEADS):
        for n in range(GROUP_SIZE):
            at = slice(n * rows, (n + 1) * rows)
            att_ref[:, head_columns(g, n)] = att_t[g, :, at].T
            dq_ref[:, head_columns(g, n)] = dq_t[g, :, at].T


def row_results(att_t, dq_t):
    rows = att_t.shape[2] // GROUP_SIZE
    width = QUERY_HEADS * HEAD_SIZE
    vmem = pl.BlockSpec(memory_space=pltpu.VMEM)
    return pl.pallas_call(
        rows_kernel,
        out_shape=(jax.ShapeDtypeStruct((rows, width), jnp.bfloat16),) * 2,
        in_specs=[vmem] * 2,
        out_specs=(vmem,) * 2,
        compiler_params=pltpu.CompilerParams(vmem_limit_bytes=8 * 1024 * 1024),
        cost_estimate=pl.CostEstimate(
            flops=2 * rows * width, bytes_accessed=8 * rows * width, transcendentals=0
        ),
        name="row_results",
    )(att_t, dq_t)


def attention(rank, q_all, do_all, kv_near, p_near, stats, acc_near, far):
    lanes = q_all.shape[1]
    rows = lanes // GROUP_SIZE
    width = QUERY_HEADS * HEAD_SIZE
    packed = rows + DOC_ROWS
    depth, chunk = p_near.shape[:2]
    vmem = pl.BlockSpec(memory_space=pltpu.VMEM)
    smem = pl.BlockSpec(memory_space=pltpu.SMEM)
    heads = KEY_VALUE_HEADS
    return pl.pallas_call(
        kernel,
        out_shape=(
            jax.ShapeDtypeStruct((heads, HEAD_SIZE, lanes), jnp.bfloat16),
            jax.ShapeDtypeStruct((heads, HEAD_SIZE, lanes), jnp.bfloat16),
            jax.ShapeDtypeStruct((1, chunk, heads * lanes), jnp.bfloat16),
            jax.ShapeDtypeStruct((depth + 1, chunk, heads * lanes), jnp.bfloat16),
            jax.ShapeDtypeStruct((heads, HEAD_SIZE, lanes), jnp.bfloat16),
            jax.ShapeDtypeStruct((heads, HEAD_SIZE, lanes), jnp.bfloat16),
            jax.ShapeDtypeStruct((-(-width // KV_WIDTH), KV_WIDTH), jnp.float32),
            jax.ShapeDtypeStruct((1,), jnp.int32),
        ),
        in_specs=[smem] + [vmem] * (6 + len(far)),
        out_specs=(vmem,) * 7 + (smem,),
        scratch_shapes=[
            pltpu.VMEM((LEVEL, packed, KV_WIDTH), jnp.bfloat16),
            pltpu.VMEM((heads, chunk, lanes), jnp.float32),
            pltpu.VMEM((heads, 8, lanes), jnp.float32),
            pltpu.VMEM((heads, 8, lanes), jnp.float32),
            pltpu.VMEM((heads, 8, lanes), jnp.float32),
            pltpu.VMEM((heads, HEAD_SIZE, lanes), jnp.float32),
            pltpu.VMEM((heads, HEAD_SIZE, lanes), jnp.float32),
        ],
        compiler_params=pltpu.CompilerParams(vmem_limit_bytes=28 * 1024 * 1024),
        cost_estimate=pl.CostEstimate(
            flops=2 * 2 * width * HEAD_SIZE * (depth + 2) * chunk,
            bytes_accessed=8 * rows * width,
            transcendentals=0,
        ),
        name="attention",
    )(rank, q_all, do_all, kv_near, p_near, stats, acc_near, *far)


def level_kernel(
    level, p_at, rank_ref, span_ref, p_buf, ds_buf, q_all, do_t, keep_ref, send_ref
):
    chunk = p_buf.shape[1]
    rows = chunk // PAIR
    lanes = GROUP_SIZE * rows
    inner = rank_ref[0] % LEVEL
    my_core = inner % 2
    my_x = inner // 2
    active = level >= span_ref[0]

    @pl.when(active)
    def _():
        for g in range(KEY_VALUE_HEADS):
            where = slice(g * lanes, (g + 1) * lanes)
            d_key = jnp.dot(
                ds_buf[level, :, where], q_all[g], preferred_element_type=jnp.float32
            ) * SCALE
            d_value = lax.dot_general(
                p_buf[p_at, :, where], do_t[g], NT, preferred_element_type=jnp.float32
            )
            for value, column in ((d_key, g), (d_value, KEY_VALUE_HEADS + g)):
                columns = slice(column * HEAD_SIZE, (column + 1) * HEAD_SIZE)
                for x_at in range(2):
                    one = value[2 * x_at * rows:(2 * x_at + 1) * rows]
                    two = value[(2 * x_at + 1) * rows:(2 * x_at + 2) * rows]
                    place = (x_at + my_x) % 2
                    at = pl.ds(pl.multiple_of(place * rows, rows), rows)
                    keep_ref[at, columns] = jnp.where(my_core == 0, one, two)
                    send_ref[at, columns] = jnp.where(my_core == 0, two, one).astype(jnp.bfloat16)

    @pl.when(jnp.logical_not(active))
    def _():
        keep_ref[...] = jnp.zeros_like(keep_ref)
        send_ref[...] = jnp.zeros_like(send_ref)


def level_gradients(level, p_at, rank, span, p_all, ds_all, q_all, do_t):
    chunk, width = p_all.shape[1:]
    rows = chunk // PAIR
    vmem = pl.BlockSpec(memory_space=pltpu.VMEM)
    smem = pl.BlockSpec(memory_space=pltpu.SMEM)
    return pl.pallas_call(
        functools.partial(level_kernel, level, p_at),
        out_shape=(
            jax.ShapeDtypeStruct((2 * rows, KV_WIDTH), jnp.float32),
            jax.ShapeDtypeStruct((2 * rows, KV_WIDTH), jnp.bfloat16),
        ),
        in_specs=[smem, smem] + [vmem] * 4,
        out_specs=(vmem, vmem),
        compiler_params=pltpu.CompilerParams(vmem_limit_bytes=28 * 1024 * 1024),
        cost_estimate=pl.CostEstimate(
            flops=LEVEL * rows * width * HEAD_SIZE // 4,
            bytes_accessed=LEVEL * rows * width // 4,
            transcendentals=0,
        ),
        name="level_gradients",
    )(rank, span, p_all, ds_all, q_all, do_t)


def shifted(value, steps):
    count = lax.axis_size("ctx")
    first, last = max(0, -steps), min(count, count - steps)
    return lax.ppermute(value, "ctx", [(at, at + steps) for at in range(first, last)])


def rotated(value, steps):
    count = lax.axis_size("ctx")
    return lax.ppermute(value, "ctx", [(at, (at + steps) % count) for at in range(count)])


def swapped(value, bit, axis="ctx"):
    return lax.ppermute(value, axis, [(at, at ^ bit) for at in range(lax.axis_size(axis))])


def bias_rows(rows):
    high = lax.reduce_precision(rows, 8, 7)
    both = jnp.concatenate([high, rows - high]).astype(jnp.bfloat16)
    return jnp.pad(both, ((0, -both.shape[0] % 16), (0, 0)))


def local(query_in, key_in, value_input, output_gradient, doc_ids, query_bias):
    rows = query_in.shape[1]
    shards = lax.axis_size("ctx")
    depth = window_levels(shards)
    rank = lax.axis_index("ctx").astype(jnp.int32)
    own = pack(key_in[0], value_input[0], doc_ids)

    ups = [shifted(own, LEVEL * step) for step in range(1, depth + 1)]
    x_own = swapped(own, 2)
    q_all, do_all, own = prepare(query_in[0], query_bias[None], output_gradient[0], own)
    ups[0], x_own, q_all, do_all = lax.optimization_barrier((ups[0], x_own, q_all, do_all))
    near = [own, x_own]
    for up in ups[:-1]:
        near += [up, swapped(up, 2)]
    x_far = swapped(ups[-1], 2)
    far_up, near = lax.optimization_barrier((ups[-1], near))
    near = jnp.concatenate(near, axis=0)
    near_core = swapped(near, 1)
    core_far = swapped(far_up, 1)
    rank = rank.reshape(1)
    kv_near, p_near, stats, acc_near = near_attention(rank, q_all, near, near_core, depth)
    x_far, p_near = lax.optimization_barrier((x_far, p_near))
    far = [far_up, x_far, core_far, swapped(x_far, 1)]
    att_t, dq_t, p_far, ds_all, do_near, do_far, bias_part, span = attention(
        rank, q_all, do_all, kv_near, p_near, stats, acc_near, far
    )

    levels = shards // LEVEL
    carried = levels == 4 and depth == 2
    bit = 1
    while bit < lax.axis_size("dp"):
        bias_part = bias_part + swapped(bias_part, bit, "dp")
        bit *= 2
    bias_total = bias_part

    def joined(value):
        return jnp.concatenate([value, bias_rows(bias_total)], axis=0) if carried else value

    def bias_of(got):
        return got[rows:rows + half_rows].astype(jnp.float32) + got[
            rows + half_rows:rows + 2 * half_rows
        ].astype(jnp.float32)

    half_rows = bias_part.shape[0]
    sends = [None] * (depth + 1)
    keeps = [None] * (depth + 1)
    for step in range(depth, -1, -1):
        if step == depth:
            keep, send = level_gradients(0, 0, rank, span, p_far, ds_all, q_all, do_far)
        else:
            level = depth - step
            keep, send = level_gradients(
                level, level - 1, rank, span, p_near, ds_all, q_all, do_near
            )
        send, ds_all = lax.optimization_barrier((send, ds_all))
        if step == max(depth - 1, 0) and carried:
            got = swapped(jnp.concatenate([send, bias_rows(bias_total)], axis=0), 1)
            bias_total = bias_total + bias_of(got[rows:])
            got = got[:2 * rows]
        else:
            got = swapped(send, 1)
        keeps[step] = keep + got.astype(jnp.float32)
        sends[step] = send

    across = [None] * (depth + 1)
    for step in range(depth, -1, -1):
        away = keeps[step][rows:].astype(jnp.bfloat16)
        if step == depth:
            away, att_t = lax.optimization_barrier((away, att_t))
            away = joined(away)
        across[step] = swapped(away, 2)
    attended, grad_query = row_results(att_t, dq_t)
    down = [None] * (depth + 1)
    total = None
    for step in range(depth, -1, -1):
        if step == depth and carried:
            bias_total = bias_total + bias_of(across[step])
        total = keeps[step][:rows] + across[step][:rows].astype(jnp.float32)
        if step:
            sent = joined(total.astype(jnp.bfloat16))
            down[step] = (rotated if carried else shifted)(sent, -LEVEL * step)
            across[step - 1], _ = lax.optimization_barrier((across[step - 1], sent))
    if carried:
        bias_total = (
            bias_total + rotated(bias_total, LEVEL) + bias_of(down[1]) + bias_of(down[2])
        )
    else:
        bit = 1
        while bit < shards:
            bias_total = bias_total + swapped(bias_total, bit)
            bit *= 2
    bias_total = bias_total.reshape(-1)[:query_bias.shape[0]]
    down = [None if part is None else part[:rows] for part in down]
    for step in range(depth, 0, -1):
        total = total + down[step].astype(jnp.float32)
    total = total.astype(jnp.bfloat16)
    half = KEY_VALUE_HEADS * HEAD_SIZE
    return (
        attended[None],
        grad_query[None],
        total[:, :half][None],
        total[:, half:][None],
        bias_total,
    )


def solution(mesh):
    placed = (
        P("dp", "ctx", None),
        P("dp", "ctx", None),
        P("dp", "ctx", None),
        P("dp", "ctx", None),
        P("dp", "ctx"),
        P(),
    )
    return jax.shard_map(
        local,
        mesh=mesh,
        in_specs=placed,
        out_specs=(
            P("dp", "ctx", None),
            P("dp", "ctx", None),
            P("dp", "ctx", None),
            P("dp", "ctx", None),
            P(),
        ),
        check_vma=False,
    )
```

```python
import functools
import math

import jax
import jax.numpy as jnp
from jax import lax
from jax.experimental import pallas as pl
from jax.experimental.pallas import tpu as pltpu
from jax.sharding import PartitionSpec as P

QUERY_HEADS = 14
KEY_VALUE_HEADS = 2
HEAD_SIZE = 128
GROUP_SIZE = 7
BLK = 128
WB = 16
DOC_ROWS = 16
PAIR = 4
LEVEL = 4
LANE_TILE = 896
KV_WIDTH = 2 * KEY_VALUE_HEADS * HEAD_SIZE
SCALE = 1.0 / math.sqrt(HEAD_SIZE)
SCALE_LOG2 = SCALE * math.log2(math.e)
LOW = -1e30

NT = (((1,), (1,)), ((), ()))


def fold(value, op):
    keys, lanes = value.shape
    return op(value.reshape(keys // 8, 8, lanes), axis=0)


def window_levels(shards):
    levels = max(shards // LEVEL, 1)
    return min((WB - 2 + LEVEL) // LEVEL, max(3 * levels // 4 - 1, 0) if levels % 4 == 0 else levels - 1)


def pack_kernel(key_hbm, value_hbm, docs_hbm, own_ref, docs, sems):
    rows, half = key_hbm.shape
    copies = [
        pltpu.make_async_copy(docs_hbm, docs, sems.at[0]),
        pltpu.make_async_copy(key_hbm, own_ref.at[0:rows, 0:half], sems.at[1]),
        pltpu.make_async_copy(value_hbm, own_ref.at[0:rows, half:2 * half], sems.at[2]),
    ]
    for copy in copies:
        copy.start()
    copies[0].wait()
    count = jnp.sum((docs[...] == 0).astype(jnp.float32), axis=1, keepdims=True)
    own_ref[rows:rows + DOC_ROWS, :] = jnp.broadcast_to(count, (DOC_ROWS, 2 * half)).astype(
        jnp.bfloat16
    )
    copies[1].wait()
    copies[2].wait()


def pack(key_in, value_input, doc_ids):
    rows, half = key_in.shape
    return pl.pallas_call(
        pack_kernel,
        out_shape=jax.ShapeDtypeStruct((rows + DOC_ROWS, 2 * half), jnp.bfloat16),
        in_specs=[pl.BlockSpec(memory_space=pltpu.HBM)] * 3,
        out_specs=pl.BlockSpec(memory_space=pltpu.VMEM),
        scratch_shapes=[pltpu.VMEM((1, rows), jnp.int32), pltpu.SemaphoreType.DMA((3,))],
        compiler_params=pltpu.CompilerParams(vmem_limit_bytes=60 * 1024 * 1024),
        name="pack",
    )(key_in, value_input, doc_ids)


def head_columns(g, n):
    head = g * GROUP_SIZE + n
    return slice(head * HEAD_SIZE, (head + 1) * HEAD_SIZE)


def prepare_kernel(q_hbm, bias_ref, do_hbm, own_hbm, q_st, do_t, own_ref, q_buf, do_buf, sems):
    rows = q_buf.shape[0]
    first = pltpu.make_async_copy(q_hbm, q_buf, sems.at[0])
    second = pltpu.make_async_copy(do_hbm, do_buf, sems.at[1])
    third = pltpu.make_async_copy(own_hbm, own_ref, sems.at[2])
    first.start()
    second.start()
    third.start()
    first.wait()
    for g in range(KEY_VALUE_HEADS):
        for n in range(GROUP_SIZE):
            columns = head_columns(g, n)
            q_st[g, n * rows:(n + 1) * rows, :] = (
                q_buf[:, columns].astype(jnp.float32) + bias_ref[:, columns]
            ).astype(jnp.bfloat16)
    second.wait()
    for g in range(KEY_VALUE_HEADS):
        for n in range(GROUP_SIZE):
            do_t[g, :, n * rows:(n + 1) * rows] = do_buf[:, head_columns(g, n)].T
    third.wait()


def prepare(query_in, query_bias, output_gradient, own):
    rows, width = query_in.shape
    lanes = GROUP_SIZE * rows
    anywhere = pl.BlockSpec(memory_space=pltpu.HBM)
    vmem = pl.BlockSpec(memory_space=pltpu.VMEM)
    return pl.pallas_call(
        prepare_kernel,
        out_shape=(
            jax.ShapeDtypeStruct((KEY_VALUE_HEADS, lanes, HEAD_SIZE), jnp.bfloat16),
            jax.ShapeDtypeStruct((KEY_VALUE_HEADS, HEAD_SIZE, lanes), jnp.bfloat16),
            jax.ShapeDtypeStruct(own.shape, own.dtype),
        ),
        in_specs=[anywhere, vmem, anywhere, anywhere],
        out_specs=(vmem, vmem, vmem),
        scratch_shapes=[
            pltpu.VMEM((rows, width), jnp.bfloat16),
            pltpu.VMEM((rows, width), jnp.bfloat16),
            pltpu.SemaphoreType.DMA((3,)),
        ],
        compiler_params=pltpu.CompilerParams(vmem_limit_bytes=8 * 1024 * 1024),
        cost_estimate=pl.CostEstimate(
            flops=4 * rows * width, bytes_accessed=8 * rows * width, transcendentals=0
        ),
        name="prepare",
    )(query_in, query_bias, output_gradient, own)


def keys_of(kv_buf, c, rows, column):
    columns = slice(column * HEAD_SIZE, (column + 1) * HEAD_SIZE)
    return jnp.concatenate([kv_buf[PAIR * c + i, 0:rows, columns] for i in range(PAIR)], axis=0)


def spread(kv_buf, slot, pieces, inner):
    core = inner % 2
    x = inner // 2
    for at, piece in enumerate(pieces):
        place_x = 1 - x if at % 2 else x
        place_core = 1 - core if at // 2 else core
        kv_buf[slot * LEVEL + 2 * place_x + place_core] = piece[...]


def doc_count(kv_buf, rows):
    counts = kv_buf[:, rows:rows + DOC_ROWS, 0:128].astype(jnp.float32)
    return jnp.sum(counts) * (1.0 / (DOC_ROWS * 128))


def window_start(rank, rows, first, count):
    boundary = (count + 0.5).astype(jnp.int32) + jnp.maximum(first, 0) * rows
    low_block = jnp.maximum(rank - (WB - 1), 0)
    in_second = rank * rows >= boundary
    return boundary, jnp.where(in_second, jnp.maximum(low_block, boundary // rows), low_block)


def mask_bias(key_first, q_first, boundary, chunk, rows):
    key_pos = key_first + lax.broadcasted_iota(jnp.int32, (chunk, rows), 0)
    query_pos = q_first + lax.broadcasted_iota(jnp.int32, (chunk, rows), 1)
    allowed = (key_pos <= query_pos) & (query_pos // BLK - key_pos // BLK < WB)
    allowed = allowed & ((key_pos >= boundary) == (query_pos >= boundary))
    return jnp.where(allowed, 0.0, LOW)


def lane_tiles(lanes):
    return [(at, min(at + LANE_TILE, lanes)) for at in range(0, lanes, LANE_TILE)]


def near_kernel(
    rank_ref, q_all, near_ref, near_core_ref,
    kv_buf, p_buf, stats_ref, acc,
    s_buf,
):
    packed = kv_buf.shape[1]
    depth, chunk = p_buf.shape[:2]
    rows = chunk // PAIR
    lanes = q_all.shape[1]
    tiles = lane_tiles(lanes)
    rank = rank_ref[0]
    first = (rank // LEVEL - (depth - 1)) * LEVEL
    for level in range(depth):
        pieces = [
            ref.at[at * packed:(at + 1) * packed]
            for ref in (near_ref, near_core_ref) for at in (2 * level, 2 * level + 1)
        ]
        spread(kv_buf, depth - 1 - level, pieces, rank % LEVEL)
    boundary, low_block = window_start(rank, rows, first, doc_count(kv_buf, rows))
    low = jnp.maximum(low_block - first, 0) // PAIR

    for g in range(KEY_VALUE_HEADS):
        stats_ref[g, 0:8, :] = jnp.full((8, lanes), LOW, jnp.float32)
        stats_ref[g, 8:16, :] = jnp.zeros((8, lanes), jnp.float32)
    acc[...] = jnp.zeros_like(acc)

    def score_steps(c, g):
        bias = mask_bias((first + PAIR * c) * rows, rank * rows, boundary, chunk, rows)
        k_c = keys_of(kv_buf, c, rows, g)

        def step(a, b):
            s = lax.dot_general(k_c, q_all[g, a:b, :], NT, preferred_element_type=jnp.float32)
            s = s + jnp.concatenate([bias] * ((b - a) // rows), axis=1)
            s_buf[c, :, a:b] = s
            stats_ref[g, 0:8, a:b] = jnp.maximum(stats_ref[g, 0:8, a:b], fold(s, jnp.max))

        return step

    def weight_steps(c, g, row_max):
        v_t = keys_of(kv_buf, c, rows, KEY_VALUE_HEADS + g).T

        def step(a, b):
            p = jnp.exp2(s_buf[c, :, a:b] * SCALE_LOG2 - row_max[:, a:b])
            stats_ref[g, 8:16, a:b] += fold(p, jnp.sum)
            p_bf = p.astype(jnp.bfloat16)
            p_buf[c, :, g * lanes + a:g * lanes + b] = p_bf
            acc[g, :, a:b] += jnp.dot(v_t, p_bf, preferred_element_type=jnp.float32)

        return step

    def over_chunks(*makers):
        @pl.loop(low, depth)
        def _(c):
            steps = [make(c) for make in makers]
            for a, b in tiles:
                for step in steps:
                    step(a, b)

    over_chunks(lambda c: score_steps(c, 0))
    for g in range(KEY_VALUE_HEADS):
        row_max = jnp.max(stats_ref[g, 0:8, :], axis=0, keepdims=True) * SCALE_LOG2
        makers = [lambda c: weight_steps(c, g, row_max)]
        if g + 1 < KEY_VALUE_HEADS:
            makers.append(lambda c: score_steps(c, g + 1))
        over_chunks(*makers)
        stats_ref[g, 0:1, :] = row_max
        stats_ref[g, 8:9, :] = jnp.sum(stats_ref[g, 8:16, :], axis=0, keepdims=True)


def near_attention(rank, q_all, near, near_core, depth):
    lanes = q_all.shape[1]
    rows = lanes // GROUP_SIZE
    packed = rows + DOC_ROWS
    chunk = PAIR * rows
    vmem = pl.BlockSpec(memory_space=pltpu.VMEM)
    smem = pl.BlockSpec(memory_space=pltpu.SMEM)
    heads = KEY_VALUE_HEADS
    return pl.pallas_call(
        near_kernel,
        out_shape=(
            jax.ShapeDtypeStruct((depth * LEVEL, packed, KV_WIDTH), jnp.bfloat16),
            jax.ShapeDtypeStruct((depth, chunk, heads * lanes), jnp.bfloat16),
            jax.ShapeDtypeStruct((heads, 16, lanes), jnp.float32),
            jax.ShapeDtypeStruct((heads, HEAD_SIZE, lanes), jnp.float32),
        ),
        in_specs=[smem] + [vmem] * 3,
        out_specs=(vmem,) * 4,
        scratch_shapes=[pltpu.VMEM((depth, chunk, lanes), jnp.float32)],
        compiler_params=pltpu.CompilerParams(vmem_limit_bytes=28 * 1024 * 1024),
        cost_estimate=pl.CostEstimate(
            flops=2 * 2 * heads * lanes * HEAD_SIZE * depth * chunk,
            bytes_accessed=4 * heads * lanes * HEAD_SIZE,
            transcendentals=heads * lanes * depth * chunk,
        ),
        name="near_attention",
    )(rank, q_all, near, near_core)


def kernel(
    rank_ref, q_all, do_all, kv_near, p_near, stats_ref, acc_near, far_0, far_1, far_2, far_3,
    att_t, dq_t, p_far, ds_buf, do_near, do_far, gb_ref, span_ref,
    kv_far, s_buf, sum_buf, factor_buf, dot_buf, acc, dq_acc,
):
    depth, chunk = p_near.shape[:2]
    rows = chunk // PAIR
    lanes = GROUP_SIZE * rows
    tiles = lane_tiles(lanes)
    rank = rank_ref[0]
    first = (rank // LEVEL - depth) * LEVEL
    spread(kv_far, 0, (far_0, far_1, far_2, far_3), rank % LEVEL)
    count = doc_count(kv_far, rows) + doc_count(kv_near, rows)
    boundary, low_block = window_start(rank, rows, first, count)
    low = jnp.maximum(low_block - first, 0) // PAIR
    span_ref[0] = low
    with_far = low == 0

    dq_acc[...] = jnp.zeros_like(dq_acc)

    @pl.when(with_far)
    def _():
        bias = mask_bias(first * rows, rank * rows, boundary, chunk, rows)

        def score(g, a, b):
            k_c = keys_of(kv_far, 0, rows, g)
            s = lax.dot_general(k_c, q_all[g, a:b, :], NT, preferred_element_type=jnp.float32)
            s = s + jnp.concatenate([bias] * ((b - a) // rows), axis=1)
            s_buf[g, :, a:b] = s
            far_max = jnp.max(fold(s, jnp.max), axis=0, keepdims=True) * SCALE_LOG2
            factor_buf[g, 0:1, a:b] = jnp.maximum(stats_ref[g, 0:1, a:b], far_max)

        def weight(g, a, b):
            v_t = keys_of(kv_far, 0, rows, KEY_VALUE_HEADS + g).T
            top = factor_buf[g, 0:1, a:b]
            factor = jnp.exp2(stats_ref[g, 0:1, a:b] - top)
            p = jnp.exp2(s_buf[g, :, a:b] * SCALE_LOG2 - top)
            p_bf = p.astype(jnp.bfloat16)
            p_far[0, :, g * lanes + a:g * lanes + b] = p_bf
            total = jnp.sum(fold(p, jnp.sum), axis=0, keepdims=True)
            sum_buf[g, 0:1, a:b] = stats_ref[g, 8:9, a:b] * factor + total
            factor_buf[g, 0:1, a:b] = factor
            acc[g, :, a:b] = acc_near[g, :, a:b] * factor + jnp.dot(
                v_t, p_bf, preferred_element_type=jnp.float32
            )

        for a, b in tiles:
            score(0, a, b)
        for g in range(KEY_VALUE_HEADS):
            for a, b in tiles:
                weight(g, a, b)
                if g + 1 < KEY_VALUE_HEADS:
                    score(g + 1, a, b)

    @pl.when(jnp.logical_not(with_far))
    def _():
        sum_buf[:, 0:1, :] = stats_ref[:, 8:9, :]
        factor_buf[:, 0:1, :] = jnp.ones((KEY_VALUE_HEADS, 1, lanes), jnp.float32)
        acc[...] = acc_near[...]

    for g in range(KEY_VALUE_HEADS):
        inverse = 1.0 / sum_buf[g, 0:1, :]
        factor = factor_buf[g, 0:1, :]
        for n in range(GROUP_SIZE):
            at = slice(n * rows, (n + 1) * rows)
            att = (acc[g, :, at] * inverse[:, at]).astype(jnp.bfloat16)
            att_t[g, :, at] = att
            do_n = do_all[g, :, at].astype(jnp.float32)
            dot_n = jnp.sum(do_n * att.astype(jnp.float32), axis=0, keepdims=True) * inverse[:, at]
            do_n = do_n * inverse[:, at]
            dot_buf[g, 0:1, at] = dot_n
            dot_buf[g, 1:2, at] = dot_n * factor[:, at]
            do_far[g, :, at] = do_n.astype(jnp.bfloat16)
            do_near[g, :, at] = (do_n * factor[:, at]).astype(jnp.bfloat16)

    def gradient_steps(g, c, kv_buf, at, p_buf, do_t, row):
        v_c = keys_of(kv_buf, at, rows, KEY_VALUE_HEADS + g)
        k_t = keys_of(kv_buf, at, rows, g).T

        def step(a, b):
            where = slice(g * lanes + a, g * lanes + b)
            d_p = jnp.dot(v_c, do_t[g, :, a:b], preferred_element_type=jnp.float32)
            p = p_buf[at, :, where].astype(jnp.float32)
            d_s = (p * (d_p - dot_buf[g, row:row + 1, a:b])).astype(jnp.bfloat16)
            ds_buf[c, :, where] = d_s
            dq_acc[g, :, a:b] += jnp.dot(k_t, d_s, preferred_element_type=jnp.float32)

        return step

    def gradients(c, kv_buf, at, p_buf, do_t, row):
        steps = [
            gradient_steps(g, c, kv_buf, at, p_buf, do_t, row) for g in range(KEY_VALUE_HEADS)
        ]
        for a, b in tiles:
            for step in steps:
                step(a, b)

    @pl.when(with_far)
    def _():
        gradients(0, kv_far, 0, p_far, do_far, 0)

    @pl.loop(jnp.maximum(low, 1), depth + 1)
    def _(c):
        gradients(c, kv_near, c - 1, p_near, do_near, 1)

    gb_ref[...] = jnp.zeros_like(gb_ref)
    ones = jnp.ones((8, rows), jnp.bfloat16)
    for g in range(KEY_VALUE_HEADS):
        for n in range(GROUP_SIZE):
            columns = slice(n * rows, (n + 1) * rows)
            d_q = (dq_acc[g, :, columns] * SCALE).astype(jnp.bfloat16)
            dq_t[g, :, columns] = d_q
            row, at = divmod(head_columns(g, n).start, KV_WIDTH)
            sums = lax.dot_general(ones, d_q, NT, preferred_element_type=jnp.float32)
            gb_ref[row:row + 1, at:at + HEAD_SIZE] = sums[0:1]


def rows_kernel(att_t, dq_t, att_ref, dq_ref):
    rows = att_ref.shape[0]
    for g in range(KEY_VALUE_HEADS):
        for n in range(GROUP_SIZE):
            at = slice(n * rows, (n + 1) * rows)
            att_ref[:, head_columns(g, n)] = att_t[g, :, at].T
            dq_ref[:, head_columns(g, n)] = dq_t[g, :, at].T


def row_results(att_t, dq_t):
    rows = att_t.shape[2] // GROUP_SIZE
    width = QUERY_HEADS * HEAD_SIZE
    vmem = pl.BlockSpec(memory_space=pltpu.VMEM)
    return pl.pallas_call(
        rows_kernel,
        out_shape=(jax.ShapeDtypeStruct((rows, width), jnp.bfloat16),) * 2,
        in_specs=[vmem] * 2,
        out_specs=(vmem,) * 2,
        compiler_params=pltpu.CompilerParams(vmem_limit_bytes=8 * 1024 * 1024),
        cost_estimate=pl.CostEstimate(
            flops=2 * rows * width, bytes_accessed=8 * rows * width, transcendentals=0
        ),
        name="row_results",
    )(att_t, dq_t)


def attention(rank, q_all, do_all, kv_near, p_near, stats, acc_near, far):
    lanes = q_all.shape[1]
    rows = lanes // GROUP_SIZE
    width = QUERY_HEADS * HEAD_SIZE
    packed = rows + DOC_ROWS
    depth, chunk = p_near.shape[:2]
    vmem = pl.BlockSpec(memory_space=pltpu.VMEM)
    smem = pl.BlockSpec(memory_space=pltpu.SMEM)
    heads = KEY_VALUE_HEADS
    return pl.pallas_call(
        kernel,
        out_shape=(
            jax.ShapeDtypeStruct((heads, HEAD_SIZE, lanes), jnp.bfloat16),
            jax.ShapeDtypeStruct((heads, HEAD_SIZE, lanes), jnp.bfloat16),
            jax.ShapeDtypeStruct((1, chunk, heads * lanes), jnp.bfloat16),
            jax.ShapeDtypeStruct((depth + 1, chunk, heads * lanes), jnp.bfloat16),
            jax.ShapeDtypeStruct((heads, HEAD_SIZE, lanes), jnp.bfloat16),
            jax.ShapeDtypeStruct((heads, HEAD_SIZE, lanes), jnp.bfloat16),
            jax.ShapeDtypeStruct((-(-width // KV_WIDTH), KV_WIDTH), jnp.float32),
            jax.ShapeDtypeStruct((1,), jnp.int32),
        ),
        in_specs=[smem] + [vmem] * (6 + len(far)),
        out_specs=(vmem,) * 7 + (smem,),
        scratch_shapes=[
            pltpu.VMEM((LEVEL, packed, KV_WIDTH), jnp.bfloat16),
            pltpu.VMEM((heads, chunk, lanes), jnp.float32),
            pltpu.VMEM((heads, 8, lanes), jnp.float32),
            pltpu.VMEM((heads, 8, lanes), jnp.float32),
            pltpu.VMEM((heads, 8, lanes), jnp.float32),
            pltpu.VMEM((heads, HEAD_SIZE, lanes), jnp.float32),
            pltpu.VMEM((heads, HEAD_SIZE, lanes), jnp.float32),
        ],
        compiler_params=pltpu.CompilerParams(vmem_limit_bytes=28 * 1024 * 1024),
        cost_estimate=pl.CostEstimate(
            flops=2 * 2 * width * HEAD_SIZE * (depth + 2) * chunk,
            bytes_accessed=8 * rows * width,
            transcendentals=0,
        ),
        name="attention",
    )(rank, q_all, do_all, kv_near, p_near, stats, acc_near, *far)


def level_kernel(
    level, p_at, rank_ref, span_ref, p_buf, ds_buf, q_all, do_t, keep_ref, send_ref
):
    chunk = p_buf.shape[1]
    rows = chunk // PAIR
    lanes = GROUP_SIZE * rows
    inner = rank_ref[0] % LEVEL
    my_core = inner % 2
    my_x = inner // 2
    active = level >= span_ref[0]

    @pl.when(active)
    def _():
        for g in range(KEY_VALUE_HEADS):
            where = slice(g * lanes, (g + 1) * lanes)
            d_key = jnp.dot(
                ds_buf[level, :, where], q_all[g], preferred_element_type=jnp.float32
            ) * SCALE
            d_value = lax.dot_general(
                p_buf[p_at, :, where], do_t[g], NT, preferred_element_type=jnp.float32
            )
            for value, column in ((d_key, g), (d_value, KEY_VALUE_HEADS + g)):
                columns = slice(column * HEAD_SIZE, (column + 1) * HEAD_SIZE)
                for x_at in range(2):
                    one = value[2 * x_at * rows:(2 * x_at + 1) * rows]
                    two = value[(2 * x_at + 1) * rows:(2 * x_at + 2) * rows]
                    place = (x_at + my_x) % 2
                    at = pl.ds(pl.multiple_of(place * rows, rows), rows)
                    keep_ref[at, columns] = jnp.where(my_core == 0, one, two)
                    send_ref[at, columns] = jnp.where(my_core == 0, two, one).astype(jnp.bfloat16)

    @pl.when(jnp.logical_not(active))
    def _():
        keep_ref[...] = jnp.zeros_like(keep_ref)
        send_ref[...] = jnp.zeros_like(send_ref)


def level_gradients(level, p_at, rank, span, p_all, ds_all, q_all, do_t):
    chunk, width = p_all.shape[1:]
    rows = chunk // PAIR
    vmem = pl.BlockSpec(memory_space=pltpu.VMEM)
    smem = pl.BlockSpec(memory_space=pltpu.SMEM)
    return pl.pallas_call(
        functools.partial(level_kernel, level, p_at),
        out_shape=(
            jax.ShapeDtypeStruct((2 * rows, KV_WIDTH), jnp.float32),
            jax.ShapeDtypeStruct((2 * rows, KV_WIDTH), jnp.bfloat16),
        ),
        in_specs=[smem, smem] + [vmem] * 4,
        out_specs=(vmem, vmem),
        compiler_params=pltpu.CompilerParams(vmem_limit_bytes=28 * 1024 * 1024),
        cost_estimate=pl.CostEstimate(
            flops=LEVEL * rows * width * HEAD_SIZE // 4,
            bytes_accessed=LEVEL * rows * width // 4,
            transcendentals=0,
        ),
        name="level_gradients",
    )(rank, span, p_all, ds_all, q_all, do_t)


def shifted(value, steps):
    count = lax.axis_size("ctx")
    first, last = max(0, -steps), min(count, count - steps)
    return lax.ppermute(value, "ctx", [(at, at + steps) for at in range(first, last)])


def rotated(value, steps):
    count = lax.axis_size("ctx")
    return lax.ppermute(value, "ctx", [(at, (at + steps) % count) for at in range(count)])


def swapped(value, bit, axis="ctx"):
    return lax.ppermute(value, axis, [(at, at ^ bit) for at in range(lax.axis_size(axis))])


def bias_rows(rows):
    high = lax.reduce_precision(rows, 8, 7)
    both = jnp.concatenate([high, rows - high]).astype(jnp.bfloat16)
    return jnp.pad(both, ((0, -both.shape[0] % 16), (0, 0)))


def local(query_in, key_in, value_input, output_gradient, doc_ids, query_bias):
    rows = query_in.shape[1]
    shards = lax.axis_size("ctx")
    depth = window_levels(shards)
    rank = lax.axis_index("ctx").astype(jnp.int32)
    own = pack(key_in[0], value_input[0], doc_ids)

    ups = [shifted(own, LEVEL * step) for step in range(1, depth + 1)]
    x_own = swapped(own, 2)
    q_all, do_all, own = prepare(query_in[0], query_bias[None], output_gradient[0], own)
    ups[0], x_own, q_all, do_all = lax.optimization_barrier((ups[0], x_own, q_all, do_all))
    near = [own, x_own]
    for up in ups[:-1]:
        near += [up, swapped(up, 2)]
    x_far = swapped(ups[-1], 2)
    far_up, near = lax.optimization_barrier((ups[-1], near))
    near = jnp.concatenate(near, axis=0)
    near_core = swapped(near, 1)
    core_far = swapped(far_up, 1)
    rank = rank.reshape(1)
    kv_near, p_near, stats, acc_near = near_attention(rank, q_all, near, near_core, depth)
    x_far, p_near = lax.optimization_barrier((x_far, p_near))
    far = [far_up, x_far, core_far, swapped(x_far, 1)]
    att_t, dq_t, p_far, ds_all, do_near, do_far, bias_part, span = attention(
        rank, q_all, do_all, kv_near, p_near, stats, acc_near, far
    )

    levels = shards // LEVEL
    carried = levels == 4 and depth == 2
    bit = 1
    while bit < lax.axis_size("dp"):
        bias_part = bias_part + swapped(bias_part, bit, "dp")
        bit *= 2
    bias_total = bias_part

    def joined(value):
        return jnp.concatenate([value, bias_rows(bias_total)], axis=0) if carried else value

    def bias_of(got):
        return got[rows:rows + half_rows].astype(jnp.float32) + got[
            rows + half_rows:rows + 2 * half_rows
        ].astype(jnp.float32)

    half_rows = bias_part.shape[0]
    sends = [None] * (depth + 1)
    keeps = [None] * (depth + 1)
    for step in range(depth, -1, -1):
        if step == depth:
            keep, send = level_gradients(0, 0, rank, span, p_far, ds_all, q_all, do_far)
        else:
            level = depth - step
            keep, send = level_gradients(
                level, level - 1, rank, span, p_near, ds_all, q_all, do_near
            )
        send, ds_all = lax.optimization_barrier((send, ds_all))
        if step == max(depth - 1, 0) and carried:
            got = swapped(jnp.concatenate([send, bias_rows(bias_total)], axis=0), 1)
            bias_total = bias_total + bias_of(got[rows:])
            got = got[:2 * rows]
        else:
            got = swapped(send, 1)
        keeps[step] = keep + got.astype(jnp.float32)
        sends[step] = send

    across = [None] * (depth + 1)
    for step in range(depth, -1, -1):
        away = keeps[step][rows:].astype(jnp.bfloat16)
        if step == depth:
            away, att_t = lax.optimization_barrier((away, att_t))
            away = joined(away)
        across[step] = swapped(away, 2)
    attended, grad_query = row_results(att_t, dq_t)
    down = [None] * (depth + 1)
    total = None
    for step in range(depth, -1, -1):
        if step == depth and carried:
            bias_total = bias_total + bias_of(across[step])
        total = keeps[step][:rows] + across[step][:rows].astype(jnp.float32)
        if step:
            sent = joined(total.astype(jnp.bfloat16))
            down[step] = (rotated if carried else shifted)(sent, -LEVEL * step)
            across[step - 1], _ = lax.optimization_barrier((across[step - 1], sent))
    if carried:
        bias_total = (
            bias_total + rotated(bias_total, LEVEL) + bias_of(down[1]) + bias_of(down[2])
        )
    else:
        bit = 1
        while bit < shards:
            bias_total = bias_total + swapped(bias_total, bit)
            bit *= 2
    bias_total = bias_total.reshape(-1)[:query_bias.shape[0]]
    down = [None if part is None else part[:rows] for part in down]
    for step in range(depth, 0, -1):
        total = total + down[step].astype(jnp.float32)
    total = total.astype(jnp.bfloat16)
    half = KEY_VALUE_HEADS * HEAD_SIZE
    return (
        attended[None],
        grad_query[None],
        total[:, :half][None],
        total[:, half:][None],
        bias_total,
    )


def solution(mesh):
    placed = (
        P("dp", "ctx", None),
        P("dp", "ctx", None),
        P("dp", "ctx", None),
        P("dp", "ctx", None),
        P("dp", "ctx"),
        P(),
    )
    return jax.shard_map(
        local,
        mesh=mesh,
        in_specs=placed,
        out_specs=(
            P("dp", "ctx", None),
            P("dp", "ctx", None),
            P("dp", "ctx", None),
            P("dp", "ctx", None),
            P(),
        ),
        check_vma=False,
    )
```
